32 devices in a mesh: sample: 4 (over y, x), gz: 8 (over z, core).
Axes of the slice: x: 2, y: 2, z: 4, core: 2. Of those that a mesh axis runs over, the one named last changes fastest.
Arguments:
- cubes: bfloat16 [8, 32, 32, 1024], P('sample', 'gz'), may hold values from -6 to 6
- weight_a: bfloat16 [27, 2048], replicated, may hold values from -0.21875 to 0.21875
- weight_b: bfloat16 [27, 8192], replicated, may hold values from -0.15625 to 0.15625
- cotangent: bfloat16 [8, 8, 8, 1024], P('sample', 'gz'), may hold values from -6 to 6
Outputs:
- input_grad: bfloat16 [8, 32, 32, 1024], P('sample', 'gz')
- weight_grad_a: float32 [27, 2048], replicated
- weight_grad_b: float32 [27, 8192], replicated
The draws below stay inside these ranges and needn't reach their ends.
All inputs are finite; a program needn't handle non-finite values.
Results may differ from the reference program's by a relative error of at most 0.012.
Values may be sent and summed in bfloat16 or wider, within the bound.
No kernel may reach another device: no remote copies, remote signals or barrier semaphores. Data moves between devices by JAX's collectives and lax.ppermute only.
A program may use at most 192 MiB of HBM per device.

```python
import jax
import jax.numpy as jnp
from jax import lax

C1 = 32
C2 = 64
C3 = 128
SIDE = 32
BATCH = 8
ZTOT = 32


def shard_levels(stream_key, shape, split, least, top_value):
    gain, own = 1.0, jax.random.fold_in(stream_key, 6)
    for dim, shards_of in split:
        draws = jnp.exp(jax.random.uniform(jax.random.fold_in(own, dim), (shards_of,), jnp.float32, least / len(split), top_value / len(split)))
        gain = gain * jnp.repeat(draws, shape[dim] // shards_of).reshape([-1 if axis == dim else 1 for axis in range(len(shape))])
    return gain


def scatter_about(own_key, shape, scale, most, split=(), kind=jnp.bfloat16):
    factor_of = shard_levels(own_key, shape, split, -0.22, 0.18) if split else 1.0
    drawn = jax.random.normal(own_key, shape, jnp.float32) * scale * factor_of
    return jnp.minimum(jnp.maximum(drawn, -most), most).astype(kind)


def setup_inputs(seed: int = 0) -> dict:
    splits = jax.random.split(jax.random.key(seed), 5)
    cubes = scatter_about(splits[0], (BATCH, ZTOT, SIDE, SIDE * C1), 1.0, 6.0, ((0, 4), (1, 8)))
    weight_a = scatter_about(splits[1], (27, C1 * C2), (27 * C1) ** -0.5, 0.21875)
    weight_b = scatter_about(splits[2], (27, C2 * C3), (27 * C2) ** -0.5, 0.15625)
    cotangent = scatter_about(splits[3], (BATCH, ZTOT // 4, SIDE // 4, SIDE // 4 * C3), 1.0, 6.0, ((0, 4), (1, 8)))
    return {"cubes": cubes, "weight_a": weight_a, "weight_b": weight_b, "cotangent": cotangent}


def activate(values):
    return values * jax.nn.sigmoid(values)


def slope(values):
    squash = jax.nn.sigmoid(values)
    return squash + values * squash * (1.0 - squash)


def rounded(values):
    return lax.optimization_barrier(values.astype(jnp.bfloat16)).astype(jnp.float32)


def correlate(volume, kernel):
    return lax.conv_general_dilated(volume[None], kernel, (1, 1, 1), ((1, 1), (1, 1), (1, 1)),
                                    dimension_numbers=("NDHWC", "DHWIO", "NDHWC"),
                                    precision=lax.Precision.HIGHEST)[0]


def shrink(values):
    planes, extent_y, extent_x, channels = values.shape
    return values.reshape(planes // 2, 2, extent_y // 2, 2, extent_x // 2, 2, channels).mean(axis=(1, 3, 5))


def spread(values):
    planes, extent_y, extent_x, channels = values.shape
    widened = jnp.broadcast_to(values[:, None, :, None, :, None, :], (planes, 2, extent_y, 2, extent_x, 2, channels))
    return widened.reshape(planes * 2, extent_y * 2, extent_x * 2, channels) * 0.125


def kernel_terms(volume, gradient):
    planes, extent_y, extent_x, channels = volume.shape
    padded = jnp.pad(volume, ((1, 1), (1, 1), (1, 1), (0, 0)))
    flat_grad = gradient.reshape(-1, gradient.shape[-1])
    partials = []
    for offset in range(27):
        shift_z, shift_y, shift_x = offset // 9, (offset // 3) % 3, offset % 3
        window = padded[shift_z:shift_z + planes, shift_y:shift_y + extent_y, shift_x:shift_x + extent_x]
        partials.append(lax.dot_general(window.reshape(-1, channels), flat_grad, (((0,), (0,)), ((), ())),
                                        precision=lax.Precision.HIGHEST))
    return jnp.stack(partials).reshape(27, -1)


def reference(cubes, weight_a, weight_b, cotangent):
    kernel_a = weight_a.astype(jnp.float32).reshape(3, 3, 3, C1, C2)
    kernel_b = weight_b.astype(jnp.float32).reshape(3, 3, 3, C2, C3)
    back_a = jnp.transpose(kernel_a[::-1, ::-1, ::-1], (0, 1, 2, 4, 3))
    back_b = jnp.transpose(kernel_b[::-1, ::-1, ::-1], (0, 1, 2, 4, 3))

    def one_cube(pair):
        sample_cube, upstream = pair
        volume = sample_cube.astype(jnp.float32).reshape(ZTOT, SIDE, SIDE, C1)
        pre_a = correlate(volume, kernel_a)
        pooled_a = rounded(shrink(activate(pre_a)))
        pre_b = correlate(pooled_a, kernel_b)
        coarse = upstream.astype(jnp.float32).reshape(ZTOT // 4, SIDE // 4, SIDE // 4, C3)
        grad_pre_b = rounded(spread(coarse) * slope(pre_b))
        term_b = kernel_terms(pooled_a, grad_pre_b)
        grad_pooled_a = correlate(grad_pre_b, back_b)
        grad_pre_a = rounded(spread(grad_pooled_a) * slope(pre_a))
        term_a = kernel_terms(volume, grad_pre_a)
        input_grad = correlate(grad_pre_a, back_a).astype(jnp.bfloat16).reshape(ZTOT, SIDE, SIDE * C1)
        return input_grad, term_a, term_b

    input_grad, terms_a, terms_b = lax.map(one_cube, (cubes, cotangent))
    weight_grad_a = jnp.sum(terms_a, axis=0) / BATCH
    weight_grad_b = jnp.sum(terms_b, axis=0) / BATCH
    return input_grad, weight_grad_a, weight_grad_b
```

```python
import jax
import jax.numpy as jnp
from jax import lax
from jax.experimental import pallas as pl
from jax.experimental.pallas import tpu as pltpu
from jax.sharding import PartitionSpec as P

C1 = 32
C2 = 64
C3 = 128
SIDE = 32
ZD = 4
HALO = 3
BF = jnp.bfloat16
F32 = jnp.float32
AXES = ("sample", "gz")
VMEM = pl.BlockSpec(memory_space=pltpu.VMEM)
SMEM = pl.BlockSpec(memory_space=pltpu.SMEM)


def dot(a, b):
    return jnp.dot(a, b, preferred_element_type=F32)


def dot_t(a, b):
    return lax.dot_general(a, b, (((0,), (0,)), ((), ())), preferred_element_type=F32)


def row_picker(variants, stride, columns):
    shape = (variants * 16, columns)
    row = lax.broadcasted_iota(jnp.int32, shape, 0)
    col = lax.broadcasted_iota(jnp.int32, shape, 1)
    return jnp.where(col == stride * (row % 16) + row // 16 - 1, 1.0, 0.0).astype(BF)


def rows_at(block, before, total):
    rows, lanes = block.shape
    parts = []
    if before:
        parts.append(jnp.zeros((before, lanes), block.dtype))
    parts.append(block)
    if total - before - rows:
        parts.append(jnp.zeros((total - before - rows, lanes), block.dtype))
    return jnp.concatenate(parts, axis=0) if len(parts) > 1 else block


def lanes_below(shape, bound):
    return lax.broadcasted_iota(jnp.int32, shape, 1) < bound


def halves(left, right):
    return jnp.where(lanes_below(left.shape, 64), left.astype(F32), right.astype(F32)).astype(BF)


def forward_kernel(where, cubes, recv_a, recv_b, wa, wb, cot, xs, dsl, pools, grad_b, ta, tb, pooled):
    cube_count = cubes.shape[0]
    even = where[0] % 2 == 0
    picker = row_picker(4, 2, 32)

    def spread_plane(b, zz, plane):
        plane = jnp.concatenate([jnp.zeros((32, 32), BF), plane, jnp.zeros((32, 96), BF)], axis=1)
        moved = dot(picker, plane).astype(BF)
        for v in range(4):
            xs[b, zz, v] = moved[16 * v : 16 * v + 16]

    for b in range(cube_count):
        for z in range(ZD):
            spread_plane(b, HALO + z, cubes[b, z])

        for z in range(HALO):
            from_a, from_b = recv_a[b, z].astype(F32), recv_b[b, z].astype(F32)
            spread_plane(b, z, jnp.where(even, from_b, from_a).astype(BF))
            spread_plane(b, HALO + ZD + z, jnp.where(even, from_a, from_b).astype(BF))

    for d in range(9):
        block = wa[d]
        for px in range(2):
            ta[256 * d : 256 * d + 256, 128 * px : 128 * px + 128] = halves(
                rows_at(block, 32 * px, 256), rows_at(block, 64 + 32 * px, 256)
            )
        block = wb[d]
        for e in range(2):
            tb[256 * d : 256 * d + 256, 128 * e : 128 * e + 128] = rows_at(block, 64 * e, 256)

    low = jnp.where(where[0] == 0, 0.0, 1.0)
    high = jnp.where(where[0] == where[1] - 1, 0.0, 1.0)
    rows = cube_count * 8 * 16

    def group(g, carry):
        lanes = pl.ds(pl.multiple_of(128 * g, 128), 256)
        stacks = []
        for p in range(2):
            stacks.append(
                jnp.concatenate(
                    [
                        xs[:, dz : dz + 8, p + dy, :, lanes].reshape(rows, 256)
                        for dz in range(3)
                        for dy in range(3)
                    ],
                    axis=1,
                )
            )
        pre = dot(jnp.concatenate(stacks, axis=0), ta[...])
        squash = jax.nn.sigmoid(pre)
        act = pre * squash
        slope = (squash + act * (1.0 - squash)).astype(BF).reshape(2, cube_count, 8, 16, 256)
        for p in range(2):
            dsl[:, :, p, :, pl.ds(pl.multiple_of(256 * g, 256), 256)] = slope[p][:, 1:7]
        act = act.reshape(2, cube_count, 4, 2, 16, 256)
        act = act[0] + act[1]
        act = act[:, :, 0] + act[:, :, 1]
        act = (act[..., :128] + act[..., 128:]) * 0.125
        out = pl.ds(pl.multiple_of(128 * g, 128), 128)
        for z in range(4):
            part = act[:, z]
            if z == 0:
                part = part * low
            if z == 3:
                part = part * high
            pooled[:, z, :, out] = part.astype(BF)
        return carry

    lax.fori_loop(0, 8, group, 0)

    shifter = row_picker(3, 1, 16)
    for b in range(cube_count):
        for z in range(4):
            plane = jnp.concatenate([jnp.zeros((16, 64), BF), pooled[b, z], jnp.zeros((16, 64), BF)], axis=1)
            moved = dot(shifter, plane).astype(BF)
            for v in range(3):
                pools[b, z, v] = moved[16 * v : 16 * v + 16]

    rows_b = cube_count * 2 * 16
    columns = []
    for dz in range(3):
        for dy in range(3):
            columns.append(
                jnp.concatenate(
                    [
                        pools[:, dz : dz + 2, dy, :, 128 * g : 128 * g + 256].reshape(rows_b, 256)
                        for g in range(8)
                    ],
                    axis=0,
                )
            )
    pre_b = dot(jnp.concatenate(columns, axis=1), tb[...])
    squash = jax.nn.sigmoid(pre_b)
    slope_b = squash + pre_b * squash * (1.0 - squash)
    for g in range(8):
        part = slope_b[rows_b * g : rows_b * g + rows_b].reshape(cube_count, 2, 16, 256)
        up = cot[:, :, 128 * g : 128 * g + 128].astype(F32) * 0.125
        for z in range(2):
            for e in range(2):
                at = 256 * g + 128 * e
                grad_b[:, z, :, at : at + 128] = (up * part[:, z, :, 128 * e : 128 * e + 128]).astype(BF)


def terms_b_kernel(pools, grad_b, out):
    cube_count = grad_b.shape[0]
    rows_b = cube_count * 2 * 16
    grads = jnp.concatenate(
        [grad_b[:, :, :, 256 * g : 256 * g + 256].reshape(rows_b, 256) for g in range(8)], axis=0
    )
    for dz in range(3):
        for dy in range(3):
            windows = jnp.concatenate(
                [
                    pools[:, dz : dz + 2, dy, :, 128 * g : 128 * g + 256].reshape(rows_b, 256)
                    for g in range(8)
                ],
                axis=0,
            )
            full = dot_t(windows, grads)
            for dx in range(3):
                at = 64 * (9 * dz + 3 * dy + dx)
                term = full[64 * dx : 64 * dx + 64, :128] + full[64 * dx + 64 : 64 * dx + 128, 128:]
                out[at : at + 64] = term.astype(BF)
    if out.shape[0] > 27 * 64:
        out[27 * 64 :] = jnp.zeros((out.shape[0] - 27 * 64, 128), BF)


def backward_kernel(where, grad_b, recv_a, recv_b, wbt, dsl, xs, ga, out, gs, tbt, gpool, acc):
    cube_count = grad_b.shape[0]
    even = where[0] % 2 == 0
    shifter = row_picker(3, 1, 16)

    def spread_plane(b, zz, plane):
        moved = dot(shifter, plane).astype(BF)
        for v in range(3):
            gs[b, zz, v, :, 128:2176] = moved[16 * v : 16 * v + 16]
            gs[b, zz, v, :, :128] = jnp.zeros((16, 128), BF)
            gs[b, zz, v, :, 2176:] = jnp.zeros((16, 128), BF)

    for b in range(cube_count):
        for z in range(2):
            spread_plane(b, 2 + z, grad_b[b, z])
            from_a, from_b = recv_a[b, z].astype(F32), recv_b[b, z].astype(F32)
            spread_plane(b, z, jnp.where(even, from_b, from_a).astype(BF))
            spread_plane(b, 4 + z, jnp.where(even, from_a, from_b).astype(BF))

    for d in range(9):
        block = wbt[d]
        for e in range(2):
            tbt[768 * d : 768 * d + 768, 128 * e : 128 * e + 128] = halves(
                rows_at(block, 256 * e, 768), rows_at(block, 256 * e + 128, 768)
            )

    low = jnp.where(where[0] == 0, 0.0, 0.125)
    high = jnp.where(where[0] == where[1] - 1, 0.0, 0.125)
    rows = cube_count * 4 * 16
    columns = []
    for dz in range(3):
        for dy in range(3):
            columns.append(
                jnp.concatenate(
                    [gs[:, dz : dz + 4, dy, :, 512 * q : 512 * q + 768].reshape(rows, 768) for q in range(4)],
                    axis=0,
                )
            )
    back = dot(jnp.concatenate(columns, axis=1), tbt[...])
    for q in range(4):
        part = back[rows * q : rows * q + rows].reshape(cube_count, 4, 16, 256)
        for z in range(4):
            scale = low if z == 0 else high if z == 3 else 0.125
            gpool[:, z, :, 256 * q : 256 * q + 256] = part[:, z] * scale

    acc[...] = jnp.zeros_like(acc)
    ga[:, :, :, :, :128] = jnp.zeros((cube_count, 6, 4, 16, 128), BF)
    ga[:, :, :, :, 2176:] = jnp.zeros((cube_count, 6, 4, 16, 128), BF)
    rows_a = cube_count * 6 * 16
    own = cube_count * 4 * 16
    place = lax.broadcasted_iota(jnp.int32, (rows_a, 128), 0) % 16

    def group(g, carry):
        lanes = pl.ds(pl.multiple_of(128 * g, 128), 128)
        up = gpool[:, :, :, lanes]
        up = jnp.concatenate(
            [up[:, 0:1], up[:, 1:2], up[:, 1:2], up[:, 2:3], up[:, 2:3], up[:, 3:4]], axis=1
        ).reshape(rows_a, 128)
        sides = []
        for p in range(2):
            pair = []
            for px in range(2):
                at = pl.ds(pl.multiple_of(256 * g + 128 * px, 128), 128)
                grad = up * dsl[:, :, p, :, at].astype(F32).reshape(rows_a, 128)
                to = pl.ds(pl.multiple_of(256 * g + 128 * px + 128, 128), 128)
                kept = grad.astype(BF).reshape(cube_count, 6, 16, 128)
                ga[:, :, 1 + p, :, to] = kept
                pair.append(kept[:, 1:5].reshape(own, 128))
                if p == 1:
                    moved = jnp.where(place == 0, 0.0, pltpu.roll(grad, 1, 0))
                else:
                    moved = jnp.where(place == 15, 0.0, pltpu.roll(grad, rows_a - 1, 0))
                ga[:, :, 0 if p else 3, :, to] = moved.astype(BF).reshape(cube_count, 6, 16, 128)
            sides.append(jnp.concatenate(pair, axis=1))
        grads = jnp.concatenate(sides, axis=0)
        wide = pl.ds(pl.multiple_of(128 * g, 128), 256)
        windows = jnp.concatenate(
            [
                jnp.concatenate(
                    [
                        xs[:, HALO - 1 + dz : HALO + 3 + dz, p + dy, :, wide].reshape(own, 256)
                        for dz in range(3)
                        for dy in range(3)
                    ],
                    axis=1,
                )
                for p in range(2)
            ],
            axis=0,
        )
        acc[...] += dot_t(grads, windows)
        return carry

    lax.fori_loop(0, 8, group, 0)

    pending = None
    for d in range(9):
        full = acc[:, 256 * d : 256 * d + 256].T
        for dx in range(3):
            left = full[32 * dx : 32 * dx + 32, :128] + full[32 * dx + 32 : 32 * dx + 64, 128:]
            right = full[32 * dx + 64 : 32 * dx + 96, :128] + full[32 * dx + 96 : 32 * dx + 128, 128:]
            mask = lanes_below((32, 128), 64)
            merged = jnp.where(mask, left, right)
            total = merged + pltpu.roll(merged, 64, 1)
            at = 3 * d + dx
            if at % 2 == 0:
                pending = total
            else:
                out[16 * (at - 1) : 16 * (at + 1)] = jnp.where(mask, pending, total).astype(BF)
    out[416:448] = pending.astype(BF)
    out[448:] = jnp.zeros((out.shape[0] - 448, 128), BF)


RANKS = (-3, -1, 0, 2, 1, 3, 4, 6, 5, 7, 8, 10)


def input_kernel(ga, wat, out, tat):
    cube_count = ga.shape[0]
    lane = lax.broadcasted_iota(jnp.int32, (64, 128), 1)
    for d in range(9):
        block = wat[d].astype(F32)
        turned = [block if s == 0 else pltpu.roll(block, 32 * s, 1) for s in range(4)]
        for slot, rank in enumerate(RANKS):
            for half in range(2):
                start = 32 * (rank - 1 - 4 * half)
                keep = (lane >= start) & (lane < start + 96)
                value = jnp.where(keep, turned[(rank - 1) % 4], 0.0).astype(BF)
                tat[768 * d + 64 * slot : 768 * d + 64 * slot + 64, 128 * half : 128 * half + 128] = value

    rows = cube_count * ZD * 16
    sides = []
    for p in range(2):
        columns = []
        for dz in range(3):
            for dy in range(3):
                columns.append(
                    jnp.concatenate(
                        [
                            ga[:, dz : dz + ZD, p + dy, :, 512 * q : 512 * q + 768].reshape(rows, 768)
                            for q in range(4)
                        ],
                        axis=0,
                    )
                )
        sides.append(dot(jnp.concatenate(columns, axis=1), tat[...]).astype(BF).reshape(4, cube_count, ZD, 16, 256))
    row = lax.broadcasted_iota(jnp.int32, (32, 32), 0)
    col = lax.broadcasted_iota(jnp.int32, (32, 32), 1)
    mixer = jnp.where(col == row // 2 + 16 * (row % 2), 1.0, 0.0).astype(BF)
    for b in range(cube_count):
        for z in range(ZD):
            for q in range(4):
                both = jnp.concatenate([sides[0][q, b, z], sides[1][q, b, z]], axis=0)
                out[b, z, :, 256 * q : 256 * q + 256] = dot(mixer, both).astype(BF)


def call(kernel, args, outs, scratch, flops, smem=0, limit=32):
    specs = [SMEM] * smem + [VMEM] * (len(args) - smem)
    outs = [jax.ShapeDtypeStruct(shape, dtype) for shape, dtype in outs]
    return pl.pallas_call(
        kernel,
        out_shape=outs,
        in_specs=specs,
        out_specs=[VMEM] * len(outs),
        scratch_shapes=[pltpu.VMEM(shape, dtype) for shape, dtype in scratch],
        compiler_params=pltpu.CompilerParams(vmem_limit_bytes=limit * 1024 * 1024),
        cost_estimate=pl.CostEstimate(flops=flops, bytes_accessed=4_000_000, transcendentals=0),
    )(*args)


def swap(first, second, count):
    pairs_a = [(i, i ^ 1) for i in range(count)]
    pairs_b = [(i, ((i + 1) ^ 1) - 1) for i in range(1, count - 1)]
    return lax.ppermute(first, "gz", pairs_a), lax.ppermute(second, "gz", pairs_b)


def total_of(partial, count):
    rows, lanes = partial.shape
    pieces = lax.all_to_all(partial.reshape(count, rows // count, lanes), AXES, 0, 0)
    mine = jnp.sum(pieces.astype(F32), axis=0).astype(BF)
    return lax.all_gather(mine, AXES, axis=0, tiled=True).astype(F32)


def shards(cubes, weight_a, weight_b, cotangent):
    cube_count = cubes.shape[0]
    ring = lax.axis_size("gz")
    count = lax.axis_size("sample") * ring
    me = lax.axis_index("gz")
    where = jnp.stack([me, jnp.int32(ring)]).astype(jnp.int32)
    odd = me % 2
    first = lax.dynamic_slice_in_dim(cubes, 1 - odd, HALO, axis=1)
    second = lax.dynamic_slice_in_dim(cubes, odd, HALO, axis=1)
    recv_a, recv_b = swap(first, second, ring)

    wa = weight_a.reshape(9, 96, C2)
    wa2 = jnp.concatenate([wa, wa], axis=-1)
    wb = weight_b.reshape(9, 192, C3)
    wbt = weight_b.reshape(3, 3, 3, C2, C3)[::-1, ::-1, ::-1].transpose(0, 1, 2, 4, 3).reshape(9, 384, C2)
    wbt2 = jnp.concatenate([wbt, wbt], axis=-1)
    wat = weight_a.reshape(3, 3, 3, C1, C2)[::-1, ::-1].transpose(0, 1, 4, 2, 3).reshape(9, C2, 96)
    wat = jnp.pad(wat, ((0, 0), (0, 0), (0, 32)))
    cot = jnp.repeat(cotangent.reshape(cube_count, SIDE // 4, SIDE // 4 * C3), 2, axis=1)

    xs, dsl, pools, grad_b = call(
        forward_kernel,
        [where, cubes, recv_a, recv_b, wa2, wb, cot],
        [
            ((cube_count, ZD + 2 * HALO, 4, 16, 1152), BF),
            ((cube_count, 6, 2, 16, 2048), BF),
            ((cube_count, 4, 3, 16, 1152), BF),
            ((cube_count, 2, 16, 2048), BF),
        ],
        [((2304, 256), BF), ((2304, 256), BF), ((cube_count, 4, 16, 1024), BF)],
        8_000_000_000,
        smem=1,
    )
    back_a, back_b = swap(grad_b, grad_b, ring)
    unit = 16 * count
    rows_b = -(-27 * C2 // unit) * unit
    (partial_b,) = call(terms_b_kernel, [pools, grad_b], [((rows_b, 128), BF)], [], 2_000_000_000)
    rows_a = -(-448 // unit) * unit
    ga, partial_a = call(
        backward_kernel,
        [where, grad_b, back_a, back_b, wbt2, dsl, xs],
        [((cube_count, 6, 4, 16, 2304), BF), ((rows_a, 128), BF)],
        [
            ((cube_count, 6, 3, 16, 2304), BF),
            ((6912, 256), BF),
            ((cube_count, 4, 16, 1024), F32),
            ((256, 2304), F32),
        ],
        6_000_000_000,
        smem=1,
    )
    (input_grad,) = call(
        input_kernel, [ga, wat], [((cube_count, ZD, SIDE, SIDE * C1), BF)], [((6912, 256), BF)], 4_000_000_000
    )
    scale = 1.0 / (cube_count * lax.axis_size("sample"))
    total_b = total_of(partial_b, count)[: 27 * C2].reshape(27, C2 * C3) * scale
    total_a = total_of(partial_a, count)[:448].reshape(14, C1, 2, C2).transpose(0, 2, 1, 3)
    total_a = total_a.reshape(28, C1 * C2)[:27] * scale
    return input_grad, total_a, total_b


def solution(mesh):
    in_specs = (P("sample", "gz", None, None), P(), P(), P("sample", "gz", None, None))
    out_specs = (P("sample", "gz", None, None), P(), P())
    return jax.shard_map(shards, mesh=mesh, in_specs=in_specs, out_specs=out_specs, check_vma=False)
```

```python
import jax
import jax.numpy as jnp
from jax import lax
from jax.experimental import pallas as pl
from jax.experimental.pallas import tpu as pltpu
from jax.sharding import PartitionSpec as P

C1 = 32
C2 = 64
C3 = 128
SIDE = 32
ZD = 4
HALO = 3
TERMS_B = 27 * 64
TERMS_A = 14 * 32
BF = jnp.bfloat16
F32 = jnp.float32
AXES = ("sample", "gz")
VMEM = pl.BlockSpec(memory_space=pltpu.VMEM)
SMEM = pl.BlockSpec(memory_space=pltpu.SMEM)
ANY = pl.BlockSpec(memory_space=pl.ANY)


def dot(a, b):
    return jnp.dot(a, b, preferred_element_type=F32)


def dot_t(a, b):
    return lax.dot_general(a, b, (((0,), (0,)), ((), ())), preferred_element_type=F32)


def row_picker(variants, stride, columns):
    shape = (variants * 16, columns)
    row = lax.broadcasted_iota(jnp.int32, shape, 0)
    col = lax.broadcasted_iota(jnp.int32, shape, 1)
    return jnp.where(col == stride * (row % 16) + row // 16 - 1, 1.0, 0.0).astype(BF)


def rows_at(block, before, total):
    rows, lanes = block.shape
    parts = []
    if before:
        parts.append(jnp.zeros((before, lanes), block.dtype))
    parts.append(block)
    if total - before - rows:
        parts.append(jnp.zeros((total - before - rows, lanes), block.dtype))
    return jnp.concatenate(parts, axis=0) if len(parts) > 1 else block


def lanes_below(shape, bound):
    return lax.broadcasted_iota(jnp.int32, shape, 1) < bound


def halves(left, right):
    return jnp.where(lanes_below(left.shape, 64), left.astype(F32), right.astype(F32)).astype(BF)


def spread_input(target, b, zz, plane, picker):
    plane = jnp.concatenate([jnp.zeros((32, 32), BF), plane, jnp.zeros((32, 96), BF)], axis=1)
    moved = dot(picker, plane).astype(BF)
    for v in range(4):
        target[b, zz, v] = moved[16 * v : 16 * v + 16]


def prepare_kernel(cubes, wa, wb, wbt, xs, ta, tb, tbt):
    picker = row_picker(4, 2, 32)
    for b in range(cubes.shape[0]):
        for z in range(ZD):
            spread_input(xs, b, HALO + z, cubes[b, z], picker)
    for d in range(9):
        block = wa[d]
        for px in range(2):
            ta[256 * d : 256 * d + 256, 128 * px : 128 * px + 128] = halves(
                rows_at(block, 32 * px, 256), rows_at(block, 64 + 32 * px, 256)
            )
        block = wb[d]
        for e in range(2):
            tb[256 * d : 256 * d + 256, 128 * e : 128 * e + 128] = rows_at(block, 64 * e, 256)
        block = wbt[d]
        for e in range(2):
            tbt[768 * d : 768 * d + 768, 128 * e : 128 * e + 128] = halves(
                rows_at(block, 256 * e, 768), rows_at(block, 256 * e + 128, 768)
            )


def forward_kernel(where, own, recv_a, recv_b, ta, tb, cot, xs, dsl, pools, grad_b, pooled):
    del own
    cube_count = xs.shape[0]
    even = where[0] % 2 == 0
    picker = row_picker(4, 2, 32)
    for b in range(cube_count):
        for z in range(HALO):
            from_a, from_b = recv_a[b, z].astype(F32), recv_b[b, z].astype(F32)
            spread_input(xs, b, z, jnp.where(even, from_b, from_a).astype(BF), picker)
            spread_input(xs, b, HALO + ZD + z, jnp.where(even, from_a, from_b).astype(BF), picker)

    low = jnp.where(where[0] == 0, 0.0, 1.0)
    high = jnp.where(where[0] == where[1] - 1, 0.0, 1.0)
    rows = cube_count * 8 * 16

    def group(g, carry):
        lanes = pl.ds(pl.multiple_of(128 * g, 128), 256)
        stacks = []
        for p in range(2):
            stacks.append(
                jnp.concatenate(
                    [
                        xs[:, dz : dz + 8, p + dy, :, lanes].reshape(rows, 256)
                        for dz in range(3)
                        for dy in range(3)
                    ],
                    axis=1,
                )
            )
        pre = dot(jnp.concatenate(stacks, axis=0), ta[...])
        squash = jax.nn.sigmoid(pre)
        act = pre * squash
        slope = (squash + act * (1.0 - squash)).astype(BF).reshape(2, cube_count, 8, 16, 256)
        for p in range(2):
            dsl[:, :, p, :, pl.ds(pl.multiple_of(256 * g, 256), 256)] = slope[p][:, 1:7]
        act = act.reshape(2, cube_count, 4, 2, 16, 256)
        act = act[0] + act[1]
        act = act[:, :, 0] + act[:, :, 1]
        act = (act[..., :128] + act[..., 128:]) * 0.125
        out = pl.ds(pl.multiple_of(128 * g, 128), 128)
        for z in range(4):
            part = act[:, z]
            if z == 0:
                part = part * low
            if z == 3:
                part = part * high
            pooled[:, z, :, out] = part.astype(BF)
        return carry

    lax.fori_loop(0, 8, group, 0)

    shifter = row_picker(3, 1, 16)
    for b in range(cube_count):
        for z in range(4):
            plane = jnp.concatenate([jnp.zeros((16, 64), BF), pooled[b, z], jnp.zeros((16, 64), BF)], axis=1)
            moved = dot(shifter, plane).astype(BF)
            for v in range(3):
                pools[b, z, v] = moved[16 * v : 16 * v + 16]

    rows_b = cube_count * 2 * 16
    columns = []
    for dz in range(3):
        for dy in range(3):
            columns.append(
                jnp.concatenate(
                    [
                        pools[:, dz : dz + 2, dy, :, 128 * g : 128 * g + 256].reshape(rows_b, 256)
                        for g in range(8)
                    ],
                    axis=0,
                )
            )
    pre_b = dot(jnp.concatenate(columns, axis=1), tb[...])
    squash = jax.nn.sigmoid(pre_b)
    slope_b = squash + pre_b * squash * (1.0 - squash)
    for g in range(8):
        part = slope_b[rows_b * g : rows_b * g + rows_b].reshape(cube_count, 2, 16, 256)
        up = cot[:, :, 128 * g : 128 * g + 128].astype(F32) * 0.125
        for z in range(2):
            for e in range(2):
                at = 256 * g + 128 * e
                grad_b[:, z, :, at : at + 128] = (up * part[:, z, :, 128 * e : 128 * e + 128]).astype(BF)


def terms_b_kernel(pools, grad_b, out):
    cube_count = grad_b.shape[0]
    rows_b = cube_count * 2 * 16
    grads = jnp.concatenate(
        [grad_b[:, :, :, 256 * g : 256 * g + 256].reshape(rows_b, 256) for g in range(8)], axis=0
    )
    for dz in range(3):
        for dy in range(3):
            windows = jnp.concatenate(
                [
                    pools[:, dz : dz + 2, dy, :, 128 * g : 128 * g + 256].reshape(rows_b, 256)
                    for g in range(8)
                ],
                axis=0,
            )
            full = dot_t(windows, grads)
            for dx in range(3):
                at = 64 * (9 * dz + 3 * dy + dx)
                term = full[64 * dx : 64 * dx + 64, :128] + full[64 * dx + 64 : 64 * dx + 128, 128:]
                out[at : at + 64] = term.astype(BF)


def backward_kernel(where, grad_b, recv_a, recv_b, tbt, dsl, xs, terms_b, ga_out, out, gs, ga, gpool, acc, sem):
    cube_count = grad_b.shape[0]
    even = where[0] % 2 == 0
    shifter = row_picker(3, 1, 16)

    def spread_plane(b, zz, plane):
        moved = dot(shifter, plane).astype(BF)
        for v in range(3):
            gs[b, zz, v, :, 128:2176] = moved[16 * v : 16 * v + 16]
            gs[b, zz, v, :, :128] = jnp.zeros((16, 128), BF)
            gs[b, zz, v, :, 2176:] = jnp.zeros((16, 128), BF)

    for b in range(cube_count):
        for z in range(2):
            spread_plane(b, 2 + z, grad_b[b, z])
            from_a, from_b = recv_a[b, z].astype(F32), recv_b[b, z].astype(F32)
            spread_plane(b, z, jnp.where(even, from_b, from_a).astype(BF))
            spread_plane(b, 4 + z, jnp.where(even, from_a, from_b).astype(BF))

    low = jnp.where(where[0] == 0, 0.0, 0.125)
    high = jnp.where(where[0] == where[1] - 1, 0.0, 0.125)
    rows = cube_count * 4 * 16
    columns = []
    for dz in range(3):
        for dy in range(3):
            columns.append(
                jnp.concatenate(
                    [gs[:, dz : dz + 4, dy, :, 512 * q : 512 * q + 768].reshape(rows, 768) for q in range(4)],
                    axis=0,
                )
            )
    back = dot(jnp.concatenate(columns, axis=1), tbt[...])
    for q in range(4):
        part = back[rows * q : rows * q + rows].reshape(cube_count, 4, 16, 256)
        for z in range(4):
            scale = low if z == 0 else high if z == 3 else 0.125
            gpool[:, z, :, 256 * q : 256 * q + 256] = part[:, z] * scale

    acc[...] = jnp.zeros_like(acc)
    ga[:, :, :, :, :128] = jnp.zeros((cube_count, 6, 4, 16, 128), BF)
    ga[:, :, :, :, 2176:] = jnp.zeros((cube_count, 6, 4, 16, 128), BF)
    rows_a = cube_count * 6 * 16
    own = cube_count * 4 * 16
    place = lax.broadcasted_iota(jnp.int32, (rows_a, 128), 0) % 16

    def group(g, carry):
        lanes = pl.ds(pl.multiple_of(128 * g, 128), 128)
        up = gpool[:, :, :, lanes]
        up = jnp.concatenate(
            [up[:, 0:1], up[:, 1:2], up[:, 1:2], up[:, 2:3], up[:, 2:3], up[:, 3:4]], axis=1
        ).reshape(rows_a, 128)
        sides = []
        for p in range(2):
            pair = []
            for px in range(2):
                at = pl.ds(pl.multiple_of(256 * g + 128 * px, 128), 128)
                grad = up * dsl[:, :, p, :, at].astype(F32).reshape(rows_a, 128)
                to = pl.ds(pl.multiple_of(256 * g + 128 * px + 128, 128), 128)
                kept = grad.astype(BF).reshape(cube_count, 6, 16, 128)
                ga[:, :, 1 + p, :, to] = kept
                pair.append(kept[:, 1:5].reshape(own, 128))
                if p == 1:
                    moved = jnp.where(place == 0, 0.0, pltpu.roll(grad, 1, 0))
                else:
                    moved = jnp.where(place == 15, 0.0, pltpu.roll(grad, rows_a - 1, 0))
                ga[:, :, 0 if p else 3, :, to] = moved.astype(BF).reshape(cube_count, 6, 16, 128)
            sides.append(jnp.concatenate(pair, axis=1))
        grads = jnp.concatenate(sides, axis=0)
        wide = pl.ds(pl.multiple_of(128 * g, 128), 256)
        windows = jnp.concatenate(
            [
                jnp.concatenate(
                    [
                        xs[:, HALO - 1 + dz : HALO + 3 + dz, p + dy, :, wide].reshape(own, 256)
                        for dz in range(3)
                        for dy in range(3)
                    ],
                    axis=1,
                )
                for p in range(2)
            ],
            axis=0,
        )
        acc[...] += dot_t(grads, windows)
        return carry

    lax.fori_loop(0, 8, group, 0)

    leave = pltpu.make_async_copy(ga, ga_out, sem)
    leave.start()
    out[:TERMS_B] = terms_b[...]
    pending = None
    for d in range(9):
        full = acc[:, 256 * d : 256 * d + 256].T
        for dx in range(3):
            left = full[32 * dx : 32 * dx + 32, :128] + full[32 * dx + 32 : 32 * dx + 64, 128:]
            right = full[32 * dx + 64 : 32 * dx + 96, :128] + full[32 * dx + 96 : 32 * dx + 128, 128:]
            mask = lanes_below((32, 128), 64)
            merged = jnp.where(mask, left, right)
            total = merged + pltpu.roll(merged, 64, 1)
            at = 3 * d + dx
            if at % 2 == 0:
                pending = total
            else:
                to = TERMS_B + 16 * (at - 1)
                out[to : to + 32] = jnp.where(mask, pending, total).astype(BF)
    out[TERMS_B + 416 : TERMS_B + TERMS_A] = pending.astype(BF)
    out[TERMS_B + TERMS_A :] = jnp.zeros((out.shape[0] - TERMS_B - TERMS_A, 128), BF)
    leave.wait()


RANKS = (-3, -1, 0, 2, 1, 3, 4, 6, 5, 7, 8, 10)


def input_kernel(ga_in, wat, out, tat, ga, sem):
    arrive = pltpu.make_async_copy(ga_in, ga, sem)
    arrive.start()
    cube_count = ga.shape[0]
    lane = lax.broadcasted_iota(jnp.int32, (64, 128), 1)
    for d in range(9):
        block = wat[d].astype(F32)
        turned = [block if s == 0 else pltpu.roll(block, 32 * s, 1) for s in range(4)]
        for slot, rank in enumerate(RANKS):
            for half in range(2):
                start = 32 * (rank - 1 - 4 * half)
                keep = (lane >= start) & (lane < start + 96)
                value = jnp.where(keep, turned[(rank - 1) % 4], 0.0).astype(BF)
                tat[768 * d + 64 * slot : 768 * d + 64 * slot + 64, 128 * half : 128 * half + 128] = value

    arrive.wait()
    rows = cube_count * ZD * 16
    sides = []
    for p in range(2):
        columns = []
        for dz in range(3):
            for dy in range(3):
                columns.append(
                    jnp.concatenate(
                        [
                            ga[:, dz : dz + ZD, p + dy, :, 512 * q : 512 * q + 768].reshape(rows, 768)
                            for q in range(4)
                        ],
                        axis=0,
                    )
                )
        sides.append(dot(jnp.concatenate(columns, axis=1), tat[...]).astype(BF).reshape(4, cube_count, ZD, 16, 256))
    row = lax.broadcasted_iota(jnp.int32, (32, 32), 0)
    col = lax.broadcasted_iota(jnp.int32, (32, 32), 1)
    mixer = jnp.where(col == row // 2 + 16 * (row % 2), 1.0, 0.0).astype(BF)
    for b in range(cube_count):
        for z in range(ZD):
            for q in range(4):
                both = jnp.concatenate([sides[0][q, b, z], sides[1][q, b, z]], axis=0)
                out[b, z, :, 256 * q : 256 * q + 256] = dot(mixer, both).astype(BF)


def call(kernel, args, outs, scratch, flops, smem=0, any_in=(), any_out=(), aliases=None):
    specs = [SMEM if i < smem else ANY if i in any_in else VMEM for i in range(len(args))]
    return pl.pallas_call(
        kernel,
        out_shape=[jax.ShapeDtypeStruct(shape, dtype) for shape, dtype in outs],
        in_specs=specs,
        out_specs=[ANY if i in any_out else VMEM for i in range(len(outs))],
        scratch_shapes=scratch,
        input_output_aliases=aliases or {},
        compiler_params=pltpu.CompilerParams(vmem_limit_bytes=28 * 1024 * 1024),
        cost_estimate=pl.CostEstimate(flops=flops, bytes_accessed=1_000_000, transcendentals=0),
    )(*args)


def swap(first, second, count):
    pairs_a = [(i, i ^ 1) for i in range(count)]
    pairs_b = [(i, ((i + 1) ^ 1) - 1) for i in range(1, count - 1)]
    return lax.ppermute(first, "gz", pairs_a), lax.ppermute(second, "gz", pairs_b)


def gather_kernel(pieces, out):
    mine = jnp.sum(pieces[...].astype(F32), axis=0).astype(BF)
    for i in range(out.shape[0]):
        out[i] = mine


def total_of(partial, count):
    rows, lanes = partial.shape
    shape = (count, rows // count, lanes)
    pieces = lax.all_to_all(partial.reshape(shape), AXES, 0, 0)
    (copies,) = call(gather_kernel, [pieces], [(shape, BF)], [], 1_000_000)
    return lax.all_to_all(copies, AXES, 0, 0).reshape(rows, lanes)


def shards(cubes, weight_a, weight_b, cotangent):
    cube_count = cubes.shape[0]
    ring = lax.axis_size("gz")
    count = lax.axis_size("sample") * ring
    me = lax.axis_index("gz")
    where = jnp.stack([me, jnp.int32(ring)]).astype(jnp.int32)
    odd = me % 2
    first = lax.dynamic_slice_in_dim(cubes, 1 - odd, HALO, axis=1)
    second = lax.dynamic_slice_in_dim(cubes, odd, HALO, axis=1)
    recv_a, recv_b = swap(first, second, ring)

    wa = weight_a.reshape(9, 96, C2)
    wa2 = jnp.concatenate([wa, wa], axis=-1)
    wb = weight_b.reshape(9, 192, C3)
    wbt = weight_b.reshape(3, 3, 3, C2, C3)[::-1, ::-1, ::-1].transpose(0, 1, 2, 4, 3).reshape(9, 384, C2)
    wbt2 = jnp.concatenate([wbt, wbt], axis=-1)
    wat = weight_a.reshape(3, 3, 3, C1, C2)[::-1, ::-1].transpose(0, 1, 4, 2, 3).reshape(9, C2, 96)
    wat = jnp.pad(wat, ((0, 0), (0, 0), (0, 32)))
    cot = jnp.repeat(cotangent.reshape(cube_count, SIDE // 4, SIDE // 4 * C3), 2, axis=1)

    own_xs, ta, tb, tbt = call(
        prepare_kernel,
        [cubes, wa2, wb, wbt2],
        [
            ((cube_count, ZD + 2 * HALO, 4, 16, 1152), BF),
            ((2304, 256), BF),
            ((2304, 256), BF),
            ((6912, 256), BF),
        ],
        [],
        1_000_000_000,
    )
    xs, dsl, pools, grad_b = call(
        forward_kernel,
        [where, own_xs, recv_a, recv_b, ta, tb, cot],
        [
            ((cube_count, ZD + 2 * HALO, 4, 16, 1152), BF),
            ((cube_count, 6, 2, 16, 2048), BF),
            ((cube_count, 4, 3, 16, 1152), BF),
            ((cube_count, 2, 16, 2048), BF),
        ],
        [pltpu.VMEM((cube_count, 4, 16, 1024), BF)],
        8_000_000_000,
        smem=1,
        aliases={1: 0},
    )
    back_a, back_b = swap(grad_b, grad_b, ring)
    (terms_b,) = call(terms_b_kernel, [pools, grad_b], [((TERMS_B, 128), BF)], [], 1_000_000_000)
    rows = -(-(TERMS_B + TERMS_A) // (8 * count)) * 8 * count
    rows = -(-rows // (16 * count)) * 16 * count if count > 32 else rows
    ga, partial = call(
        backward_kernel,
        [where, grad_b, back_a, back_b, tbt, dsl, xs, terms_b],
        [((cube_count, 6, 4, 16, 2304), BF), ((rows, 128), BF)],
        [
            pltpu.VMEM((cube_count, 6, 3, 16, 2304), BF),
            pltpu.VMEM((cube_count, 6, 4, 16, 2304), BF),
            pltpu.VMEM((cube_count, 4, 16, 1024), F32),
            pltpu.VMEM((256, 2304), F32),
            pltpu.SemaphoreType.DMA,
        ],
        6_000_000_000,
        smem=1,
        any_out=(0,),
    )
    (input_grad,) = call(
        input_kernel,
        [ga, wat],
        [((cube_count, ZD, SIDE, SIDE * C1), BF)],
        [
            pltpu.VMEM((6912, 256), BF),
            pltpu.VMEM((cube_count, 6, 4, 16, 2304), BF),
            pltpu.SemaphoreType.DMA,
        ],
        4_000_000_000,
        any_in=(0,),
    )
    scale = 1.0 / (cube_count * lax.axis_size("sample"))
    total = total_of(partial, count)
    total_b = total[:TERMS_B].astype(F32).reshape(27, C2 * C3) * scale
    total_a = total[TERMS_B : TERMS_B + TERMS_A].astype(F32).reshape(14, C1, 2, C2).transpose(0, 2, 1, 3)
    total_a = total_a.reshape(28, C1 * C2)[:27] * scale
    return input_grad, total_a, total_b


def solution(mesh):
    in_specs = (P("sample", "gz", None, None), P(), P(), P("sample", "gz", None, None))
    out_specs = (P("sample", "gz", None, None), P(), P())
    return jax.shard_map(shards, mesh=mesh, in_specs=in_specs, out_specs=out_specs, check_vma=False)
```

```python
import jax
import jax.numpy as jnp
from jax import lax
from jax.experimental import pallas as pl
from jax.experimental.pallas import tpu as pltpu
from jax.sharding import PartitionSpec as P

C1 = 32
C2 = 64
C3 = 128
SIDE = 32
ZD = 4
HALO = 3
ROWS_B = C1 * 2 * 28
ROWS_A = C1 // 2 * 28
BF = jnp.bfloat16
F32 = jnp.float32
AXES = ("sample", "gz")
VMEM = pl.BlockSpec(memory_space=pltpu.VMEM)
SMEM = pl.BlockSpec(memory_space=pltpu.SMEM)
ANY = pl.BlockSpec(memory_space=pl.ANY)


def dot(a, b):
    return jnp.dot(a, b, preferred_element_type=F32)


def dot_t(a, b):
    return lax.dot_general(a, b, (((0,), (0,)), ((), ())), preferred_element_type=F32)


def sigmoid(v):
    return pl.reciprocal(1.0 + jnp.exp(-v), approx=True)


def row_picker(variants, stride, columns):
    shape = (variants * 16, columns)
    row = lax.broadcasted_iota(jnp.int32, shape, 0)
    col = lax.broadcasted_iota(jnp.int32, shape, 1)
    return jnp.where(col == stride * (row % 16) + row // 16 - 1, 1.0, 0.0).astype(BF)


def rows_at(block, before, total):
    rows, lanes = block.shape
    parts = []
    if before:
        parts.append(jnp.zeros((before, lanes), block.dtype))
    parts.append(block)
    if total - before - rows:
        parts.append(jnp.zeros((total - before - rows, lanes), block.dtype))
    return jnp.concatenate(parts, axis=0) if len(parts) > 1 else block


def lanes_below(shape, bound):
    return lax.broadcasted_iota(jnp.int32, shape, 1) < bound


def halves(left, right):
    return jnp.where(lanes_below(left.shape, 64), left, right).astype(BF)


def spread_input(target, b, zz, plane, picker):
    plane = jnp.concatenate([jnp.zeros((32, 32), BF), plane, jnp.zeros((32, 96), BF)], axis=1)
    moved = dot(picker, plane).astype(BF)
    for v in range(4):
        target[b, zz, v] = moved[16 * v : 16 * v + 16]


def prepare_kernel(cubes, wa, wb, xs, ta, tb, tbt, wat):
    picker = row_picker(4, 2, 32)
    for b in range(cubes.shape[0]):
        for z in range(ZD):
            spread_input(xs, b, HALO + z, cubes[b, z], picker)
    for d in range(9):
        block = wa[d].astype(F32)
        block = jnp.concatenate([block, block], axis=1)
        for px in range(2):
            ta[256 * d : 256 * d + 256, 128 * px : 128 * px + 128] = halves(
                rows_at(block, 32 * px, 256), rows_at(block, 64 + 32 * px, 256)
            )
        wat[8 - d] = rows_at(block, 0, 128).T[:64].astype(BF)
        block = wb[d]
        for e in range(2):
            tb[256 * d : 256 * d + 256, 128 * e : 128 * e + 128] = rows_at(block, 64 * e, 256)
        turned = []
        for dx in (2, 1, 0):
            part = block[64 * dx : 64 * dx + 64].astype(F32)
            turned.append(jnp.concatenate([part, part], axis=0).T)
        block = jnp.concatenate(turned, axis=0)
        to = 768 * (8 - d)
        for e in range(2):
            tbt[to : to + 768, 128 * e : 128 * e + 128] = halves(
                rows_at(block, 256 * e, 768), rows_at(block, 256 * e + 128, 768)
            )


def forward_kernel(where, own, recv_a, recv_b, ta, tb, cot, xs, dsl, pools, grad_b, pooled):
    del own
    cube_count = xs.shape[0]
    even = where[0] % 2 == 0
    picker = row_picker(4, 2, 32)
    for b in range(cube_count):
        for z in range(HALO):
            far = ZD - HALO + z
            below = jnp.where(even, recv_b[b, far].astype(F32), recv_a[b, far].astype(F32)).astype(BF)
            above = jnp.where(even, recv_a[b, z].astype(F32), recv_b[b, z].astype(F32)).astype(BF)
            spread_input(xs, b, z, below, picker)
            spread_input(xs, b, HALO + ZD + z, above, picker)

    low = jnp.where(where[0] == 0, 0.0, 1.0)
    high = jnp.where(where[0] == where[1] - 1, 0.0, 1.0)
    rows = cube_count * 8 * 16

    def group(g, carry):
        lanes = pl.ds(pl.multiple_of(128 * g, 128), 256)
        stacks = []
        for p in range(2):
            stacks.append(
                jnp.concatenate(
                    [
                        xs[:, dz : dz + 8, p + dy, :, lanes].reshape(rows, 256)
                        for dz in range(3)
                        for dy in range(3)
                    ],
                    axis=1,
                )
            )
        pre = dot(jnp.concatenate(stacks, axis=0), ta[...])
        squash = sigmoid(pre)
        act = pre * squash
        slope = (squash + act * (1.0 - squash)).astype(BF).reshape(2, cube_count, 8, 16, 256)
        for p in range(2):
            dsl[:, :, p, :, pl.ds(pl.multiple_of(256 * g, 256), 256)] = slope[p][:, 1:7]
        act = act.reshape(2, cube_count, 4, 2, 16, 256)
        act = act[0] + act[1]
        act = act[:, :, 0] + act[:, :, 1]
        act = (act[..., :128] + act[..., 128:]) * 0.125
        out = pl.ds(pl.multiple_of(128 * g, 128), 128)
        for z in range(4):
            part = act[:, z]
            if z == 0:
                part = part * low
            if z == 3:
                part = part * high
            pooled[:, z, :, out] = part.astype(BF)
        return carry

    lax.fori_loop(0, 8, group, 0)

    shifter = row_picker(3, 1, 16)
    for b in range(cube_count):
        for z in range(4):
            plane = jnp.concatenate([jnp.zeros((16, 64), BF), pooled[b, z], jnp.zeros((16, 64), BF)], axis=1)
            moved = dot(shifter, plane).astype(BF)
            for v in range(3):
                pools[b, z, v] = moved[16 * v : 16 * v + 16]

    rows_b = cube_count * 2 * 16
    columns = []
    for dz in range(3):
        for dy in range(3):
            columns.append(
                jnp.concatenate(
                    [
                        pools[:, dz : dz + 2, dy, :, 128 * g : 128 * g + 256].reshape(rows_b, 256)
                        for g in range(8)
                    ],
                    axis=0,
                )
            )
    pre_b = dot(jnp.concatenate(columns, axis=1), tb[...])
    squash = sigmoid(pre_b)
    slope_b = squash + pre_b * squash * (1.0 - squash)
    row = lax.broadcasted_iota(jnp.int32, (16, 8), 0)
    twice = jnp.where(row // 2 == lax.broadcasted_iota(jnp.int32, (16, 8), 1), 0.125, 0.0).astype(BF)
    ups = [dot(twice, cot[b, 0]) for b in range(cube_count)]
    for g in range(8):
        part = slope_b[rows_b * g : rows_b * g + rows_b].reshape(cube_count, 2, 16, 256)
        up = jnp.stack([ups[b][:, 128 * g : 128 * g + 128] for b in range(cube_count)])
        for z in range(2):
            for e in range(2):
                at = 256 * g + 128 * e
                grad_b[:, z, :, at : at + 128] = (up * part[:, z, :, 128 * e : 128 * e + 128]).astype(BF)


def terms_b_kernel(where, pools, grad_b, *rest):
    outs, terms = rest[:-1], rest[-1]
    cube_count = grad_b.shape[0]
    rows_b = cube_count * 2 * 16
    grads = jnp.concatenate(
        [grad_b[:, :, :, 256 * g : 256 * g + 256].reshape(rows_b, 256) for g in range(8)], axis=0
    )
    terms[pl.ds(27, C2, stride=28), :] = jnp.zeros((C2, 128), F32)
    for dz in range(3):
        for dy in range(3):
            windows = jnp.concatenate(
                [
                    pools[:, dz : dz + 2, dy, :, 128 * g : 128 * g + 256].reshape(rows_b, 256)
                    for g in range(8)
                ],
                axis=0,
            )
            full = dot_t(windows, grads)
            for dx in range(3):
                term = full[64 * dx : 64 * dx + 64, :128] + full[64 * dx + 64 : 64 * dx + 128, 128:]
                terms[pl.ds(9 * dz + 3 * dy + dx, C2, stride=28), :] = term
    share = ROWS_B // len(outs)
    for k, out in enumerate(outs):
        chunk = where[2] ^ k
        out[...] = terms[pl.ds(pl.multiple_of(chunk * share, 8), share), :].astype(BF)


def scatter_b_kernel(*refs):
    parts, out = refs[1:-1], refs[-1]
    total = parts[0][...].astype(F32)
    for part in parts[1:]:
        total = total + part[...].astype(F32)
    out[...] = total.reshape(out.shape).astype(BF)


def exchange_kernel(after, pieces_b, pieces_a, out):
    del after
    mine = jnp.concatenate(
        [jnp.sum(pieces_b[...].astype(F32), axis=0), jnp.sum(pieces_a[...].astype(F32), axis=0)], axis=0
    ).astype(BF)
    for i in range(out.shape[0]):
        out[i] = mine


def collect_kernel(pieces, out):
    count, rows, lanes = pieces.shape
    piece = out.shape[0] - ROWS_A * out.shape[0] // (ROWS_A + ROWS_B)
    piece = piece // count
    parts = pieces[...].astype(F32)
    whole = jnp.concatenate([parts[:, :piece].reshape(count * piece, lanes), jnp.sum(parts[:, piece:], axis=0)], axis=0)
    out[...] = whole.astype(BF)


def finish_kernel(where, scale, *refs):
    parts, out_a, out_b, whole = refs[:-3], refs[-3], refs[-2], refs[-1]
    for k, part in enumerate(parts):
        whole[where[2] ^ k] = part[...].astype(F32)
    for rows, width, base, out in ((ROWS_B, C2, 0, out_b), (ROWS_A, C1 // 2, ROWS_B // len(parts), out_a)):
        each = width // len(parts)
        for i in range(width):
            start = base + 28 * (i % each)
            out[:, 128 * i : 128 * i + 128] = whole[i // each, start : start + 27] * scale[0]


def backward_kernel(where, grad_b, recv_a, recv_b, tbt, dsl, xs, after, ga_out, out, gs, ga, gpool, acc, term, terms, sem):
    del after
    cube_count = grad_b.shape[0]
    even = where[0] % 2 == 0
    shifter = row_picker(3, 1, 16)

    def spread_plane(b, zz, plane):
        moved = dot(shifter, plane).astype(BF)
        for v in range(3):
            gs[b, zz, v, :, 128:2176] = moved[16 * v : 16 * v + 16]
            gs[b, zz, v, :, :128] = jnp.zeros((16, 128), BF)
            gs[b, zz, v, :, 2176:] = jnp.zeros((16, 128), BF)

    for b in range(cube_count):
        for z in range(2):
            spread_plane(b, 2 + z, grad_b[b, z])
            from_a, from_b = recv_a[b, z].astype(F32), recv_b[b, z].astype(F32)
            spread_plane(b, z, jnp.where(even, from_b, from_a).astype(BF))
            spread_plane(b, 4 + z, jnp.where(even, from_a, from_b).astype(BF))

    low = jnp.where(where[0] == 0, 0.0, 0.125)
    high = jnp.where(where[0] == where[1] - 1, 0.0, 0.125)
    rows = cube_count * 4 * 16
    columns = []
    for dz in range(3):
        for dy in range(3):
            columns.append(
                jnp.concatenate(
                    [gs[:, dz : dz + 4, dy, :, 512 * q : 512 * q + 768].reshape(rows, 768) for q in range(4)],
                    axis=0,
                )
            )
    back = dot(jnp.concatenate(columns, axis=1), tbt[...])
    for q in range(4):
        part = back[rows * q : rows * q + rows].reshape(cube_count, 4, 16, 256)
        for z in range(4):
            scale = low if z == 0 else high if z == 3 else 0.125
            gpool[:, z, :, 256 * q : 256 * q + 256] = part[:, z] * scale

    acc[...] = jnp.zeros_like(acc)
    ga[:, :, :, :, :128] = jnp.zeros((cube_count, 6, 4, 16, 128), BF)
    ga[:, :, :, :, 2176:] = jnp.zeros((cube_count, 6, 4, 16, 128), BF)
    rows_a = cube_count * 6 * 16
    own = cube_count * 4 * 16
    place = lax.broadcasted_iota(jnp.int32, (rows_a, 128), 0) % 16

    def group(g, carry):
        lanes = pl.ds(pl.multiple_of(128 * g, 128), 128)
        up = gpool[:, :, :, lanes]
        up = jnp.concatenate(
            [up[:, 0:1], up[:, 1:2], up[:, 1:2], up[:, 2:3], up[:, 2:3], up[:, 3:4]], axis=1
        ).reshape(rows_a, 128)
        sides = []
        for p in range(2):
            pair = []
            for px in range(2):
                at = pl.ds(pl.multiple_of(256 * g + 128 * px, 128), 128)
                grad = up * dsl[:, :, p, :, at].astype(F32).reshape(rows_a, 128)
                to = pl.ds(pl.multiple_of(256 * g + 128 * px + 128, 128), 128)
                kept = grad.astype(BF).reshape(cube_count, 6, 16, 128)
                ga[:, :, 1 + p, :, to] = kept
                pair.append(kept[:, 1:5].reshape(own, 128))
                if p == 1:
                    moved = jnp.where(place == 0, 0.0, pltpu.roll(grad, 1, 0))
                else:
                    moved = jnp.where(place == 15, 0.0, pltpu.roll(grad, rows_a - 1, 0))
                ga[:, :, 0 if p else 3, :, to] = moved.astype(BF).reshape(cube_count, 6, 16, 128)
            sides.append(jnp.concatenate(pair, axis=1))
        grads = jnp.concatenate(sides, axis=0)
        wide = pl.ds(pl.multiple_of(128 * g, 128), 256)
        windows = jnp.concatenate(
            [
                jnp.concatenate(
                    [
                        xs[:, HALO - 1 + dz : HALO + 3 + dz, p + dy, :, wide].reshape(own, 256)
                        for dz in range(3)
                        for dy in range(3)
                    ],
                    axis=1,
                )
                for p in range(2)
            ],
            axis=0,
        )
        acc[...] += dot_t(grads, windows)
        return carry

    lax.fori_loop(0, 8, group, 0)

    leave = pltpu.make_async_copy(ga, ga_out, sem)
    leave.start()
    terms[pl.ds(27, C1 // 2, stride=28), :] = jnp.zeros((C1 // 2, 128), F32)
    mask = lanes_below((32, 128), 64)
    for d in range(9):
        full = acc[:, 256 * d : 256 * d + 256].T
        for dx in range(3):
            left = full[32 * dx : 32 * dx + 32, :128] + full[32 * dx + 32 : 32 * dx + 64, 128:]
            right = full[32 * dx + 64 : 32 * dx + 96, :128] + full[32 * dx + 96 : 32 * dx + 128, 128:]
            merged = jnp.where(mask, left, right)
            slot = (3 * d + dx) % 4
            term[slot] = merged + pltpu.roll(merged, 64, 1)
            evens = term[slot, pl.ds(0, C1 // 2, stride=2), :]
            odds = term[slot, pl.ds(1, C1 // 2, stride=2), :]
            terms[pl.ds(3 * d + dx, C1 // 2, stride=28), :] = jnp.where(mask[:16], evens, odds)
    out[...] = terms[...].reshape(out.shape).astype(BF)
    leave.wait()


RANKS = (-3, -1, 0, 2, 1, 3, 4, 6, 5, 7, 8, 10)


def input_kernel(ga_in, wat, out, tat, ga, sem):
    arrive = pltpu.make_async_copy(ga_in, ga, sem)
    arrive.start()
    cube_count = ga.shape[0]
    lane = lax.broadcasted_iota(jnp.int32, (64, 128), 1)
    for d in range(9):
        block = wat[d].astype(F32)
        turned = [block if s == 0 else pltpu.roll(block, 32 * s, 1) for s in range(4)]
        for slot, rank in enumerate(RANKS):
            for half in range(2):
                start = 32 * (rank - 1 - 4 * half)
                keep = (lane >= start) & (lane < start + 96)
                value = jnp.where(keep, turned[(rank - 1) % 4], 0.0).astype(BF)
                tat[768 * d + 64 * slot : 768 * d + 64 * slot + 64, 128 * half : 128 * half + 128] = value

    arrive.wait()
    rows = cube_count * ZD * 16
    sides = []
    for p in range(2):
        columns = []
        for dz in range(3):
            for dy in range(3):
                columns.append(
                    jnp.concatenate(
                        [
                            ga[:, dz : dz + ZD, p + dy, :, 512 * q : 512 * q + 768].reshape(rows, 768)
                            for q in range(4)
                        ],
                        axis=0,
                    )
                )
        sides.append(dot(jnp.concatenate(columns, axis=1), tat[...]).astype(BF).reshape(4, cube_count, ZD, 16, 256))
    row = lax.broadcasted_iota(jnp.int32, (32, 32), 0)
    col = lax.broadcasted_iota(jnp.int32, (32, 32), 1)
    mixer = jnp.where(col == row // 2 + 16 * (row % 2), 1.0, 0.0).astype(BF)
    for b in range(cube_count):
        for z in range(ZD):
            for q in range(4):
                both = jnp.concatenate([sides[0][q, b, z], sides[1][q, b, z]], axis=0)
                out[b, z, :, 256 * q : 256 * q + 256] = dot(mixer, both).astype(BF)


def call(kernel, args, outs, scratch, flops, smem=0, any_in=(), any_out=(), aliases=None):
    specs = [SMEM if i < smem else ANY if i in any_in else VMEM for i in range(len(args))]
    return pl.pallas_call(
        kernel,
        out_shape=[jax.ShapeDtypeStruct(shape, dtype) for shape, dtype in outs],
        in_specs=specs,
        out_specs=[ANY if i in any_out else VMEM for i in range(len(outs))],
        scratch_shapes=scratch,
        input_output_aliases=aliases or {},
        compiler_params=pltpu.CompilerParams(vmem_limit_bytes=28 * 1024 * 1024),
        cost_estimate=pl.CostEstimate(flops=flops, bytes_accessed=1_000_000, transcendentals=0),
    )(*args)


def swap(first, second, count):
    pairs_a = [(i, i ^ 1) for i in range(count)]
    pairs_b = [(i, ((i + 1) ^ 1) - 1) for i in range(1, count - 1)]
    return lax.ppermute(first, "gz", pairs_a), lax.ppermute(second, "gz", pairs_b)


def swap_samples(parts, count):
    return [
        lax.ppermute(part, "sample", [(i, i ^ k) for i in range(count)]) for k, part in enumerate(parts) if k
    ]


def shards(cubes, weight_a, weight_b, cotangent):
    cube_count = cubes.shape[0]
    ring = lax.axis_size("gz")
    samples = lax.axis_size("sample")
    where = jnp.stack([lax.axis_index("gz"), jnp.int32(ring), lax.axis_index("sample")]).astype(jnp.int32)
    recv_a, recv_b = swap(cubes, cubes, ring)

    own_xs, ta, tb, tbt, wat = call(
        prepare_kernel,
        [cubes, weight_a.reshape(9, 96, C2), weight_b.reshape(9, 192, C3)],
        [
            ((cube_count, ZD + 2 * HALO, 4, 16, 1152), BF),
            ((2304, 256), BF),
            ((2304, 256), BF),
            ((6912, 256), BF),
            ((9, C2, 128), BF),
        ],
        [],
        1_000_000_000,
    )
    xs, dsl, pools, grad_b = call(
        forward_kernel,
        [where, own_xs, recv_a, recv_b, ta, tb, cotangent],
        [
            ((cube_count, ZD + 2 * HALO, 4, 16, 1152), BF),
            ((cube_count, 6, 2, 16, 2048), BF),
            ((cube_count, 4, 3, 16, 1152), BF),
            ((cube_count, 2, 16, 2048), BF),
        ],
        [pltpu.VMEM((cube_count, 4, 16, 1024), BF)],
        8_000_000_000,
        smem=1,
        aliases={1: 0},
    )
    back_a, back_b = swap(grad_b, grad_b, ring)
    share_b, share_a = ROWS_B // samples, ROWS_A // samples
    parts_b = call(
        terms_b_kernel,
        [where, pools, grad_b],
        [((share_b, 128), BF)] * samples,
        [pltpu.VMEM((ROWS_B, 128), F32)],
        1_000_000_000,
        smem=1,
    )
    others_b = swap_samples(parts_b, samples)
    ga, partial_a = call(
        backward_kernel,
        [where, grad_b, back_a, back_b, tbt, dsl, xs, parts_b[0]],
        [((cube_count, 6, 4, 16, 2304), BF), ((samples, share_a, 128), BF)],
        [
            pltpu.VMEM((cube_count, 6, 3, 16, 2304), BF),
            pltpu.VMEM((cube_count, 6, 4, 16, 2304), BF),
            pltpu.VMEM((cube_count, 4, 16, 1024), F32),
            pltpu.VMEM((256, 2304), F32),
            pltpu.VMEM((4, C1, 128), F32),
            pltpu.VMEM((ROWS_A, 128), F32),
            pltpu.SemaphoreType.DMA,
        ],
        6_000_000_000,
        smem=1,
        any_in=(7,),
        any_out=(0,),
    )
    (scattered_b,) = call(
        scatter_b_kernel,
        [partial_a, parts_b[0], *others_b],
        [((ring, share_b // ring, 128), BF)],
        [],
        1_000_000,
        any_in=(0,),
    )
    pieces_a = lax.all_to_all(partial_a, "sample", 0, 0)
    pieces_b = lax.all_to_all(scattered_b, "gz", 0, 0)
    (input_grad,) = call(
        input_kernel,
        [ga, wat],
        [((cube_count, ZD, SIDE, SIDE * C1), BF)],
        [
            pltpu.VMEM((6912, 256), BF),
            pltpu.VMEM((cube_count, 6, 4, 16, 2304), BF),
            pltpu.SemaphoreType.DMA,
        ],
        4_000_000_000,
        any_in=(0,),
    )
    (copies,) = call(
        exchange_kernel,
        [input_grad, pieces_b, pieces_a],
        [((ring, share_b // ring + share_a, 128), BF)],
        [],
        1_000_000,
        any_in=(0,),
    )
    pieces = lax.all_to_all(copies, "gz", 0, 0)
    (mine,) = call(collect_kernel, [pieces], [((share_b + share_a, 128), BF)], [], 1_000_000)
    scale = jnp.full((1,), 1.0 / (cube_count * samples), F32)
    total_a, total_b = call(
        finish_kernel,
        [where, scale, mine, *swap_samples([mine] * samples, samples)],
        [((27, C1 * C2), F32), ((27, C2 * C3), F32)],
        [pltpu.VMEM((samples, share_b + share_a, 128), F32)],
        1_000_000,
        smem=2,
    )
    return input_grad, total_a, total_b


def solution(mesh):
    in_specs = (P("sample", "gz", None, None), P(), P(), P("sample", "gz", None, None))
    out_specs = (P("sample", "gz", None, None), P(), P())
    return jax.shard_map(shards, mesh=mesh, in_specs=in_specs, out_specs=out_specs, check_vma=False)
```

```python
import jax
import jax.numpy as jnp
from jax import lax
from jax.experimental import pallas as pl
from jax.experimental.pallas import tpu as pltpu
from jax.sharding import PartitionSpec as P

C1 = 32
C2 = 64
C3 = 128
SIDE = 32
ZD = 4
HALO = 3
ROWS_B = C1 * 2 * 28
ROWS_A = C1 // 2 * 28
BF = jnp.bfloat16
F32 = jnp.float32
VMEM = pl.BlockSpec(memory_space=pltpu.VMEM)
SMEM = pl.BlockSpec(memory_space=pltpu.SMEM)
ANY = pl.BlockSpec(memory_space=pl.ANY)


def dot(a, b):
    return jnp.dot(a, b, preferred_element_type=F32)


def dot_t(a, b):
    return lax.dot_general(a, b, (((0,), (0,)), ((), ())), preferred_element_type=F32)


def sigmoid(v):
    return pl.reciprocal(1.0 + jnp.exp(-v), approx=True)


def row_picker(variants, stride, columns):
    shape = (variants * 16, columns)
    row = lax.broadcasted_iota(jnp.int32, shape, 0)
    col = lax.broadcasted_iota(jnp.int32, shape, 1)
    return jnp.where(col == stride * (row % 16) + row // 16 - 1, 1.0, 0.0).astype(BF)


def rows_at(block, before, total):
    rows, lanes = block.shape
    parts = []
    if before:
        parts.append(jnp.zeros((before, lanes), block.dtype))
    parts.append(block)
    if total - before - rows:
        parts.append(jnp.zeros((total - before - rows, lanes), block.dtype))
    return jnp.concatenate(parts, axis=0) if len(parts) > 1 else block


def lanes_below(shape, bound):
    return lax.broadcasted_iota(jnp.int32, shape, 1) < bound


def halves(left, right):
    return jnp.where(lanes_below(left.shape, 64), left, right).astype(BF)


def spread_input(target, b, zz, plane, picker):
    plane = jnp.concatenate([jnp.zeros((32, 32), BF), plane, jnp.zeros((32, 96), BF)], axis=1)
    moved = dot(picker, plane).astype(BF)
    for v in range(4):
        target[b, zz, v] = moved[16 * v : 16 * v + 16]


def prepare_kernel(cubes, wa, wb, xs, ta, tb, tbt, wat):
    picker = row_picker(4, 2, 32)
    for b in range(cubes.shape[0]):
        for z in range(ZD):
            spread_input(xs, b, HALO + z, cubes[b, z], picker)
    for d in range(9):
        block = wa[d].astype(F32)
        block = jnp.concatenate([block, block], axis=1)
        for px in range(2):
            ta[256 * d : 256 * d + 256, 128 * px : 128 * px + 128] = halves(
                rows_at(block, 32 * px, 256), rows_at(block, 64 + 32 * px, 256)
            )
        wat[8 - d] = rows_at(block, 0, 128).T[:64].astype(BF)
        block = wb[d]
        for e in range(2):
            tb[256 * d : 256 * d + 256, 128 * e : 128 * e + 128] = rows_at(block, 64 * e, 256)
        turned = []
        for dx in (2, 1, 0):
            part = block[64 * dx : 64 * dx + 64].astype(F32)
            turned.append(jnp.concatenate([part, part], axis=0).T)
        block = jnp.concatenate(turned, axis=0)
        to = 768 * (8 - d)
        for e in range(2):
            tbt[to : to + 768, 128 * e : 128 * e + 128] = halves(
                rows_at(block, 256 * e, 768), rows_at(block, 256 * e + 128, 768)
            )


def forward_kernel(where, own, recv_a, recv_b, ta, tb, cot, xs, dsl, pools, grad_b, pooled):
    del own
    cube_count = xs.shape[0]
    even = where[0] % 2 == 0
    picker = row_picker(4, 2, 32)
    for b in range(cube_count):
        for z in range(HALO):
            far = ZD - HALO + z
            below = jnp.where(even, recv_b[b, far].astype(F32), recv_a[b, far].astype(F32)).astype(BF)
            above = jnp.where(even, recv_a[b, z].astype(F32), recv_b[b, z].astype(F32)).astype(BF)
            spread_input(xs, b, z, below, picker)
            spread_input(xs, b, HALO + ZD + z, above, picker)

    low = jnp.where(where[0] == 0, 0.0, 1.0)
    high = jnp.where(where[0] == where[1] - 1, 0.0, 1.0)
    rows = cube_count * 8 * 16

    def group(g, carry):
        lanes = pl.ds(pl.multiple_of(128 * g, 128), 256)
        stacks = []
        for p in range(2):
            stacks.append(
                jnp.concatenate(
                    [
                        xs[:, dz : dz + 8, p + dy, :, lanes].reshape(rows, 256)
                        for dz in range(3)
                        for dy in range(3)
                    ],
                    axis=1,
                )
            )
        pre = dot(jnp.concatenate(stacks, axis=0), ta[...])
        squash = sigmoid(pre)
        act = pre * squash
        slope = (squash + act * (1.0 - squash)).astype(BF).reshape(2, cube_count, 8, 16, 256)
        for p in range(2):
            dsl[:, :, p, :, pl.ds(pl.multiple_of(256 * g, 256), 256)] = slope[p][:, 1:7]
        act = act.reshape(2, cube_count, 4, 2, 16, 256)
        act = act[0] + act[1]
        act = act[:, :, 0] + act[:, :, 1]
        act = (act[..., :128] + act[..., 128:]) * 0.125
        out = pl.ds(pl.multiple_of(128 * g, 128), 128)
        for z in range(4):
            part = act[:, z]
            if z == 0:
                part = part * low
            if z == 3:
                part = part * high
            pooled[:, z, :, out] = part.astype(BF)
        return carry

    lax.fori_loop(0, 8, group, 0)

    shifter = row_picker(3, 1, 16)
    for b in range(cube_count):
        for z in range(4):
            plane = jnp.concatenate([jnp.zeros((16, 64), BF), pooled[b, z], jnp.zeros((16, 64), BF)], axis=1)
            moved = dot(shifter, plane).astype(BF)
            for v in range(3):
                pools[b, z, v] = moved[16 * v : 16 * v + 16]

    rows_b = cube_count * 2 * 16
    columns = []
    for dz in range(3):
        for dy in range(3):
            columns.append(
                jnp.concatenate(
                    [
                        pools[:, dz : dz + 2, dy, :, 128 * g : 128 * g + 256].reshape(rows_b, 256)
                        for g in range(8)
                    ],
                    axis=0,
                )
            )
    pre_b = dot(jnp.concatenate(columns, axis=1), tb[...])
    squash = sigmoid(pre_b)
    slope_b = squash + pre_b * squash * (1.0 - squash)
    row = lax.broadcasted_iota(jnp.int32, (16, 8), 0)
    twice = jnp.where(row // 2 == lax.broadcasted_iota(jnp.int32, (16, 8), 1), 0.125, 0.0).astype(BF)
    ups = [dot(twice, cot[b, 0]) for b in range(cube_count)]
    for g in range(8):
        part = slope_b[rows_b * g : rows_b * g + rows_b].reshape(cube_count, 2, 16, 256)
        up = jnp.stack([ups[b][:, 128 * g : 128 * g + 128] for b in range(cube_count)])
        for z in range(2):
            for e in range(2):
                at = 256 * g + 128 * e
                grad_b[:, z, :, at : at + 128] = (up * part[:, z, :, 128 * e : 128 * e + 128]).astype(BF)


def terms_b_kernel(where, pools, grad_b, *rest):
    outs, terms = rest[:-1], rest[-1]
    cube_count = grad_b.shape[0]
    rows_b = cube_count * 2 * 16
    grads = jnp.concatenate(
        [grad_b[:, :, :, 256 * g : 256 * g + 256].reshape(rows_b, 256) for g in range(8)], axis=0
    )
    terms[pl.ds(27, C2, stride=28), :] = jnp.zeros((C2, 128), F32)
    for dz in range(3):
        for dy in range(3):
            windows = jnp.concatenate(
                [
                    pools[:, dz : dz + 2, dy, :, 128 * g : 128 * g + 256].reshape(rows_b, 256)
                    for g in range(8)
                ],
                axis=0,
            )
            full = dot_t(windows, grads)
            for dx in range(3):
                term = full[64 * dx : 64 * dx + 64, :128] + full[64 * dx + 64 : 64 * dx + 128, 128:]
                terms[pl.ds(9 * dz + 3 * dy + dx, C2, stride=28), :] = term
    share = ROWS_B // len(outs)
    for k, out in enumerate(outs):
        chunk = where[2] ^ k
        out[...] = terms[pl.ds(pl.multiple_of(chunk * share, 8), share), :].astype(BF)


def tree(parts):
    while len(parts) > 1:
        parts = [left + right for left, right in zip(parts[::2], parts[1::2])]
    return parts[0]


def halve_kernel(where, after, *refs):
    del after
    parts, keep, send = refs[:-2], refs[-2], refs[-1]
    count = len(parts) // 2
    mine = jnp.concatenate(
        [
            tree([part[...].astype(F32) for part in parts[:count]]),
            tree([part[...].astype(F32) for part in parts[count:]]),
        ],
        axis=0,
    )
    half = keep.shape[0]
    low = where[0] % 2 == 0
    keep[...] = jnp.where(low, mine[:half], mine[half:]).astype(BF)
    send[...] = jnp.where(low, mine[half:], mine[:half]).astype(BF)


def add_kernel(after, *refs):
    del after
    parts, out = refs[:-1], refs[-1]
    out[...] = tree([part[...].astype(F32) for part in parts]).astype(BF)


def stack_kernel(where, *refs):
    parts, out = refs[:-1], refs[-1]
    for k, part in enumerate(parts):
        out[where[2] ^ k] = part[...]


def finish_kernel(where, scale, own, other, out_a, out_b, whole):
    core = where[0] % 2
    whole[core] = own[...].astype(F32)
    whole[1 - core] = other[...].astype(F32)
    count, half = own.shape[0], own.shape[1]
    for width, base, out in ((C2, 0, out_b), (C1 // 2, ROWS_B // count, out_a)):
        each = width // count
        for i in range(width):
            start = base + 28 * (i % each)
            piece = whole[start // half, i // each, start % half : start % half + 27]
            out[:, 128 * i : 128 * i + 128] = piece * scale[0]


def backward_kernel(where, grad_b, recv_a, recv_b, tbt, dsl, xs, after, ga, *rest):
    outs, (gs, gpool, acc, term, terms) = rest[:-5], rest[-5:]
    del after
    cube_count = grad_b.shape[0]
    even = where[0] % 2 == 0
    shifter = row_picker(3, 1, 16)

    def spread_plane(b, zz, plane):
        moved = dot(shifter, plane).astype(BF)
        for v in range(3):
            gs[b, zz, v, :, 128:2176] = moved[16 * v : 16 * v + 16]
            gs[b, zz, v, :, :128] = jnp.zeros((16, 128), BF)
            gs[b, zz, v, :, 2176:] = jnp.zeros((16, 128), BF)

    for b in range(cube_count):
        for z in range(2):
            spread_plane(b, 2 + z, grad_b[b, z])
            from_a, from_b = recv_a[b, z].astype(F32), recv_b[b, z].astype(F32)
            spread_plane(b, z, jnp.where(even, from_b, from_a).astype(BF))
            spread_plane(b, 4 + z, jnp.where(even, from_a, from_b).astype(BF))

    low = jnp.where(where[0] == 0, 0.0, 0.125)
    high = jnp.where(where[0] == where[1] - 1, 0.0, 0.125)
    rows = cube_count * 4 * 16
    columns = []
    for dz in range(3):
        for dy in range(3):
            columns.append(
                jnp.concatenate(
                    [gs[:, dz : dz + 4, dy, :, 512 * q : 512 * q + 768].reshape(rows, 768) for q in range(4)],
                    axis=0,
                )
            )
    back = dot(jnp.concatenate(columns, axis=1), tbt[...])
    for q in range(4):
        part = back[rows * q : rows * q + rows].reshape(cube_count, 4, 16, 256)
        for z in range(4):
            scale = low if z == 0 else high if z == 3 else 0.125
            gpool[:, z, :, 256 * q : 256 * q + 256] = part[:, z] * scale

    acc[...] = jnp.zeros_like(acc)
    ga[:, :, :, :, :128] = jnp.zeros((cube_count, 6, 4, 16, 128), BF)
    ga[:, :, :, :, 2176:] = jnp.zeros((cube_count, 6, 4, 16, 128), BF)
    rows_a = cube_count * 6 * 16
    own = cube_count * 4 * 16
    place = lax.broadcasted_iota(jnp.int32, (rows_a, 128), 0) % 16

    def group(g, carry):
        lanes = pl.ds(pl.multiple_of(128 * g, 128), 128)
        up = gpool[:, :, :, lanes]
        up = jnp.concatenate(
            [up[:, 0:1], up[:, 1:2], up[:, 1:2], up[:, 2:3], up[:, 2:3], up[:, 3:4]], axis=1
        ).reshape(rows_a, 128)
        sides = []
        for p in range(2):
            pair = []
            for px in range(2):
                at = pl.ds(pl.multiple_of(256 * g + 128 * px, 128), 128)
                grad = up * dsl[:, :, p, :, at].astype(F32).reshape(rows_a, 128)
                to = pl.ds(pl.multiple_of(256 * g + 128 * px + 128, 128), 128)
                kept = grad.astype(BF).reshape(cube_count, 6, 16, 128)
                ga[:, :, 1 + p, :, to] = kept
                pair.append(kept[:, 1:5].reshape(own, 128))
                if p == 1:
                    moved = jnp.where(place == 0, 0.0, pltpu.roll(grad, 1, 0))
                else:
                    moved = jnp.where(place == 15, 0.0, pltpu.roll(grad, rows_a - 1, 0))
                ga[:, :, 0 if p else 3, :, to] = moved.astype(BF).reshape(cube_count, 6, 16, 128)
            sides.append(jnp.concatenate(pair, axis=1))
        grads = jnp.concatenate(sides, axis=0)
        wide = pl.ds(pl.multiple_of(128 * g, 128), 256)
        windows = jnp.concatenate(
            [
                jnp.concatenate(
                    [
                        xs[:, HALO - 1 + dz : HALO + 3 + dz, p + dy, :, wide].reshape(own, 256)
                        for dz in range(3)
                        for dy in range(3)
                    ],
                    axis=1,
                )
                for p in range(2)
            ],
            axis=0,
        )
        acc[...] += dot_t(grads, windows)
        return carry

    lax.fori_loop(0, 8, group, 0)

    terms[pl.ds(27, C1 // 2, stride=28), :] = jnp.zeros((C1 // 2, 128), F32)
    mask = lanes_below((32, 128), 64)
    for d in range(9):
        full = acc[:, 256 * d : 256 * d + 256].T
        for dx in range(3):
            left = full[32 * dx : 32 * dx + 32, :128] + full[32 * dx + 32 : 32 * dx + 64, 128:]
            right = full[32 * dx + 64 : 32 * dx + 96, :128] + full[32 * dx + 96 : 32 * dx + 128, 128:]
            merged = jnp.where(mask, left, right)
            slot = (3 * d + dx) % 4
            term[slot] = merged + pltpu.roll(merged, 64, 1)
            evens = term[slot, pl.ds(0, C1 // 2, stride=2), :]
            odds = term[slot, pl.ds(1, C1 // 2, stride=2), :]
            terms[pl.ds(3 * d + dx, C1 // 2, stride=28), :] = jnp.where(mask[:16], evens, odds)
    share = ROWS_A // len(outs)
    for k, out in enumerate(outs):
        chunk = where[2] ^ k
        out[...] = terms[pl.ds(pl.multiple_of(chunk * share, 8), share), :].astype(BF)


RANKS = (-3, -1, 0, 2, 1, 3, 4, 6, 5, 7, 8, 10)


def mirror_kernel(wat, tat):
    lane = lax.broadcasted_iota(jnp.int32, (64, 128), 1)
    for d in range(9):
        block = wat[d].astype(F32)
        turned = [block if s == 0 else pltpu.roll(block, 32 * s, 1) for s in range(4)]
        for slot, rank in enumerate(RANKS):
            for half in range(2):
                start = 32 * (rank - 1 - 4 * half)
                keep = (lane >= start) & (lane < start + 96)
                value = jnp.where(keep, turned[(rank - 1) % 4], 0.0).astype(BF)
                tat[768 * d + 64 * slot : 768 * d + 64 * slot + 64, 128 * half : 128 * half + 128] = value


def one_cube(b, ga, tat, out, token, block, sem):
    rows = ZD * 16
    sides = []
    for p in range(2):
        columns = []
        for dz in range(3):
            for dy in range(3):
                columns.append(
                    jnp.concatenate(
                        [ga[b, dz : dz + ZD, p + dy, :, 512 * q : 512 * q + 768].reshape(rows, 768) for q in range(4)],
                        axis=0,
                    )
                )
        sides.append(jnp.concatenate(columns, axis=1))
    both = dot(jnp.concatenate(sides, axis=0), tat[...]).astype(BF).reshape(2, 4, ZD, 16, 256)
    row = lax.broadcasted_iota(jnp.int32, (32, 32), 0)
    col = lax.broadcasted_iota(jnp.int32, (32, 32), 1)
    mixer = jnp.where(col == row // 2 + 16 * (row % 2), 1.0, 0.0).astype(BF)
    for z in range(ZD):
        for q in range(4):
            pair = jnp.concatenate([both[0, q, z], both[1, q, z]], axis=0)
            block[z, :, 256 * q : 256 * q + 256] = dot(mixer, pair).astype(BF)
    leave = pltpu.make_async_copy(block, out.at[b], sem)
    leave.start()
    token[...] = jnp.zeros_like(token)
    leave.wait()


def first_cube_kernel(ga, wat, out, tat, token, block, sem):
    mirror_kernel(wat, tat)
    one_cube(0, ga, tat, out, token, block, sem)


def later_cube_kernel(b):
    def kernel(before, ga, tat, out, token, block, sem):
        del before
        one_cube(b, ga, tat, out, token, block, sem)

    return kernel


def call(kernel, args, outs, scratch, flops, smem=0, any_in=(), any_out=(), aliases=None):
    specs = [SMEM if i < smem else ANY if i in any_in else VMEM for i in range(len(args))]
    return pl.pallas_call(
        kernel,
        out_shape=[jax.ShapeDtypeStruct(shape, dtype) for shape, dtype in outs],
        in_specs=specs,
        out_specs=[ANY if i in any_out else VMEM for i in range(len(outs))],
        scratch_shapes=scratch,
        input_output_aliases=aliases or {},
        compiler_params=pltpu.CompilerParams(vmem_limit_bytes=28 * 1024 * 1024),
        cost_estimate=pl.CostEstimate(flops=flops, bytes_accessed=1_000_000, transcendentals=0),
    )(*args)


def swap(first, second, count):
    pairs_a = [(i, i ^ 1) for i in range(count)]
    pairs_b = [(i, ((i + 1) ^ 1) - 1) for i in range(1, count - 1)]
    return lax.ppermute(first, "gz", pairs_a), lax.ppermute(second, "gz", pairs_b)


def swap_along(parts, axis, step):
    count = lax.axis_size(axis)
    return [
        lax.ppermute(part, axis, [(i, i ^ (k * step)) for i in range(count)]) for k, part in enumerate(parts) if k
    ]


def shards(cubes, weight_a, weight_b, cotangent):
    cube_count = cubes.shape[0]
    ring = lax.axis_size("gz")
    samples = lax.axis_size("sample")
    where = jnp.stack([lax.axis_index("gz"), jnp.int32(ring), lax.axis_index("sample")]).astype(jnp.int32)
    recv_a, recv_b = swap(cubes, cubes, ring)

    own_xs, ta, tb, tbt, wat = call(
        prepare_kernel,
        [cubes, weight_a.reshape(9, 96, C2), weight_b.reshape(9, 192, C3)],
        [
            ((cube_count, ZD + 2 * HALO, 4, 16, 1152), BF),
            ((2304, 256), BF),
            ((2304, 256), BF),
            ((6912, 256), BF),
            ((9, C2, 128), BF),
        ],
        [],
        1_000_000_000,
    )
    xs, dsl, pools, grad_b = call(
        forward_kernel,
        [where, own_xs, recv_a, recv_b, ta, tb, cotangent],
        [
            ((cube_count, ZD + 2 * HALO, 4, 16, 1152), BF),
            ((cube_count, 6, 2, 16, 2048), BF),
            ((cube_count, 4, 3, 16, 1152), BF),
            ((cube_count, 2, 16, 2048), BF),
        ],
        [pltpu.VMEM((cube_count, 4, 16, 1024), BF)],
        8_000_000_000,
        smem=1,
        aliases={1: 0},
    )
    back_a, back_b = swap(grad_b, grad_b, ring)
    share_b, share_a = ROWS_B // samples, ROWS_A // samples
    parts_b = call(
        terms_b_kernel,
        [where, pools, grad_b],
        [((share_b, 128), BF)] * samples,
        [pltpu.VMEM((ROWS_B, 128), F32)],
        1_000_000_000,
        smem=1,
    )
    others_b = swap_along(parts_b, "sample", 1)
    ga, *parts_a = call(
        backward_kernel,
        [where, grad_b, back_a, back_b, tbt, dsl, xs, parts_b[0]],
        [((cube_count, 6, 4, 16, 2304), BF)] + [((share_a, 128), BF)] * samples,
        [
            pltpu.VMEM((cube_count, 6, 3, 16, 2304), BF),
            pltpu.VMEM((cube_count, 4, 16, 1024), F32),
            pltpu.VMEM((256, 2304), F32),
            pltpu.VMEM((4, C1, 128), F32),
            pltpu.VMEM((ROWS_A, 128), F32),
        ],
        6_000_000_000,
        smem=1,
    )
    others_a = swap_along(parts_a, "sample", 1)
    whole = ((cube_count, ZD, SIDE, SIDE * C1), BF)
    token = ((8, 128), F32)
    block = [pltpu.VMEM((ZD, SIDE, SIDE * C1), BF), pltpu.SemaphoreType.DMA]
    input_grad, tat, done = call(
        first_cube_kernel, [ga, wat], [whole, ((6912, 256), BF), token], block, 2_000_000_000, any_out=(0,)
    )
    half = (share_b + share_a) // 2
    small = [((half, 128), BF)]
    keep, send = call(
        halve_kernel, [where, done, parts_b[0], *others_b, parts_a[0], *others_a], small * 2, [], 1_000_000, smem=1
    )
    (keep,) = call(add_kernel, [done, keep, *swap_along([send] * 2, "gz", 1)], small, [], 1_000_000)
    others = swap_along([keep] * (ring // 2), "gz", 2)
    for b in range(1, cube_count):
        input_grad, done = call(
            later_cube_kernel(b),
            [input_grad, ga, tat],
            [whole, token],
            block,
            2_000_000_000,
            any_in=(0,),
            any_out=(0,),
            aliases={0: 0},
        )
    (keep,) = call(add_kernel, [done, keep, *others], small, [], 1_000_000)
    shape = (samples, half, 128)
    (own,) = call(
        stack_kernel, [where, keep, *swap_along([keep] * samples, "sample", 1)], [(shape, BF)], [], 1_000_000, smem=1
    )
    (other,) = swap_along([own] * 2, "gz", 1)
    scale = jnp.full((1,), 1.0 / (cube_count * samples), F32)
    total_a, total_b = call(
        finish_kernel,
        [where, scale, own, other],
        [((27, C1 * C2), F32), ((27, C2 * C3), F32)],
        [pltpu.VMEM((2, *shape), F32)],
        1_000_000,
        smem=2,
    )
    return input_grad, total_a, total_b


def solution(mesh):
    in_specs = (P("sample", "gz", None, None), P(), P(), P("sample", "gz", None, None))
    out_specs = (P("sample", "gz", None, None), P(), P())
    return jax.shard_map(shards, mesh=mesh, in_specs=in_specs, out_specs=out_specs, check_vma=False)
```

```python
import jax
import jax.numpy as jnp
from jax import lax
from jax.experimental import pallas as pl
from jax.experimental.pallas import tpu as pltpu
from jax.sharding import PartitionSpec as P

C1 = 32
C2 = 64
C3 = 128
SIDE = 32
ZD = 4
HALO = 3
ROWS_B = C1 * 2 * 28
ROWS_A = C1 // 2 * 28
BF = jnp.bfloat16
F32 = jnp.float32
VMEM = pl.BlockSpec(memory_space=pltpu.VMEM)
SMEM = pl.BlockSpec(memory_space=pltpu.SMEM)
ANY = pl.BlockSpec(memory_space=pl.ANY)


def dot(a, b):
    return jnp.dot(a, b, preferred_element_type=F32)


def dot_t(a, b):
    return lax.dot_general(a, b, (((0,), (0,)), ((), ())), preferred_element_type=F32)


def sigmoid(v):
    return pl.reciprocal(1.0 + jnp.exp(-v), approx=True)


def row_picker(variants, stride, columns):
    shape = (variants * 16, columns)
    row = lax.broadcasted_iota(jnp.int32, shape, 0)
    col = lax.broadcasted_iota(jnp.int32, shape, 1)
    return jnp.where(col == stride * (row % 16) + row // 16 - 1, 1.0, 0.0).astype(BF)


def rows_at(block, before, total):
    rows, lanes = block.shape
    parts = []
    if before:
        parts.append(jnp.zeros((before, lanes), block.dtype))
    parts.append(block)
    if total - before - rows:
        parts.append(jnp.zeros((total - before - rows, lanes), block.dtype))
    return jnp.concatenate(parts, axis=0) if len(parts) > 1 else block


def lanes_below(shape, bound):
    return lax.broadcasted_iota(jnp.int32, shape, 1) < bound


def halves(left, right):
    return jnp.where(lanes_below(left.shape, 64), left, right).astype(BF)


def spread_input(target, b, zz, plane, picker):
    plane = jnp.concatenate([jnp.zeros((32, 32), BF), plane, jnp.zeros((32, 96), BF)], axis=1)
    moved = dot(picker, plane).astype(BF)
    for v in range(4):
        target[b, zz, v] = moved[16 * v : 16 * v + 16]


RANKS = (-3, -1, 0, 2, 1, 3, 4, 6, 5, 7, 8, 10)


def mirror(d, block, tat):
    lane = lax.broadcasted_iota(jnp.int32, (64, 128), 1)
    turned = [block if s == 0 else pltpu.roll(block, 32 * s, 1) for s in range(4)]
    for slot, rank in enumerate(RANKS):
        for half in range(2):
            start = 32 * (rank - 1 - 4 * half)
            keep = (lane >= start) & (lane < start + 96)
            value = jnp.where(keep, turned[(rank - 1) % 4], 0.0).astype(BF)
            tat[768 * d + 64 * slot : 768 * d + 64 * slot + 64, 128 * half : 128 * half + 128] = value


def prepare_kernel(cubes, wa, wb, xs, ta, tb, tbt, tat):
    picker = row_picker(4, 2, 32)
    for b in range(cubes.shape[0]):
        for z in range(ZD):
            spread_input(xs, b, HALO + z, cubes[b, z], picker)
    for d in range(9):
        block = wa[d].astype(F32)
        block = jnp.concatenate([block, block], axis=1)
        for px in range(2):
            ta[256 * d : 256 * d + 256, 128 * px : 128 * px + 128] = halves(
                rows_at(block, 32 * px, 256), rows_at(block, 64 + 32 * px, 256)
            )
        mirror(8 - d, rows_at(block, 0, 128).T[:64], tat)
        block = wb[d]
        for e in range(2):
            tb[256 * d : 256 * d + 256, 128 * e : 128 * e + 128] = rows_at(block, 64 * e, 256)
        turned = []
        for dx in (2, 1, 0):
            part = block[64 * dx : 64 * dx + 64].astype(F32)
            turned.append(jnp.concatenate([part, part], axis=0).T)
        block = jnp.concatenate(turned, axis=0)
        to = 768 * (8 - d)
        for e in range(2):
            tbt[to : to + 768, 128 * e : 128 * e + 128] = halves(
                rows_at(block, 256 * e, 768), rows_at(block, 256 * e + 128, 768)
            )


def forward_kernel(where, own, recv_a, recv_b, ta, tb, cot, xs, dsl, pools, grad_b, pooled, pre_even, pre_odd):
    del own
    cube_count = xs.shape[0]
    even = where[0] % 2 == 0
    picker = row_picker(4, 2, 32)
    for b in range(cube_count):
        for z in range(HALO):
            far = ZD - HALO + z
            below = jnp.where(even, recv_b[b, far].astype(F32), recv_a[b, far].astype(F32)).astype(BF)
            above = jnp.where(even, recv_a[b, z].astype(F32), recv_b[b, z].astype(F32)).astype(BF)
            spread_input(xs, b, z, below, picker)
            spread_input(xs, b, HALO + ZD + z, above, picker)

    low = jnp.where(where[0] == 0, 0.0, 1.0)
    high = jnp.where(where[0] == where[1] - 1, 0.0, 1.0)
    rows = cube_count * 8 * 16

    def product(g, target):
        lanes = pl.ds(128 * g if isinstance(g, int) else pl.multiple_of(128 * g, 128), 256)
        stacks = []
        for p in range(2):
            stacks.append(
                jnp.concatenate(
                    [
                        xs[:, dz : dz + 8, p + dy, :, lanes].reshape(rows, 256)
                        for dz in range(3)
                        for dy in range(3)
                    ],
                    axis=1,
                )
            )
        target[...] = dot(jnp.concatenate(stacks, axis=0), ta[...])

    def pool(g, source):
        pre = source[...]
        squash = sigmoid(pre)
        act = pre * squash
        slope = (squash + act * (1.0 - squash)).astype(BF).reshape(2, cube_count, 8, 16, 256)
        for p in range(2):
            to = pl.ds(256 * g if isinstance(g, int) else pl.multiple_of(256 * g, 256), 256)
            dsl[:, :, p, :, to] = slope[p][:, 1:7]
        act = act.reshape(2, cube_count, 4, 2, 16, 256)
        act = act[0] + act[1]
        act = act[:, :, 0] + act[:, :, 1]
        act = (act[..., :128] + act[..., 128:]) * 0.125
        out = pl.ds(128 * g if isinstance(g, int) else pl.multiple_of(128 * g, 128), 128)
        for z in range(4):
            part = act[:, z]
            if z == 0:
                part = part * low
            if z == 3:
                part = part * high
            pooled[:, z, :, out] = part.astype(BF)

    def pair(i, carry):
        product(2 * i + 1, pre_odd)
        pool(2 * i, pre_even)
        product(2 * i + 2, pre_even)
        pool(2 * i + 1, pre_odd)
        return carry

    product(0, pre_even)
    lax.fori_loop(0, 3, pair, 0)
    product(7, pre_odd)
    pool(6, pre_even)
    pool(7, pre_odd)

    shifter = row_picker(3, 1, 16)
    for b in range(cube_count):
        for z in range(4):
            plane = jnp.concatenate([jnp.zeros((16, 64), BF), pooled[b, z], jnp.zeros((16, 64), BF)], axis=1)
            moved = dot(shifter, plane).astype(BF)
            for v in range(3):
                pools[b, z, v] = moved[16 * v : 16 * v + 16]

    rows_b = cube_count * 2 * 16
    columns = []
    for dz in range(3):
        for dy in range(3):
            columns.append(
                jnp.concatenate(
                    [
                        pools[:, dz : dz + 2, dy, :, 128 * g : 128 * g + 256].reshape(rows_b, 256)
                        for g in range(8)
                    ],
                    axis=0,
                )
            )
    pre_b = dot(jnp.concatenate(columns, axis=1), tb[...])
    squash = sigmoid(pre_b)
    slope_b = squash + pre_b * squash * (1.0 - squash)
    row = lax.broadcasted_iota(jnp.int32, (16, 8), 0)
    twice = jnp.where(row // 2 == lax.broadcasted_iota(jnp.int32, (16, 8), 1), 0.125, 0.0).astype(BF)
    ups = [dot(twice, cot[b, 0]) for b in range(cube_count)]
    for g in range(8):
        part = slope_b[rows_b * g : rows_b * g + rows_b].reshape(cube_count, 2, 16, 256)
        up = jnp.stack([ups[b][:, 128 * g : 128 * g + 128] for b in range(cube_count)])
        for z in range(2):
            for e in range(2):
                at = 256 * g + 128 * e
                grad_b[:, z, :, at : at + 128] = (up * part[:, z, :, 128 * e : 128 * e + 128]).astype(BF)


def terms_b_kernel(where, pools, grad_b, *rest):
    outs, terms = rest[:-1], rest[-1]
    cube_count = grad_b.shape[0]
    rows_b = cube_count * 2 * 16
    grads = jnp.concatenate(
        [grad_b[:, :, :, 256 * g : 256 * g + 256].reshape(rows_b, 256) for g in range(8)], axis=0
    )
    terms[pl.ds(27, C2, stride=28), :] = jnp.zeros((C2, 128), F32)
    for dz in range(3):
        for dy in range(3):
            windows = jnp.concatenate(
                [
                    pools[:, dz : dz + 2, dy, :, 128 * g : 128 * g + 256].reshape(rows_b, 256)
                    for g in range(8)
                ],
                axis=0,
            )
            full = dot_t(windows, grads)
            for dx in range(3):
                term = full[64 * dx : 64 * dx + 64, :128] + full[64 * dx + 64 : 64 * dx + 128, 128:]
                terms[pl.ds(9 * dz + 3 * dy + dx, C2, stride=28), :] = term
    share = ROWS_B // len(outs)
    for k, out in enumerate(outs):
        chunk = where[2] ^ k
        out[...] = terms[pl.ds(pl.multiple_of(chunk * share, 8), share), :].astype(BF)


def tree(parts):
    while len(parts) > 1:
        parts = [left + right for left, right in zip(parts[::2], parts[1::2])]
    return parts[0]


def halve_kernel(where, after, *refs):
    del after
    parts, keep, send = refs[:-2], refs[-2], refs[-1]
    count = len(parts) // 2
    mine = jnp.concatenate(
        [
            tree([part[...].astype(F32) for part in parts[:count]]),
            tree([part[...].astype(F32) for part in parts[count:]]),
        ],
        axis=0,
    )
    half = keep.shape[0]
    low = where[0] % 2 == 0
    keep[...] = jnp.where(low, mine[:half], mine[half:]).astype(BF)
    send[...] = jnp.where(low, mine[half:], mine[:half]).astype(BF)


def add_kernel(after, *refs):
    del after
    parts, out = refs[:-1], refs[-1]
    out[...] = tree([part[...].astype(F32) for part in parts]).astype(BF)


def stack_kernel(where, *refs):
    parts, out = refs[:-1], refs[-1]
    for k, part in enumerate(parts):
        out[where[2] ^ k] = part[...]


def finish_kernel(where, scale, own, other, out_a, out_b, whole):
    core = where[0] % 2
    whole[core] = own[...].astype(F32)
    whole[1 - core] = other[...].astype(F32)
    count, half = own.shape[0], own.shape[1]
    for width, base, out in ((C2, 0, out_b), (C1 // 2, ROWS_B // count, out_a)):
        each = width // count
        for i in range(width):
            start = base + 28 * (i % each)
            piece = whole[start // half, i // each, start % half : start % half + 27]
            out[:, 128 * i : 128 * i + 128] = piece * scale[0]


def backward_kernel(where, grad_b, recv_a, recv_b, tbt, dsl, xs, after, ga, *rest):
    outs, (gs, gpool, turned, term, terms) = rest[:-5], rest[-5:]
    del after
    cube_count = grad_b.shape[0]
    even = where[0] % 2 == 0
    shifter = row_picker(3, 1, 16)

    def spread_plane(b, zz, plane):
        moved = dot(shifter, plane).astype(BF)
        for v in range(3):
            gs[b, zz, v, :, 128:2176] = moved[16 * v : 16 * v + 16]
            gs[b, zz, v, :, :128] = jnp.zeros((16, 128), BF)
            gs[b, zz, v, :, 2176:] = jnp.zeros((16, 128), BF)

    for b in range(cube_count):
        for z in range(2):
            spread_plane(b, 2 + z, grad_b[b, z])
            from_a, from_b = recv_a[b, z].astype(F32), recv_b[b, z].astype(F32)
            spread_plane(b, z, jnp.where(even, from_b, from_a).astype(BF))
            spread_plane(b, 4 + z, jnp.where(even, from_a, from_b).astype(BF))

    low = jnp.where(where[0] == 0, 0.0, 0.125)
    high = jnp.where(where[0] == where[1] - 1, 0.0, 0.125)
    rows = cube_count * 4 * 16
    columns = []
    for dz in range(3):
        for dy in range(3):
            columns.append(
                jnp.concatenate(
                    [gs[:, dz : dz + 4, dy, :, 512 * q : 512 * q + 768].reshape(rows, 768) for q in range(4)],
                    axis=0,
                )
            )
    back = dot(jnp.concatenate(columns, axis=1), tbt[...])
    for q in range(4):
        part = back[rows * q : rows * q + rows].reshape(cube_count, 4, 16, 256)
        for z in range(4):
            scale = low if z == 0 else high if z == 3 else 0.125
            gpool[:, z, :, 256 * q : 256 * q + 256] = part[:, z] * scale

    ga[:, :, :, :, :128] = jnp.zeros((cube_count, 6, 4, 16, 128), BF)
    ga[:, :, :, :, 2176:] = jnp.zeros((cube_count, 6, 4, 16, 128), BF)
    rows_a = cube_count * 6 * 16
    own = cube_count * 4 * 16
    place = lax.broadcasted_iota(jnp.int32, (rows_a, 128), 0) % 16

    def group(g, carry):
        lanes = pl.ds(pl.multiple_of(128 * g, 128), 128)
        up = gpool[:, :, :, lanes]
        up = jnp.concatenate(
            [up[:, 0:1], up[:, 1:2], up[:, 1:2], up[:, 2:3], up[:, 2:3], up[:, 3:4]], axis=1
        ).reshape(rows_a, 128)
        for p in range(2):
            for px in range(2):
                at = pl.ds(pl.multiple_of(256 * g + 128 * px, 128), 128)
                grad = up * dsl[:, :, p, :, at].astype(F32).reshape(rows_a, 128)
                to = pl.ds(pl.multiple_of(256 * g + 128 * px + 128, 128), 128)
                kept = grad.astype(BF).reshape(cube_count, 6, 16, 128)
                ga[:, :, 1 + p, :, to] = kept
                turned[g, 128 * px : 128 * px + 128, own * p : own * p + own] = kept[:, 1:5].reshape(own, 128).T
                if p == 1:
                    moved = jnp.where(place == 0, 0.0, pltpu.roll(grad, 1, 0))
                else:
                    moved = jnp.where(place == 15, 0.0, pltpu.roll(grad, rows_a - 1, 0))
                ga[:, :, 0 if p else 3, :, to] = moved.astype(BF).reshape(cube_count, 6, 16, 128)
        return carry

    lax.fori_loop(0, 8, group, 0)

    terms[pl.ds(27, C1 // 2, stride=28), :] = jnp.zeros((C1 // 2, 128), F32)
    mask = lanes_below((32, 128), 64)
    for d in range(9):
        dz, dy = d // 3, d % 3
        windows = jnp.concatenate(
            [
                xs[:, HALO - 1 + dz : HALO + 3 + dz, p + dy, :, 128 * g : 128 * g + 256].reshape(own, 256)
                for g in range(8)
                for p in range(2)
            ],
            axis=0,
        )
        full = dot(jnp.concatenate([turned[g] for g in range(8)], axis=1), windows).T
        for dx in range(3):
            left = full[32 * dx : 32 * dx + 32, :128] + full[32 * dx + 32 : 32 * dx + 64, 128:]
            right = full[32 * dx + 64 : 32 * dx + 96, :128] + full[32 * dx + 96 : 32 * dx + 128, 128:]
            merged = jnp.where(mask, left, right)
            slot = (3 * d + dx) % 4
            term[slot] = merged + pltpu.roll(merged, 64, 1)
            evens = term[slot, pl.ds(0, C1 // 2, stride=2), :]
            odds = term[slot, pl.ds(1, C1 // 2, stride=2), :]
            terms[pl.ds(3 * d + dx, C1 // 2, stride=28), :] = jnp.where(mask[:16], evens, odds)
    share = ROWS_A // len(outs)
    for k, out in enumerate(outs):
        chunk = where[2] ^ k
        out[...] = terms[pl.ds(pl.multiple_of(chunk * share, 8), share), :].astype(BF)


def one_cube(b, ga, tat, out, landed):
    rows = ZD * 16
    sides = []
    for p in range(2):
        columns = []
        for dz in range(3):
            for dy in range(3):
                columns.append(
                    jnp.concatenate(
                        [ga[b, dz : dz + ZD, p + dy, :, 512 * q : 512 * q + 768].reshape(rows, 768) for q in range(4)],
                        axis=0,
                    )
                )
        sides.append(jnp.concatenate(columns, axis=1))
    both = dot(jnp.concatenate(sides, axis=0), tat[...]).astype(BF).reshape(2, 4, ZD, 16, 256)
    row = lax.broadcasted_iota(jnp.int32, (32, 32), 0)
    col = lax.broadcasted_iota(jnp.int32, (32, 32), 1)
    mixer = jnp.where(col == row // 2 + 16 * (row % 2), 1.0, 0.0).astype(BF)
    for z in range(ZD):
        for q in range(4):
            pair = jnp.concatenate([both[0, q, z], both[1, q, z]], axis=0)
            out[z, :, 256 * q : 256 * q + 256] = dot(mixer, pair).astype(BF)
        if landed is not None:
            landed(z)


def early_cube_kernel(b):
    def kernel(ga, tat, out):
        one_cube(b, ga, tat, out, None)

    return kernel


def last_cube_kernel(ga, tat, *rest):
    early, (out, token, block, sems) = rest[:-4], rest[-4:]
    last = len(early)
    copies = [pltpu.make_async_copy(cube, out.at[b], sems.at[b]) for b, cube in enumerate(early)]
    for copy in copies:
        copy.start()

    def landed(z):
        copy = pltpu.make_async_copy(block.at[z], out.at[last, z], sems.at[last + z])
        copy.start()
        copies.append(copy)

    one_cube(last, ga, tat, block, landed)
    token[...] = jnp.zeros_like(token)
    for copy in copies:
        copy.wait()


def call(kernel, args, outs, scratch, flops, smem=0, any_in=(), any_out=(), aliases=None):
    specs = [SMEM if i < smem else ANY if i in any_in else VMEM for i in range(len(args))]
    return pl.pallas_call(
        kernel,
        out_shape=[jax.ShapeDtypeStruct(shape, dtype) for shape, dtype in outs],
        in_specs=specs,
        out_specs=[ANY if i in any_out else VMEM for i in range(len(outs))],
        scratch_shapes=scratch,
        input_output_aliases=aliases or {},
        compiler_params=pltpu.CompilerParams(vmem_limit_bytes=28 * 1024 * 1024),
        cost_estimate=pl.CostEstimate(flops=flops, bytes_accessed=1_000_000, transcendentals=0),
    )(*args)


def swap(first, second, count):
    pairs_a = [(i, i ^ 1) for i in range(count)]
    pairs_b = [(i, ((i + 1) ^ 1) - 1) for i in range(1, count - 1)]
    return lax.ppermute(first, "gz", pairs_a), lax.ppermute(second, "gz", pairs_b)


def swap_along(parts, axis, step):
    count = lax.axis_size(axis)
    return [
        lax.ppermute(part, axis, [(i, i ^ (k * step)) for i in range(count)]) for k, part in enumerate(parts) if k
    ]


def shards(cubes, weight_a, weight_b, cotangent):
    cube_count = cubes.shape[0]
    ring = lax.axis_size("gz")
    samples = lax.axis_size("sample")
    where = jnp.stack([lax.axis_index("gz"), jnp.int32(ring), lax.axis_index("sample")]).astype(jnp.int32)
    recv_a, recv_b = swap(cubes, cubes, ring)

    own_xs, ta, tb, tbt, tat = call(
        prepare_kernel,
        [cubes, weight_a.reshape(9, 96, C2), weight_b.reshape(9, 192, C3)],
        [
            ((cube_count, ZD + 2 * HALO, 4, 16, 1152), BF),
            ((2304, 256), BF),
            ((2304, 256), BF),
            ((6912, 256), BF),
            ((6912, 256), BF),
        ],
        [],
        1_000_000_000,
    )
    xs, dsl, pools, grad_b = call(
        forward_kernel,
        [where, own_xs, recv_a, recv_b, ta, tb, cotangent],
        [
            ((cube_count, ZD + 2 * HALO, 4, 16, 1152), BF),
            ((cube_count, 6, 2, 16, 2048), BF),
            ((cube_count, 4, 3, 16, 1152), BF),
            ((cube_count, 2, 16, 2048), BF),
        ],
        [pltpu.VMEM((cube_count, 4, 16, 1024), BF)] + [pltpu.VMEM((cube_count * 256, 256), F32)] * 2,
        8_000_000_000,
        smem=1,
        aliases={1: 0},
    )
    back_a, back_b = swap(grad_b, grad_b, ring)
    share_b, share_a = ROWS_B // samples, ROWS_A // samples
    parts_b = call(
        terms_b_kernel,
        [where, pools, grad_b],
        [((share_b, 128), BF)] * samples,
        [pltpu.VMEM((ROWS_B, 128), F32)],
        1_000_000_000,
        smem=1,
    )
    others_b = swap_along(parts_b, "sample", 1)
    ga, *parts_a = call(
        backward_kernel,
        [where, grad_b, back_a, back_b, tbt, dsl, xs, parts_b[0]],
        [((cube_count, 6, 4, 16, 2304), BF)] + [((share_a, 128), BF)] * samples,
        [
            pltpu.VMEM((cube_count, 6, 3, 16, 2304), BF),
            pltpu.VMEM((cube_count, 4, 16, 1024), F32),
            pltpu.VMEM((8, 256, cube_count * 128), BF),
            pltpu.VMEM((4, C1, 128), F32),
            pltpu.VMEM((ROWS_A, 128), F32),
        ],
        6_000_000_000,
        smem=1,
    )
    others_a = swap_along(parts_a, "sample", 1)
    cube = (ZD, SIDE, SIDE * C1)
    early = [
        call(early_cube_kernel(b), [ga, tat], [(cube, BF)], [], 2_000_000_000)[0] for b in range(cube_count - 1)
    ]
    half = (share_b + share_a) // 2
    small = [((half, 128), BF)]
    keep, send = call(
        halve_kernel, [where, early[0], parts_b[0], *others_b, parts_a[0], *others_a], small * 2, [], 1_000_000, smem=1
    )
    (keep,) = call(add_kernel, [where, keep, *swap_along([send] * 2, "gz", 1)], small, [], 1_000_000, smem=1)
    others = swap_along([keep] * (ring // 2), "gz", 2)
    input_grad, done = call(
        last_cube_kernel,
        [ga, tat, *early],
        [((cube_count, *cube), BF), ((8, 128), F32)],
        [pltpu.VMEM(cube, BF), pltpu.SemaphoreType.DMA((cube_count - 1 + ZD,))],
        2_000_000_000,
        any_out=(0,),
    )
    (keep,) = call(add_kernel, [done, keep, *others], small, [], 1_000_000)
    shape = (samples, half, 128)
    (own,) = call(
        stack_kernel, [where, keep, *swap_along([keep] * samples, "sample", 1)], [(shape, BF)], [], 1_000_000, smem=1
    )
    (other,) = swap_along([own] * 2, "gz", 1)
    scale = jnp.full((1,), 1.0 / (cube_count * samples), F32)
    total_a, total_b = call(
        finish_kernel,
        [where, scale, own, other],
        [((27, C1 * C2), F32), ((27, C2 * C3), F32)],
        [pltpu.VMEM((2, *shape), F32)],
        1_000_000,
        smem=2,
    )
    return input_grad, total_a, total_b


def solution(mesh):
    in_specs = (P("sample", "gz", None, None), P(), P(), P("sample", "gz", None, None))
    out_specs = (P("sample", "gz", None, None), P(), P())
    return jax.shard_map(shards, mesh=mesh, in_specs=in_specs, out_specs=out_specs, check_vma=False)
```

```python
import jax
import jax.numpy as jnp
from jax import lax
from jax.experimental import pallas as pl
from jax.experimental.pallas import tpu as pltpu
from jax.sharding import PartitionSpec as P

C1 = 32
C2 = 64
C3 = 128
SIDE = 32
ZD = 4
HALO = 3
ROWS_B = C1 * 2 * 28
ROWS_A = C1 // 2 * 28
BF = jnp.bfloat16
F32 = jnp.float32
VMEM = pl.BlockSpec(memory_space=pltpu.VMEM)
SMEM = pl.BlockSpec(memory_space=pltpu.SMEM)
ANY = pl.BlockSpec(memory_space=pl.ANY)


def dot(a, b):
    return jnp.dot(a, b, preferred_element_type=F32)


def dot_t(a, b):
    return lax.dot_general(a, b, (((0,), (0,)), ((), ())), preferred_element_type=F32)


def sigmoid(v):
    return pl.reciprocal(1.0 + jnp.exp(-v), approx=True)


def row_picker(variants, stride, columns):
    shape = (variants * 16, columns)
    row = lax.broadcasted_iota(jnp.int32, shape, 0)
    col = lax.broadcasted_iota(jnp.int32, shape, 1)
    return jnp.where(col == stride * (row % 16) + row // 16 - 1, 1.0, 0.0).astype(BF)


def rows_at(block, before, total):
    rows, lanes = block.shape
    parts = []
    if before:
        parts.append(jnp.zeros((before, lanes), block.dtype))
    parts.append(block)
    if total - before - rows:
        parts.append(jnp.zeros((total - before - rows, lanes), block.dtype))
    return jnp.concatenate(parts, axis=0) if len(parts) > 1 else block


def lanes_below(shape, bound):
    return lax.broadcasted_iota(jnp.int32, shape, 1) < bound


def halves(left, right):
    return jnp.where(lanes_below(left.shape, 64), left, right).astype(BF)


def spread_input(target, b, zz, plane, picker):
    plane = jnp.concatenate([jnp.zeros((32, 32), BF), plane, jnp.zeros((32, 96), BF)], axis=1)
    moved = dot(picker, plane).astype(BF)
    for v in range(4):
        target[b, zz, v] = moved[16 * v : 16 * v + 16]


RANKS = (-3, -1, 0, 2, 1, 3, 4, 6, 5, 7, 8, 10)


def mirror(d, block, tat):
    lane = lax.broadcasted_iota(jnp.int32, (64, 128), 1)
    turned = [block if s == 0 else pltpu.roll(block, 32 * s, 1) for s in range(4)]
    for slot, rank in enumerate(RANKS):
        for half in range(2):
            start = 32 * (rank - 1 - 4 * half)
            keep = (lane >= start) & (lane < start + 96)
            value = jnp.where(keep, turned[(rank - 1) % 4], 0.0).astype(BF)
            tat[768 * d + 64 * slot : 768 * d + 64 * slot + 64, 128 * half : 128 * half + 128] = value


def prepare_kernel(cubes, wa, wb, xs, ta, tb, tbt, tat):
    picker = row_picker(4, 2, 32)
    for b in range(cubes.shape[0]):
        for z in range(ZD):
            spread_input(xs, b, HALO + z, cubes[b, z], picker)
    for d in range(9):
        block = wa[d].astype(F32)
        block = jnp.concatenate([block, block], axis=1)
        for px in range(2):
            ta[256 * d : 256 * d + 256, 128 * px : 128 * px + 128] = halves(
                rows_at(block, 32 * px, 256), rows_at(block, 64 + 32 * px, 256)
            )
        mirror(8 - d, rows_at(block, 0, 128).T[:64], tat)
        block = wb[d]
        for e in range(2):
            tb[256 * d : 256 * d + 256, 128 * e : 128 * e + 128] = rows_at(block, 64 * e, 256)
        turned = []
        for dx in (2, 1, 0):
            part = block[64 * dx : 64 * dx + 64].astype(F32)
            turned.append(jnp.concatenate([part, part], axis=0).T)
        block = jnp.concatenate(turned, axis=0)
        to = 768 * (8 - d)
        for e in range(2):
            tbt[to : to + 768, 128 * e : 128 * e + 128] = halves(
                rows_at(block, 256 * e, 768), rows_at(block, 256 * e + 128, 768)
            )


def forward_kernel(where, own, recv_a, recv_b, ta, tb, cot, xs, dsl, pools, grad_b, pooled):
    del own
    cube_count = xs.shape[0]
    even = where[0] % 2 == 0
    picker = row_picker(4, 2, 32)
    for b in range(cube_count):
        for z in range(HALO):
            far = ZD - HALO + z
            below = jnp.where(even, recv_b[b, far].astype(F32), recv_a[b, far].astype(F32)).astype(BF)
            above = jnp.where(even, recv_a[b, z].astype(F32), recv_b[b, z].astype(F32)).astype(BF)
            spread_input(xs, b, z, below, picker)
            spread_input(xs, b, HALO + ZD + z, above, picker)

    low = jnp.where(where[0] == 0, 0.0, 1.0)
    high = jnp.where(where[0] == where[1] - 1, 0.0, 1.0)
    rows = cube_count * 8 * 16

    def groups(i, carry):
        stacks = []
        for j in range(2):
            lanes = pl.ds(pl.multiple_of(256 * i + 128 * j, 128), 256)
            for p in range(2):
                stacks.append(
                    jnp.concatenate(
                        [
                            xs[:, dz : dz + 8, p + dy, :, lanes].reshape(rows, 256)
                            for dz in range(3)
                            for dy in range(3)
                        ],
                        axis=1,
                    )
                )
        pre = dot(jnp.concatenate(stacks, axis=0), ta[...])
        squash = sigmoid(pre)
        act = pre * squash
        slope = (squash + act * (1.0 - squash)).astype(BF).reshape(2, 2, cube_count, 8, 16, 256)
        act = act.reshape(2, 2, cube_count, 4, 2, 16, 256)
        for j in range(2):
            for p in range(2):
                to = pl.ds(pl.multiple_of(512 * i + 256 * j, 256), 256)
                dsl[:, :, p, :, to] = slope[j, p][:, 1:7]
            part = act[j, 0] + act[j, 1]
            part = part[:, :, 0] + part[:, :, 1]
            part = (part[..., :128] + part[..., 128:]) * 0.125
            out = pl.ds(pl.multiple_of(256 * i + 128 * j, 128), 128)
            for z in range(4):
                plane = part[:, z]
                if z == 0:
                    plane = plane * low
                if z == 3:
                    plane = plane * high
                pooled[:, z, :, out] = plane.astype(BF)
        return carry

    lax.fori_loop(0, 4, groups, 0)

    shifter = row_picker(3, 1, 16)
    for b in range(cube_count):
        for z in range(4):
            plane = jnp.concatenate([jnp.zeros((16, 64), BF), pooled[b, z], jnp.zeros((16, 64), BF)], axis=1)
            moved = dot(shifter, plane).astype(BF)
            for v in range(3):
                pools[b, z, v] = moved[16 * v : 16 * v + 16]

    rows_b = cube_count * 2 * 16
    columns = []
    for dz in range(3):
        for dy in range(3):
            columns.append(
                jnp.concatenate(
                    [
                        pools[:, dz : dz + 2, dy, :, 128 * g : 128 * g + 256].reshape(rows_b, 256)
                        for g in range(8)
                    ],
                    axis=0,
                )
            )
    pre_b = dot(jnp.concatenate(columns, axis=1), tb[...])
    squash = sigmoid(pre_b)
    slope_b = squash + pre_b * squash * (1.0 - squash)
    row = lax.broadcasted_iota(jnp.int32, (16, 8), 0)
    twice = jnp.where(row // 2 == lax.broadcasted_iota(jnp.int32, (16, 8), 1), 0.125, 0.0).astype(BF)
    ups = [dot(twice, cot[b, 0]) for b in range(cube_count)]
    for g in range(8):
        part = slope_b[rows_b * g : rows_b * g + rows_b].reshape(cube_count, 2, 16, 256)
        up = jnp.stack([ups[b][:, 128 * g : 128 * g + 128] for b in range(cube_count)])
        for z in range(2):
            for e in range(2):
                at = 256 * g + 128 * e
                grad_b[:, z, :, at : at + 128] = (up * part[:, z, :, 128 * e : 128 * e + 128]).astype(BF)


def terms_b_kernel(pools, grad_b, terms):
    cube_count = grad_b.shape[0]
    rows_b = cube_count * 2 * 16
    grads = jnp.concatenate(
        [grad_b[:, :, :, 256 * g : 256 * g + 256].reshape(rows_b, 256) for g in range(8)], axis=0
    )
    terms[pl.ds(27, C2, stride=28), :] = jnp.zeros((C2, 128), F32)
    for dz in range(3):
        for dy in range(3):
            windows = jnp.concatenate(
                [
                    pools[:, dz : dz + 2, dy, :, 128 * g : 128 * g + 256].reshape(rows_b, 256)
                    for g in range(8)
                ],
                axis=0,
            )
            full = dot_t(windows, grads)
            for dx in range(3):
                term = full[64 * dx : 64 * dx + 64, :128] + full[64 * dx + 64 : 64 * dx + 128, 128:]
                terms[pl.ds(9 * dz + 3 * dy + dx, C2, stride=28), :] = term


def tree(parts):
    while len(parts) > 1:
        parts = [left + right for left, right in zip(parts[::2], parts[1::2])]
    return parts[0]


def scatter_kernel(where, keep, recv, *outs):
    for k, out in enumerate(outs):
        part = where[2] ^ k
        out[...] = (keep[part].astype(F32) + recv[part].astype(F32)).astype(BF)


def add_kernel(after, *refs):
    del after
    parts, out = refs[:-1], refs[-1]
    out[...] = tree([part[...].astype(F32) for part in parts]).astype(BF)


def stack_kernel(where, *refs):
    parts, out = refs[:-1], refs[-1]
    for k, part in enumerate(parts):
        out[where[2] ^ k] = part[...]


def finish_kernel(where, scale, own, other, out_a, out_b, whole):
    core = where[0] % 2
    whole[core] = own[...].astype(F32)
    whole[1 - core] = other[...].astype(F32)
    count = own.shape[0]
    for width, base, out in ((C2, 0, out_b), (C1 // 2, ROWS_B // (2 * count), out_a)):
        each = width // (2 * count)
        for i in range(width):
            start = base + 28 * (i % each)
            piece = whole[i // each // count, i // each % count, start : start + 27]
            out[:, 128 * i : 128 * i + 128] = piece * scale[0]


def backward_kernel(where, grad_b, recv_a, recv_b, tbt, dsl, xs, terms_b, ga, keep, send, gs, gpool, acc, term, terms):
    cube_count = grad_b.shape[0]
    even = where[0] % 2 == 0
    shifter = row_picker(3, 1, 16)

    def spread_plane(b, zz, plane):
        moved = dot(shifter, plane).astype(BF)
        for v in range(3):
            gs[b, zz, v, :, 128:2176] = moved[16 * v : 16 * v + 16]
            gs[b, zz, v, :, :128] = jnp.zeros((16, 128), BF)
            gs[b, zz, v, :, 2176:] = jnp.zeros((16, 128), BF)

    for b in range(cube_count):
        for z in range(2):
            spread_plane(b, 2 + z, grad_b[b, z])
            from_a, from_b = recv_a[b, z].astype(F32), recv_b[b, z].astype(F32)
            spread_plane(b, z, jnp.where(even, from_b, from_a).astype(BF))
            spread_plane(b, 4 + z, jnp.where(even, from_a, from_b).astype(BF))

    low = jnp.where(where[0] == 0, 0.0, 0.125)
    high = jnp.where(where[0] == where[1] - 1, 0.0, 0.125)
    rows = cube_count * 4 * 16
    columns = []
    for dz in range(3):
        for dy in range(3):
            columns.append(
                jnp.concatenate(
                    [gs[:, dz : dz + 4, dy, :, 512 * q : 512 * q + 768].reshape(rows, 768) for q in range(4)],
                    axis=0,
                )
            )
    back = dot(jnp.concatenate(columns, axis=1), tbt[...])
    for q in range(4):
        part = back[rows * q : rows * q + rows].reshape(cube_count, 4, 16, 256)
        for z in range(4):
            scale = low if z == 0 else high if z == 3 else 0.125
            gpool[:, z, :, 256 * q : 256 * q + 256] = part[:, z] * scale

    ga[:, :, :, :, :128] = jnp.zeros((cube_count, 6, 4, 16, 128), BF)
    ga[:, :, :, :, 2176:] = jnp.zeros((cube_count, 6, 4, 16, 128), BF)
    rows_a = cube_count * 6 * 16
    own = cube_count * 4 * 16
    place = lax.broadcasted_iota(jnp.int32, (rows_a, 128), 0) % 16

    def one_group(g):
        lanes = pl.ds(pl.multiple_of(128 * g, 128), 128)
        up = gpool[:, :, :, lanes]
        up = jnp.concatenate(
            [up[:, 0:1], up[:, 1:2], up[:, 1:2], up[:, 2:3], up[:, 2:3], up[:, 3:4]], axis=1
        ).reshape(rows_a, 128)
        sides = []
        for p in range(2):
            pair = []
            for px in range(2):
                at = pl.ds(pl.multiple_of(256 * g + 128 * px, 128), 128)
                grad = up * dsl[:, :, p, :, at].astype(F32).reshape(rows_a, 128)
                to = pl.ds(pl.multiple_of(256 * g + 128 * px + 128, 128), 128)
                kept = grad.astype(BF).reshape(cube_count, 6, 16, 128)
                ga[:, :, 1 + p, :, to] = kept
                pair.append(kept[:, 1:5].reshape(own, 128))
                if p == 1:
                    moved = jnp.where(place == 0, 0.0, pltpu.roll(grad, 1, 0))
                else:
                    moved = jnp.where(place == 15, 0.0, pltpu.roll(grad, rows_a - 1, 0))
                ga[:, :, 0 if p else 3, :, to] = moved.astype(BF).reshape(cube_count, 6, 16, 128)
            sides.append(jnp.concatenate(pair, axis=1))
        wide = pl.ds(pl.multiple_of(128 * g, 128), 256)
        windows = [
            jnp.concatenate(
                [
                    xs[:, HALO - 1 + dz : HALO + 3 + dz, p + dy, :, wide].reshape(own, 256)
                    for dz in range(3)
                    for dy in range(3)
                ],
                axis=1,
            )
            for p in range(2)
        ]
        return sides, windows

    def groups(i, carry):
        first, second = one_group(2 * i), one_group(2 * i + 1)
        grads = jnp.concatenate(first[0] + second[0], axis=0)
        acc[...] += dot_t(grads, jnp.concatenate(first[1] + second[1], axis=0))
        return carry

    acc[...] = jnp.zeros_like(acc)
    lax.fori_loop(0, 4, groups, 0)

    terms[pl.ds(27, C1 // 2, stride=28), :] = jnp.zeros((C1 // 2, 128), F32)
    mask = lanes_below((32, 128), 64)
    for d in range(9):
        full = acc[:, 256 * d : 256 * d + 256].T
        for dx in range(3):
            left = full[32 * dx : 32 * dx + 32, :128] + full[32 * dx + 32 : 32 * dx + 64, 128:]
            right = full[32 * dx + 64 : 32 * dx + 96, :128] + full[32 * dx + 96 : 32 * dx + 128, 128:]
            merged = jnp.where(mask, left, right)
            slot = (3 * d + dx) % 4
            term[slot] = merged + pltpu.roll(merged, 64, 1)
            evens = term[slot, pl.ds(0, C1 // 2, stride=2), :]
            odds = term[slot, pl.ds(1, C1 // 2, stride=2), :]
            terms[pl.ds(3 * d + dx, C1 // 2, stride=28), :] = jnp.where(mask[:16], evens, odds)
    low = where[0] % 2 == 0
    count = keep.shape[0]
    for part in range(count):
        sides = []
        for core in range(2):
            at = core * count + part
            rows_b, rows_a = ROWS_B // (2 * count), ROWS_A // (2 * count)
            sides.append(
                jnp.concatenate(
                    [terms_b[rows_b * at : rows_b * at + rows_b], terms[rows_a * at : rows_a * at + rows_a]], axis=0
                )
            )
        keep[part] = jnp.where(low, sides[0], sides[1]).astype(BF)
        send[part] = jnp.where(low, sides[1], sides[0]).astype(BF)


def one_cube(b, ga, tat, out, landed):
    rows = ZD * 16
    sides = []
    for p in range(2):
        columns = []
        for dz in range(3):
            for dy in range(3):
                columns.append(
                    jnp.concatenate(
                        [ga[b, dz : dz + ZD, p + dy, :, 512 * q : 512 * q + 768].reshape(rows, 768) for q in range(4)],
                        axis=0,
                    )
                )
        sides.append(jnp.concatenate(columns, axis=1))
    both = dot(jnp.concatenate(sides, axis=0), tat[...]).astype(BF).reshape(2, 4, ZD, 16, 256)
    row = lax.broadcasted_iota(jnp.int32, (32, 32), 0)
    col = lax.broadcasted_iota(jnp.int32, (32, 32), 1)
    mixer = jnp.where(col == row // 2 + 16 * (row % 2), 1.0, 0.0).astype(BF)
    for z in range(ZD):
        for q in range(4):
            pair = jnp.concatenate([both[0, q, z], both[1, q, z]], axis=0)
            out[z, :, 256 * q : 256 * q + 256] = dot(mixer, pair).astype(BF)
        if landed is not None:
            landed(z)


def early_cube_kernel(b):
    def kernel(ga, tat, out):
        one_cube(b, ga, tat, out, None)

    return kernel


def last_cube_kernel(ga, tat, *rest):
    early, (out, token, block, sems) = rest[:-4], rest[-4:]
    last = len(early)
    copies = [pltpu.make_async_copy(cube, out.at[b], sems.at[b]) for b, cube in enumerate(early)]
    for copy in copies:
        copy.start()

    def landed(z):
        copy = pltpu.make_async_copy(block.at[z], out.at[last, z], sems.at[last + z])
        copy.start()
        copies.append(copy)

    one_cube(last, ga, tat, block, landed)
    token[...] = jnp.zeros_like(token)
    for copy in copies:
        copy.wait()


def call(kernel, args, outs, scratch, flops, smem=0, any_in=(), any_out=(), aliases=None):
    specs = [SMEM if i < smem else ANY if i in any_in else VMEM for i in range(len(args))]
    return pl.pallas_call(
        kernel,
        out_shape=[jax.ShapeDtypeStruct(shape, dtype) for shape, dtype in outs],
        in_specs=specs,
        out_specs=[ANY if i in any_out else VMEM for i in range(len(outs))],
        scratch_shapes=scratch,
        input_output_aliases=aliases or {},
        compiler_params=pltpu.CompilerParams(vmem_limit_bytes=28 * 1024 * 1024),
        cost_estimate=pl.CostEstimate(flops=flops, bytes_accessed=1_000_000, transcendentals=0),
    )(*args)


def swap(first, second, count):
    pairs_a = [(i, i ^ 1) for i in range(count)]
    pairs_b = [(i, ((i + 1) ^ 1) - 1) for i in range(1, count - 1)]
    return lax.ppermute(first, "gz", pairs_a), lax.ppermute(second, "gz", pairs_b)


def swap_along(parts, axis, step):
    count = lax.axis_size(axis)
    return [
        lax.ppermute(part, axis, [(i, i ^ (k * step)) for i in range(count)]) for k, part in enumerate(parts) if k
    ]


def shards(cubes, weight_a, weight_b, cotangent):
    cube_count = cubes.shape[0]
    ring = lax.axis_size("gz")
    samples = lax.axis_size("sample")
    where = jnp.stack([lax.axis_index("gz"), jnp.int32(ring), lax.axis_index("sample")]).astype(jnp.int32)
    recv_a, recv_b = swap(cubes, cubes, ring)

    own_xs, ta, tb, tbt, tat = call(
        prepare_kernel,
        [cubes, weight_a.reshape(9, 96, C2), weight_b.reshape(9, 192, C3)],
        [
            ((cube_count, ZD + 2 * HALO, 4, 16, 1152), BF),
            ((2304, 256), BF),
            ((2304, 256), BF),
            ((6912, 256), BF),
            ((6912, 256), BF),
        ],
        [],
        1_000_000_000,
    )
    xs, dsl, pools, grad_b = call(
        forward_kernel,
        [where, own_xs, recv_a, recv_b, ta, tb, cotangent],
        [
            ((cube_count, ZD + 2 * HALO, 4, 16, 1152), BF),
            ((cube_count, 6, 2, 16, 2048), BF),
            ((cube_count, 4, 3, 16, 1152), BF),
            ((cube_count, 2, 16, 2048), BF),
        ],
        [pltpu.VMEM((cube_count, 4, 16, 1024), BF)],
        8_000_000_000,
        smem=1,
        aliases={1: 0},
    )
    back_a, back_b = swap(grad_b, grad_b, ring)
    (terms_b,) = call(terms_b_kernel, [pools, grad_b], [((ROWS_B, 128), F32)], [], 1_000_000_000)
    piece = (ROWS_A + ROWS_B) // (2 * samples)
    pieces = ((samples, piece, 128), BF)
    ga, keep, send = call(
        backward_kernel,
        [where, grad_b, back_a, back_b, tbt, dsl, xs, terms_b],
        [((cube_count, 6, 4, 16, 2304), BF), pieces, pieces],
        [
            pltpu.VMEM((cube_count, 6, 3, 16, 2304), BF),
            pltpu.VMEM((cube_count, 4, 16, 1024), F32),
            pltpu.VMEM((256, 2304), F32),
            pltpu.VMEM((4, C1, 128), F32),
            pltpu.VMEM((ROWS_A, 128), F32),
        ],
        6_000_000_000,
        smem=1,
    )
    small = [((piece, 128), BF)]
    (recv,) = swap_along([send] * 2, "gz", 1)
    parts = call(scatter_kernel, [where, keep, recv], small * samples, [], 1_000_000, smem=1)
    others = swap_along(parts, "sample", 1)
    cube = (ZD, SIDE, SIDE * C1)
    early = [
        call(early_cube_kernel(b), [ga, tat], [(cube, BF)], [], 2_000_000_000)[0] for b in range(cube_count - 1)
    ]
    (mine,) = call(add_kernel, [early[0], parts[0], *others], small, [], 1_000_000)
    others = swap_along([mine] * (ring // 2), "gz", 2)
    input_grad, done = call(
        last_cube_kernel,
        [ga, tat, *early],
        [((cube_count, *cube), BF), ((8, 128), F32)],
        [pltpu.VMEM(cube, BF), pltpu.SemaphoreType.DMA((cube_count - 1 + ZD,))],
        2_000_000_000,
        any_out=(0,),
    )
    (mine,) = call(add_kernel, [done, mine, *others], small, [], 1_000_000)
    (own,) = call(
        stack_kernel, [where, mine, *swap_along([mine] * samples, "sample", 1)], [pieces], [], 1_000_000, smem=1
    )
    (other,) = swap_along([own] * 2, "gz", 1)
    scale = jnp.full((1,), 1.0 / (cube_count * samples), F32)
    total_a, total_b = call(
        finish_kernel,
        [where, scale, own, other],
        [((27, C1 * C2), F32), ((27, C2 * C3), F32)],
        [pltpu.VMEM((2, samples, piece, 128), F32)],
        1_000_000,
        smem=2,
    )
    return input_grad, total_a, total_b


def solution(mesh):
    in_specs = (P("sample", "gz", None, None), P(), P(), P("sample", "gz", None, None))
    out_specs = (P("sample", "gz", None, None), P(), P())
    return jax.shard_map(shards, mesh=mesh, in_specs=in_specs, out_specs=out_specs, check_vma=False)
```

```python
import jax
import jax.numpy as jnp
from jax import lax
from jax.experimental import pallas as pl
from jax.experimental.pallas import tpu as pltpu
from jax.sharding import PartitionSpec as P

C1 = 32
C2 = 64
C3 = 128
SIDE = 32
ZD = 4
HALO = 3
ROWS_B = C1 * 2 * 28
ROWS_A = C1 // 2 * 28
BF = jnp.bfloat16
F32 = jnp.float32
VMEM = pl.BlockSpec(memory_space=pltpu.VMEM)
SMEM = pl.BlockSpec(memory_space=pltpu.SMEM)
ANY = pl.BlockSpec(memory_space=pl.ANY)


def dot(a, b):
    return jnp.dot(a, b, preferred_element_type=F32)


def dot_t(a, b):
    return lax.dot_general(a, b, (((0,), (0,)), ((), ())), preferred_element_type=F32)


def sigmoid(v):
    return pl.reciprocal(1.0 + jnp.exp(-v), approx=True)


def row_picker(variants, stride, columns):
    shape = (variants * 16, columns)
    row = lax.broadcasted_iota(jnp.int32, shape, 0)
    col = lax.broadcasted_iota(jnp.int32, shape, 1)
    return jnp.where(col == stride * (row % 16) + row // 16 - 1, 1.0, 0.0).astype(BF)


def rows_at(block, before, total):
    rows, lanes = block.shape
    parts = []
    if before:
        parts.append(jnp.zeros((before, lanes), block.dtype))
    parts.append(block)
    if total - before - rows:
        parts.append(jnp.zeros((total - before - rows, lanes), block.dtype))
    return jnp.concatenate(parts, axis=0) if len(parts) > 1 else block


def lanes_below(shape, bound):
    return lax.broadcasted_iota(jnp.int32, shape, 1) < bound


def halves(left, right):
    return jnp.where(lanes_below(left.shape, 64), left, right).astype(BF)


def silu(pre):
    squash = sigmoid(pre)
    act = pre * squash
    return act, (squash + act * (1.0 - squash)).astype(BF)


def windows_a(xs, spans, p, start):
    lanes = pl.ds(start if isinstance(start, int) else pl.multiple_of(start, 128), 256)
    columns = []
    for dz in range(3):
        for dy in range(3):
            parts = [xs[:, first + dz : first + dz + planes, p + dy, :, lanes] for first, planes in spans]
            whole = jnp.concatenate(parts, axis=1) if len(parts) > 1 else parts[0]
            columns.append(whole.reshape(whole.shape[0] * whole.shape[1] * 16, 256))
    return jnp.concatenate(columns, axis=1)


def spread_input(target, b, zz, plane, picker):
    plane = jnp.concatenate([jnp.zeros((32, 32), BF), plane, jnp.zeros((32, 96), BF)], axis=1)
    moved = dot(picker, plane).astype(BF)
    for v in range(4):
        target[b, zz, v] = moved[16 * v : 16 * v + 16]


RANKS = (-3, -1, 0, 2, 1, 3, 4, 6, 5, 7, 8, 10)


def mirror(d, block, tat):
    lane = lax.broadcasted_iota(jnp.int32, (64, 128), 1)
    turned = [block if s == 0 else pltpu.roll(block, 32 * s, 1) for s in range(4)]
    for slot, rank in enumerate(RANKS):
        for half in range(2):
            start = 32 * (rank - 1 - 4 * half)
            keep = (lane >= start) & (lane < start + 96)
            value = jnp.where(keep, turned[(rank - 1) % 4], 0.0).astype(BF)
            tat[768 * d + 64 * slot : 768 * d + 64 * slot + 64, 128 * half : 128 * half + 128] = value


def prepare_kernel(cubes, wa, wb, xs, ta, tb, tbt, dsl, inner):
    picker = row_picker(4, 2, 32)
    for b in range(cubes.shape[0]):
        for z in range(ZD):
            spread_input(xs, b, HALO + z, cubes[b, z], picker)
    for d in range(9):
        block = wa[d].astype(F32)
        block = jnp.concatenate([block, block], axis=1)
        for px in range(2):
            ta[256 * d : 256 * d + 256, 128 * px : 128 * px + 128] = halves(
                rows_at(block, 32 * px, 256), rows_at(block, 64 + 32 * px, 256)
            )
        block = wb[d]
        for e in range(2):
            tb[256 * d : 256 * d + 256, 128 * e : 128 * e + 128] = rows_at(block, 64 * e, 256)
        turned = []
        for dx in (2, 1, 0):
            part = block[64 * dx : 64 * dx + 64].astype(F32)
            turned.append(jnp.concatenate([part, part], axis=0).T)
        block = jnp.concatenate(turned, axis=0)
        to = 768 * (8 - d)
        for e in range(2):
            tbt[to : to + 768, 128 * e : 128 * e + 128] = halves(
                rows_at(block, 256 * e, 768), rows_at(block, 256 * e + 128, 768)
            )

    cube_count = cubes.shape[0]
    pre = dot(
        jnp.concatenate(
            [windows_a(xs, ((HALO, 2),), p, 128 * g) for g in range(8) for p in range(2)], axis=0
        ),
        ta[...],
    )
    act, slope = silu(pre)
    slope = slope.reshape(8, 2, cube_count, 2, 16, 256)
    act = act.reshape(8, 2, cube_count, 2, 16, 256)
    for g in range(8):
        for p in range(2):
            dsl[:, 2:4, p, :, 256 * g : 256 * g + 256] = slope[g, p]
        part = act[g, 0] + act[g, 1]
        inner[:, :, :, 128 * g : 128 * g + 128] = part[..., :128] + part[..., 128:]


def forward_kernel(where, own, own_slope, inner, recv_a, recv_b, ta, tb, cot, xs, dsl, pools, grad_b, pooled):
    del own, own_slope
    cube_count = xs.shape[0]
    even = where[0] % 2 == 0
    picker = row_picker(4, 2, 32)
    for b in range(cube_count):
        for z in range(HALO):
            far = ZD - HALO + z
            below = jnp.where(even, recv_b[b, far].astype(F32), recv_a[b, far].astype(F32)).astype(BF)
            above = jnp.where(even, recv_a[b, z].astype(F32), recv_b[b, z].astype(F32)).astype(BF)
            spread_input(xs, b, z, below, picker)
            spread_input(xs, b, HALO + ZD + z, above, picker)

    low = jnp.where(where[0] == 0, 0.0, 0.125)
    high = jnp.where(where[0] == where[1] - 1, 0.0, 0.125)

    def groups(i, carry):
        pre = dot(
            jnp.concatenate(
                [
                    windows_a(xs, ((0, 3), (HALO + ZD - 2, 3)), p, 512 * i + 128 * j)
                    for j in range(4)
                    for p in range(2)
                ],
                axis=0,
            ),
            ta[...],
        )
        act, slope = silu(pre)
        slope = slope.reshape(4, 2, cube_count, 6, 16, 256)
        act = act.reshape(4, 2, cube_count, 6, 16, 256)
        for j in range(4):
            for p in range(2):
                to = pl.ds(pl.multiple_of(1024 * i + 256 * j, 256), 256)
                dsl[:, 0:2, p, :, to] = slope[j, p][:, 1:3]
                dsl[:, 4:6, p, :, to] = slope[j, p][:, 3:5]
            part = act[j, 0] + act[j, 1]
            part = part[..., :128] + part[..., 128:]
            out = pl.ds(pl.multiple_of(512 * i + 128 * j, 128), 128)
            pooled[:, 0, :, out] = ((part[:, 0] + part[:, 1]) * low).astype(BF)
            pooled[:, 1, :, out] = ((part[:, 2] + inner[:, 0, :, out]) * 0.125).astype(BF)
            pooled[:, 2, :, out] = ((part[:, 3] + inner[:, 1, :, out]) * 0.125).astype(BF)
            pooled[:, 3, :, out] = ((part[:, 4] + part[:, 5]) * high).astype(BF)
        return carry

    lax.fori_loop(0, 2, groups, 0)

    shifter = row_picker(3, 1, 16)
    for b in range(cube_count):
        for z in range(4):
            plane = jnp.concatenate([jnp.zeros((16, 64), BF), pooled[b, z], jnp.zeros((16, 64), BF)], axis=1)
            moved = dot(shifter, plane).astype(BF)
            for v in range(3):
                pools[b, z, v] = moved[16 * v : 16 * v + 16]

    rows_b = cube_count * 2 * 16
    columns = []
    for dz in range(3):
        for dy in range(3):
            columns.append(
                jnp.concatenate(
                    [
                        pools[:, dz : dz + 2, dy, :, 128 * g : 128 * g + 256].reshape(rows_b, 256)
                        for g in range(8)
                    ],
                    axis=0,
                )
            )
    pre_b = dot(jnp.concatenate(columns, axis=1), tb[...])
    squash = sigmoid(pre_b)
    slope_b = squash + pre_b * squash * (1.0 - squash)
    row = lax.broadcasted_iota(jnp.int32, (16, 8), 0)
    twice = jnp.where(row // 2 == lax.broadcasted_iota(jnp.int32, (16, 8), 1), 0.125, 0.0).astype(BF)
    ups = [dot(twice, cot[b, 0]) for b in range(cube_count)]
    for g in range(8):
        part = slope_b[rows_b * g : rows_b * g + rows_b].reshape(cube_count, 2, 16, 256)
        up = jnp.stack([ups[b][:, 128 * g : 128 * g + 128] for b in range(cube_count)])
        for z in range(2):
            for e in range(2):
                at = 256 * g + 128 * e
                grad_b[:, z, :, at : at + 128] = (up * part[:, z, :, 128 * e : 128 * e + 128]).astype(BF)


def spread_grad(target, b, zz, plane, shifter):
    moved = dot(shifter, plane).astype(BF)
    for v in range(3):
        target[b, zz, v, :, 128:2176] = moved[16 * v : 16 * v + 16]
        target[b, zz, v, :, :128] = jnp.zeros((16, 128), BF)
        target[b, zz, v, :, 2176:] = jnp.zeros((16, 128), BF)


def terms_b_kernel(pools, grad_b, wa, terms, gs, tat):
    cube_count = grad_b.shape[0]
    shifter = row_picker(3, 1, 16)
    for b in range(cube_count):
        for z in range(2):
            spread_grad(gs, b, 2 + z, grad_b[b, z], shifter)
    for d in range(9):
        block = wa[d].astype(F32)
        block = jnp.concatenate([block, block], axis=1)
        mirror(8 - d, rows_at(block, 0, 128).T[:64], tat)
    rows_b = cube_count * 2 * 16
    grads = jnp.concatenate(
        [grad_b[:, :, :, 256 * g : 256 * g + 256].reshape(rows_b, 256) for g in range(8)], axis=0
    )
    terms[pl.ds(27, C2, stride=28), :] = jnp.zeros((C2, 128), F32)
    for dz in range(3):
        for dy in range(3):
            windows = jnp.concatenate(
                [
                    pools[:, dz : dz + 2, dy, :, 128 * g : 128 * g + 256].reshape(rows_b, 256)
                    for g in range(8)
                ],
                axis=0,
            )
            full = dot_t(windows, grads)
            for dx in range(3):
                term = full[64 * dx : 64 * dx + 64, :128] + full[64 * dx + 64 : 64 * dx + 128, 128:]
                terms[pl.ds(9 * dz + 3 * dy + dx, C2, stride=28), :] = term


def tree(parts):
    while len(parts) > 1:
        parts = [left + right for left, right in zip(parts[::2], parts[1::2])]
    return parts[0]


def scatter_kernel(where, keep, recv, *outs):
    for k, out in enumerate(outs):
        part = where[2] ^ k
        out[...] = (keep[part].astype(F32) + recv[part].astype(F32)).astype(BF)


def add_kernel(after, *refs):
    del after
    parts, out = refs[:-1], refs[-1]
    out[...] = tree([part[...].astype(F32) for part in parts]).astype(BF)


def stack_kernel(where, *refs):
    parts, out = refs[:-1], refs[-1]
    for k, part in enumerate(parts):
        out[where[2] ^ k] = part[...]


def finish_kernel(where, scale, own, other, out_a, out_b, whole):
    core = where[0] % 2
    whole[core] = own[...].astype(F32)
    whole[1 - core] = other[...].astype(F32)
    count = own.shape[0]
    for width, base, out in ((C2, 0, out_b), (C1 // 2, ROWS_B // (2 * count), out_a)):
        each = width // (2 * count)
        for i in range(width):
            start = base + 28 * (i % each)
            piece = whole[i // each // count, i // each % count, start : start + 27]
            out[:, 128 * i : 128 * i + 128] = piece * scale[0]


def backward_kernel(where, own, recv_a, recv_b, tbt, dsl, xs, terms_b, ga, keep, send, gs, gpool, acc, term, terms):
    del own
    cube_count = recv_a.shape[0]
    even = where[0] % 2 == 0
    shifter = row_picker(3, 1, 16)

    for b in range(cube_count):
        for z in range(2):
            from_a, from_b = recv_a[b, z].astype(F32), recv_b[b, z].astype(F32)
            spread_grad(gs, b, z, jnp.where(even, from_b, from_a).astype(BF), shifter)
            spread_grad(gs, b, 4 + z, jnp.where(even, from_a, from_b).astype(BF), shifter)

    low = jnp.where(where[0] == 0, 0.0, 0.125)
    high = jnp.where(where[0] == where[1] - 1, 0.0, 0.125)
    rows = cube_count * 4 * 16
    columns = []
    for dz in range(3):
        for dy in range(3):
            columns.append(
                jnp.concatenate(
                    [gs[:, dz : dz + 4, dy, :, 512 * q : 512 * q + 768].reshape(rows, 768) for q in range(4)],
                    axis=0,
                )
            )
    back = dot(jnp.concatenate(columns, axis=1), tbt[...])
    for q in range(4):
        part = back[rows * q : rows * q + rows].reshape(cube_count, 4, 16, 256)
        for z in range(4):
            scale = low if z == 0 else high if z == 3 else 0.125
            gpool[:, z, :, 256 * q : 256 * q + 256] = part[:, z] * scale

    ga[:, :, :, :, :128] = jnp.zeros((cube_count, 6, 4, 16, 128), BF)
    ga[:, :, :, :, 2176:] = jnp.zeros((cube_count, 6, 4, 16, 128), BF)
    rows_a = cube_count * 6 * 16
    own_rows = cube_count * 4 * 16
    place = lax.broadcasted_iota(jnp.int32, (rows_a, 128), 0) % 16

    def one_group(g):
        lanes = pl.ds(pl.multiple_of(128 * g, 128), 128)
        up = gpool[:, :, :, lanes]
        up = jnp.concatenate(
            [up[:, 0:1], up[:, 1:2], up[:, 1:2], up[:, 2:3], up[:, 2:3], up[:, 3:4]], axis=1
        ).reshape(rows_a, 128)
        sides = []
        for p in range(2):
            pair = []
            for px in range(2):
                at = pl.ds(pl.multiple_of(256 * g + 128 * px, 128), 128)
                grad = up * dsl[:, :, p, :, at].astype(F32).reshape(rows_a, 128)
                to = pl.ds(pl.multiple_of(256 * g + 128 * px + 128, 128), 128)
                kept = grad.astype(BF).reshape(cube_count, 6, 16, 128)
                ga[:, :, 1 + p, :, to] = kept
                pair.append(kept[:, 1:5].reshape(own_rows, 128))
                if p == 1:
                    moved = jnp.where(place == 0, 0.0, pltpu.roll(grad, 1, 0))
                else:
                    moved = jnp.where(place == 15, 0.0, pltpu.roll(grad, rows_a - 1, 0))
                ga[:, :, 0 if p else 3, :, to] = moved.astype(BF).reshape(cube_count, 6, 16, 128)
            sides.append(jnp.concatenate(pair, axis=1))
        return sides, [windows_a(xs, ((HALO - 1, ZD),), p, 128 * g) for p in range(2)]

    def groups(i, carry):
        first, second = one_group(2 * i), one_group(2 * i + 1)
        grads = jnp.concatenate(first[0] + second[0], axis=0)
        acc[...] += dot_t(jnp.concatenate(first[1] + second[1], axis=0), grads)
        return carry

    acc[...] = jnp.zeros_like(acc)
    lax.fori_loop(0, 4, groups, 0)

    terms[pl.ds(27, C1 // 2, stride=28), :] = jnp.zeros((C1 // 2, 128), F32)
    mask = lanes_below((32, 128), 64)
    for d in range(9):
        full = acc[256 * d : 256 * d + 256]
        for dx in range(3):
            left = full[32 * dx : 32 * dx + 32, :128] + full[32 * dx + 32 : 32 * dx + 64, 128:]
            right = full[32 * dx + 64 : 32 * dx + 96, :128] + full[32 * dx + 96 : 32 * dx + 128, 128:]
            merged = jnp.where(mask, left, right)
            slot = (3 * d + dx) % 4
            term[slot] = merged + pltpu.roll(merged, 64, 1)
            evens = term[slot, pl.ds(0, C1 // 2, stride=2), :]
            odds = term[slot, pl.ds(1, C1 // 2, stride=2), :]
            terms[pl.ds(3 * d + dx, C1 // 2, stride=28), :] = jnp.where(mask[:16], evens, odds)
    low = where[0] % 2 == 0
    count = keep.shape[0]
    for part in range(count):
        sides = []
        for core in range(2):
            at = core * count + part
            rows_b, rows_a = ROWS_B // (2 * count), ROWS_A // (2 * count)
            sides.append(
                jnp.concatenate(
                    [terms_b[rows_b * at : rows_b * at + rows_b], terms[rows_a * at : rows_a * at + rows_a]], axis=0
                )
            )
        keep[part] = jnp.where(low, sides[0], sides[1]).astype(BF)
        send[part] = jnp.where(low, sides[1], sides[0]).astype(BF)


def one_cube(b, ga, tat, out, landed):
    rows = ZD * 16
    sides = []
    for p in range(2):
        columns = []
        for dz in range(3):
            for dy in range(3):
                columns.append(
                    jnp.concatenate(
                        [ga[b, dz : dz + ZD, p + dy, :, 512 * q : 512 * q + 768].reshape(rows, 768) for q in range(4)],
                        axis=0,
                    )
                )
        sides.append(jnp.concatenate(columns, axis=1))
    both = dot(jnp.concatenate(sides, axis=0), tat[...]).astype(BF).reshape(2, 4, ZD, 16, 256)
    row = lax.broadcasted_iota(jnp.int32, (32, 32), 0)
    col = lax.broadcasted_iota(jnp.int32, (32, 32), 1)
    mixer = jnp.where(col == row // 2 + 16 * (row % 2), 1.0, 0.0).astype(BF)
    for z in range(ZD):
        for q in range(4):
            pair = jnp.concatenate([both[0, q, z], both[1, q, z]], axis=0)
            out[z, :, 256 * q : 256 * q + 256] = dot(mixer, pair).astype(BF)
        if landed is not None:
            landed(z)


def early_cube_kernel(b):
    def kernel(ga, tat, out):
        one_cube(b, ga, tat, out, None)

    return kernel


def last_cube_kernel(ga, tat, *rest):
    early, (out, token, block, sems) = rest[:-4], rest[-4:]
    last = len(early)
    copies = [pltpu.make_async_copy(cube, out.at[b], sems.at[b]) for b, cube in enumerate(early)]
    for copy in copies:
        copy.start()

    def landed(z):
        copy = pltpu.make_async_copy(block.at[z], out.at[last, z], sems.at[last + z])
        copy.start()
        copies.append(copy)

    one_cube(last, ga, tat, block, landed)
    token[...] = jnp.zeros_like(token)
    for copy in copies:
        copy.wait()


def call(kernel, args, outs, scratch, flops, smem=0, any_in=(), any_out=(), aliases=None):
    specs = [SMEM if i < smem else ANY if i in any_in else VMEM for i in range(len(args))]
    return pl.pallas_call(
        kernel,
        out_shape=[jax.ShapeDtypeStruct(shape, dtype) for shape, dtype in outs],
        in_specs=specs,
        out_specs=[ANY if i in any_out else VMEM for i in range(len(outs))],
        scratch_shapes=scratch,
        input_output_aliases=aliases or {},
        compiler_params=pltpu.CompilerParams(vmem_limit_bytes=28 * 1024 * 1024),
        cost_estimate=pl.CostEstimate(flops=flops, bytes_accessed=1_000_000, transcendentals=0),
    )(*args)


def swap(first, second, count):
    pairs_a = [(i, i ^ 1) for i in range(count)]
    pairs_b = [(i, ((i + 1) ^ 1) - 1) for i in range(1, count - 1)]
    return lax.ppermute(first, "gz", pairs_a), lax.ppermute(second, "gz", pairs_b)


def swap_along(parts, axis, step):
    count = lax.axis_size(axis)
    return [
        lax.ppermute(part, axis, [(i, i ^ (k * step)) for i in range(count)]) for k, part in enumerate(parts) if k
    ]


def shards(cubes, weight_a, weight_b, cotangent):
    cube_count = cubes.shape[0]
    ring = lax.axis_size("gz")
    samples = lax.axis_size("sample")
    where = jnp.stack([lax.axis_index("gz"), jnp.int32(ring), lax.axis_index("sample")]).astype(jnp.int32)
    recv_a, recv_b = swap(cubes, cubes, ring)

    wa = weight_a.reshape(9, 96, C2)
    own_xs, ta, tb, tbt, own_slope, inner = call(
        prepare_kernel,
        [cubes, wa, weight_b.reshape(9, 192, C3)],
        [
            ((cube_count, ZD + 2 * HALO, 4, 16, 1152), BF),
            ((2304, 256), BF),
            ((2304, 256), BF),
            ((6912, 256), BF),
            ((cube_count, 6, 2, 16, 2048), BF),
            ((cube_count, 2, 16, 1024), F32),
        ],
        [],
        1_000_000_000,
    )
    xs, dsl, pools, grad_b = call(
        forward_kernel,
        [where, own_xs, own_slope, inner, recv_a, recv_b, ta, tb, cotangent],
        [
            ((cube_count, ZD + 2 * HALO, 4, 16, 1152), BF),
            ((cube_count, 6, 2, 16, 2048), BF),
            ((cube_count, 4, 3, 16, 1152), BF),
            ((cube_count, 2, 16, 2048), BF),
        ],
        [pltpu.VMEM((cube_count, 4, 16, 1024), BF)],
        8_000_000_000,
        smem=1,
        aliases={1: 0, 2: 1},
    )
    back_a, back_b = swap(grad_b, grad_b, ring)
    spread = ((cube_count, 6, 3, 16, 2304), BF)
    terms_b, own_gs, tat = call(
        terms_b_kernel, [pools, grad_b, wa], [((ROWS_B, 128), F32), spread, ((6912, 256), BF)], [], 1_000_000_000
    )
    piece = (ROWS_A + ROWS_B) // (2 * samples)
    pieces = ((samples, piece, 128), BF)
    ga, keep, send, _ = call(
        backward_kernel,
        [where, own_gs, back_a, back_b, tbt, dsl, xs, terms_b],
        [((cube_count, 6, 4, 16, 2304), BF), pieces, pieces, spread],
        [
            pltpu.VMEM((cube_count, 4, 16, 1024), F32),
            pltpu.VMEM((2304, 256), F32),
            pltpu.VMEM((4, C1, 128), F32),
            pltpu.VMEM((ROWS_A, 128), F32),
        ],
        6_000_000_000,
        smem=1,
        aliases={1: 3},
    )
    small = [((piece, 128), BF)]
    (recv,) = swap_along([send] * 2, "gz", 1)
    parts = call(scatter_kernel, [where, keep, recv], small * samples, [], 1_000_000, smem=1)
    others = swap_along(parts, "sample", 1)
    cube = (ZD, SIDE, SIDE * C1)
    early = [
        call(early_cube_kernel(b), [ga, tat], [(cube, BF)], [], 2_000_000_000)[0] for b in range(cube_count - 1)
    ]
    (mine,) = call(add_kernel, [early[0], parts[0], *others], small, [], 1_000_000)
    others = swap_along([mine] * (ring // 2), "gz", 2)
    input_grad, done = call(
        last_cube_kernel,
        [ga, tat, *early],
        [((cube_count, *cube), BF), ((8, 128), F32)],
        [pltpu.VMEM(cube, BF), pltpu.SemaphoreType.DMA((cube_count - 1 + ZD,))],
        2_000_000_000,
        any_out=(0,),
    )
    (mine,) = call(add_kernel, [done, mine, *others], small, [], 1_000_000)
    (own,) = call(
        stack_kernel, [where, mine, *swap_along([mine] * samples, "sample", 1)], [pieces], [], 1_000_000, smem=1
    )
    (other,) = swap_along([own] * 2, "gz", 1)
    scale = jnp.full((1,), 1.0 / (cube_count * samples), F32)
    total_a, total_b = call(
        finish_kernel,
        [where, scale, own, other],
        [((27, C1 * C2), F32), ((27, C2 * C3), F32)],
        [pltpu.VMEM((2, samples, piece, 128), F32)],
        1_000_000,
        smem=2,
    )
    return input_grad, total_a, total_b


def solution(mesh):
    in_specs = (P("sample", "gz", None, None), P(), P(), P("sample", "gz", None, None))
    out_specs = (P("sample", "gz", None, None), P(), P())
    return jax.shard_map(shards, mesh=mesh, in_specs=in_specs, out_specs=out_specs, check_vma=False)
```

```python
import jax
import jax.numpy as jnp
from jax import lax
from jax.experimental import pallas as pl
from jax.experimental.pallas import tpu as pltpu
from jax.sharding import PartitionSpec as P

C1 = 32
C2 = 64
C3 = 128
SIDE = 32
ZD = 4
HALO = 3
ROWS_B = C1 * 2 * 28
ROWS_A = C1 // 2 * 28
BF = jnp.bfloat16
F32 = jnp.float32
VMEM = pl.BlockSpec(memory_space=pltpu.VMEM)
SMEM = pl.BlockSpec(memory_space=pltpu.SMEM)
HBM = pl.BlockSpec(memory_space=pltpu.HBM)


def dot(a, b):
    return jnp.dot(a, b, preferred_element_type=F32)


def dot_t(a, b):
    return lax.dot_general(a, b, (((0,), (0,)), ((), ())), preferred_element_type=F32)


def sigmoid(v):
    return pl.reciprocal(1.0 + jnp.exp(-v), approx=True)


def row_picker(variants, stride, columns):
    shape = (variants * 16, columns)
    row = lax.broadcasted_iota(jnp.int32, shape, 0)
    col = lax.broadcasted_iota(jnp.int32, shape, 1)
    return jnp.where(col == stride * (row % 16) + row // 16 - 1, 1.0, 0.0).astype(BF)


def rows_at(block, before, total):
    rows, lanes = block.shape
    parts = []
    if before:
        parts.append(jnp.zeros((before, lanes), block.dtype))
    parts.append(block)
    if total - before - rows:
        parts.append(jnp.zeros((total - before - rows, lanes), block.dtype))
    return jnp.concatenate(parts, axis=0) if len(parts) > 1 else block


def lanes_below(shape, bound):
    return lax.broadcasted_iota(jnp.int32, shape, 1) < bound


def halves(left, right):
    return jnp.where(lanes_below(left.shape, 64), left, right).astype(BF)


def silu(pre):
    squash = sigmoid(pre)
    act = pre * squash
    return act, (squash + act * (1.0 - squash)).astype(BF)


def windows_a(xs, spans, p, start):
    lanes = pl.ds(start if isinstance(start, int) else pl.multiple_of(start, 128), 256)
    columns = []
    for dz in range(3):
        for dy in range(3):
            parts = [xs[:, first + dz : first + dz + planes, p + dy, :, lanes] for first, planes in spans]
            whole = jnp.concatenate(parts, axis=1) if len(parts) > 1 else parts[0]
            columns.append(whole.reshape(whole.shape[0] * whole.shape[1] * 16, 256))
    return jnp.concatenate(columns, axis=1)


def spread_input(target, b, zz, plane, picker):
    plane = jnp.concatenate([jnp.zeros((32, 32), BF), plane, jnp.zeros((32, 96), BF)], axis=1)
    moved = dot(picker, plane).astype(BF)
    for v in range(4):
        target[b, zz, v] = moved[16 * v : 16 * v + 16]


RANKS = (-3, -1, 0, 2, 1, 3, 4, 6, 5, 7, 8, 10)


def mirror(d, block, tat):
    lane = lax.broadcasted_iota(jnp.int32, (64, 128), 1)
    turned = [block if s == 0 else pltpu.roll(block, 32 * s, 1) for s in range(4)]
    for slot, rank in enumerate(RANKS):
        for half in range(2):
            start = 32 * (rank - 1 - 4 * half)
            keep = (lane >= start) & (lane < start + 96)
            value = jnp.where(keep, turned[(rank - 1) % 4], 0.0).astype(BF)
            tat[768 * d + 64 * slot : 768 * d + 64 * slot + 64, 128 * half : 128 * half + 128] = value


def prepare_kernel(cubes_in, wa, wb, xs, ta, tb, dsl, inner, cubes, sem):
    arrive = pltpu.make_async_copy(cubes_in, cubes, sem)
    arrive.start()
    picker = row_picker(4, 2, 32)
    for d in range(9):
        block = wa[d].astype(F32)
        block = jnp.concatenate([block, block], axis=1)
        for px in range(2):
            ta[256 * d : 256 * d + 256, 128 * px : 128 * px + 128] = halves(
                rows_at(block, 32 * px, 256), rows_at(block, 64 + 32 * px, 256)
            )
        block = wb[d]
        for e in range(2):
            tb[256 * d : 256 * d + 256, 128 * e : 128 * e + 128] = rows_at(block, 64 * e, 256)
    arrive.wait()
    for b in range(cubes.shape[0]):
        for z in range(ZD):
            spread_input(xs, b, HALO + z, cubes[b, z], picker)

    cube_count = cubes.shape[0]
    pre = dot(
        jnp.concatenate(
            [windows_a(xs, ((HALO, 2),), p, 128 * g) for g in range(8) for p in range(2)], axis=0
        ),
        ta[...],
    )
    act, slope = silu(pre)
    slope = slope.reshape(8, 2, cube_count, 2, 16, 256)
    act = act.reshape(8, 2, cube_count, 2, 16, 256)
    for g in range(8):
        for p in range(2):
            dsl[:, 2:4, p, :, 256 * g : 256 * g + 256] = slope[g, p]
        part = act[g, 0] + act[g, 1]
        inner[:, :, :, 128 * g : 128 * g + 128] = part[..., :128] + part[..., 128:]


def forward_kernel(where, own, own_slope, inner, recv_a, recv_b, ta, tb, cot, xs, dsl, pools, grad_b, pooled):
    del own, own_slope
    cube_count = xs.shape[0]
    even = where[0] % 2 == 0
    picker = row_picker(4, 2, 32)
    for b in range(cube_count):
        for z in range(HALO):
            far = ZD - HALO + z
            below = jnp.where(even, recv_b[b, far].astype(F32), recv_a[b, far].astype(F32)).astype(BF)
            above = jnp.where(even, recv_a[b, z].astype(F32), recv_b[b, z].astype(F32)).astype(BF)
            spread_input(xs, b, z, below, picker)
            spread_input(xs, b, HALO + ZD + z, above, picker)

    low = jnp.where(where[0] == 0, 0.0, 0.125)
    high = jnp.where(where[0] == where[1] - 1, 0.0, 0.125)

    def groups(i, carry):
        pre = dot(
            jnp.concatenate(
                [
                    windows_a(xs, ((0, 3), (HALO + ZD - 2, 3)), p, 512 * i + 128 * j)
                    for j in range(4)
                    for p in range(2)
                ],
                axis=0,
            ),
            ta[...],
        )
        act, slope = silu(pre)
        slope = slope.reshape(4, 2, cube_count, 6, 16, 256)
        act = act.reshape(4, 2, cube_count, 6, 16, 256)
        for j in range(4):
            for p in range(2):
                to = pl.ds(pl.multiple_of(1024 * i + 256 * j, 256), 256)
                dsl[:, 0:2, p, :, to] = slope[j, p][:, 1:3]
                dsl[:, 4:6, p, :, to] = slope[j, p][:, 3:5]
            part = act[j, 0] + act[j, 1]
            part = part[..., :128] + part[..., 128:]
            out = pl.ds(pl.multiple_of(512 * i + 128 * j, 128), 128)
            pooled[:, 0, :, out] = ((part[:, 0] + part[:, 1]) * low).astype(BF)
            pooled[:, 1, :, out] = ((part[:, 2] + inner[:, 0, :, out]) * 0.125).astype(BF)
            pooled[:, 2, :, out] = ((part[:, 3] + inner[:, 1, :, out]) * 0.125).astype(BF)
            pooled[:, 3, :, out] = ((part[:, 4] + part[:, 5]) * high).astype(BF)
        return carry

    lax.fori_loop(0, 2, groups, 0)

    shifter = row_picker(3, 1, 16)
    for b in range(cube_count):
        for z in range(4):
            plane = jnp.concatenate([jnp.zeros((16, 64), BF), pooled[b, z], jnp.zeros((16, 64), BF)], axis=1)
            moved = dot(shifter, plane).astype(BF)
            for v in range(3):
                pools[b, z, v] = moved[16 * v : 16 * v + 16]

    rows_b = cube_count * 2 * 16
    columns = []
    for dz in range(3):
        for dy in range(3):
            columns.append(
                jnp.concatenate(
                    [
                        pools[:, dz : dz + 2, dy, :, 128 * g : 128 * g + 256].reshape(rows_b, 256)
                        for g in range(8)
                    ],
                    axis=0,
                )
            )
    pre_b = dot(jnp.concatenate(columns, axis=1), tb[...])
    squash = sigmoid(pre_b)
    slope_b = squash + pre_b * squash * (1.0 - squash)
    row = lax.broadcasted_iota(jnp.int32, (16, 8), 0)
    twice = jnp.where(row // 2 == lax.broadcasted_iota(jnp.int32, (16, 8), 1), 0.125, 0.0).astype(BF)
    ups = [dot(twice, cot[b, 0]) for b in range(cube_count)]
    for g in range(8):
        part = slope_b[rows_b * g : rows_b * g + rows_b].reshape(cube_count, 2, 16, 256)
        up = jnp.stack([ups[b][:, 128 * g : 128 * g + 128] for b in range(cube_count)])
        for z in range(2):
            for e in range(2):
                at = 256 * g + 128 * e
                grad_b[:, z, :, at : at + 128] = (up * part[:, z, :, 128 * e : 128 * e + 128]).astype(BF)


def spread_grad(target, b, zz, plane, shifter):
    moved = dot(shifter, plane).astype(BF)
    for v in range(3):
        target[b, zz, v, :, 128:2176] = moved[16 * v : 16 * v + 16]
        target[b, zz, v, :, :128] = jnp.zeros((16, 128), BF)
        target[b, zz, v, :, 2176:] = jnp.zeros((16, 128), BF)


def terms_b_kernel(pools, grad_b, wa, wb, terms, gs, tat, tbt):
    cube_count = grad_b.shape[0]
    shifter = row_picker(3, 1, 16)
    for b in range(cube_count):
        for z in range(2):
            spread_grad(gs, b, 2 + z, grad_b[b, z], shifter)
    for d in range(9):
        block = wa[d].astype(F32)
        block = jnp.concatenate([block, block], axis=1)
        mirror(8 - d, rows_at(block, 0, 128).T[:64], tat)
        block = wb[d]
        turned = []
        for dx in (2, 1, 0):
            part = block[64 * dx : 64 * dx + 64].astype(F32)
            turned.append(jnp.concatenate([part, part], axis=0).T)
        block = jnp.concatenate(turned, axis=0)
        to = 768 * (8 - d)
        for e in range(2):
            tbt[to : to + 768, 128 * e : 128 * e + 128] = halves(
                rows_at(block, 256 * e, 768), rows_at(block, 256 * e + 128, 768)
            )
    rows_b = cube_count * 2 * 16
    grads = jnp.concatenate(
        [grad_b[:, :, :, 256 * g : 256 * g + 256].reshape(rows_b, 256) for g in range(8)], axis=0
    )
    terms[pl.ds(27, C2, stride=28), :] = jnp.zeros((C2, 128), F32)
    for dz in range(3):
        for dy in range(3):
            windows = jnp.concatenate(
                [
                    pools[:, dz : dz + 2, dy, :, 128 * g : 128 * g + 256].reshape(rows_b, 256)
                    for g in range(8)
                ],
                axis=0,
            )
            full = dot_t(windows, grads)
            for dx in range(3):
                term = full[64 * dx : 64 * dx + 64, :128] + full[64 * dx + 64 : 64 * dx + 128, 128:]
                terms[pl.ds(9 * dz + 3 * dy + dx, C2, stride=28), :] = term


def tree(parts):
    while len(parts) > 1:
        parts = [left + right for left, right in zip(parts[::2], parts[1::2])]
    return parts[0]


def scatter_kernel(where, keep, recv, *outs):
    for k, out in enumerate(outs):
        part = where[2] ^ k
        out[...] = (keep[part].astype(F32) + recv[part].astype(F32)).astype(BF)


def add_kernel(after, *refs):
    del after
    parts, out = refs[:-1], refs[-1]
    out[...] = tree([part[...].astype(F32) for part in parts]).astype(BF)


def finish_kernel(where, scale, *refs):
    parts, (out_a, out_b, whole, total_a, total_b, sems) = refs[:-6], refs[-6:]
    core, sample, count = where[0] % 2, where[2], len(parts) // 2
    for i, part in enumerate(parts):
        whole[core ^ (i % 2), sample ^ (i // 2)] = part[...].astype(F32)
    copies = []
    for width, base, total, out in (
        (C2, 0, total_b, out_b),
        (C1 // 2, ROWS_B // (2 * count), total_a, out_a),
    ):
        each = width // (2 * count)
        for unit in range(2 * count):
            for i in range(each):
                piece = whole[unit // count, unit % count, base + 28 * i : base + 28 * i + 27]
                at = 128 * (unit * each + i)
                total[:, at : at + 128] = piece * scale[0]
            if (unit + 1) * each % 8 == 0:
                at = 128 * ((unit + 1) * each - 8)
                copy = pltpu.make_async_copy(
                    total.at[:, at : at + 1024], out.at[:, at : at + 1024], sems.at[len(copies)]
                )
                copy.start()
                copies.append(copy)
    for copy in copies:
        copy.wait()


def backward_kernel(where, own, recv_a, recv_b, tbt, dsl, xs, terms_b, ga, keep, send, gs, gpool, acc, term, terms):
    del own
    cube_count = recv_a.shape[0]
    even = where[0] % 2 == 0
    shifter = row_picker(3, 1, 16)

    for b in range(cube_count):
        for z in range(2):
            from_a, from_b = recv_a[b, z].astype(F32), recv_b[b, z].astype(F32)
            spread_grad(gs, b, z, jnp.where(even, from_b, from_a).astype(BF), shifter)
            spread_grad(gs, b, 4 + z, jnp.where(even, from_a, from_b).astype(BF), shifter)

    low = jnp.where(where[0] == 0, 0.0, 0.125)
    high = jnp.where(where[0] == where[1] - 1, 0.0, 0.125)
    rows = cube_count * 4 * 16
    columns = []
    for dz in range(3):
        for dy in range(3):
            columns.append(
                jnp.concatenate(
                    [gs[:, dz : dz + 4, dy, :, 512 * q : 512 * q + 768].reshape(rows, 768) for q in range(4)],
                    axis=0,
                )
            )
    back = dot(jnp.concatenate(columns, axis=1), tbt[...])
    for q in range(4):
        part = back[rows * q : rows * q + rows].reshape(cube_count, 4, 16, 256)
        for z in range(4):
            scale = low if z == 0 else high if z == 3 else 0.125
            gpool[:, z, :, 256 * q : 256 * q + 256] = part[:, z] * scale

    ga[:, :, :, :, :128] = jnp.zeros((cube_count, 6, 4, 16, 128), BF)
    ga[:, :, :, :, 2176:] = jnp.zeros((cube_count, 6, 4, 16, 128), BF)
    rows_a = cube_count * 6 * 16
    own_rows = cube_count * 4 * 16
    place = lax.broadcasted_iota(jnp.int32, (rows_a, 128), 0) % 16

    def one_group(g):
        lanes = pl.ds(pl.multiple_of(128 * g, 128), 128)
        up = gpool[:, :, :, lanes]
        up = jnp.concatenate(
            [up[:, 0:1], up[:, 1:2], up[:, 1:2], up[:, 2:3], up[:, 2:3], up[:, 3:4]], axis=1
        ).reshape(rows_a, 128)
        sides = []
        for p in range(2):
            pair = []
            for px in range(2):
                at = pl.ds(pl.multiple_of(256 * g + 128 * px, 128), 128)
                grad = up * dsl[:, :, p, :, at].astype(F32).reshape(rows_a, 128)
                to = pl.ds(pl.multiple_of(256 * g + 128 * px + 128, 128), 128)
                kept = grad.astype(BF).reshape(cube_count, 6, 16, 128)
                ga[:, :, 1 + p, :, to] = kept
                pair.append(kept[:, 1:5].reshape(own_rows, 128))
                if p == 1:
                    moved = jnp.where(place == 0, 0.0, pltpu.roll(grad, 1, 0))
                else:
                    moved = jnp.where(place == 15, 0.0, pltpu.roll(grad, rows_a - 1, 0))
                ga[:, :, 0 if p else 3, :, to] = moved.astype(BF).reshape(cube_count, 6, 16, 128)
            sides.append(jnp.concatenate(pair, axis=1))
        return sides, [windows_a(xs, ((HALO - 1, ZD),), p, 128 * g) for p in range(2)]

    def groups(i, carry):
        first, second = one_group(2 * i), one_group(2 * i + 1)
        grads = jnp.concatenate(first[0] + second[0], axis=0)
        acc[...] += dot_t(jnp.concatenate(first[1] + second[1], axis=0), grads)
        return carry

    acc[...] = jnp.zeros_like(acc)
    lax.fori_loop(0, 4, groups, 0)

    terms[pl.ds(27, C1 // 2, stride=28), :] = jnp.zeros((C1 // 2, 128), F32)
    mask = lanes_below((32, 128), 64)
    for d in range(9):
        full = acc[256 * d : 256 * d + 256]
        for dx in range(3):
            left = full[32 * dx : 32 * dx + 32, :128] + full[32 * dx + 32 : 32 * dx + 64, 128:]
            right = full[32 * dx + 64 : 32 * dx + 96, :128] + full[32 * dx + 96 : 32 * dx + 128, 128:]
            merged = jnp.where(mask, left, right)
            slot = (3 * d + dx) % 4
            term[slot] = merged + pltpu.roll(merged, 64, 1)
            evens = term[slot, pl.ds(0, C1 // 2, stride=2), :]
            odds = term[slot, pl.ds(1, C1 // 2, stride=2), :]
            terms[pl.ds(3 * d + dx, C1 // 2, stride=28), :] = jnp.where(mask[:16], evens, odds)
    low = where[0] % 2 == 0
    count = keep.shape[0]
    for part in range(count):
        sides = []
        for core in range(2):
            at = core * count + part
            rows_b, rows_a = ROWS_B // (2 * count), ROWS_A // (2 * count)
            sides.append(
                jnp.concatenate(
                    [terms_b[rows_b * at : rows_b * at + rows_b], terms[rows_a * at : rows_a * at + rows_a]], axis=0
                )
            )
        keep[part] = jnp.where(low, sides[0], sides[1]).astype(BF)
        send[part] = jnp.where(low, sides[1], sides[0]).astype(BF)


def one_cube(b, ga, tat, out, landed):
    rows = ZD * 16
    sides = []
    for p in range(2):
        columns = []
        for dz in range(3):
            for dy in range(3):
                columns.append(
                    jnp.concatenate(
                        [ga[b, dz : dz + ZD, p + dy, :, 512 * q : 512 * q + 768].reshape(rows, 768) for q in range(4)],
                        axis=0,
                    )
                )
        sides.append(jnp.concatenate(columns, axis=1))
    both = dot(jnp.concatenate(sides, axis=0), tat[...]).astype(BF).reshape(2, 4, ZD, 16, 256)
    row = lax.broadcasted_iota(jnp.int32, (32, 32), 0)
    col = lax.broadcasted_iota(jnp.int32, (32, 32), 1)
    mixer = jnp.where(col == row // 2 + 16 * (row % 2), 1.0, 0.0).astype(BF)
    for z in range(ZD):
        for q in range(4):
            pair = jnp.concatenate([both[0, q, z], both[1, q, z]], axis=0)
            out[z, :, 256 * q : 256 * q + 256] = dot(mixer, pair).astype(BF)
        if landed is not None:
            landed(z)


def early_cube_kernel(b):
    def kernel(ga, tat, out):
        one_cube(b, ga, tat, out, None)

    return kernel


def last_cube_kernel(ga, tat, *rest):
    early, (out, token, block, sems) = rest[:-4], rest[-4:]
    last = len(early)
    copies = [pltpu.make_async_copy(cube, out.at[b], sems.at[b]) for b, cube in enumerate(early)]
    for copy in copies:
        copy.start()

    def landed(z):
        copy = pltpu.make_async_copy(block.at[z], out.at[last, z], sems.at[last + z])
        copy.start()
        copies.append(copy)

    one_cube(last, ga, tat, block, landed)
    token[...] = jnp.zeros_like(token)
    for copy in copies:
        copy.wait()


def call(kernel, args, outs, scratch, flops, smem=0, any_in=(), any_out=(), aliases=None, limit=28):
    specs = [SMEM if i < smem else HBM if i in any_in else VMEM for i in range(len(args))]
    return pl.pallas_call(
        kernel,
        out_shape=[jax.ShapeDtypeStruct(shape, dtype) for shape, dtype in outs],
        in_specs=specs,
        out_specs=[HBM if i in any_out else VMEM for i in range(len(outs))],
        scratch_shapes=scratch,
        input_output_aliases=aliases or {},
        compiler_params=pltpu.CompilerParams(vmem_limit_bytes=limit * 1024 * 1024),
        cost_estimate=pl.CostEstimate(flops=flops, bytes_accessed=1_000_000, transcendentals=0),
    )(*args)


def swap(first, second, count):
    pairs_a = [(i, i ^ 1) for i in range(count)]
    pairs_b = [(i, ((i + 1) ^ 1) - 1) for i in range(1, count - 1)]
    return lax.ppermute(first, "gz", pairs_a), lax.ppermute(second, "gz", pairs_b)


def swap_along(parts, axis, step):
    count = lax.axis_size(axis)
    return [
        lax.ppermute(part, axis, [(i, i ^ (k * step)) for i in range(count)]) for k, part in enumerate(parts) if k
    ]


def shards(cubes, weight_a, weight_b, cotangent):
    cube_count = cubes.shape[0]
    ring = lax.axis_size("gz")
    samples = lax.axis_size("sample")
    where = jnp.stack([lax.axis_index("gz"), jnp.int32(ring), lax.axis_index("sample")]).astype(jnp.int32)
    recv_a, recv_b = swap(cubes, cubes, ring)

    wa = weight_a.reshape(9, 96, C2)
    wb = weight_b.reshape(9, 192, C3)
    own_xs, ta, tb, own_slope, inner = call(
        prepare_kernel,
        [cubes, wa, wb],
        [
            ((cube_count, ZD + 2 * HALO, 4, 16, 1152), BF),
            ((2304, 256), BF),
            ((2304, 256), BF),
            ((cube_count, 6, 2, 16, 2048), BF),
            ((cube_count, 2, 16, 1024), F32),
        ],
        [pltpu.VMEM(cubes.shape, BF), pltpu.SemaphoreType.DMA],
        1_000_000_000,
        any_in=(0,),
        limit=52,
    )
    xs, dsl, pools, grad_b = call(
        forward_kernel,
        [where, own_xs, own_slope, inner, recv_a, recv_b, ta, tb, cotangent],
        [
            ((cube_count, ZD + 2 * HALO, 4, 16, 1152), BF),
            ((cube_count, 6, 2, 16, 2048), BF),
            ((cube_count, 4, 3, 16, 1152), BF),
            ((cube_count, 2, 16, 2048), BF),
        ],
        [pltpu.VMEM((cube_count, 4, 16, 1024), BF)],
        8_000_000_000,
        smem=1,
        aliases={1: 0, 2: 1},
    )
    back_a, back_b = swap(grad_b, grad_b, ring)
    spread = ((cube_count, 6, 3, 16, 2304), BF)
    wide = ((6912, 256), BF)
    terms_b, own_gs, tat, tbt = call(
        terms_b_kernel, [pools, grad_b, wa, wb], [((ROWS_B, 128), F32), spread, wide, wide], [], 1_000_000_000
    )
    piece = (ROWS_A + ROWS_B) // (2 * samples)
    pieces = ((samples, piece, 128), BF)
    ga, keep, send, _ = call(
        backward_kernel,
        [where, own_gs, back_a, back_b, tbt, dsl, xs, terms_b],
        [((cube_count, 6, 4, 16, 2304), BF), pieces, pieces, spread],
        [
            pltpu.VMEM((cube_count, 4, 16, 1024), F32),
            pltpu.VMEM((2304, 256), F32),
            pltpu.VMEM((4, C1, 128), F32),
            pltpu.VMEM((ROWS_A, 128), F32),
        ],
        6_000_000_000,
        smem=1,
        aliases={1: 3},
    )
    small = [((piece, 128), BF)]
    (recv,) = swap_along([send] * 2, "gz", 1)
    parts = call(scatter_kernel, [where, keep, recv], small * samples, [], 1_000_000, smem=1)
    others = swap_along(parts, "sample", 1)
    cube = (ZD, SIDE, SIDE * C1)
    early = [
        call(early_cube_kernel(b), [ga, tat], [(cube, BF)], [], 2_000_000_000)[0] for b in range(cube_count - 1)
    ]
    (mine,) = call(add_kernel, [early[0], parts[0], *others], small, [], 1_000_000)
    others = swap_along([mine] * (ring // 2), "gz", 2)
    input_grad, done = call(
        last_cube_kernel,
        [ga, tat, *early],
        [((cube_count, *cube), BF), ((8, 128), F32)],
        [pltpu.VMEM(cube, BF), pltpu.SemaphoreType.DMA((cube_count - 1 + ZD,))],
        2_000_000_000,
        any_out=(0,),
    )
    (mine,) = call(add_kernel, [done, mine, *others], small, [], 1_000_000)
    gathered = [
        lax.ppermute(
            mine,
            ("sample", "gz"),
            [(i * ring + j, (i ^ k) * ring + (j ^ c)) for i in range(samples) for j in range(ring)],
        )
        for k in range(samples)
        for c in range(2)
        if k or c
    ]
    scale = jnp.full((1,), 1.0 / (cube_count * samples), F32)
    shape_a, shape_b = (27, C1 * C2), (27, C2 * C3)
    total_a, total_b = call(
        finish_kernel,
        [where, scale, mine, *gathered],
        [(shape_a, F32), (shape_b, F32)],
        [
            pltpu.VMEM((2, samples, piece, 128), F32),
            pltpu.VMEM(shape_a, F32),
            pltpu.VMEM(shape_b, F32),
            pltpu.SemaphoreType.DMA((10,)),
        ],
        1_000_000,
        smem=2,
        any_out=(0, 1),
    )
    return input_grad, total_a, total_b


def solution(mesh):
    in_specs = (P("sample", "gz", None, None), P(), P(), P("sample", "gz", None, None))
    out_specs = (P("sample", "gz", None, None), P(), P())
    return jax.shard_map(shards, mesh=mesh, in_specs=in_specs, out_specs=out_specs, check_vma=False)
```

```python
import jax
import jax.numpy as jnp
from jax import lax
from jax.experimental import pallas as pl
from jax.experimental.pallas import tpu as pltpu
from jax.sharding import PartitionSpec as P

C1 = 32
C2 = 64
C3 = 128
SIDE = 32
ZD = 4
HALO = 3
ROWS_B = C1 * 2 * 28
ROWS_A = C1 // 2 * 28
BF = jnp.bfloat16
F32 = jnp.float32
VMEM = pl.BlockSpec(memory_space=pltpu.VMEM)
SMEM = pl.BlockSpec(memory_space=pltpu.SMEM)
ANY = pl.BlockSpec(memory_space=pl.ANY)


def dot(a, b):
    return jnp.dot(a, b, preferred_element_type=F32)


def dot_t(a, b):
    return lax.dot_general(a, b, (((0,), (0,)), ((), ())), preferred_element_type=F32)


def sigmoid(v):
    return pl.reciprocal(1.0 + jnp.exp(-v), approx=True)


def row_picker(variants, stride, columns):
    shape = (variants * 16, columns)
    row = lax.broadcasted_iota(jnp.int32, shape, 0)
    col = lax.broadcasted_iota(jnp.int32, shape, 1)
    return jnp.where(col == stride * (row % 16) + row // 16 - 1, 1.0, 0.0).astype(BF)


def rows_at(block, before, total):
    rows, lanes = block.shape
    parts = []
    if before:
        parts.append(jnp.zeros((before, lanes), block.dtype))
    parts.append(block)
    if total - before - rows:
        parts.append(jnp.zeros((total - before - rows, lanes), block.dtype))
    return jnp.concatenate(parts, axis=0) if len(parts) > 1 else block


def lanes_below(shape, bound):
    return lax.broadcasted_iota(jnp.int32, shape, 1) < bound


def halves(left, right):
    return jnp.where(lanes_below(left.shape, 64), left, right).astype(BF)


def silu(pre):
    squash = sigmoid(pre)
    act = pre * squash
    return act, (squash + act * (1.0 - squash)).astype(BF)


def windows_a(xs, spans, p, start):
    lanes = pl.ds(start if isinstance(start, int) else pl.multiple_of(start, 128), 256)
    columns = []
    for dz in range(3):
        for dy in range(3):
            parts = [xs[:, first + dz : first + dz + planes, p + dy, :, lanes] for first, planes in spans]
            whole = jnp.concatenate(parts, axis=1) if len(parts) > 1 else parts[0]
            columns.append(whole.reshape(whole.shape[0] * whole.shape[1] * 16, 256))
    return jnp.concatenate(columns, axis=1)


def spread_input(target, b, zz, plane, picker):
    plane = jnp.concatenate([jnp.zeros((32, 32), BF), plane, jnp.zeros((32, 96), BF)], axis=1)
    moved = dot(picker, plane).astype(BF)
    for v in range(4):
        target[b, zz, v] = moved[16 * v : 16 * v + 16]


RANKS = (-3, -1, 0, 2, 1, 3, 4, 6, 5, 7, 8, 10)


def mirror(d, block, tat):
    lane = lax.broadcasted_iota(jnp.int32, (64, 128), 1)
    turned = [block if s == 0 else pltpu.roll(block, 32 * s, 1) for s in range(4)]
    for slot, rank in enumerate(RANKS):
        for half in range(2):
            start = 32 * (rank - 1 - 4 * half)
            keep = (lane >= start) & (lane < start + 96)
            value = jnp.where(keep, turned[(rank - 1) % 4], 0.0).astype(BF)
            tat[768 * d + 64 * slot : 768 * d + 64 * slot + 64, 128 * half : 128 * half + 128] = value


def prepare_kernel(cubes, wa, wb, xs, ta, tb, dsl, inner):
    picker = row_picker(4, 2, 32)
    for b in range(cubes.shape[0]):
        for z in range(ZD):
            spread_input(xs, b, HALO + z, cubes[b, z], picker)
    for d in range(9):
        block = wa[d].astype(F32)
        block = jnp.concatenate([block, block], axis=1)
        for px in range(2):
            ta[256 * d : 256 * d + 256, 128 * px : 128 * px + 128] = halves(
                rows_at(block, 32 * px, 256), rows_at(block, 64 + 32 * px, 256)
            )
        block = wb[d]
        for e in range(2):
            tb[256 * d : 256 * d + 256, 128 * e : 128 * e + 128] = rows_at(block, 64 * e, 256)

    cube_count = cubes.shape[0]
    pre = dot(
        jnp.concatenate(
            [windows_a(xs, ((HALO, 2),), p, 128 * g) for g in range(8) for p in range(2)], axis=0
        ),
        ta[...],
    )
    act, slope = silu(pre)
    slope = slope.reshape(8, 2, cube_count, 2, 16, 256)
    act = act.reshape(8, 2, cube_count, 2, 16, 256)
    for g in range(8):
        for p in range(2):
            dsl[:, 2:4, p, :, 256 * g : 256 * g + 256] = slope[g, p]
        part = act[g, 0] + act[g, 1]
        inner[:, :, :, 128 * g : 128 * g + 128] = part[..., :128] + part[..., 128:]


def forward_kernel(where, own, own_slope, inner, recv_a, recv_b, ta, tb, cot, xs, dsl, pools, grad_b, pooled):
    del own, own_slope
    cube_count = xs.shape[0]
    even = where[0] % 2 == 0
    picker = row_picker(4, 2, 32)
    for b in range(cube_count):
        for z in range(HALO):
            far = ZD - HALO + z
            below = jnp.where(even, recv_b[b, far].astype(F32), recv_a[b, far].astype(F32)).astype(BF)
            above = jnp.where(even, recv_a[b, z].astype(F32), recv_b[b, z].astype(F32)).astype(BF)
            spread_input(xs, b, z, below, picker)
            spread_input(xs, b, HALO + ZD + z, above, picker)

    low = jnp.where(where[0] == 0, 0.0, 0.125)
    high = jnp.where(where[0] == where[1] - 1, 0.0, 0.125)

    def groups(i, carry):
        pre = dot(
            jnp.concatenate(
                [
                    windows_a(xs, ((0, 3), (HALO + ZD - 2, 3)), p, 512 * i + 128 * j)
                    for j in range(4)
                    for p in range(2)
                ],
                axis=0,
            ),
            ta[...],
        )
        act, slope = silu(pre)
        slope = slope.reshape(4, 2, cube_count, 6, 16, 256)
        act = act.reshape(4, 2, cube_count, 6, 16, 256)
        for j in range(4):
            for p in range(2):
                to = pl.ds(pl.multiple_of(1024 * i + 256 * j, 256), 256)
                dsl[:, 0:2, p, :, to] = slope[j, p][:, 1:3]
                dsl[:, 4:6, p, :, to] = slope[j, p][:, 3:5]
            part = act[j, 0] + act[j, 1]
            part = part[..., :128] + part[..., 128:]
            out = pl.ds(pl.multiple_of(512 * i + 128 * j, 128), 128)
            pooled[:, 0, :, out] = ((part[:, 0] + part[:, 1]) * low).astype(BF)
            pooled[:, 1, :, out] = ((part[:, 2] + inner[:, 0, :, out]) * 0.125).astype(BF)
            pooled[:, 2, :, out] = ((part[:, 3] + inner[:, 1, :, out]) * 0.125).astype(BF)
            pooled[:, 3, :, out] = ((part[:, 4] + part[:, 5]) * high).astype(BF)
        return carry

    lax.fori_loop(0, 2, groups, 0, unroll=True)

    shifter = row_picker(3, 1, 16)
    for b in range(cube_count):
        for z in range(4):
            plane = jnp.concatenate([jnp.zeros((16, 64), BF), pooled[b, z], jnp.zeros((16, 64), BF)], axis=1)
            moved = dot(shifter, plane).astype(BF)
            for v in range(3):
                pools[b, z, v] = moved[16 * v : 16 * v + 16]

    rows_b = cube_count * 2 * 16
    columns = []
    for dz in range(3):
        for dy in range(3):
            columns.append(
                jnp.concatenate(
                    [
                        pools[:, dz : dz + 2, dy, :, 128 * g : 128 * g + 256].reshape(rows_b, 256)
                        for g in range(8)
                    ],
                    axis=0,
                )
            )
    pre_b = dot(jnp.concatenate(columns, axis=1), tb[...])
    squash = sigmoid(pre_b)
    slope_b = squash + pre_b * squash * (1.0 - squash)
    row = lax.broadcasted_iota(jnp.int32, (16, 8), 0)
    twice = jnp.where(row // 2 == lax.broadcasted_iota(jnp.int32, (16, 8), 1), 0.125, 0.0).astype(BF)
    ups = [dot(twice, cot[b, 0]) for b in range(cube_count)]
    for g in range(8):
        part = slope_b[rows_b * g : rows_b * g + rows_b].reshape(cube_count, 2, 16, 256)
        up = jnp.stack([ups[b][:, 128 * g : 128 * g + 128] for b in range(cube_count)])
        for z in range(2):
            for e in range(2):
                at = 256 * g + 128 * e
                grad_b[:, z, :, at : at + 128] = (up * part[:, z, :, 128 * e : 128 * e + 128]).astype(BF)


def spread_grad(target, b, zz, plane, shifter):
    moved = dot(shifter, plane).astype(BF)
    for v in range(3):
        target[b, zz, v, :, 128:2176] = moved[16 * v : 16 * v + 16]
        target[b, zz, v, :, :128] = jnp.zeros((16, 128), BF)
        target[b, zz, v, :, 2176:] = jnp.zeros((16, 128), BF)


def terms_b_kernel(pools, grad_b, wa, wb, terms, gs, tat, tbt):
    cube_count = grad_b.shape[0]
    shifter = row_picker(3, 1, 16)
    for b in range(cube_count):
        for z in range(2):
            spread_grad(gs, b, 2 + z, grad_b[b, z], shifter)
    for d in range(9):
        block = wa[d].astype(F32)
        block = jnp.concatenate([block, block], axis=1)
        mirror(8 - d, rows_at(block, 0, 128).T[:64], tat)
        block = wb[d]
        turned = []
        for dx in (2, 1, 0):
            part = block[64 * dx : 64 * dx + 64].astype(F32)
            turned.append(jnp.concatenate([part, part], axis=0).T)
        block = jnp.concatenate(turned, axis=0)
        to = 768 * (8 - d)
        for e in range(2):
            tbt[to : to + 768, 128 * e : 128 * e + 128] = halves(
                rows_at(block, 256 * e, 768), rows_at(block, 256 * e + 128, 768)
            )
    rows_b = cube_count * 2 * 16
    grads = jnp.concatenate(
        [grad_b[:, :, :, 256 * g : 256 * g + 256].reshape(rows_b, 256) for g in range(8)], axis=0
    )
    terms[pl.ds(27, C2, stride=28), :] = jnp.zeros((C2, 128), F32)
    for dz in range(3):
        for dy in range(3):
            windows = jnp.concatenate(
                [
                    pools[:, dz : dz + 2, dy, :, 128 * g : 128 * g + 256].reshape(rows_b, 256)
                    for g in range(8)
                ],
                axis=0,
            )
            full = dot_t(windows, grads)
            for dx in range(3):
                term = full[64 * dx : 64 * dx + 64, :128] + full[64 * dx + 64 : 64 * dx + 128, 128:]
                terms[pl.ds(9 * dz + 3 * dy + dx, C2, stride=28), :] = term


def tree(parts):
    while len(parts) > 1:
        parts = [left + right for left, right in zip(parts[::2], parts[1::2])]
    return parts[0]


def scatter_kernel(where, keep, recv, *outs):
    for k, out in enumerate(outs):
        part = where[2] ^ k
        out[...] = (keep[part].astype(F32) + recv[part].astype(F32)).astype(BF)


def add_kernel(after, *refs):
    del after
    parts, out = refs[:-1], refs[-1]
    out[...] = tree([part[...].astype(F32) for part in parts]).astype(BF)


def stack_kernel(where, *refs):
    parts, out = refs[:-1], refs[-1]
    for k, part in enumerate(parts):
        out[where[2] ^ k] = part[...]


def finish_kernel(where, scale, own, other, out_a, out_b, whole):
    core = where[0] % 2
    whole[core] = own[...].astype(F32)
    whole[1 - core] = other[...].astype(F32)
    count = own.shape[0]
    for width, base, out in ((C2, 0, out_b), (C1 // 2, ROWS_B // (2 * count), out_a)):
        each = width // (2 * count)
        for i in range(width):
            start = base + 28 * (i % each)
            piece = whole[i // each // count, i // each % count, start : start + 27]
            out[:, 128 * i : 128 * i + 128] = piece * scale[0]


def backward_kernel(where, own, recv_a, recv_b, tbt, dsl, xs, terms_b, ga, keep, send, gs, gpool, acc, term, terms):
    del own
    cube_count = recv_a.shape[0]
    even = where[0] % 2 == 0
    shifter = row_picker(3, 1, 16)

    for b in range(cube_count):
        for z in range(2):
            from_a, from_b = recv_a[b, z].astype(F32), recv_b[b, z].astype(F32)
            spread_grad(gs, b, z, jnp.where(even, from_b, from_a).astype(BF), shifter)
            spread_grad(gs, b, 4 + z, jnp.where(even, from_a, from_b).astype(BF), shifter)

    low = jnp.where(where[0] == 0, 0.0, 0.125)
    high = jnp.where(where[0] == where[1] - 1, 0.0, 0.125)
    rows = cube_count * 4 * 16
    columns = []
    for dz in range(3):
        for dy in range(3):
            columns.append(
                jnp.concatenate(
                    [gs[:, dz : dz + 4, dy, :, 512 * q : 512 * q + 768].reshape(rows, 768) for q in range(4)],
                    axis=0,
                )
            )
    back = dot(jnp.concatenate(columns, axis=1), tbt[...])
    for q in range(4):
        part = back[rows * q : rows * q + rows].reshape(cube_count, 4, 16, 256)
        for z in range(4):
            scale = low if z == 0 else high if z == 3 else 0.125
            gpool[:, z, :, 256 * q : 256 * q + 256] = part[:, z] * scale

    ga[:, :, :, :, :128] = jnp.zeros((cube_count, 6, 4, 16, 128), BF)
    ga[:, :, :, :, 2176:] = jnp.zeros((cube_count, 6, 4, 16, 128), BF)
    rows_a = cube_count * 6 * 16
    own_rows = cube_count * 4 * 16
    place = lax.broadcasted_iota(jnp.int32, (rows_a, 128), 0) % 16

    def one_group(g):
        lanes = pl.ds(pl.multiple_of(128 * g, 128), 128)
        up = gpool[:, :, :, lanes]
        up = jnp.concatenate(
            [up[:, 0:1], up[:, 1:2], up[:, 1:2], up[:, 2:3], up[:, 2:3], up[:, 3:4]], axis=1
        ).reshape(rows_a, 128)
        sides = []
        for p in range(2):
            pair = []
            for px in range(2):
                at = pl.ds(pl.multiple_of(256 * g + 128 * px, 128), 128)
                grad = up * dsl[:, :, p, :, at].astype(F32).reshape(rows_a, 128)
                to = pl.ds(pl.multiple_of(256 * g + 128 * px + 128, 128), 128)
                kept = grad.astype(BF).reshape(cube_count, 6, 16, 128)
                ga[:, :, 1 + p, :, to] = kept
                pair.append(kept[:, 1:5].reshape(own_rows, 128))
                if p == 1:
                    moved = jnp.where(place == 0, 0.0, pltpu.roll(grad, 1, 0))
                else:
                    moved = jnp.where(place == 15, 0.0, pltpu.roll(grad, rows_a - 1, 0))
                ga[:, :, 0 if p else 3, :, to] = moved.astype(BF).reshape(cube_count, 6, 16, 128)
            sides.append(jnp.concatenate(pair, axis=1))
        return sides, [windows_a(xs, ((HALO - 1, ZD),), p, 128 * g) for p in range(2)]

    def groups(i, carry):
        first, second = one_group(2 * i), one_group(2 * i + 1)
        grads = jnp.concatenate(first[0] + second[0], axis=0)
        acc[...] += dot_t(jnp.concatenate(first[1] + second[1], axis=0), grads)
        return carry

    acc[...] = jnp.zeros_like(acc)
    lax.fori_loop(0, 4, groups, 0, unroll=True)

    terms[pl.ds(27, C1 // 2, stride=28), :] = jnp.zeros((C1 // 2, 128), F32)
    mask = lanes_below((32, 128), 64)
    for d in range(9):
        full = acc[256 * d : 256 * d + 256]
        for dx in range(3):
            left = full[32 * dx : 32 * dx + 32, :128] + full[32 * dx + 32 : 32 * dx + 64, 128:]
            right = full[32 * dx + 64 : 32 * dx + 96, :128] + full[32 * dx + 96 : 32 * dx + 128, 128:]
            merged = jnp.where(mask, left, right)
            slot = (3 * d + dx) % 4
            term[slot] = merged + pltpu.roll(merged, 64, 1)
            evens = term[slot, pl.ds(0, C1 // 2, stride=2), :]
            odds = term[slot, pl.ds(1, C1 // 2, stride=2), :]
            terms[pl.ds(3 * d + dx, C1 // 2, stride=28), :] = jnp.where(mask[:16], evens, odds)
    low = where[0] % 2 == 0
    count = keep.shape[0]
    for part in range(count):
        sides = []
        for core in range(2):
            at = core * count + part
            rows_b, rows_a = ROWS_B // (2 * count), ROWS_A // (2 * count)
            sides.append(
                jnp.concatenate(
                    [terms_b[rows_b * at : rows_b * at + rows_b], terms[rows_a * at : rows_a * at + rows_a]], axis=0
                )
            )
        keep[part] = jnp.where(low, sides[0], sides[1]).astype(BF)
        send[part] = jnp.where(low, sides[1], sides[0]).astype(BF)


def one_cube(b, ga, tat, out, landed):
    rows = ZD * 16
    sides = []
    for p in range(2):
        columns = []
        for dz in range(3):
            for dy in range(3):
                columns.append(
                    jnp.concatenate(
                        [ga[b, dz : dz + ZD, p + dy, :, 512 * q : 512 * q + 768].reshape(rows, 768) for q in range(4)],
                        axis=0,
                    )
                )
        sides.append(jnp.concatenate(columns, axis=1))
    both = dot(jnp.concatenate(sides, axis=0), tat[...]).astype(BF).reshape(2, 4, ZD, 16, 256)
    row = lax.broadcasted_iota(jnp.int32, (32, 32), 0)
    col = lax.broadcasted_iota(jnp.int32, (32, 32), 1)
    mixer = jnp.where(col == row // 2 + 16 * (row % 2), 1.0, 0.0).astype(BF)
    for z in range(ZD):
        for q in range(4):
            pair = jnp.concatenate([both[0, q, z], both[1, q, z]], axis=0)
            out[z, :, 256 * q : 256 * q + 256] = dot(mixer, pair).astype(BF)
        if landed is not None:
            landed(z)


def early_cube_kernel(b):
    def kernel(ga, tat, out):
        one_cube(b, ga, tat, out, None)

    return kernel


def last_cube_kernel(ga, tat, *rest):
    early, (out, token, block, sems) = rest[:-4], rest[-4:]
    last = len(early)
    copies = [pltpu.make_async_copy(cube, out.at[b], sems.at[b]) for b, cube in enumerate(early)]
    for copy in copies:
        copy.start()

    def landed(z):
        copy = pltpu.make_async_copy(block.at[z], out.at[last, z], sems.at[last + z])
        copy.start()
        copies.append(copy)

    one_cube(last, ga, tat, block, landed)
    token[...] = jnp.zeros_like(token)
    for copy in copies:
        copy.wait()


def call(kernel, args, outs, scratch, flops, smem=0, any_in=(), any_out=(), aliases=None):
    specs = [SMEM if i < smem else ANY if i in any_in else VMEM for i in range(len(args))]
    return pl.pallas_call(
        kernel,
        out_shape=[jax.ShapeDtypeStruct(shape, dtype) for shape, dtype in outs],
        in_specs=specs,
        out_specs=[ANY if i in any_out else VMEM for i in range(len(outs))],
        scratch_shapes=scratch,
        input_output_aliases=aliases or {},
        compiler_params=pltpu.CompilerParams(vmem_limit_bytes=28 * 1024 * 1024),
        cost_estimate=pl.CostEstimate(flops=flops, bytes_accessed=1_000_000, transcendentals=0),
    )(*args)


def swap(first, second, count):
    pairs_a = [(i, i ^ 1) for i in range(count)]
    pairs_b = [(i, ((i + 1) ^ 1) - 1) for i in range(1, count - 1)]
    return lax.ppermute(first, "gz", pairs_a), lax.ppermute(second, "gz", pairs_b)


def swap_along(parts, axis, step):
    count = lax.axis_size(axis)
    return [
        lax.ppermute(part, axis, [(i, i ^ (k * step)) for i in range(count)]) for k, part in enumerate(parts) if k
    ]


def shards(cubes, weight_a, weight_b, cotangent):
    cube_count = cubes.shape[0]
    ring = lax.axis_size("gz")
    samples = lax.axis_size("sample")
    where = jnp.stack([lax.axis_index("gz"), jnp.int32(ring), lax.axis_index("sample")]).astype(jnp.int32)
    recv_a, recv_b = swap(cubes, cubes, ring)

    wa = weight_a.reshape(9, 96, C2)
    wb = weight_b.reshape(9, 192, C3)
    own_xs, ta, tb, own_slope, inner = call(
        prepare_kernel,
        [cubes, wa, wb],
        [
            ((cube_count, ZD + 2 * HALO, 4, 16, 1152), BF),
            ((2304, 256), BF),
            ((2304, 256), BF),
            ((cube_count, 6, 2, 16, 2048), BF),
            ((cube_count, 2, 16, 1024), F32),
        ],
        [],
        1_000_000_000,
    )
    xs, dsl, pools, grad_b = call(
        forward_kernel,
        [where, own_xs, own_slope, inner, recv_a, recv_b, ta, tb, cotangent],
        [
            ((cube_count, ZD + 2 * HALO, 4, 16, 1152), BF),
            ((cube_count, 6, 2, 16, 2048), BF),
            ((cube_count, 4, 3, 16, 1152), BF),
            ((cube_count, 2, 16, 2048), BF),
        ],
        [pltpu.VMEM((cube_count, 4, 16, 1024), BF)],
        8_000_000_000,
        smem=1,
        aliases={1: 0, 2: 1},
    )
    back_a, back_b = swap(grad_b, grad_b, ring)
    spread = ((cube_count, 6, 3, 16, 2304), BF)
    wide = ((6912, 256), BF)
    terms_b, own_gs, tat, tbt = call(
        terms_b_kernel, [pools, grad_b, wa, wb], [((ROWS_B, 128), F32), spread, wide, wide], [], 1_000_000_000
    )
    piece = (ROWS_A + ROWS_B) // (2 * samples)
    pieces = ((samples, piece, 128), BF)
    ga, keep, send, _ = call(
        backward_kernel,
        [where, own_gs, back_a, back_b, tbt, dsl, xs, terms_b],
        [((cube_count, 6, 4, 16, 2304), BF), pieces, pieces, spread],
        [
            pltpu.VMEM((cube_count, 4, 16, 1024), F32),
            pltpu.VMEM((2304, 256), F32),
            pltpu.VMEM((4, C1, 128), F32),
            pltpu.VMEM((ROWS_A, 128), F32),
        ],
        6_000_000_000,
        smem=1,
        aliases={1: 3},
    )
    small = [((piece, 128), BF)]
    (recv,) = swap_along([send] * 2, "gz", 1)
    parts = call(scatter_kernel, [where, keep, recv], small * samples, [], 1_000_000, smem=1)
    others = swap_along(parts, "sample", 1)
    cube = (ZD, SIDE, SIDE * C1)
    early = [
        call(early_cube_kernel(b), [ga, tat], [(cube, BF)], [], 2_000_000_000)[0] for b in range(cube_count - 1)
    ]
    (mine,) = call(add_kernel, [early[0], parts[0], *others], small, [], 1_000_000)
    others = swap_along([mine] * (ring // 2), "gz", 2)
    input_grad, done = call(
        last_cube_kernel,
        [ga, tat, *early],
        [((cube_count, *cube), BF), ((8, 128), F32)],
        [pltpu.VMEM(cube, BF), pltpu.SemaphoreType.DMA((cube_count - 1 + ZD,))],
        2_000_000_000,
        any_out=(0,),
    )
    (mine,) = call(add_kernel, [done, mine, *others], small, [], 1_000_000)
    (own,) = call(
        stack_kernel, [where, mine, *swap_along([mine] * samples, "sample", 1)], [pieces], [], 1_000_000, smem=1
    )
    (other,) = swap_along([own] * 2, "gz", 1)
    scale = jnp.full((1,), 1.0 / (cube_count * samples), F32)
    total_a, total_b = call(
        finish_kernel,
        [where, scale, own, other],
        [((27, C1 * C2), F32), ((27, C2 * C3), F32)],
        [pltpu.VMEM((2, samples, piece, 128), F32)],
        1_000_000,
        smem=2,
    )
    return input_grad, total_a, total_b


def solution(mesh):
    in_specs = (P("sample", "gz", None, None), P(), P(), P("sample", "gz", None, None))
    out_specs = (P("sample", "gz", None, None), P(), P())
    return jax.shard_map(shards, mesh=mesh, in_specs=in_specs, out_specs=out_specs, check_vma=False)
```

```python
import jax
import jax.numpy as jnp
from jax import lax
from jax.experimental import pallas as pl
from jax.experimental.pallas import tpu as pltpu
from jax.sharding import PartitionSpec as P

C1 = 32
C2 = 64
C3 = 128
SIDE = 32
ZD = 4
HALO = 3
ROWS_B = C1 * 2 * 28
ROWS_A = C1 // 2 * 28
BF = jnp.bfloat16
F32 = jnp.float32
VMEM = pl.BlockSpec(memory_space=pltpu.VMEM)
SMEM = pl.BlockSpec(memory_space=pltpu.SMEM)
ANY = pl.BlockSpec(memory_space=pl.ANY)


def dot(a, b):
    return jnp.dot(a, b, preferred_element_type=F32)


def dot_t(a, b):
    return lax.dot_general(a, b, (((0,), (0,)), ((), ())), preferred_element_type=F32)


def sigmoid(v):
    return pl.reciprocal(1.0 + jnp.exp(-v), approx=True)


def row_picker(variants, stride, columns):
    shape = (variants * 16, columns)
    row = lax.broadcasted_iota(jnp.int32, shape, 0)
    col = lax.broadcasted_iota(jnp.int32, shape, 1)
    return jnp.where(col == stride * (row % 16) + row // 16 - 1, 1.0, 0.0).astype(BF)


def rows_at(block, before, total):
    rows, lanes = block.shape
    parts = []
    if before:
        parts.append(jnp.zeros((before, lanes), block.dtype))
    parts.append(block)
    if total - before - rows:
        parts.append(jnp.zeros((total - before - rows, lanes), block.dtype))
    return jnp.concatenate(parts, axis=0) if len(parts) > 1 else block


def lanes_below(shape, bound):
    return lax.broadcasted_iota(jnp.int32, shape, 1) < bound


def halves(left, right):
    return jnp.where(lanes_below(left.shape, 64), left, right).astype(BF)


def loop(count, body):
    def step(i, carry):
        body(i)
        return carry

    lax.fori_loop(0, count, step, 0)


def aligned(start, size):
    return pl.ds(start if isinstance(start, int) else pl.multiple_of(start, size), size)


def silu(pre):
    squash = sigmoid(pre)
    act = pre * squash
    return act, (squash + act * (1.0 - squash)).astype(BF)


def windows_a(xs, spans, p, start):
    lanes = pl.ds(start if isinstance(start, int) else pl.multiple_of(start, 128), 256)
    columns = []
    for dz in range(3):
        for dy in range(3):
            parts = [xs[:, first + dz : first + dz + planes, p + dy, :, lanes] for first, planes in spans]
            whole = jnp.concatenate(parts, axis=1) if len(parts) > 1 else parts[0]
            columns.append(whole.reshape(whole.shape[0] * whole.shape[1] * 16, 256))
    return jnp.concatenate(columns, axis=1)


def spread_input(target, b, zz, plane, picker):
    plane = jnp.concatenate([jnp.zeros((32, 32), BF), plane, jnp.zeros((32, 96), BF)], axis=1)
    moved = dot(picker, plane).astype(BF)
    for v in range(4):
        target[b, zz, v] = moved[16 * v : 16 * v + 16]


RANKS = (-3, -1, 0, 2, 1, 3, 4, 6, 5, 7, 8, 10)


def mirror(d, block, tat):
    lane = lax.broadcasted_iota(jnp.int32, (64, 128), 1)
    turned = [block if s == 0 else pltpu.roll(block, 32 * s, 1) for s in range(4)]
    for slot, rank in enumerate(RANKS):
        for half in range(2):
            start = 32 * (rank - 1 - 4 * half)
            keep = (lane >= start) & (lane < start + 96)
            value = jnp.where(keep, turned[(rank - 1) % 4], 0.0).astype(BF)
            tat[aligned(768 * d + 64 * slot, 64), 128 * half : 128 * half + 128] = value


def prepare_kernel(cubes, wa, wb, xs, ta, tb, dsl, inner):
    cube_count = cubes.shape[0]
    picker = row_picker(4, 2, 32)

    def plane(i):
        spread_input(xs, i // ZD, HALO + i % ZD, cubes[i // ZD, i % ZD], picker)

    def weights(d):
        rows = aligned(256 * d, 256)
        block = wa[d].astype(F32)
        block = jnp.concatenate([block, block], axis=1)
        for px in range(2):
            ta[rows, 128 * px : 128 * px + 128] = halves(
                rows_at(block, 32 * px, 256), rows_at(block, 64 + 32 * px, 256)
            )
        block = wb[d]
        for e in range(2):
            tb[rows, 128 * e : 128 * e + 128] = rows_at(block, 64 * e, 256)

    loop(cube_count * ZD, plane)
    loop(9, weights)

    pre = dot(
        jnp.concatenate(
            [windows_a(xs, ((HALO, 2),), p, 128 * g) for g in range(8) for p in range(2)], axis=0
        ),
        ta[...],
    )
    act, slope = silu(pre)
    slope = slope.reshape(8, 2, cube_count, 2, 16, 256)
    act = act.reshape(8, 2, cube_count, 2, 16, 256)
    for g in range(8):
        for p in range(2):
            dsl[:, 2:4, p, :, 256 * g : 256 * g + 256] = slope[g, p]
        part = act[g, 0] + act[g, 1]
        inner[:, :, :, 128 * g : 128 * g + 128] = part[..., :128] + part[..., 128:]


def forward_kernel(where, own, own_slope, inner, recv_a, recv_b, ta, tb, cot, xs, dsl, pools, grad_b, pooled):
    del own, own_slope
    cube_count = xs.shape[0]
    even = where[0] % 2 == 0
    picker = row_picker(4, 2, 32)

    def planes(i):
        b, z = i // HALO, i % HALO
        far = ZD - HALO + z
        below = jnp.where(even, recv_b[b, far].astype(F32), recv_a[b, far].astype(F32)).astype(BF)
        above = jnp.where(even, recv_a[b, z].astype(F32), recv_b[b, z].astype(F32)).astype(BF)
        spread_input(xs, b, z, below, picker)
        spread_input(xs, b, HALO + ZD + z, above, picker)

    loop(cube_count * HALO, planes)

    low = jnp.where(where[0] == 0, 0.0, 0.125)
    high = jnp.where(where[0] == where[1] - 1, 0.0, 0.125)

    def groups(i, carry):
        pre = dot(
            jnp.concatenate(
                [
                    windows_a(xs, ((0, 3), (HALO + ZD - 2, 3)), p, 512 * i + 128 * j)
                    for j in range(4)
                    for p in range(2)
                ],
                axis=0,
            ),
            ta[...],
        )
        act, slope = silu(pre)
        slope = slope.reshape(4, 2, cube_count, 6, 16, 256)
        act = act.reshape(4, 2, cube_count, 6, 16, 256)
        for j in range(4):
            for p in range(2):
                to = pl.ds(pl.multiple_of(1024 * i + 256 * j, 256), 256)
                dsl[:, 0:2, p, :, to] = slope[j, p][:, 1:3]
                dsl[:, 4:6, p, :, to] = slope[j, p][:, 3:5]
            part = act[j, 0] + act[j, 1]
            part = part[..., :128] + part[..., 128:]
            out = pl.ds(pl.multiple_of(512 * i + 128 * j, 128), 128)
            pooled[:, 0, :, out] = ((part[:, 0] + part[:, 1]) * low).astype(BF)
            pooled[:, 1, :, out] = ((part[:, 2] + inner[:, 0, :, out]) * 0.125).astype(BF)
            pooled[:, 2, :, out] = ((part[:, 3] + inner[:, 1, :, out]) * 0.125).astype(BF)
            pooled[:, 3, :, out] = ((part[:, 4] + part[:, 5]) * high).astype(BF)
        return carry

    lax.fori_loop(0, 2, groups, 0)

    shifter = row_picker(3, 1, 16)

    def pool_plane(i):
        b, z = i // 4, i % 4
        plane = jnp.concatenate([jnp.zeros((16, 64), BF), pooled[b, z], jnp.zeros((16, 64), BF)], axis=1)
        moved = dot(shifter, plane).astype(BF)
        for v in range(3):
            pools[b, z, v] = moved[16 * v : 16 * v + 16]

    loop(cube_count * 4, pool_plane)

    rows_b = cube_count * 2 * 16
    columns = []
    for dz in range(3):
        for dy in range(3):
            columns.append(
                jnp.concatenate(
                    [
                        pools[:, dz : dz + 2, dy, :, 128 * g : 128 * g + 256].reshape(rows_b, 256)
                        for g in range(8)
                    ],
                    axis=0,
                )
            )
    pre_b = dot(jnp.concatenate(columns, axis=1), tb[...])
    squash = sigmoid(pre_b)
    slope_b = squash + pre_b * squash * (1.0 - squash)
    row = lax.broadcasted_iota(jnp.int32, (16, 8), 0)
    twice = jnp.where(row // 2 == lax.broadcasted_iota(jnp.int32, (16, 8), 1), 0.125, 0.0).astype(BF)
    ups = [dot(twice, cot[b, 0]) for b in range(cube_count)]
    for g in range(8):
        part = slope_b[rows_b * g : rows_b * g + rows_b].reshape(cube_count, 2, 16, 256)
        up = jnp.stack([ups[b][:, 128 * g : 128 * g + 128] for b in range(cube_count)])
        for z in range(2):
            for e in range(2):
                at = 256 * g + 128 * e
                grad_b[:, z, :, at : at + 128] = (up * part[:, z, :, 128 * e : 128 * e + 128]).astype(BF)


def spread_grad(target, b, zz, plane, shifter):
    moved = dot(shifter, plane).astype(BF)
    for v in range(3):
        target[b, zz, v, :, 128:2176] = moved[16 * v : 16 * v + 16]
        target[b, zz, v, :, :128] = jnp.zeros((16, 128), BF)
        target[b, zz, v, :, 2176:] = jnp.zeros((16, 128), BF)


def terms_b_kernel(pools, grad_b, wa, wb, terms, gs, tat, tbt):
    cube_count = grad_b.shape[0]
    shifter = row_picker(3, 1, 16)
    loop(cube_count * 2, lambda i: spread_grad(gs, i // 2, 2 + i % 2, grad_b[i // 2, i % 2], shifter))
    rows_b = cube_count * 2 * 16
    grads = jnp.concatenate(
        [grad_b[:, :, :, 256 * g : 256 * g + 256].reshape(rows_b, 256) for g in range(8)], axis=0
    )
    terms[pl.ds(27, C2, stride=28), :] = jnp.zeros((C2, 128), F32)

    def offset(d):
        block = wa[d].astype(F32)
        block = jnp.concatenate([block, block], axis=1)
        mirror(8 - d, rows_at(block, 0, 128).T[:64], tat)
        block = wb[d]
        turned = []
        for dx in (2, 1, 0):
            part = block[64 * dx : 64 * dx + 64].astype(F32)
            turned.append(jnp.concatenate([part, part], axis=0).T)
        block = jnp.concatenate(turned, axis=0)
        to = aligned(768 * (8 - d), 768)
        for e in range(2):
            tbt[to, 128 * e : 128 * e + 128] = halves(
                rows_at(block, 256 * e, 768), rows_at(block, 256 * e + 128, 768)
            )
        windows = jnp.concatenate(
            [pools[:, pl.ds(d // 3, 2), d % 3, :, 128 * g : 128 * g + 256].reshape(rows_b, 256) for g in range(8)],
            axis=0,
        )
        full = dot_t(windows, grads)
        for dx in range(3):
            term = full[64 * dx : 64 * dx + 64, :128] + full[64 * dx + 64 : 64 * dx + 128, 128:]
            terms[pl.ds(3 * d + dx, C2, stride=28), :] = term

    loop(9, offset)


def tree(parts):
    while len(parts) > 1:
        parts = [left + right for left, right in zip(parts[::2], parts[1::2])]
    return parts[0]


def scatter_kernel(where, keep, recv, *outs):
    for k, out in enumerate(outs):
        part = where[2] ^ k
        out[...] = (keep[part].astype(F32) + recv[part].astype(F32)).astype(BF)


def add_kernel(after, *refs):
    del after
    parts, out = refs[:-1], refs[-1]
    out[...] = tree([part[...].astype(F32) for part in parts]).astype(BF)


def stack_kernel(where, *refs):
    parts, out = refs[:-1], refs[-1]
    for k, part in enumerate(parts):
        out[where[2] ^ k] = part[...]


def finish_kernel(where, scale, own, other, out_a, out_b, whole):
    core = where[0] % 2
    whole[core] = own[...].astype(F32)
    whole[1 - core] = other[...].astype(F32)
    count = own.shape[0]
    for width, base, out in ((C2, 0, out_b), (C1 // 2, ROWS_B // (2 * count), out_a)):
        each = width // (2 * count)
        for i in range(width):
            start = base + 28 * (i % each)
            piece = whole[i // each // count, i // each % count, start : start + 27]
            out[:, 128 * i : 128 * i + 128] = piece * scale[0]


def backward_kernel(where, own, recv_a, recv_b, tbt, dsl, xs, terms_b, ga, keep, send, gs, back, gpool, acc, term, terms):
    del own
    cube_count = recv_a.shape[0]
    even = where[0] % 2 == 0
    shifter = row_picker(3, 1, 16)


    def planes(i):
        b, z = i // 2, i % 2
        from_a, from_b = recv_a[b, z].astype(F32), recv_b[b, z].astype(F32)
        spread_grad(gs, b, z, jnp.where(even, from_b, from_a).astype(BF), shifter)
        spread_grad(gs, b, 4 + z, jnp.where(even, from_a, from_b).astype(BF), shifter)

    loop(cube_count * 2, planes)

    low = jnp.where(where[0] == 0, 0.0, 0.125)
    high = jnp.where(where[0] == where[1] - 1, 0.0, 0.125)
    rows = cube_count * 4 * 16

    def back_dz(dz):
        columns = [
            jnp.concatenate(
                [gs[:, pl.ds(dz, 4), dy, :, 512 * q : 512 * q + 768].reshape(rows, 768) for q in range(4)], axis=0
            )
            for dy in range(3)
        ]
        part = dot(jnp.concatenate(columns, axis=1), tbt[aligned(2304 * dz, 2304)])
        back[...] = jnp.where(dz == 0, part, back[...] + part)

    loop(3, back_dz)
    for q in range(4):
        part = back[rows * q : rows * q + rows].reshape(cube_count, 4, 16, 256)
        for z in range(4):
            scale = low if z == 0 else high if z == 3 else 0.125
            gpool[:, z, :, 256 * q : 256 * q + 256] = part[:, z] * scale

    ga[:, :, :, :, :128] = jnp.zeros((cube_count, 6, 4, 16, 128), BF)
    ga[:, :, :, :, 2176:] = jnp.zeros((cube_count, 6, 4, 16, 128), BF)
    rows_a = cube_count * 6 * 16
    own_rows = cube_count * 4 * 16
    place = lax.broadcasted_iota(jnp.int32, (rows_a, 128), 0) % 16

    def one_group(g):
        lanes = pl.ds(pl.multiple_of(128 * g, 128), 128)
        up = gpool[:, :, :, lanes]
        up = jnp.concatenate(
            [up[:, 0:1], up[:, 1:2], up[:, 1:2], up[:, 2:3], up[:, 2:3], up[:, 3:4]], axis=1
        ).reshape(rows_a, 128)
        sides = []
        for p in range(2):
            pair = []
            for px in range(2):
                at = pl.ds(pl.multiple_of(256 * g + 128 * px, 128), 128)
                grad = up * dsl[:, :, p, :, at].astype(F32).reshape(rows_a, 128)
                to = pl.ds(pl.multiple_of(256 * g + 128 * px + 128, 128), 128)
                kept = grad.astype(BF).reshape(cube_count, 6, 16, 128)
                ga[:, :, 1 + p, :, to] = kept
                pair.append(kept[:, 1:5].reshape(own_rows, 128))
                if p == 1:
                    moved = jnp.where(place == 0, 0.0, pltpu.roll(grad, 1, 0))
                else:
                    moved = jnp.where(place == 15, 0.0, pltpu.roll(grad, rows_a - 1, 0))
                ga[:, :, 0 if p else 3, :, to] = moved.astype(BF).reshape(cube_count, 6, 16, 128)
            sides.append(jnp.concatenate(pair, axis=1))
        return sides, [windows_a(xs, ((HALO - 1, ZD),), p, 128 * g) for p in range(2)]

    def groups(i, carry):
        first, second = one_group(2 * i), one_group(2 * i + 1)
        grads = jnp.concatenate(first[0] + second[0], axis=0)
        acc[...] += dot_t(jnp.concatenate(first[1] + second[1], axis=0), grads)
        return carry

    acc[...] = jnp.zeros_like(acc)
    lax.fori_loop(0, 4, groups, 0)

    terms[pl.ds(27, C1 // 2, stride=28), :] = jnp.zeros((C1 // 2, 128), F32)
    mask = lanes_below((32, 128), 64)

    def extract(d):
        full = acc[aligned(256 * d, 256)]
        for dx in range(3):
            left = full[32 * dx : 32 * dx + 32, :128] + full[32 * dx + 32 : 32 * dx + 64, 128:]
            right = full[32 * dx + 64 : 32 * dx + 96, :128] + full[32 * dx + 96 : 32 * dx + 128, 128:]
            merged = jnp.where(mask, left, right)
            term[dx] = merged + pltpu.roll(merged, 64, 1)
            evens = term[dx, pl.ds(0, C1 // 2, stride=2), :]
            odds = term[dx, pl.ds(1, C1 // 2, stride=2), :]
            terms[pl.ds(3 * d + dx, C1 // 2, stride=28), :] = jnp.where(mask[:16], evens, odds)

    loop(9, extract)
    low = where[0] % 2 == 0
    count = keep.shape[0]
    for part in range(count):
        sides = []
        for core in range(2):
            at = core * count + part
            rows_b, rows_a = ROWS_B // (2 * count), ROWS_A // (2 * count)
            sides.append(
                jnp.concatenate(
                    [terms_b[rows_b * at : rows_b * at + rows_b], terms[rows_a * at : rows_a * at + rows_a]], axis=0
                )
            )
        keep[part] = jnp.where(low, sides[0], sides[1]).astype(BF)
        send[part] = jnp.where(low, sides[1], sides[0]).astype(BF)


def one_cube(b, ga, tat, out, acc, landed):
    rows = ZD * 16

    def step(dz):
        sides = []
        for p in range(2):
            columns = [
                jnp.concatenate(
                    [
                        ga[b, pl.ds(dz, ZD), p + dy, :, 512 * q : 512 * q + 768].reshape(rows, 768)
                        for q in range(4)
                    ],
                    axis=0,
                )
                for dy in range(3)
            ]
            sides.append(jnp.concatenate(columns, axis=1))
        part = dot(jnp.concatenate(sides, axis=0), tat[aligned(2304 * dz, 2304)])
        acc[...] = jnp.where(dz == 0, part, acc[...] + part)

    loop(3, step)
    both = acc[...].astype(BF).reshape(2, 4, ZD, 16, 256)
    row = lax.broadcasted_iota(jnp.int32, (32, 32), 0)
    col = lax.broadcasted_iota(jnp.int32, (32, 32), 1)
    mixer = jnp.where(col == row // 2 + 16 * (row % 2), 1.0, 0.0).astype(BF)
    for z in range(ZD):
        for q in range(4):
            pair = jnp.concatenate([both[0, q, z], both[1, q, z]], axis=0)
            out[z, :, 256 * q : 256 * q + 256] = dot(mixer, pair).astype(BF)
        if landed is not None:
            landed(z)


def early_cube_kernel(b):
    def kernel(ga, tat, out, acc):
        one_cube(b, ga, tat, out, acc, None)

    return kernel


def last_cube_kernel(ga, tat, *rest):
    early, (out, token, block, acc, sems) = rest[:-5], rest[-5:]
    last = len(early)
    copies = [pltpu.make_async_copy(cube, out.at[b], sems.at[b]) for b, cube in enumerate(early)]
    for copy in copies:
        copy.start()

    def landed(z):
        copy = pltpu.make_async_copy(block.at[z], out.at[last, z], sems.at[last + z])
        copy.start()
        copies.append(copy)

    one_cube(last, ga, tat, block, acc, landed)
    token[...] = jnp.zeros_like(token)
    for copy in copies:
        copy.wait()


def call(kernel, args, outs, scratch, flops, smem=0, any_in=(), any_out=(), aliases=None):
    specs = [SMEM if i < smem else ANY if i in any_in else VMEM for i in range(len(args))]
    return pl.pallas_call(
        kernel,
        out_shape=[jax.ShapeDtypeStruct(shape, dtype) for shape, dtype in outs],
        in_specs=specs,
        out_specs=[ANY if i in any_out else VMEM for i in range(len(outs))],
        scratch_shapes=scratch,
        input_output_aliases=aliases or {},
        compiler_params=pltpu.CompilerParams(vmem_limit_bytes=28 * 1024 * 1024),
        cost_estimate=pl.CostEstimate(flops=flops, bytes_accessed=1_000_000, transcendentals=0),
    )(*args)


def swap(first, second, count):
    pairs_a = [(i, i ^ 1) for i in range(count)]
    pairs_b = [(i, ((i + 1) ^ 1) - 1) for i in range(1, count - 1)]
    return lax.ppermute(first, "gz", pairs_a), lax.ppermute(second, "gz", pairs_b)


def swap_along(parts, axis, step):
    count = lax.axis_size(axis)
    return [
        lax.ppermute(part, axis, [(i, i ^ (k * step)) for i in range(count)]) for k, part in enumerate(parts) if k
    ]


def shards(cubes, weight_a, weight_b, cotangent):
    cube_count = cubes.shape[0]
    ring = lax.axis_size("gz")
    samples = lax.axis_size("sample")
    where = jnp.stack([lax.axis_index("gz"), jnp.int32(ring), lax.axis_index("sample")]).astype(jnp.int32)
    recv_a, recv_b = swap(cubes, cubes, ring)

    wa = weight_a.reshape(9, 96, C2)
    wb = weight_b.reshape(9, 192, C3)
    own_xs, ta, tb, own_slope, inner = call(
        prepare_kernel,
        [cubes, wa, wb],
        [
            ((cube_count, ZD + 2 * HALO, 4, 16, 1152), BF),
            ((2304, 256), BF),
            ((2304, 256), BF),
            ((cube_count, 6, 2, 16, 2048), BF),
            ((cube_count, 2, 16, 1024), F32),
        ],
        [],
        1_000_000_000,
    )
    xs, dsl, pools, grad_b = call(
        forward_kernel,
        [where, own_xs, own_slope, inner, recv_a, recv_b, ta, tb, cotangent],
        [
            ((cube_count, ZD + 2 * HALO, 4, 16, 1152), BF),
            ((cube_count, 6, 2, 16, 2048), BF),
            ((cube_count, 4, 3, 16, 1152), BF),
            ((cube_count, 2, 16, 2048), BF),
        ],
        [pltpu.VMEM((cube_count, 4, 16, 1024), BF)],
        8_000_000_000,
        smem=1,
        aliases={1: 0, 2: 1},
    )
    back_a, back_b = swap(grad_b, grad_b, ring)
    spread = ((cube_count, 6, 3, 16, 2304), BF)
    wide = ((6912, 256), BF)
    terms_b, own_gs, tat, tbt = call(
        terms_b_kernel, [pools, grad_b, wa, wb], [((ROWS_B, 128), F32), spread, wide, wide], [], 1_000_000_000
    )
    piece = (ROWS_A + ROWS_B) // (2 * samples)
    pieces = ((samples, piece, 128), BF)
    ga, keep, send, _ = call(
        backward_kernel,
        [where, own_gs, back_a, back_b, tbt, dsl, xs, terms_b],
        [((cube_count, 6, 4, 16, 2304), BF), pieces, pieces, spread],
        [
            pltpu.VMEM((cube_count * 256, 256), F32),
            pltpu.VMEM((cube_count, 4, 16, 1024), F32),
            pltpu.VMEM((2304, 256), F32),
            pltpu.VMEM((4, C1, 128), F32),
            pltpu.VMEM((ROWS_A, 128), F32),
        ],
        6_000_000_000,
        smem=1,
        aliases={1: 3},
    )
    small = [((piece, 128), BF)]
    (recv,) = swap_along([send] * 2, "gz", 1)
    parts = call(scatter_kernel, [where, keep, recv], small * samples, [], 1_000_000, smem=1)
    others = swap_along(parts, "sample", 1)
    cube = (ZD, SIDE, SIDE * C1)
    early = [
        call(early_cube_kernel(b), [ga, tat], [(cube, BF)], [pltpu.VMEM((512, 256), F32)], 2_000_000_000)[0] for b in range(cube_count - 1)
    ]
    (mine,) = call(add_kernel, [early[0], parts[0], *others], small, [], 1_000_000)
    others = swap_along([mine] * (ring // 2), "gz", 2)
    input_grad, done = call(
        last_cube_kernel,
        [ga, tat, *early],
        [((cube_count, *cube), BF), ((8, 128), F32)],
        [
            pltpu.VMEM(cube, BF),
            pltpu.VMEM((512, 256), F32),
            pltpu.SemaphoreType.DMA((cube_count - 1 + ZD,)),
        ],
        2_000_000_000,
        any_out=(0,),
    )
    (mine,) = call(add_kernel, [done, mine, *others], small, [], 1_000_000)
    (own,) = call(
        stack_kernel, [where, mine, *swap_along([mine] * samples, "sample", 1)], [pieces], [], 1_000_000, smem=1
    )
    (other,) = swap_along([own] * 2, "gz", 1)
    scale = jnp.full((1,), 1.0 / (cube_count * samples), F32)
    total_a, total_b = call(
        finish_kernel,
        [where, scale, own, other],
        [((27, C1 * C2), F32), ((27, C2 * C3), F32)],
        [pltpu.VMEM((2, samples, piece, 128), F32)],
        1_000_000,
        smem=2,
    )
    return input_grad, total_a, total_b


def solution(mesh):
    in_specs = (P("sample", "gz", None, None), P(), P(), P("sample", "gz", None, None))
    out_specs = (P("sample", "gz", None, None), P(), P())
    return jax.shard_map(shards, mesh=mesh, in_specs=in_specs, out_specs=out_specs, check_vma=False)
```

```python
import jax
import jax.numpy as jnp
from jax import lax
from jax.experimental import pallas as pl
from jax.experimental.pallas import tpu as pltpu
from jax.sharding import PartitionSpec as P

C1 = 32
C2 = 64
C3 = 128
SIDE = 32
ZD = 4
HALO = 3
ROWS_B = C1 * 2 * 28
ROWS_A = C1 // 2 * 28
BF = jnp.bfloat16
F32 = jnp.float32
VMEM = pl.BlockSpec(memory_space=pltpu.VMEM)
SMEM = pl.BlockSpec(memory_space=pltpu.SMEM)
ANY = pl.BlockSpec(memory_space=pl.ANY)


def dot(a, b):
    return jnp.dot(a, b, preferred_element_type=F32)


def dot_t(a, b):
    return lax.dot_general(a, b, (((0,), (0,)), ((), ())), preferred_element_type=F32)


def sigmoid(v):
    return pl.reciprocal(1.0 + jnp.exp(-v), approx=True)


def row_picker(variants, stride, columns):
    shape = (variants * 16, columns)
    row = lax.broadcasted_iota(jnp.int32, shape, 0)
    col = lax.broadcasted_iota(jnp.int32, shape, 1)
    return jnp.where(col == stride * (row % 16) + row // 16 - 1, 1.0, 0.0).astype(BF)


def rows_at(block, before, total):
    rows, lanes = block.shape
    parts = []
    if before:
        parts.append(jnp.zeros((before, lanes), block.dtype))
    parts.append(block)
    if total - before - rows:
        parts.append(jnp.zeros((total - before - rows, lanes), block.dtype))
    return jnp.concatenate(parts, axis=0) if len(parts) > 1 else block


def lanes_below(shape, bound):
    return lax.broadcasted_iota(jnp.int32, shape, 1) < bound


def halves(left, right):
    return jnp.where(lanes_below(left.shape, 64), left, right).astype(BF)


def silu(pre):
    squash = sigmoid(pre)
    act = pre * squash
    return act, (squash + act * (1.0 - squash)).astype(BF)


def windows_a(xs, spans, p, start, offsets=(0, 1, 2)):
    lanes = pl.ds(start if isinstance(start, int) else pl.multiple_of(start, 128), 256)
    columns = []
    for dz in offsets:
        for dy in range(3):
            parts = [xs[:, first + dz : first + dz + planes, p + dy, :, lanes] for first, planes in spans]
            whole = jnp.concatenate(parts, axis=1) if len(parts) > 1 else parts[0]
            columns.append(whole.reshape(whole.shape[0] * whole.shape[1] * 16, 256))
    return jnp.concatenate(columns, axis=1)


def spread_input(target, b, zz, plane, picker):
    plane = jnp.concatenate([jnp.zeros((32, 32), BF), plane, jnp.zeros((32, 96), BF)], axis=1)
    moved = dot(picker, plane).astype(BF)
    for v in range(4):
        target[b, zz, v] = moved[16 * v : 16 * v + 16]


RANKS = (-3, -1, 0, 2, 1, 3, 4, 6, 5, 7, 8, 10)


def mirror(d, block, tat):
    lane = lax.broadcasted_iota(jnp.int32, (64, 128), 1)
    turned = [block if s == 0 else pltpu.roll(block, 32 * s, 1) for s in range(4)]
    for slot, rank in enumerate(RANKS):
        for half in range(2):
            start = 32 * (rank - 1 - 4 * half)
            keep = (lane >= start) & (lane < start + 96)
            value = jnp.where(keep, turned[(rank - 1) % 4], 0.0).astype(BF)
            tat[768 * d + 64 * slot : 768 * d + 64 * slot + 64, 128 * half : 128 * half + 128] = value


def prepare_kernel(cubes, weight_a, weight_b, xs, ta, tb, dsl, inner, edge_low, edge_high, wa, wb):
    mask = lanes_below((27, 128), 64)
    for j in range(C1 // 2):
        both = weight_a[:, 128 * j : 128 * j + 128].astype(F32)
        other = pltpu.roll(both, 64, 1)
        wa[pl.ds(2 * j, 27, stride=C1), :] = jnp.where(mask, both, other)
        wa[pl.ds(2 * j + 1, 27, stride=C1), :] = jnp.where(mask, other, both)
    for i in range(C2):
        wb[pl.ds(i, 27, stride=C2), :] = weight_b[:, 128 * i : 128 * i + 128].astype(F32)
    picker = row_picker(4, 2, 32)
    for b in range(cubes.shape[0]):
        for z in range(ZD):
            spread_input(xs, b, HALO + z, cubes[b, z], picker)
    for d in range(9):
        block = wa[96 * d : 96 * d + 96]
        for px in range(2):
            ta[256 * d : 256 * d + 256, 128 * px : 128 * px + 128] = halves(
                rows_at(block, 32 * px, 256), rows_at(block, 64 + 32 * px, 256)
            )
        block = wb[192 * d : 192 * d + 192].astype(BF)
        for e in range(2):
            tb[256 * d : 256 * d + 256, 128 * e : 128 * e + 128] = rows_at(block, 64 * e, 256)

    cube_count = cubes.shape[0]
    pre = dot(
        jnp.concatenate(
            [windows_a(xs, ((HALO, 2),), p, 128 * g) for g in range(8) for p in range(2)], axis=0
        ),
        ta[...],
    )
    act, slope = silu(pre)
    slope = slope.reshape(8, 2, cube_count, 2, 16, 256)
    act = act.reshape(8, 2, cube_count, 2, 16, 256)
    for g in range(8):
        for p in range(2):
            dsl[:, 2:4, p, :, 256 * g : 256 * g + 256] = slope[g, p]
        part = act[g, 0] + act[g, 1]
        inner[:, :, :, 128 * g : 128 * g + 128] = part[..., :128] + part[..., 128:]
    for edge, first, offsets in ((edge_low, HALO - 1, (1, 2)), (edge_high, HALO + 2, (0, 1))):
        rows = jnp.concatenate(
            [windows_a(xs, ((first, 1),), p, 128 * g, offsets) for g in range(8) for p in range(2)], axis=0
        )
        edge[...] = dot(rows, ta[768 * offsets[0] : 768 * offsets[0] + 1536])


def forward_kernel(where, own, own_slope, inner, edge_low, edge_high, recv_a, recv_b, ta, tb, cot, xs, dsl, pools, grad_b, pooled):
    del own, own_slope
    cube_count = xs.shape[0]
    even = where[0] % 2 == 0
    picker = row_picker(4, 2, 32)
    for b in range(cube_count):
        for z in range(HALO):
            far = ZD - HALO + z
            below = jnp.where(even, recv_b[b, far].astype(F32), recv_a[b, far].astype(F32)).astype(BF)
            above = jnp.where(even, recv_a[b, z].astype(F32), recv_b[b, z].astype(F32)).astype(BF)
            spread_input(xs, b, z, below, picker)
            spread_input(xs, b, HALO + ZD + z, above, picker)

    low = jnp.where(where[0] == 0, 0.0, 0.125)
    high = jnp.where(where[0] == where[1] - 1, 0.0, 0.125)

    def groups(i, carry):
        def stack(spans, offsets=(0, 1, 2)):
            return jnp.concatenate(
                [windows_a(xs, spans, p, 512 * i + 128 * j, offsets) for j in range(4) for p in range(2)], axis=0
            )

        act, slope = silu(dot(stack(((0, 2), (HALO + ZD - 1, 2))), ta[...]))
        slope = slope.reshape(4, 2, cube_count, 4, 16, 256)
        act = act.reshape(4, 2, cube_count, 4, 16, 256)
        rows = cube_count * 128
        here = pl.ds(pl.multiple_of(rows * i, rows), rows)
        sides = []
        for edge, first, dz in ((edge_low, HALO - 1, 0), (edge_high, HALO + 2, 2)):
            pre = edge[here] + dot(stack(((first, 1),), (dz,)), ta[768 * dz : 768 * dz + 768])
            edge_act, edge_slope = silu(pre)
            edge_act = edge_act.reshape(4, 2, cube_count, 16, 256)
            sides.append((edge_act, edge_slope.reshape(4, 2, cube_count, 16, 256)))
        for j in range(4):
            for p in range(2):
                to = pl.ds(pl.multiple_of(1024 * i + 256 * j, 256), 256)
                dsl[:, 0, p, :, to] = slope[j, p][:, 1]
                dsl[:, 1, p, :, to] = sides[0][1][j, p]
                dsl[:, 4, p, :, to] = sides[1][1][j, p]
                dsl[:, 5, p, :, to] = slope[j, p][:, 2]
            part = act[j, 0] + act[j, 1]
            part = part[..., :128] + part[..., 128:]
            ends = [side[0][j, 0] + side[0][j, 1] for side in sides]
            ends = [end[..., :128] + end[..., 128:] for end in ends]
            out = pl.ds(pl.multiple_of(512 * i + 128 * j, 128), 128)
            pooled[:, 0, :, out] = ((part[:, 0] + part[:, 1]) * low).astype(BF)
            pooled[:, 1, :, out] = ((ends[0] + inner[:, 0, :, out]) * 0.125).astype(BF)
            pooled[:, 2, :, out] = ((ends[1] + inner[:, 1, :, out]) * 0.125).astype(BF)
            pooled[:, 3, :, out] = ((part[:, 2] + part[:, 3]) * high).astype(BF)
        return carry

    lax.fori_loop(0, 2, groups, 0)

    shifter = row_picker(3, 1, 16)
    for b in range(cube_count):
        for z in range(4):
            plane = jnp.concatenate([jnp.zeros((16, 64), BF), pooled[b, z], jnp.zeros((16, 64), BF)], axis=1)
            moved = dot(shifter, plane).astype(BF)
            for v in range(3):
                pools[b, z, v] = moved[16 * v : 16 * v + 16]

    rows_b = cube_count * 2 * 16
    columns = []
    for dz in range(3):
        for dy in range(3):
            columns.append(
                jnp.concatenate(
                    [
                        pools[:, dz : dz + 2, dy, :, 128 * g : 128 * g + 256].reshape(rows_b, 256)
                        for g in range(8)
                    ],
                    axis=0,
                )
            )
    pre_b = dot(jnp.concatenate(columns, axis=1), tb[...])
    squash = sigmoid(pre_b)
    slope_b = squash + pre_b * squash * (1.0 - squash)
    row = lax.broadcasted_iota(jnp.int32, (16, 8), 0)
    twice = jnp.where(row // 2 == lax.broadcasted_iota(jnp.int32, (16, 8), 1), 0.125, 0.0).astype(BF)
    ups = [dot(twice, cot[b, 0]) for b in range(cube_count)]
    for g in range(8):
        part = slope_b[rows_b * g : rows_b * g + rows_b].reshape(cube_count, 2, 16, 256)
        up = jnp.stack([ups[b][:, 128 * g : 128 * g + 128] for b in range(cube_count)])
        for z in range(2):
            for e in range(2):
                at = 256 * g + 128 * e
                grad_b[:, z, :, at : at + 128] = (up * part[:, z, :, 128 * e : 128 * e + 128]).astype(BF)


def spread_grad(target, b, zz, plane, shifter):
    moved = dot(shifter, plane).astype(BF)
    for v in range(3):
        target[b, zz, v, :, 128:2176] = moved[16 * v : 16 * v + 16]
        target[b, zz, v, :, :128] = jnp.zeros((16, 128), BF)
        target[b, zz, v, :, 2176:] = jnp.zeros((16, 128), BF)


def terms_b_kernel(pools, grad_b, wa, wb, terms, gs, tat, tbt):
    cube_count = grad_b.shape[0]
    shifter = row_picker(3, 1, 16)
    for b in range(cube_count):
        for z in range(2):
            spread_grad(gs, b, 2 + z, grad_b[b, z], shifter)
    for d in range(9):
        mirror(8 - d, rows_at(wa[96 * d : 96 * d + 96], 0, 128).T[:64], tat)
        block = wb[192 * d : 192 * d + 192]
        turned = []
        for dx in (2, 1, 0):
            part = block[64 * dx : 64 * dx + 64]
            turned.append(jnp.concatenate([part, part], axis=0).T)
        block = jnp.concatenate(turned, axis=0)
        to = 768 * (8 - d)
        for e in range(2):
            tbt[to : to + 768, 128 * e : 128 * e + 128] = halves(
                rows_at(block, 256 * e, 768), rows_at(block, 256 * e + 128, 768)
            )
    rows_b = cube_count * 2 * 16
    grads = jnp.concatenate(
        [grad_b[:, :, :, 256 * g : 256 * g + 256].reshape(rows_b, 256) for g in range(8)], axis=0
    )
    terms[pl.ds(27, C2, stride=28), :] = jnp.zeros((C2, 128), F32)
    for dz in range(3):
        for dy in range(3):
            windows = jnp.concatenate(
                [
                    pools[:, dz : dz + 2, dy, :, 128 * g : 128 * g + 256].reshape(rows_b, 256)
                    for g in range(8)
                ],
                axis=0,
            )
            full = dot_t(windows, grads)
            for dx in range(3):
                term = full[64 * dx : 64 * dx + 64, :128] + full[64 * dx + 64 : 64 * dx + 128, 128:]
                terms[pl.ds(9 * dz + 3 * dy + dx, C2, stride=28), :] = term


def tree(parts):
    while len(parts) > 1:
        parts = [left + right for left, right in zip(parts[::2], parts[1::2])]
    return parts[0]


def scatter_kernel(where, keep, recv, *outs):
    for k, out in enumerate(outs):
        part = where[2] ^ k
        out[...] = (keep[part].astype(F32) + recv[part].astype(F32)).astype(BF)


def add_kernel(after, *refs):
    del after
    parts, out = refs[:-1], refs[-1]
    out[...] = tree([part[...].astype(F32) for part in parts]).astype(BF)


def stack_kernel(where, *refs):
    parts, out = refs[:-1], refs[-1]
    for k, part in enumerate(parts):
        out[where[2] ^ k] = part[...]


def finish_kernel(where, scale, own, other, out_a, out_b, whole):
    core = where[0] % 2
    whole[core] = own[...].astype(F32)
    whole[1 - core] = other[...].astype(F32)
    count = own.shape[0]
    for width, base, out in ((C2, 0, out_b), (C1 // 2, ROWS_B // (2 * count), out_a)):
        each = width // (2 * count)
        for i in range(width):
            start = base + 28 * (i % each)
            piece = whole[i // each // count, i // each % count, start : start + 27]
            out[:, 128 * i : 128 * i + 128] = piece * scale[0]


def backward_kernel(where, own, recv_a, recv_b, tbt, dsl, xs, terms_b, ga, keep, send, gs, gpool, acc, term, terms):
    del own
    cube_count = recv_a.shape[0]
    even = where[0] % 2 == 0
    shifter = row_picker(3, 1, 16)

    for b in range(cube_count):
        for z in range(2):
            from_a, from_b = recv_a[b, z].astype(F32), recv_b[b, z].astype(F32)
            spread_grad(gs, b, z, jnp.where(even, from_b, from_a).astype(BF), shifter)
            spread_grad(gs, b, 4 + z, jnp.where(even, from_a, from_b).astype(BF), shifter)

    low = jnp.where(where[0] == 0, 0.0, 0.125)
    high = jnp.where(where[0] == where[1] - 1, 0.0, 0.125)
    rows = cube_count * 4 * 16
    columns = []
    for dz in range(3):
        for dy in range(3):
            columns.append(
                jnp.concatenate(
                    [gs[:, dz : dz + 4, dy, :, 512 * q : 512 * q + 768].reshape(rows, 768) for q in range(4)],
                    axis=0,
                )
            )
    back = dot(jnp.concatenate(columns, axis=1), tbt[...])
    for q in range(4):
        part = back[rows * q : rows * q + rows].reshape(cube_count, 4, 16, 256)
        for z in range(4):
            scale = low if z == 0 else high if z == 3 else 0.125
            gpool[:, z, :, 256 * q : 256 * q + 256] = part[:, z] * scale

    ga[:, :, :, :, :128] = jnp.zeros((cube_count, 6, 4, 16, 128), BF)
    ga[:, :, :, :, 2176:] = jnp.zeros((cube_count, 6, 4, 16, 128), BF)
    rows_a = cube_count * 6 * 16
    own_rows = cube_count * 4 * 16
    place = lax.broadcasted_iota(jnp.int32, (rows_a, 128), 0) % 16

    def one_group(g):
        lanes = pl.ds(pl.multiple_of(128 * g, 128), 128)
        up = gpool[:, :, :, lanes]
        up = jnp.concatenate(
            [up[:, 0:1], up[:, 1:2], up[:, 1:2], up[:, 2:3], up[:, 2:3], up[:, 3:4]], axis=1
        ).reshape(rows_a, 128)
        sides = []
        for p in range(2):
            pair = []
            for px in range(2):
                at = pl.ds(pl.multiple_of(256 * g + 128 * px, 128), 128)
                grad = up * dsl[:, :, p, :, at].astype(F32).reshape(rows_a, 128)
                to = pl.ds(pl.multiple_of(256 * g + 128 * px + 128, 128), 128)
                kept = grad.astype(BF).reshape(cube_count, 6, 16, 128)
                ga[:, :, 1 + p, :, to] = kept
                pair.append(kept[:, 1:5].reshape(own_rows, 128))
                if p == 1:
                    moved = jnp.where(place == 0, 0.0, pltpu.roll(grad, 1, 0))
                else:
                    moved = jnp.where(place == 15, 0.0, pltpu.roll(grad, rows_a - 1, 0))
                ga[:, :, 0 if p else 3, :, to] = moved.astype(BF).reshape(cube_count, 6, 16, 128)
            sides.append(jnp.concatenate(pair, axis=1))
        return sides, [windows_a(xs, ((HALO - 1, ZD),), p, 128 * g) for p in range(2)]

    def groups(i, carry):
        first, second = one_group(2 * i), one_group(2 * i + 1)
        grads = jnp.concatenate(first[0] + second[0], axis=0)
        acc[...] += dot_t(jnp.concatenate(first[1] + second[1], axis=0), grads)
        return carry

    acc[...] = jnp.zeros_like(acc)
    lax.fori_loop(0, 4, groups, 0)

    terms[pl.ds(27, C1 // 2, stride=28), :] = jnp.zeros((C1 // 2, 128), F32)
    mask = lanes_below((32, 128), 64)
    for d in range(9):
        full = acc[256 * d : 256 * d + 256]
        for dx in range(3):
            left = full[32 * dx : 32 * dx + 32, :128] + full[32 * dx + 32 : 32 * dx + 64, 128:]
            right = full[32 * dx + 64 : 32 * dx + 96, :128] + full[32 * dx + 96 : 32 * dx + 128, 128:]
            merged = jnp.where(mask, left, right)
            slot = (3 * d + dx) % 4
            term[slot] = merged + pltpu.roll(merged, 64, 1)
            evens = term[slot, pl.ds(0, C1 // 2, stride=2), :]
            odds = term[slot, pl.ds(1, C1 // 2, stride=2), :]
            terms[pl.ds(3 * d + dx, C1 // 2, stride=28), :] = jnp.where(mask[:16], evens, odds)
    low = where[0] % 2 == 0
    count = keep.shape[0]
    for part in range(count):
        sides = []
        for core in range(2):
            at = core * count + part
            rows_b, rows_a = ROWS_B // (2 * count), ROWS_A // (2 * count)
            sides.append(
                jnp.concatenate(
                    [terms_b[rows_b * at : rows_b * at + rows_b], terms[rows_a * at : rows_a * at + rows_a]], axis=0
                )
            )
        keep[part] = jnp.where(low, sides[0], sides[1]).astype(BF)
        send[part] = jnp.where(low, sides[1], sides[0]).astype(BF)


def one_cube(b, ga, tat, out, landed):
    rows = ZD * 16
    sides = []
    for p in range(2):
        columns = []
        for dz in range(3):
            for dy in range(3):
                columns.append(
                    jnp.concatenate(
                        [ga[b, dz : dz + ZD, p + dy, :, 512 * q : 512 * q + 768].reshape(rows, 768) for q in range(4)],
                        axis=0,
                    )
                )
        sides.append(jnp.concatenate(columns, axis=1))
    both = dot(jnp.concatenate(sides, axis=0), tat[...]).astype(BF).reshape(2, 4, ZD, 16, 256)
    row = lax.broadcasted_iota(jnp.int32, (32, 32), 0)
    col = lax.broadcasted_iota(jnp.int32, (32, 32), 1)
    mixer = jnp.where(col == row // 2 + 16 * (row % 2), 1.0, 0.0).astype(BF)
    for z in range(ZD):
        for q in range(4):
            pair = jnp.concatenate([both[0, q, z], both[1, q, z]], axis=0)
            out[z, :, 256 * q : 256 * q + 256] = dot(mixer, pair).astype(BF)
        if landed is not None:
            landed(z)


def early_cube_kernel(b):
    def kernel(ga, tat, out):
        one_cube(b, ga, tat, out, None)

    return kernel


def last_cube_kernel(ga, tat, *rest):
    early, (out, token, block, sems) = rest[:-4], rest[-4:]
    last = len(early)
    copies = [pltpu.make_async_copy(cube, out.at[b], sems.at[b]) for b, cube in enumerate(early)]
    for copy in copies:
        copy.start()

    def landed(z):
        copy = pltpu.make_async_copy(block.at[z], out.at[last, z], sems.at[last + z])
        copy.start()
        copies.append(copy)

    one_cube(last, ga, tat, block, landed)
    token[...] = jnp.zeros_like(token)
    for copy in copies:
        copy.wait()


def call(kernel, args, outs, scratch, flops, smem=0, any_in=(), any_out=(), aliases=None):
    specs = [SMEM if i < smem else ANY if i in any_in else VMEM for i in range(len(args))]
    return pl.pallas_call(
        kernel,
        out_shape=[jax.ShapeDtypeStruct(shape, dtype) for shape, dtype in outs],
        in_specs=specs,
        out_specs=[ANY if i in any_out else VMEM for i in range(len(outs))],
        scratch_shapes=scratch,
        input_output_aliases=aliases or {},
        compiler_params=pltpu.CompilerParams(vmem_limit_bytes=28 * 1024 * 1024),
        cost_estimate=pl.CostEstimate(flops=flops, bytes_accessed=1_000_000, transcendentals=0),
    )(*args)


def swap(first, second, count):
    pairs_a = [(i, i ^ 1) for i in range(count)]
    pairs_b = [(i, ((i + 1) ^ 1) - 1) for i in range(1, count - 1)]
    return lax.ppermute(first, "gz", pairs_a), lax.ppermute(second, "gz", pairs_b)


def swap_along(parts, axis, step):
    count = lax.axis_size(axis)
    return [
        lax.ppermute(part, axis, [(i, i ^ (k * step)) for i in range(count)]) for k, part in enumerate(parts) if k
    ]


def shards(cubes, weight_a, weight_b, cotangent):
    cube_count = cubes.shape[0]
    ring = lax.axis_size("gz")
    samples = lax.axis_size("sample")
    where = jnp.stack([lax.axis_index("gz"), jnp.int32(ring), lax.axis_index("sample")]).astype(jnp.int32)
    recv_a, recv_b = swap(cubes, cubes, ring)

    own_xs, ta, tb, own_slope, inner, edge_low, edge_high, wa, wb = call(
        prepare_kernel,
        [cubes, weight_a, weight_b],
        [
            ((cube_count, ZD + 2 * HALO, 4, 16, 1152), BF),
            ((2304, 256), BF),
            ((2304, 256), BF),
            ((cube_count, 6, 2, 16, 2048), BF),
            ((cube_count, 2, 16, 1024), F32),
            ((cube_count * 256, 256), F32),
            ((cube_count * 256, 256), F32),
            ((27 * C1, 128), F32),
            ((27 * C2, 128), F32),
        ],
        [],
        1_000_000_000,
    )
    xs, dsl, pools, grad_b = call(
        forward_kernel,
        [where, own_xs, own_slope, inner, edge_low, edge_high, recv_a, recv_b, ta, tb, cotangent],
        [
            ((cube_count, ZD + 2 * HALO, 4, 16, 1152), BF),
            ((cube_count, 6, 2, 16, 2048), BF),
            ((cube_count, 4, 3, 16, 1152), BF),
            ((cube_count, 2, 16, 2048), BF),
        ],
        [pltpu.VMEM((cube_count, 4, 16, 1024), BF)],
        8_000_000_000,
        smem=1,
        aliases={1: 0, 2: 1},
    )
    back_a, back_b = swap(grad_b, grad_b, ring)
    spread = ((cube_count, 6, 3, 16, 2304), BF)
    wide = ((6912, 256), BF)
    terms_b, own_gs, tat, tbt = call(
        terms_b_kernel, [pools, grad_b, wa, wb], [((ROWS_B, 128), F32), spread, wide, wide], [], 1_000_000_000
    )
    piece = (ROWS_A + ROWS_B) // (2 * samples)
    pieces = ((samples, piece, 128), BF)
    ga, keep, send, _ = call(
        backward_kernel,
        [where, own_gs, back_a, back_b, tbt, dsl, xs, terms_b],
        [((cube_count, 6, 4, 16, 2304), BF), pieces, pieces, spread],
        [
            pltpu.VMEM((cube_count, 4, 16, 1024), F32),
            pltpu.VMEM((2304, 256), F32),
            pltpu.VMEM((4, C1, 128), F32),
            pltpu.VMEM((ROWS_A, 128), F32),
        ],
        6_000_000_000,
        smem=1,
        aliases={1: 3},
    )
    small = [((piece, 128), BF)]
    (recv,) = swap_along([send] * 2, "gz", 1)
    parts = call(scatter_kernel, [where, keep, recv], small * samples, [], 1_000_000, smem=1)
    others = swap_along(parts, "sample", 1)
    cube = (ZD, SIDE, SIDE * C1)
    early = [
        call(early_cube_kernel(b), [ga, tat], [(cube, BF)], [], 2_000_000_000)[0] for b in range(cube_count - 1)
    ]
    (mine,) = call(add_kernel, [early[0], parts[0], *others], small, [], 1_000_000)
    others = swap_along([mine] * (ring // 2), "gz", 2)
    input_grad, done = call(
        last_cube_kernel,
        [ga, tat, *early],
        [((cube_count, *cube), BF), ((8, 128), F32)],
        [pltpu.VMEM(cube, BF), pltpu.SemaphoreType.DMA((cube_count - 1 + ZD,))],
        2_000_000_000,
        any_out=(0,),
    )
    (mine,) = call(add_kernel, [done, mine, *others], small, [], 1_000_000)
    (own,) = call(
        stack_kernel, [where, mine, *swap_along([mine] * samples, "sample", 1)], [pieces], [], 1_000_000, smem=1
    )
    (other,) = swap_along([own] * 2, "gz", 1)
    scale = jnp.full((1,), 1.0 / (cube_count * samples), F32)
    total_a, total_b = call(
        finish_kernel,
        [where, scale, own, other],
        [((27, C1 * C2), F32), ((27, C2 * C3), F32)],
        [pltpu.VMEM((2, samples, piece, 128), F32)],
        1_000_000,
        smem=2,
    )
    return input_grad, total_a, total_b


def solution(mesh):
    in_specs = (P("sample", "gz", None, None), P(), P(), P("sample", "gz", None, None))
    out_specs = (P("sample", "gz", None, None), P(), P())
    return jax.shard_map(shards, mesh=mesh, in_specs=in_specs, out_specs=out_specs, check_vma=False)
```

```python
import jax
import jax.numpy as jnp
from jax import lax
from jax.experimental import pallas as pl
from jax.experimental.pallas import tpu as pltpu
from jax.sharding import PartitionSpec as P

C1 = 32
C2 = 64
C3 = 128
SIDE = 32
ZD = 4
HALO = 3
ROWS_B = C1 * 2 * 28
ROWS_A = C1 // 2 * 28
BF = jnp.bfloat16
F32 = jnp.float32
VMEM = pl.BlockSpec(memory_space=pltpu.VMEM)
SMEM = pl.BlockSpec(memory_space=pltpu.SMEM)
ANY = pl.BlockSpec(memory_space=pl.ANY)


def dot(a, b):
    return jnp.dot(a, b, preferred_element_type=F32)


def dot_t(a, b):
    return lax.dot_general(a, b, (((0,), (0,)), ((), ())), preferred_element_type=F32)


def sigmoid(v):
    return pl.reciprocal(1.0 + jnp.exp(-v), approx=True)


def row_picker(variants, stride, columns):
    shape = (variants * 16, columns)
    row = lax.broadcasted_iota(jnp.int32, shape, 0)
    col = lax.broadcasted_iota(jnp.int32, shape, 1)
    return jnp.where(col == stride * (row % 16) + row // 16 - 1, 1.0, 0.0).astype(BF)


def rows_at(block, before, total):
    rows, lanes = block.shape
    parts = []
    if before:
        parts.append(jnp.zeros((before, lanes), block.dtype))
    parts.append(block)
    if total - before - rows:
        parts.append(jnp.zeros((total - before - rows, lanes), block.dtype))
    return jnp.concatenate(parts, axis=0) if len(parts) > 1 else block


def lanes_below(shape, bound):
    return lax.broadcasted_iota(jnp.int32, shape, 1) < bound


def halves(left, right):
    return jnp.where(lanes_below(left.shape, 64), left, right).astype(BF)


def silu(pre):
    squash = sigmoid(pre)
    act = pre * squash
    return act, (squash + act * (1.0 - squash)).astype(BF)


def windows_a(xs, spans, p, start, offsets=(0, 1, 2)):
    lanes = pl.ds(start if isinstance(start, int) else pl.multiple_of(start, 128), 256)
    columns = []
    for dz in offsets:
        for dy in range(3):
            parts = [xs[:, first + dz : first + dz + planes, p + dy, :, lanes] for first, planes in spans]
            whole = jnp.concatenate(parts, axis=1) if len(parts) > 1 else parts[0]
            columns.append(whole.reshape(whole.shape[0] * whole.shape[1] * 16, 256))
    return jnp.concatenate(columns, axis=1)


def spread_input(target, b, zz, plane, picker):
    plane = jnp.concatenate([jnp.zeros((32, 32), BF), plane, jnp.zeros((32, 96), BF)], axis=1)
    moved = dot(picker, plane).astype(BF)
    for v in range(4):
        target[b, zz, v] = moved[16 * v : 16 * v + 16]


RANKS = (-3, -1, 0, 2, 1, 3, 4, 6, 5, 7, 8, 10)


def mirror(d, block, tat):
    lane = lax.broadcasted_iota(jnp.int32, (64, 128), 1)
    turned = [block if s == 0 else pltpu.roll(block, 32 * s, 1) for s in range(4)]
    for slot, rank in enumerate(RANKS):
        for half in range(2):
            start = 32 * (rank - 1 - 4 * half)
            keep = (lane >= start) & (lane < start + 96)
            value = jnp.where(keep, turned[(rank - 1) % 4], 0.0).astype(BF)
            tat[768 * d + 64 * slot : 768 * d + 64 * slot + 64, 128 * half : 128 * half + 128] = value


def prepare_kernel(cubes, weight_a, weight_b, xs, ta, tb, dsl, inner, edge_low, edge_high, wa, wb):
    mask = lanes_below((27, 128), 64)
    for j in range(C1 // 2):
        both = weight_a[:, 128 * j : 128 * j + 128].astype(F32)
        other = pltpu.roll(both, 64, 1)
        wa[pl.ds(2 * j, 27, stride=C1), :] = jnp.where(mask, both, other)
        wa[pl.ds(2 * j + 1, 27, stride=C1), :] = jnp.where(mask, other, both)
    for i in range(C2):
        wb[pl.ds(i, 27, stride=C2), :] = weight_b[:, 128 * i : 128 * i + 128].astype(F32)
    picker = row_picker(4, 2, 32)
    for b in range(cubes.shape[0]):
        for z in range(ZD):
            spread_input(xs, b, HALO + z, cubes[b, z], picker)
    for d in range(9):
        block = wa[96 * d : 96 * d + 96]
        for px in range(2):
            ta[256 * d : 256 * d + 256, 128 * px : 128 * px + 128] = halves(
                rows_at(block, 32 * px, 256), rows_at(block, 64 + 32 * px, 256)
            )
        block = wb[192 * d : 192 * d + 192].astype(BF)
        for e in range(2):
            tb[256 * d : 256 * d + 256, 128 * e : 128 * e + 128] = rows_at(block, 64 * e, 256)

    cube_count = cubes.shape[0]
    pre = dot(
        jnp.concatenate(
            [windows_a(xs, ((HALO, 2),), p, 128 * g) for g in range(8) for p in range(2)], axis=0
        ),
        ta[...],
    )
    act, slope = silu(pre)
    slope = slope.reshape(8, 2, cube_count, 2, 16, 256)
    act = act.reshape(8, 2, cube_count, 2, 16, 256)
    for g in range(8):
        for p in range(2):
            dsl[:, 2:4, p, :, 256 * g : 256 * g + 256] = slope[g, p]
        part = act[g, 0] + act[g, 1]
        inner[:, :, :, 128 * g : 128 * g + 128] = part[..., :128] + part[..., 128:]
    for edge, first, offsets in ((edge_low, HALO - 1, (1, 2)), (edge_high, HALO + 2, (0, 1))):
        rows = jnp.concatenate(
            [windows_a(xs, ((first, 1),), p, 128 * g, offsets) for g in range(8) for p in range(2)], axis=0
        )
        edge[...] = dot(rows, ta[768 * offsets[0] : 768 * offsets[0] + 1536])


def forward_kernel(where, own, own_slope, inner, edge_low, edge_high, recv_a, recv_b, ta, tb, cot, xs, dsl, pools, grad_b, pooled):
    del own, own_slope
    cube_count = xs.shape[0]
    even = where[0] % 2 == 0
    picker = row_picker(4, 2, 32)
    for b in range(cube_count):
        for z in range(HALO):
            far = ZD - HALO + z
            below = jnp.where(even, recv_b[b, z].astype(F32), recv_a[b, far].astype(F32)).astype(BF)
            above = jnp.where(even, recv_a[b, z].astype(F32), recv_b[b, z].astype(F32)).astype(BF)
            spread_input(xs, b, z, below, picker)
            spread_input(xs, b, HALO + ZD + z, above, picker)

    low = jnp.where(where[0] == 0, 0.0, 0.125)
    high = jnp.where(where[0] == where[1] - 1, 0.0, 0.125)

    def groups(i, carry):
        def stack(spans, offsets=(0, 1, 2)):
            return jnp.concatenate(
                [windows_a(xs, spans, p, 512 * i + 128 * j, offsets) for j in range(4) for p in range(2)], axis=0
            )

        act, slope = silu(dot(stack(((0, 2), (HALO + ZD - 1, 2))), ta[...]))
        slope = slope.reshape(4, 2, cube_count, 4, 16, 256)
        act = act.reshape(4, 2, cube_count, 4, 16, 256)
        rows = cube_count * 128
        here = pl.ds(pl.multiple_of(rows * i, rows), rows)
        sides = []
        for edge, first, dz in ((edge_low, HALO - 1, 0), (edge_high, HALO + 2, 2)):
            pre = edge[here] + dot(stack(((first, 1),), (dz,)), ta[768 * dz : 768 * dz + 768])
            edge_act, edge_slope = silu(pre)
            edge_act = edge_act.reshape(4, 2, cube_count, 16, 256)
            sides.append((edge_act, edge_slope.reshape(4, 2, cube_count, 16, 256)))
        for j in range(4):
            for p in range(2):
                to = pl.ds(pl.multiple_of(1024 * i + 256 * j, 256), 256)
                dsl[:, 0, p, :, to] = slope[j, p][:, 1]
                dsl[:, 1, p, :, to] = sides[0][1][j, p]
                dsl[:, 4, p, :, to] = sides[1][1][j, p]
                dsl[:, 5, p, :, to] = slope[j, p][:, 2]
            part = act[j, 0] + act[j, 1]
            part = part[..., :128] + part[..., 128:]
            ends = [side[0][j, 0] + side[0][j, 1] for side in sides]
            ends = [end[..., :128] + end[..., 128:] for end in ends]
            out = pl.ds(pl.multiple_of(512 * i + 128 * j, 128), 128)
            pooled[:, 0, :, out] = ((part[:, 0] + part[:, 1]) * low).astype(BF)
            pooled[:, 1, :, out] = ((ends[0] + inner[:, 0, :, out]) * 0.125).astype(BF)
            pooled[:, 2, :, out] = ((ends[1] + inner[:, 1, :, out]) * 0.125).astype(BF)
            pooled[:, 3, :, out] = ((part[:, 2] + part[:, 3]) * high).astype(BF)
        return carry

    lax.fori_loop(0, 2, groups, 0)

    shifter = row_picker(3, 1, 16)
    for b in range(cube_count):
        for z in range(4):
            plane = jnp.concatenate([jnp.zeros((16, 64), BF), pooled[b, z], jnp.zeros((16, 64), BF)], axis=1)
            moved = dot(shifter, plane).astype(BF)
            for v in range(3):
                pools[b, z, v] = moved[16 * v : 16 * v + 16]

    rows_b = cube_count * 2 * 16
    columns = []
    for dz in range(3):
        for dy in range(3):
            columns.append(
                jnp.concatenate(
                    [
                        pools[:, dz : dz + 2, dy, :, 128 * g : 128 * g + 256].reshape(rows_b, 256)
                        for g in range(8)
                    ],
                    axis=0,
                )
            )
    pre_b = dot(jnp.concatenate(columns, axis=1), tb[...])
    squash = sigmoid(pre_b)
    slope_b = squash + pre_b * squash * (1.0 - squash)
    row = lax.broadcasted_iota(jnp.int32, (16, 8), 0)
    twice = jnp.where(row // 2 == lax.broadcasted_iota(jnp.int32, (16, 8), 1), 0.125, 0.0).astype(BF)
    ups = [dot(twice, cot[b, 0]) for b in range(cube_count)]
    for g in range(8):
        part = slope_b[rows_b * g : rows_b * g + rows_b].reshape(cube_count, 2, 16, 256)
        up = jnp.stack([ups[b][:, 128 * g : 128 * g + 128] for b in range(cube_count)])
        for z in range(2):
            for e in range(2):
                at = 256 * g + 128 * e
                grad_b[:, z, :, at : at + 128] = (up * part[:, z, :, 128 * e : 128 * e + 128]).astype(BF)


def spread_grad(target, b, zz, plane, shifter):
    moved = dot(shifter, plane).astype(BF)
    for v in range(3):
        target[b, zz, v, :, 128:2176] = moved[16 * v : 16 * v + 16]
        target[b, zz, v, :, :128] = jnp.zeros((16, 128), BF)
        target[b, zz, v, :, 2176:] = jnp.zeros((16, 128), BF)


def terms_b_kernel(pools, grad_b, wa, wb, terms, gs, tat, tbt, back):
    cube_count = grad_b.shape[0]
    shifter = row_picker(3, 1, 16)
    for b in range(cube_count):
        for z in range(2):
            spread_grad(gs, b, 2 + z, grad_b[b, z], shifter)
    for d in range(9):
        mirror(8 - d, rows_at(wa[96 * d : 96 * d + 96], 0, 128).T[:64], tat)
        block = wb[192 * d : 192 * d + 192]
        turned = []
        for dx in (2, 1, 0):
            part = block[64 * dx : 64 * dx + 64]
            turned.append(jnp.concatenate([part, part], axis=0).T)
        block = jnp.concatenate(turned, axis=0)
        to = 768 * (8 - d)
        for e in range(2):
            tbt[to : to + 768, 128 * e : 128 * e + 128] = halves(
                rows_at(block, 256 * e, 768), rows_at(block, 256 * e + 128, 768)
            )
    rows_b = cube_count * 2 * 16
    grads = jnp.concatenate(
        [grad_b[:, :, :, 256 * g : 256 * g + 256].reshape(rows_b, 256) for g in range(8)], axis=0
    )
    terms[pl.ds(27, C2, stride=28), :] = jnp.zeros((C2, 128), F32)
    for dz in range(3):
        for dy in range(3):
            windows = jnp.concatenate(
                [
                    pools[:, dz : dz + 2, dy, :, 128 * g : 128 * g + 256].reshape(rows_b, 256)
                    for g in range(8)
                ],
                axis=0,
            )
            full = dot_t(windows, grads)
            for dx in range(3):
                term = full[64 * dx : 64 * dx + 64, :128] + full[64 * dx + 64 : 64 * dx + 128, 128:]
                terms[pl.ds(9 * dz + 3 * dy + dx, C2, stride=28), :] = term

    sources = windows_b(gs, ((2, 2),))
    given = [
        dot(sources, tbt[2304 * dz : 2304 * dz + 2304]).reshape(4, cube_count, 2, 16, 256) for dz in range(3)
    ]
    back[:, :, 0] = given[2][:, :, 0]
    back[:, :, 1] = given[1][:, :, 0] + given[2][:, :, 1]
    back[:, :, 2] = given[0][:, :, 0] + given[1][:, :, 1]
    back[:, :, 3] = given[0][:, :, 1]


def windows_b(gs, spans):
    columns = []
    for dy in range(3):
        stacks = []
        for q in range(4):
            parts = [gs[:, first : first + planes, dy, :, 512 * q : 512 * q + 768] for first, planes in spans]
            whole = jnp.concatenate(parts, axis=1) if len(parts) > 1 else parts[0]
            stacks.append(whole.reshape(whole.shape[0] * whole.shape[1] * 16, 768))
        columns.append(jnp.concatenate(stacks, axis=0))
    return jnp.concatenate(columns, axis=1)


def tree(parts):
    while len(parts) > 1:
        parts = [left + right for left, right in zip(parts[::2], parts[1::2])]
    return parts[0]


def scatter_kernel(where, keep, recv, *outs):
    for k, out in enumerate(outs):
        part = where[2] ^ k
        out[...] = (keep[part].astype(F32) + recv[part].astype(F32)).astype(BF)


def add_kernel(after, *refs):
    del after
    parts, out = refs[:-1], refs[-1]
    out[...] = tree([part[...].astype(F32) for part in parts]).astype(BF)


def stack_kernel(where, *refs):
    parts, out = refs[:-1], refs[-1]
    for k, part in enumerate(parts):
        out[where[2] ^ k] = part[...]


def lay_out(pieces, scale, out_a, out_b, whole):
    whole[...] = pieces[...].astype(F32) * scale
    count = pieces.shape[0]
    for width, base, out in ((C2, 0, out_b), (C1 // 2, ROWS_B // (2 * count), out_a)):
        each = width // (2 * count)
        for i in range(width // 2):
            start = base + 28 * (i % each)
            out[:, 128 * i : 128 * i + 128] = whole[i // each, start : start + 27]


def first_half_kernel(scale, pieces, out_a, out_b, whole):
    lay_out(pieces, scale[0], out_a, out_b, whole)


def finish_kernel(where, scale, pieces, own_a, own_b, out_a, out_b, whole, other_a, other_b):
    lay_out(pieces, scale[0], other_a, other_b, whole)
    low = where[0] % 2 == 0
    for own, other, out in ((own_a, other_a, out_a), (own_b, other_b, out_b)):
        width = own.shape[1]
        mine, theirs = own[...], other[...]
        out[:, :width] = jnp.where(low, mine, theirs)
        out[:, width:] = jnp.where(low, theirs, mine)


def backward_kernel(where, own, recv_a, recv_b, tbt, dsl, xs, terms_b, back, ga, keep, send, gs, gpool, acc, term, terms):
    del own
    cube_count = recv_a.shape[0]
    even = where[0] % 2 == 0
    shifter = row_picker(3, 1, 16)

    for b in range(cube_count):
        for z in range(2):
            from_a, from_b = recv_a[b, z].astype(F32), recv_b[b, z].astype(F32)
            spread_grad(gs, b, z, jnp.where(even, from_b, from_a).astype(BF), shifter)
            spread_grad(gs, b, 4 + z, jnp.where(even, from_a, from_b).astype(BF), shifter)

    low = jnp.where(where[0] == 0, 0.0, 0.125)
    high = jnp.where(where[0] == where[1] - 1, 0.0, 0.125)
    parts = [
        dot(windows_b(gs, spans), tbt[2304 * dz : 2304 * dz + 2304]).reshape(4, cube_count, 2, 16, 256)
        for dz, spans in enumerate((((0, 2),), ((1, 1), (4, 1)), ((4, 2),)))
    ]
    extra = (
        parts[0][:, :, 0] + parts[1][:, :, 0],
        parts[0][:, :, 1],
        parts[2][:, :, 0],
        parts[1][:, :, 1] + parts[2][:, :, 1],
    )
    for z in range(4):
        scale = low if z == 0 else high if z == 3 else 0.125
        total = (back[:, :, z] + extra[z]) * scale
        for q in range(4):
            gpool[:, z, :, 256 * q : 256 * q + 256] = total[q]

    ga[:, :, :, :, :128] = jnp.zeros((cube_count, 6, 4, 16, 128), BF)
    ga[:, :, :, :, 2176:] = jnp.zeros((cube_count, 6, 4, 16, 128), BF)
    rows_a = cube_count * 6 * 16
    own_rows = cube_count * 4 * 16
    place = lax.broadcasted_iota(jnp.int32, (rows_a, 128), 0) % 16

    def one_group(g):
        lanes = pl.ds(pl.multiple_of(128 * g, 128), 128)
        up = gpool[:, :, :, lanes]
        up = jnp.concatenate(
            [up[:, 0:1], up[:, 1:2], up[:, 1:2], up[:, 2:3], up[:, 2:3], up[:, 3:4]], axis=1
        ).reshape(rows_a, 128)
        sides = []
        for p in range(2):
            pair = []
            for px in range(2):
                at = pl.ds(pl.multiple_of(256 * g + 128 * px, 128), 128)
                grad = up * dsl[:, :, p, :, at].astype(F32).reshape(rows_a, 128)
                to = pl.ds(pl.multiple_of(256 * g + 128 * px + 128, 128), 128)
                kept = grad.astype(BF).reshape(cube_count, 6, 16, 128)
                ga[:, :, 1 + p, :, to] = kept
                pair.append(kept[:, 1:5].reshape(own_rows, 128))
                if p == 1:
                    moved = jnp.where(place == 0, 0.0, pltpu.roll(grad, 1, 0))
                else:
                    moved = jnp.where(place == 15, 0.0, pltpu.roll(grad, rows_a - 1, 0))
                ga[:, :, 0 if p else 3, :, to] = moved.astype(BF).reshape(cube_count, 6, 16, 128)
            sides.append(jnp.concatenate(pair, axis=1))
        return sides, [windows_a(xs, ((HALO - 1, ZD),), p, 128 * g) for p in range(2)]

    def groups(i, carry):
        first, second = one_group(2 * i), one_group(2 * i + 1)
        grads = jnp.concatenate(first[0] + second[0], axis=0)
        acc[...] += dot_t(jnp.concatenate(first[1] + second[1], axis=0), grads)
        return carry

    acc[...] = jnp.zeros_like(acc)
    lax.fori_loop(0, 4, groups, 0)

    terms[pl.ds(27, C1 // 2, stride=28), :] = jnp.zeros((C1 // 2, 128), F32)
    mask = lanes_below((32, 128), 64)
    for d in range(9):
        full = acc[256 * d : 256 * d + 256]
        for dx in range(3):
            left = full[32 * dx : 32 * dx + 32, :128] + full[32 * dx + 32 : 32 * dx + 64, 128:]
            right = full[32 * dx + 64 : 32 * dx + 96, :128] + full[32 * dx + 96 : 32 * dx + 128, 128:]
            merged = jnp.where(mask, left, right)
            slot = (3 * d + dx) % 4
            term[slot] = merged + pltpu.roll(merged, 64, 1)
            evens = term[slot, pl.ds(0, C1 // 2, stride=2), :]
            odds = term[slot, pl.ds(1, C1 // 2, stride=2), :]
            terms[pl.ds(3 * d + dx, C1 // 2, stride=28), :] = jnp.where(mask[:16], evens, odds)
    low = where[0] % 2 == 0
    count = keep.shape[0]
    for part in range(count):
        sides = []
        for core in range(2):
            at = core * count + part
            rows_b, rows_a = ROWS_B // (2 * count), ROWS_A // (2 * count)
            sides.append(
                jnp.concatenate(
                    [terms_b[rows_b * at : rows_b * at + rows_b], terms[rows_a * at : rows_a * at + rows_a]], axis=0
                )
            )
        keep[part] = jnp.where(low, sides[0], sides[1]).astype(BF)
        send[part] = jnp.where(low, sides[1], sides[0]).astype(BF)


def one_cube(b, ga, tat, out, landed):
    rows = ZD * 16
    sides = []
    for p in range(2):
        columns = []
        for dz in range(3):
            for dy in range(3):
                columns.append(
                    jnp.concatenate(
                        [ga[b, dz : dz + ZD, p + dy, :, 512 * q : 512 * q + 768].reshape(rows, 768) for q in range(4)],
                        axis=0,
                    )
                )
        sides.append(jnp.concatenate(columns, axis=1))
    both = dot(jnp.concatenate(sides, axis=0), tat[...]).astype(BF).reshape(2, 4, ZD, 16, 256)
    row = lax.broadcasted_iota(jnp.int32, (32, 32), 0)
    col = lax.broadcasted_iota(jnp.int32, (32, 32), 1)
    mixer = jnp.where(col == row // 2 + 16 * (row % 2), 1.0, 0.0).astype(BF)
    for z in range(ZD):
        for q in range(4):
            pair = jnp.concatenate([both[0, q, z], both[1, q, z]], axis=0)
            out[z, :, 256 * q : 256 * q + 256] = dot(mixer, pair).astype(BF)
        if landed is not None:
            landed(z)


def early_cube_kernel(b):
    def kernel(ga, tat, out):
        one_cube(b, ga, tat, out, None)

    return kernel


def last_cube_kernel(ga, tat, *rest):
    early, (out, token, block, sems) = rest[:-4], rest[-4:]
    last = len(early)
    copies = [pltpu.make_async_copy(cube, out.at[b], sems.at[b]) for b, cube in enumerate(early)]
    for copy in copies:
        copy.start()

    def landed(z):
        copy = pltpu.make_async_copy(block.at[z], out.at[last, z], sems.at[last + z])
        copy.start()
        copies.append(copy)

    one_cube(last, ga, tat, block, landed)
    token[...] = jnp.zeros_like(token)
    for copy in copies:
        copy.wait()


def call(kernel, args, outs, scratch, flops, smem=0, any_in=(), any_out=(), aliases=None):
    specs = [SMEM if i < smem else ANY if i in any_in else VMEM for i in range(len(args))]
    return pl.pallas_call(
        kernel,
        out_shape=[jax.ShapeDtypeStruct(shape, dtype) for shape, dtype in outs],
        in_specs=specs,
        out_specs=[ANY if i in any_out else VMEM for i in range(len(outs))],
        scratch_shapes=scratch,
        input_output_aliases=aliases or {},
        compiler_params=pltpu.CompilerParams(vmem_limit_bytes=28 * 1024 * 1024),
        cost_estimate=pl.CostEstimate(flops=flops, bytes_accessed=1_000_000, transcendentals=0),
    )(*args)


def swap(first, second, count):
    pairs_a = [(i, i ^ 1) for i in range(count)]
    pairs_b = [(i, ((i + 1) ^ 1) - 1) for i in range(1, count - 1)]
    return lax.ppermute(first, "gz", pairs_a), lax.ppermute(second, "gz", pairs_b)


def swap_along(parts, axis, step):
    count = lax.axis_size(axis)
    return [
        lax.ppermute(part, axis, [(i, i ^ (k * step)) for i in range(count)]) for k, part in enumerate(parts) if k
    ]


def shards(cubes, weight_a, weight_b, cotangent):
    cube_count = cubes.shape[0]
    ring = lax.axis_size("gz")
    samples = lax.axis_size("sample")
    where = jnp.stack([lax.axis_index("gz"), jnp.int32(ring), lax.axis_index("sample")]).astype(jnp.int32)
    outer = lax.dynamic_slice_in_dim(cubes, lax.axis_index("gz") % 2, HALO, axis=1)
    recv_a, recv_b = swap(cubes, outer, ring)

    own_xs, ta, tb, own_slope, inner, edge_low, edge_high, wa, wb = call(
        prepare_kernel,
        [cubes, weight_a, weight_b],
        [
            ((cube_count, ZD + 2 * HALO, 4, 16, 1152), BF),
            ((2304, 256), BF),
            ((2304, 256), BF),
            ((cube_count, 6, 2, 16, 2048), BF),
            ((cube_count, 2, 16, 1024), F32),
            ((cube_count * 256, 256), F32),
            ((cube_count * 256, 256), F32),
            ((27 * C1, 128), F32),
            ((27 * C2, 128), F32),
        ],
        [],
        1_000_000_000,
    )
    xs, dsl, pools, grad_b = call(
        forward_kernel,
        [where, own_xs, own_slope, inner, edge_low, edge_high, recv_a, recv_b, ta, tb, cotangent],
        [
            ((cube_count, ZD + 2 * HALO, 4, 16, 1152), BF),
            ((cube_count, 6, 2, 16, 2048), BF),
            ((cube_count, 4, 3, 16, 1152), BF),
            ((cube_count, 2, 16, 2048), BF),
        ],
        [pltpu.VMEM((cube_count, 4, 16, 1024), BF)],
        8_000_000_000,
        smem=1,
        aliases={1: 0, 2: 1},
    )
    back_a, back_b = swap(grad_b, grad_b, ring)
    spread = ((cube_count, 6, 3, 16, 2304), BF)
    wide = ((6912, 256), BF)
    terms_b, own_gs, tat, tbt, back = call(
        terms_b_kernel,
        [pools, grad_b, wa, wb],
        [((ROWS_B, 128), F32), spread, wide, wide, ((4, cube_count, 4, 16, 256), F32)],
        [],
        1_000_000_000,
    )
    piece = (ROWS_A + ROWS_B) // (2 * samples)
    pieces = ((samples, piece, 128), BF)
    ga, keep, send, _ = call(
        backward_kernel,
        [where, own_gs, back_a, back_b, tbt, dsl, xs, terms_b, back],
        [((cube_count, 6, 4, 16, 2304), BF), pieces, pieces, spread],
        [
            pltpu.VMEM((cube_count, 4, 16, 1024), F32),
            pltpu.VMEM((2304, 256), F32),
            pltpu.VMEM((4, C1, 128), F32),
            pltpu.VMEM((ROWS_A, 128), F32),
        ],
        6_000_000_000,
        smem=1,
        aliases={1: 3},
    )
    small = [((piece, 128), BF)]
    (recv,) = swap_along([send] * 2, "gz", 1)
    parts = call(scatter_kernel, [where, keep, recv], small * samples, [], 1_000_000, smem=1)
    others = swap_along(parts, "sample", 1)
    cube = (ZD, SIDE, SIDE * C1)
    early = [
        call(early_cube_kernel(b), [ga, tat], [(cube, BF)], [], 2_000_000_000)[0] for b in range(cube_count - 1)
    ]
    (mine,) = call(add_kernel, [early[0], parts[0], *others], small, [], 1_000_000)
    others = swap_along([mine] * (ring // 2), "gz", 2)
    input_grad, done = call(
        last_cube_kernel,
        [ga, tat, *early],
        [((cube_count, *cube), BF), ((8, 128), F32)],
        [pltpu.VMEM(cube, BF), pltpu.SemaphoreType.DMA((cube_count - 1 + ZD,))],
        2_000_000_000,
        any_out=(0,),
    )
    (mine,) = call(add_kernel, [done, mine, *others], small, [], 1_000_000)
    (own,) = call(
        stack_kernel, [where, mine, *swap_along([mine] * samples, "sample", 1)], [pieces], [], 1_000_000, smem=1
    )
    (other,) = swap_along([own] * 2, "gz", 1)
    scale = jnp.full((1,), 1.0 / (cube_count * samples), F32)
    half_a, half_b = (27, C1 * C2 // 2), (27, C2 * C3 // 2)
    whole = pltpu.VMEM((samples, piece, 128), F32)
    own_a, own_b = call(first_half_kernel, [scale, own], [(half_a, F32), (half_b, F32)], [whole], 1_000_000, smem=1)
    total_a, total_b = call(
        finish_kernel,
        [where, scale, other, own_a, own_b],
        [((27, C1 * C2), F32), ((27, C2 * C3), F32)],
        [whole, pltpu.VMEM(half_a, F32), pltpu.VMEM(half_b, F32)],
        1_000_000,
        smem=2,
    )
    return input_grad, total_a, total_b


def solution(mesh):
    in_specs = (P("sample", "gz", None, None), P(), P(), P("sample", "gz", None, None))
    out_specs = (P("sample", "gz", None, None), P(), P())
    return jax.shard_map(shards, mesh=mesh, in_specs=in_specs, out_specs=out_specs, check_vma=False)
```

```python
import jax
import jax.numpy as jnp
from jax import lax
from jax.experimental import pallas as pl
from jax.experimental.pallas import tpu as pltpu
from jax.sharding import PartitionSpec as P

C1 = 32
C2 = 64
C3 = 128
SIDE = 32
ZD = 4
HALO = 3
ROWS_B = C1 * 2 * 28
ROWS_A = C1 // 2 * 28
BF = jnp.bfloat16
F32 = jnp.float32
VMEM = pl.BlockSpec(memory_space=pltpu.VMEM)
SMEM = pl.BlockSpec(memory_space=pltpu.SMEM)
ANY = pl.BlockSpec(memory_space=pl.ANY)


def dot(a, b):
    return jnp.dot(a, b, preferred_element_type=F32)


def dot_t(a, b):
    return lax.dot_general(a, b, (((0,), (0,)), ((), ())), preferred_element_type=F32)


def sigmoid(v):
    return pl.reciprocal(1.0 + jnp.exp(-v), approx=True)


def row_picker(variants, stride, columns):
    shape = (variants * 16, columns)
    row = lax.broadcasted_iota(jnp.int32, shape, 0)
    col = lax.broadcasted_iota(jnp.int32, shape, 1)
    return jnp.where(col == stride * (row % 16) + row // 16 - 1, 1.0, 0.0).astype(BF)


def rows_at(block, before, total):
    rows, lanes = block.shape
    parts = []
    if before:
        parts.append(jnp.zeros((before, lanes), block.dtype))
    parts.append(block)
    if total - before - rows:
        parts.append(jnp.zeros((total - before - rows, lanes), block.dtype))
    return jnp.concatenate(parts, axis=0) if len(parts) > 1 else block


def lanes_below(shape, bound):
    return lax.broadcasted_iota(jnp.int32, shape, 1) < bound


def halves(left, right):
    return jnp.where(lanes_below(left.shape, 64), left, right).astype(BF)


def silu(pre):
    squash = sigmoid(pre)
    act = pre * squash
    return act, (squash + act * (1.0 - squash)).astype(BF)


def windows_a(xs, spans, p, start, offsets=(0, 1, 2)):
    lanes = pl.ds(start if isinstance(start, int) else pl.multiple_of(start, 128), 256)
    columns = []
    for dz in offsets:
        for dy in range(3):
            parts = [xs[:, first + dz : first + dz + planes, p + dy, :, lanes] for first, planes in spans]
            whole = jnp.concatenate(parts, axis=1) if len(parts) > 1 else parts[0]
            columns.append(whole.reshape(whole.shape[0] * whole.shape[1] * 16, 256))
    return jnp.concatenate(columns, axis=1)


def spread_input(target, b, zz, plane, picker):
    plane = jnp.concatenate([jnp.zeros((32, 32), BF), plane, jnp.zeros((32, 96), BF)], axis=1)
    moved = dot(picker, plane).astype(BF)
    for v in range(4):
        target[b, zz, v] = moved[16 * v : 16 * v + 16]


RANKS = (-3, -1, 0, 2, 1, 3, 4, 6, 5, 7, 8, 10)


def mirror(d, block, tat):
    lane = lax.broadcasted_iota(jnp.int32, (64, 128), 1)
    turned = [block if s == 0 else pltpu.roll(block, 32 * s, 1) for s in range(4)]
    for slot, rank in enumerate(RANKS):
        for half in range(2):
            start = 32 * (rank - 1 - 4 * half)
            keep = (lane >= start) & (lane < start + 96)
            value = jnp.where(keep, turned[(rank - 1) % 4], 0.0).astype(BF)
            tat[768 * d + 64 * slot : 768 * d + 64 * slot + 64, 128 * half : 128 * half + 128] = value


def prepare_kernel(cubes, weight_a, xs, ta, dsl, inner, edge_low, edge_high, wa):
    mask = lanes_below((27, 128), 64)
    for j in range(C1 // 2):
        both = weight_a[:, 128 * j : 128 * j + 128].astype(F32)
        other = pltpu.roll(both, 64, 1)
        wa[pl.ds(2 * j, 27, stride=C1), :] = jnp.where(mask, both, other)
        wa[pl.ds(2 * j + 1, 27, stride=C1), :] = jnp.where(mask, other, both)
    picker = row_picker(4, 2, 32)
    for b in range(cubes.shape[0]):
        for z in range(ZD):
            spread_input(xs, b, HALO + z, cubes[b, z], picker)
    for d in range(9):
        block = wa[96 * d : 96 * d + 96]
        for px in range(2):
            ta[256 * d : 256 * d + 256, 128 * px : 128 * px + 128] = halves(
                rows_at(block, 32 * px, 256), rows_at(block, 64 + 32 * px, 256)
            )

    cube_count = cubes.shape[0]
    pre = dot(
        jnp.concatenate(
            [windows_a(xs, ((HALO, 2),), p, 128 * g) for g in range(8) for p in range(2)], axis=0
        ),
        ta[...],
    )
    act, slope = silu(pre)
    slope = slope.reshape(8, 2, cube_count, 2, 16, 256)
    act = act.reshape(8, 2, cube_count, 2, 16, 256)
    for g in range(8):
        for p in range(2):
            dsl[:, 2:4, p, :, 256 * g : 256 * g + 256] = slope[g, p]
        part = act[g, 0] + act[g, 1]
        inner[:, :, :, 128 * g : 128 * g + 128] = part[..., :128] + part[..., 128:]
    for edge, first, offsets in ((edge_low, HALO - 1, (1, 2)), (edge_high, HALO + 2, (0, 1))):
        rows = jnp.concatenate(
            [windows_a(xs, ((first, 1),), p, 128 * g, offsets) for g in range(8) for p in range(2)], axis=0
        )
        edge[...] = dot(rows, ta[768 * offsets[0] : 768 * offsets[0] + 1536])


def prepare_b_kernel(weight_b, tb, wb):
    for i in range(C2):
        wb[pl.ds(i, 27, stride=C2), :] = weight_b[:, 128 * i : 128 * i + 128].astype(F32)
    for d in range(9):
        block = wb[192 * d : 192 * d + 192].astype(BF)
        for e in range(2):
            tb[256 * d : 256 * d + 256, 128 * e : 128 * e + 128] = rows_at(block, 64 * e, 256)


def forward_kernel(where, own, own_slope, inner, edge_low, edge_high, recv_a, recv_b, ta, tb, cot, xs, dsl, pools, grad_b, pooled):
    del own, own_slope
    cube_count = xs.shape[0]
    even = where[0] % 2 == 0
    picker = row_picker(4, 2, 32)
    for b in range(cube_count):
        for z in range(HALO):
            far = ZD - HALO + z
            below = jnp.where(even, recv_b[b, z].astype(F32), recv_a[b, far].astype(F32)).astype(BF)
            above = jnp.where(even, recv_a[b, z].astype(F32), recv_b[b, z].astype(F32)).astype(BF)
            spread_input(xs, b, z, below, picker)
            spread_input(xs, b, HALO + ZD + z, above, picker)

    low = jnp.where(where[0] == 0, 0.0, 0.125)
    high = jnp.where(where[0] == where[1] - 1, 0.0, 0.125)

    def groups(i, carry):
        def stack(spans, offsets=(0, 1, 2)):
            return jnp.concatenate(
                [windows_a(xs, spans, p, 512 * i + 128 * j, offsets) for j in range(4) for p in range(2)], axis=0
            )

        act, slope = silu(dot(stack(((0, 2), (HALO + ZD - 1, 2))), ta[...]))
        slope = slope.reshape(4, 2, cube_count, 4, 16, 256)
        act = act.reshape(4, 2, cube_count, 4, 16, 256)
        rows = cube_count * 128
        here = pl.ds(pl.multiple_of(rows * i, rows), rows)
        sides = []
        for edge, first, dz in ((edge_low, HALO - 1, 0), (edge_high, HALO + 2, 2)):
            pre = edge[here] + dot(stack(((first, 1),), (dz,)), ta[768 * dz : 768 * dz + 768])
            edge_act, edge_slope = silu(pre)
            edge_act = edge_act.reshape(4, 2, cube_count, 16, 256)
            sides.append((edge_act, edge_slope.reshape(4, 2, cube_count, 16, 256)))
        for j in range(4):
            for p in range(2):
                to = pl.ds(pl.multiple_of(1024 * i + 256 * j, 256), 256)
                dsl[:, 0, p, :, to] = slope[j, p][:, 1]
                dsl[:, 1, p, :, to] = sides[0][1][j, p]
                dsl[:, 4, p, :, to] = sides[1][1][j, p]
                dsl[:, 5, p, :, to] = slope[j, p][:, 2]
            part = act[j, 0] + act[j, 1]
            part = part[..., :128] + part[..., 128:]
            ends = [side[0][j, 0] + side[0][j, 1] for side in sides]
            ends = [end[..., :128] + end[..., 128:] for end in ends]
            out = pl.ds(pl.multiple_of(512 * i + 128 * j, 128), 128)
            pooled[:, 0, :, out] = ((part[:, 0] + part[:, 1]) * low).astype(BF)
            pooled[:, 1, :, out] = ((ends[0] + inner[:, 0, :, out]) * 0.125).astype(BF)
            pooled[:, 2, :, out] = ((ends[1] + inner[:, 1, :, out]) * 0.125).astype(BF)
            pooled[:, 3, :, out] = ((part[:, 2] + part[:, 3]) * high).astype(BF)
        return carry

    lax.fori_loop(0, 2, groups, 0)

    shifter = row_picker(3, 1, 16)
    for b in range(cube_count):
        for z in range(4):
            plane = jnp.concatenate([jnp.zeros((16, 64), BF), pooled[b, z], jnp.zeros((16, 64), BF)], axis=1)
            moved = dot(shifter, plane).astype(BF)
            for v in range(3):
                pools[b, z, v] = moved[16 * v : 16 * v + 16]

    rows_b = cube_count * 2 * 16
    columns = []
    for dz in range(3):
        for dy in range(3):
            columns.append(
                jnp.concatenate(
                    [
                        pools[:, dz : dz + 2, dy, :, 128 * g : 128 * g + 256].reshape(rows_b, 256)
                        for g in range(8)
                    ],
                    axis=0,
                )
            )
    pre_b = dot(jnp.concatenate(columns, axis=1), tb[...])
    squash = sigmoid(pre_b)
    slope_b = squash + pre_b * squash * (1.0 - squash)
    row = lax.broadcasted_iota(jnp.int32, (16, 8), 0)
    twice = jnp.where(row // 2 == lax.broadcasted_iota(jnp.int32, (16, 8), 1), 0.125, 0.0).astype(BF)
    ups = [dot(twice, cot[b, 0]) for b in range(cube_count)]
    for g in range(8):
        part = slope_b[rows_b * g : rows_b * g + rows_b].reshape(cube_count, 2, 16, 256)
        up = jnp.stack([ups[b][:, 128 * g : 128 * g + 128] for b in range(cube_count)])
        for z in range(2):
            for e in range(2):
                at = 256 * g + 128 * e
                grad_b[:, z, :, at : at + 128] = (up * part[:, z, :, 128 * e : 128 * e + 128]).astype(BF)


def spread_grad(target, b, zz, plane, shifter):
    moved = dot(shifter, plane).astype(BF)
    for v in range(3):
        target[b, zz, v, :, 128:2176] = moved[16 * v : 16 * v + 16]
        target[b, zz, v, :, :128] = jnp.zeros((16, 128), BF)
        target[b, zz, v, :, 2176:] = jnp.zeros((16, 128), BF)


def terms_b_kernel(pools, grad_b, wa, wb, terms, gs, tat, tbt, back):
    cube_count = grad_b.shape[0]
    shifter = row_picker(3, 1, 16)
    for b in range(cube_count):
        for z in range(2):
            spread_grad(gs, b, 2 + z, grad_b[b, z], shifter)
    for d in range(9):
        mirror(8 - d, rows_at(wa[96 * d : 96 * d + 96], 0, 128).T[:64], tat)
        block = wb[192 * d : 192 * d + 192]
        turned = []
        for dx in (2, 1, 0):
            part = block[64 * dx : 64 * dx + 64]
            turned.append(jnp.concatenate([part, part], axis=0).T)
        block = jnp.concatenate(turned, axis=0)
        to = 768 * (8 - d)
        for e in range(2):
            tbt[to : to + 768, 128 * e : 128 * e + 128] = halves(
                rows_at(block, 256 * e, 768), rows_at(block, 256 * e + 128, 768)
            )
    rows_b = cube_count * 2 * 16
    grads = jnp.concatenate(
        [grad_b[:, :, :, 256 * g : 256 * g + 256].reshape(rows_b, 256) for g in range(8)], axis=0
    )
    terms[pl.ds(27, C2, stride=28), :] = jnp.zeros((C2, 128), F32)
    for dz in range(3):
        for dy in range(3):
            windows = jnp.concatenate(
                [
                    pools[:, dz : dz + 2, dy, :, 128 * g : 128 * g + 256].reshape(rows_b, 256)
                    for g in range(8)
                ],
                axis=0,
            )
            full = dot_t(windows, grads)
            for dx in range(3):
                term = full[64 * dx : 64 * dx + 64, :128] + full[64 * dx + 64 : 64 * dx + 128, 128:]
                terms[pl.ds(9 * dz + 3 * dy + dx, C2, stride=28), :] = term

    sources = windows_b(gs, ((2, 2),))
    given = [
        dot(sources, tbt[2304 * dz : 2304 * dz + 2304]).reshape(4, cube_count, 2, 16, 256) for dz in range(3)
    ]
    back[:, :, 0] = given[2][:, :, 0]
    back[:, :, 1] = given[1][:, :, 0] + given[2][:, :, 1]
    back[:, :, 2] = given[0][:, :, 0] + given[1][:, :, 1]
    back[:, :, 3] = given[0][:, :, 1]


def windows_b(gs, spans):
    columns = []
    for dy in range(3):
        stacks = []
        for q in range(4):
            parts = [gs[:, first : first + planes, dy, :, 512 * q : 512 * q + 768] for first, planes in spans]
            whole = jnp.concatenate(parts, axis=1) if len(parts) > 1 else parts[0]
            stacks.append(whole.reshape(whole.shape[0] * whole.shape[1] * 16, 768))
        columns.append(jnp.concatenate(stacks, axis=0))
    return jnp.concatenate(columns, axis=1)


def tree(parts):
    while len(parts) > 1:
        parts = [left + right for left, right in zip(parts[::2], parts[1::2])]
    return parts[0]


def scatter_kernel(where, keep, recv, *outs):
    for k, out in enumerate(outs):
        part = where[2] ^ k
        out[...] = (keep[part].astype(F32) + recv[part].astype(F32)).astype(BF)


def add_kernel(after, *refs):
    del after
    parts, out = refs[:-1], refs[-1]
    out[...] = tree([part[...].astype(F32) for part in parts]).astype(BF)


def stack_kernel(where, *refs):
    parts, out = refs[:-1], refs[-1]
    for k, part in enumerate(parts):
        out[where[2] ^ k] = part[...]


def lay_out(pieces, scale, out_a, out_b, whole):
    whole[...] = pieces[...].astype(F32) * scale
    count = pieces.shape[0]
    for width, base, out in ((C2, 0, out_b), (C1 // 2, ROWS_B // (2 * count), out_a)):
        each = width // (2 * count)
        for i in range(width // 2):
            start = base + 28 * (i % each)
            out[:, 128 * i : 128 * i + 128] = whole[i // each, start : start + 27]


def send_half(core, pieces, scale, outs, halves_out, whole, sems):
    lay_out(pieces, scale, *halves_out, whole)
    copies = []
    for i, (out, half) in enumerate(zip(outs, halves_out)):
        width = half.shape[1]
        copies.append(
            pltpu.make_async_copy(half, out.at[:, pl.ds(pl.multiple_of(core * width, width), width)], sems.at[i])
        )
        copies[-1].start()
    for copy in copies:
        copy.wait()


def first_half_kernel(where, scale, pieces, out_a, out_b, whole, half_a, half_b, sems):
    send_half(where[0] % 2, pieces, scale[0], (out_a, out_b), (half_a, half_b), whole, sems)


def finish_kernel(where, scale, pieces, before_a, before_b, out_a, out_b, whole, half_a, half_b, sems):
    del before_a, before_b
    send_half(1 - where[0] % 2, pieces, scale[0], (out_a, out_b), (half_a, half_b), whole, sems)


def backward_kernel(where, own, recv_a, recv_b, tbt, dsl, xs, terms_b, back, ga, keep, send, gs, gpool, acc, term, terms):
    del own
    cube_count = recv_a.shape[0]
    even = where[0] % 2 == 0
    shifter = row_picker(3, 1, 16)

    for b in range(cube_count):
        for z in range(2):
            from_a, from_b = recv_a[b, z].astype(F32), recv_b[b, z].astype(F32)
            spread_grad(gs, b, z, jnp.where(even, from_b, from_a).astype(BF), shifter)
            spread_grad(gs, b, 4 + z, jnp.where(even, from_a, from_b).astype(BF), shifter)

    low = jnp.where(where[0] == 0, 0.0, 0.125)
    high = jnp.where(where[0] == where[1] - 1, 0.0, 0.125)
    parts = [
        dot(windows_b(gs, spans), tbt[2304 * dz : 2304 * dz + 2304]).reshape(4, cube_count, 2, 16, 256)
        for dz, spans in enumerate((((0, 2),), ((1, 1), (4, 1)), ((4, 2),)))
    ]
    extra = (
        parts[0][:, :, 0] + parts[1][:, :, 0],
        parts[0][:, :, 1],
        parts[2][:, :, 0],
        parts[1][:, :, 1] + parts[2][:, :, 1],
    )
    for z in range(4):
        scale = low if z == 0 else high if z == 3 else 0.125
        total = (back[:, :, z] + extra[z]) * scale
        for q in range(4):
            gpool[:, z, :, 256 * q : 256 * q + 256] = total[q]

    ga[:, :, :, :, :128] = jnp.zeros((cube_count, 6, 4, 16, 128), BF)
    ga[:, :, :, :, 2176:] = jnp.zeros((cube_count, 6, 4, 16, 128), BF)
    rows_a = cube_count * 6 * 16
    own_rows = cube_count * 4 * 16
    place = lax.broadcasted_iota(jnp.int32, (rows_a, 128), 0) % 16

    def one_group(g):
        lanes = pl.ds(pl.multiple_of(128 * g, 128), 128)
        up = gpool[:, :, :, lanes]
        up = jnp.concatenate(
            [up[:, 0:1], up[:, 1:2], up[:, 1:2], up[:, 2:3], up[:, 2:3], up[:, 3:4]], axis=1
        ).reshape(rows_a, 128)
        sides = []
        for p in range(2):
            pair = []
            for px in range(2):
                at = pl.ds(pl.multiple_of(256 * g + 128 * px, 128), 128)
                grad = up * dsl[:, :, p, :, at].astype(F32).reshape(rows_a, 128)
                to = pl.ds(pl.multiple_of(256 * g + 128 * px + 128, 128), 128)
                kept = grad.astype(BF).reshape(cube_count, 6, 16, 128)
                ga[:, :, 1 + p, :, to] = kept
                pair.append(kept[:, 1:5].reshape(own_rows, 128))
                if p == 1:
                    moved = jnp.where(place == 0, 0.0, pltpu.roll(grad, 1, 0))
                else:
                    moved = jnp.where(place == 15, 0.0, pltpu.roll(grad, rows_a - 1, 0))
                ga[:, :, 0 if p else 3, :, to] = moved.astype(BF).reshape(cube_count, 6, 16, 128)
            sides.append(jnp.concatenate(pair, axis=1))
        return sides, [windows_a(xs, ((HALO - 1, ZD),), p, 128 * g) for p in range(2)]

    def groups(i, carry):
        first, second = one_group(2 * i), one_group(2 * i + 1)
        grads = jnp.concatenate(first[0] + second[0], axis=0)
        acc[...] += dot_t(jnp.concatenate(first[1] + second[1], axis=0), grads)
        return carry

    acc[...] = jnp.zeros_like(acc)
    lax.fori_loop(0, 4, groups, 0)

    terms[pl.ds(27, C1 // 2, stride=28), :] = jnp.zeros((C1 // 2, 128), F32)
    mask = lanes_below((32, 128), 64)
    for d in range(9):
        full = acc[256 * d : 256 * d + 256]
        for dx in range(3):
            left = full[32 * dx : 32 * dx + 32, :128] + full[32 * dx + 32 : 32 * dx + 64, 128:]
            right = full[32 * dx + 64 : 32 * dx + 96, :128] + full[32 * dx + 96 : 32 * dx + 128, 128:]
            merged = jnp.where(mask, left, right)
            slot = (3 * d + dx) % 4
            term[slot] = merged + pltpu.roll(merged, 64, 1)
            evens = term[slot, pl.ds(0, C1 // 2, stride=2), :]
            odds = term[slot, pl.ds(1, C1 // 2, stride=2), :]
            terms[pl.ds(3 * d + dx, C1 // 2, stride=28), :] = jnp.where(mask[:16], evens, odds)
    low = where[0] % 2 == 0
    count = keep.shape[0]
    for part in range(count):
        sides = []
        for core in range(2):
            at = core * count + part
            rows_b, rows_a = ROWS_B // (2 * count), ROWS_A // (2 * count)
            sides.append(
                jnp.concatenate(
                    [terms_b[rows_b * at : rows_b * at + rows_b], terms[rows_a * at : rows_a * at + rows_a]], axis=0
                )
            )
        keep[part] = jnp.where(low, sides[0], sides[1]).astype(BF)
        send[part] = jnp.where(low, sides[1], sides[0]).astype(BF)


def one_cube(b, ga, tat, out, landed):
    rows = ZD * 16
    sides = []
    for p in range(2):
        columns = []
        for dz in range(3):
            for dy in range(3):
                columns.append(
                    jnp.concatenate(
                        [ga[b, dz : dz + ZD, p + dy, :, 512 * q : 512 * q + 768].reshape(rows, 768) for q in range(4)],
                        axis=0,
                    )
                )
        sides.append(jnp.concatenate(columns, axis=1))
    both = dot(jnp.concatenate(sides, axis=0), tat[...]).astype(BF).reshape(2, 4, ZD, 16, 256)
    row = lax.broadcasted_iota(jnp.int32, (32, 32), 0)
    col = lax.broadcasted_iota(jnp.int32, (32, 32), 1)
    mixer = jnp.where(col == row // 2 + 16 * (row % 2), 1.0, 0.0).astype(BF)
    for z in range(ZD):
        for q in range(4):
            pair = jnp.concatenate([both[0, q, z], both[1, q, z]], axis=0)
            out[z, :, 256 * q : 256 * q + 256] = dot(mixer, pair).astype(BF)
        if landed is not None:
            landed(z)


def early_cube_kernel(b):
    def kernel(ga, tat, out):
        one_cube(b, ga, tat, out, None)

    return kernel


def last_cube_kernel(ga, tat, *rest):
    early, (out, token, block, sems) = rest[:-4], rest[-4:]
    last = len(early)
    copies = [pltpu.make_async_copy(cube, out.at[b], sems.at[b]) for b, cube in enumerate(early)]
    for copy in copies:
        copy.start()

    def landed(z):
        copy = pltpu.make_async_copy(block.at[z], out.at[last, z], sems.at[last + z])
        copy.start()
        copies.append(copy)

    one_cube(last, ga, tat, block, landed)
    token[...] = jnp.zeros_like(token)
    for copy in copies:
        copy.wait()


def call(kernel, args, outs, scratch, flops, smem=0, any_in=(), any_out=(), aliases=None):
    specs = [SMEM if i < smem else ANY if i in any_in else VMEM for i in range(len(args))]
    return pl.pallas_call(
        kernel,
        out_shape=[jax.ShapeDtypeStruct(shape, dtype) for shape, dtype in outs],
        in_specs=specs,
        out_specs=[ANY if i in any_out else VMEM for i in range(len(outs))],
        scratch_shapes=scratch,
        input_output_aliases=aliases or {},
        compiler_params=pltpu.CompilerParams(vmem_limit_bytes=28 * 1024 * 1024),
        cost_estimate=pl.CostEstimate(flops=flops, bytes_accessed=1_000_000, transcendentals=0),
    )(*args)


def swap(first, second, count):
    pairs_a = [(i, i ^ 1) for i in range(count)]
    pairs_b = [(i, ((i + 1) ^ 1) - 1) for i in range(1, count - 1)]
    return lax.ppermute(first, "gz", pairs_a), lax.ppermute(second, "gz", pairs_b)


def swap_along(parts, axis, step):
    count = lax.axis_size(axis)
    return [
        lax.ppermute(part, axis, [(i, i ^ (k * step)) for i in range(count)]) for k, part in enumerate(parts) if k
    ]


def shards(cubes, weight_a, weight_b, cotangent):
    cube_count = cubes.shape[0]
    ring = lax.axis_size("gz")
    samples = lax.axis_size("sample")
    where = jnp.stack([lax.axis_index("gz"), jnp.int32(ring), lax.axis_index("sample")]).astype(jnp.int32)
    outer = lax.dynamic_slice_in_dim(cubes, lax.axis_index("gz") % 2, HALO, axis=1)
    recv_a, recv_b = swap(cubes, outer, ring)

    own_xs, ta, own_slope, inner, edge_low, edge_high, wa = call(
        prepare_kernel,
        [cubes, weight_a],
        [
            ((cube_count, ZD + 2 * HALO, 4, 16, 1152), BF),
            ((2304, 256), BF),
            ((cube_count, 6, 2, 16, 2048), BF),
            ((cube_count, 2, 16, 1024), F32),
            ((cube_count * 256, 256), F32),
            ((cube_count * 256, 256), F32),
            ((27 * C1, 128), F32),
        ],
        [],
        1_000_000_000,
    )
    tb, wb = call(
        prepare_b_kernel, [weight_b], [((2304, 256), BF), ((27 * C2, 128), F32)], [], 500_000_000
    )
    xs, dsl, pools, grad_b = call(
        forward_kernel,
        [where, own_xs, own_slope, inner, edge_low, edge_high, recv_a, recv_b, ta, tb, cotangent],
        [
            ((cube_count, ZD + 2 * HALO, 4, 16, 1152), BF),
            ((cube_count, 6, 2, 16, 2048), BF),
            ((cube_count, 4, 3, 16, 1152), BF),
            ((cube_count, 2, 16, 2048), BF),
        ],
        [pltpu.VMEM((cube_count, 4, 16, 1024), BF)],
        8_000_000_000,
        smem=1,
        aliases={1: 0, 2: 1},
    )
    back_a, back_b = swap(grad_b, grad_b, ring)
    spread = ((cube_count, 6, 3, 16, 2304), BF)
    wide = ((6912, 256), BF)
    terms_b, own_gs, tat, tbt, back = call(
        terms_b_kernel,
        [pools, grad_b, wa, wb],
        [((ROWS_B, 128), F32), spread, wide, wide, ((4, cube_count, 4, 16, 256), F32)],
        [],
        1_000_000_000,
    )
    piece = (ROWS_A + ROWS_B) // (2 * samples)
    pieces = ((samples, piece, 128), BF)
    ga, keep, send, _ = call(
        backward_kernel,
        [where, own_gs, back_a, back_b, tbt, dsl, xs, terms_b, back],
        [((cube_count, 6, 4, 16, 2304), BF), pieces, pieces, spread],
        [
            pltpu.VMEM((cube_count, 4, 16, 1024), F32),
            pltpu.VMEM((2304, 256), F32),
            pltpu.VMEM((4, C1, 128), F32),
            pltpu.VMEM((ROWS_A, 128), F32),
        ],
        6_000_000_000,
        smem=1,
        aliases={1: 3},
    )
    small = [((piece, 128), BF)]
    (recv,) = swap_along([send] * 2, "gz", 1)
    parts = call(scatter_kernel, [where, keep, recv], small * samples, [], 1_000_000, smem=1)
    others = swap_along(parts, "sample", 1)
    cube = (ZD, SIDE, SIDE * C1)
    early = [
        call(early_cube_kernel(b), [ga, tat], [(cube, BF)], [], 2_000_000_000)[0] for b in range(cube_count - 1)
    ]
    (mine,) = call(add_kernel, [early[0], parts[0], *others], small, [], 1_000_000)
    others = swap_along([mine] * (ring // 2), "gz", 2)
    input_grad, done = call(
        last_cube_kernel,
        [ga, tat, *early],
        [((cube_count, *cube), BF), ((8, 128), F32)],
        [pltpu.VMEM(cube, BF), pltpu.SemaphoreType.DMA((cube_count - 1 + ZD,))],
        2_000_000_000,
        any_out=(0,),
    )
    (mine,) = call(add_kernel, [done, mine, *others], small, [], 1_000_000)
    (own,) = call(
        stack_kernel, [where, mine, *swap_along([mine] * samples, "sample", 1)], [pieces], [], 1_000_000, smem=1
    )
    (other,) = swap_along([own] * 2, "gz", 1)
    scale = jnp.full((1,), 1.0 / (cube_count * samples), F32)
    shapes = [((27, C1 * C2), F32), ((27, C2 * C3), F32)]
    scratch = [
        pltpu.VMEM((samples, piece, 128), F32),
        pltpu.VMEM((27, C1 * C2 // 2), F32),
        pltpu.VMEM((27, C2 * C3 // 2), F32),
        pltpu.SemaphoreType.DMA((2,)),
    ]
    totals = call(first_half_kernel, [where, scale, own], shapes, scratch, 1_000_000, smem=2, any_out=(0, 1))
    total_a, total_b = call(
        finish_kernel,
        [where, scale, other, *totals],
        shapes,
        scratch,
        1_000_000,
        smem=2,
        any_in=(3, 4),
        any_out=(0, 1),
        aliases={3: 0, 4: 1},
    )
    return input_grad, total_a, total_b


def solution(mesh):
    in_specs = (P("sample", "gz", None, None), P(), P(), P("sample", "gz", None, None))
    out_specs = (P("sample", "gz", None, None), P(), P())
    return jax.shard_map(shards, mesh=mesh, in_specs=in_specs, out_specs=out_specs, check_vma=False)
```

```python
import jax
import jax.numpy as jnp
from jax import lax
from jax.experimental import pallas as pl
from jax.experimental.pallas import tpu as pltpu
from jax.sharding import PartitionSpec as P

C1 = 32
C2 = 64
C3 = 128
SIDE = 32
ZD = 4
HALO = 3
ROWS_B = C1 * 2 * 28
ROWS_A = C1 // 2 * 28
BF = jnp.bfloat16
F32 = jnp.float32
VMEM = pl.BlockSpec(memory_space=pltpu.VMEM)
SMEM = pl.BlockSpec(memory_space=pltpu.SMEM)
ANY = pl.BlockSpec(memory_space=pl.ANY)


def dot(a, b):
    return jnp.dot(a, b, preferred_element_type=F32)


def dot_t(a, b):
    return lax.dot_general(a, b, (((0,), (0,)), ((), ())), preferred_element_type=F32)


def sigmoid(v):
    return pl.reciprocal(1.0 + jnp.exp(-v), approx=True)


def row_picker(variants, stride, planes):
    size = 16 * stride
    shape = (planes * variants * 16, planes * size)
    row = lax.broadcasted_iota(jnp.int32, shape, 0)
    col = lax.broadcasted_iota(jnp.int32, shape, 1)
    want = stride * (row % 16) + row // 16 % variants - 1
    hit = (col == row // (16 * variants) * size + want) & (want >= 0) & (want < size)
    return jnp.where(hit, 1.0, 0.0).astype(BF)


def rows_at(block, before, total):
    rows, lanes = block.shape
    parts = []
    if before:
        parts.append(jnp.zeros((before, lanes), block.dtype))
    parts.append(block)
    if total - before - rows:
        parts.append(jnp.zeros((total - before - rows, lanes), block.dtype))
    return jnp.concatenate(parts, axis=0) if len(parts) > 1 else block


def lanes_below(shape, bound):
    return lax.broadcasted_iota(jnp.int32, shape, 1) < bound


def halves(left, right):
    return jnp.where(lanes_below(left.shape, 64), left, right).astype(BF)


def silu(pre):
    squash = sigmoid(pre)
    act = pre * squash
    return act, (squash + act * (1.0 - squash)).astype(BF)


def windows_a(xs, spans, p, start, offsets=(0, 1, 2)):
    lanes = pl.ds(start if isinstance(start, int) else pl.multiple_of(start, 128), 256)
    columns = []
    for dz in offsets:
        for dy in range(3):
            parts = [xs[:, first + dz : first + dz + planes, p + dy, :, lanes] for first, planes in spans]
            whole = jnp.concatenate(parts, axis=1) if len(parts) > 1 else parts[0]
            columns.append(whole.reshape(whole.shape[0] * whole.shape[1] * 16, 256))
    return jnp.concatenate(columns, axis=1)


def spread_input(target, b, zz, planes, picker):
    rows = 32 * len(planes)
    block = jnp.concatenate(planes, axis=0)
    block = jnp.concatenate([jnp.zeros((rows, 32), BF), block, jnp.zeros((rows, 96), BF)], axis=1)
    moved = dot(picker, block).astype(BF)
    for i in range(len(planes)):
        for v in range(4):
            target[b, zz + i, v] = moved[64 * i + 16 * v : 64 * i + 16 * v + 16]


RANKS = (-3, -1, 0, 2, 1, 3, 4, 6, 5, 7, 8, 10)


def mirror(d, block, tat):
    lane = lax.broadcasted_iota(jnp.int32, (64, 128), 1)
    turned = [block if s == 0 else pltpu.roll(block, 32 * s, 1) for s in range(4)]
    for slot, rank in enumerate(RANKS):
        for half in range(2):
            start = 32 * (rank - 1 - 4 * half)
            keep = (lane >= start) & (lane < start + 96)
            value = jnp.where(keep, turned[(rank - 1) % 4], 0.0).astype(BF)
            tat[768 * d + 64 * slot : 768 * d + 64 * slot + 64, 128 * half : 128 * half + 128] = value


def prepare_kernel(cubes, weight_a, xs, ta, dsl, inner, edge_low, edge_high, wa):
    mask = lanes_below((27, 128), 64)
    for j in range(C1 // 2):
        both = weight_a[:, 128 * j : 128 * j + 128].astype(F32)
        other = pltpu.roll(both, 64, 1)
        wa[pl.ds(2 * j, 27, stride=C1), :] = jnp.where(mask, both, other)
        wa[pl.ds(2 * j + 1, 27, stride=C1), :] = jnp.where(mask, other, both)
    picker = row_picker(4, 2, ZD)
    for b in range(cubes.shape[0]):
        spread_input(xs, b, HALO, [cubes[b, z] for z in range(ZD)], picker)
    for d in range(9):
        block = wa[96 * d : 96 * d + 96]
        for px in range(2):
            ta[256 * d : 256 * d + 256, 128 * px : 128 * px + 128] = halves(
                rows_at(block, 32 * px, 256), rows_at(block, 64 + 32 * px, 256)
            )

    cube_count = cubes.shape[0]
    pre = dot(
        jnp.concatenate(
            [windows_a(xs, ((HALO, 2),), p, 128 * g) for g in range(8) for p in range(2)], axis=0
        ),
        ta[...],
    )
    act, slope = silu(pre)
    slope = slope.reshape(8, 2, cube_count, 2, 16, 256)
    act = act.reshape(8, 2, cube_count, 2, 16, 256)
    for g in range(8):
        for p in range(2):
            dsl[:, 2:4, p, :, 256 * g : 256 * g + 256] = slope[g, p]
        part = act[g, 0] + act[g, 1]
        inner[:, :, :, 128 * g : 128 * g + 128] = part[..., :128] + part[..., 128:]
    for edge, first, offsets in ((edge_low, HALO - 1, (1, 2)), (edge_high, HALO + 2, (0, 1))):
        rows = jnp.concatenate(
            [windows_a(xs, ((first, 1),), p, 128 * g, offsets) for g in range(8) for p in range(2)], axis=0
        )
        edge[...] = dot(rows, ta[768 * offsets[0] : 768 * offsets[0] + 1536])


def prepare_b_kernel(weight_b, tb, wb):
    for i in range(C2):
        wb[pl.ds(i, 27, stride=C2), :] = weight_b[:, 128 * i : 128 * i + 128].astype(F32)
    for d in range(9):
        block = wb[192 * d : 192 * d + 192].astype(BF)
        for e in range(2):
            tb[256 * d : 256 * d + 256, 128 * e : 128 * e + 128] = rows_at(block, 64 * e, 256)


def forward_kernel(where, own, own_slope, inner, edge_low, edge_high, recv_a, recv_b, ta, tb, cot, xs, dsl, pools, grad_b, pooled):
    del own, own_slope
    cube_count = xs.shape[0]
    even = where[0] % 2 == 0
    picker = row_picker(4, 2, HALO)
    for b in range(cube_count):
        below, above = [], []
        for z in range(HALO):
            far = ZD - HALO + z
            below.append(jnp.where(even, recv_b[b, z].astype(F32), recv_a[b, far].astype(F32)).astype(BF))
            above.append(jnp.where(even, recv_a[b, z].astype(F32), recv_b[b, z].astype(F32)).astype(BF))
        spread_input(xs, b, 0, below, picker)
        spread_input(xs, b, HALO + ZD, above, picker)

    low = jnp.where(where[0] == 0, 0.0, 0.125)
    high = jnp.where(where[0] == where[1] - 1, 0.0, 0.125)

    def groups(i, carry):
        def stack(spans, offsets=(0, 1, 2)):
            return jnp.concatenate(
                [windows_a(xs, spans, p, 512 * i + 128 * j, offsets) for j in range(4) for p in range(2)], axis=0
            )

        act, slope = silu(dot(stack(((0, 2), (HALO + ZD - 1, 2))), ta[...]))
        slope = slope.reshape(4, 2, cube_count, 4, 16, 256)
        act = act.reshape(4, 2, cube_count, 4, 16, 256)
        rows = cube_count * 128
        here = pl.ds(pl.multiple_of(rows * i, rows), rows)
        sides = []
        for edge, first, dz in ((edge_low, HALO - 1, 0), (edge_high, HALO + 2, 2)):
            pre = edge[here] + dot(stack(((first, 1),), (dz,)), ta[768 * dz : 768 * dz + 768])
            edge_act, edge_slope = silu(pre)
            edge_act = edge_act.reshape(4, 2, cube_count, 16, 256)
            sides.append((edge_act, edge_slope.reshape(4, 2, cube_count, 16, 256)))
        for j in range(4):
            for p in range(2):
                to = pl.ds(pl.multiple_of(1024 * i + 256 * j, 256), 256)
                dsl[:, 0, p, :, to] = slope[j, p][:, 1]
                dsl[:, 1, p, :, to] = sides[0][1][j, p]
                dsl[:, 4, p, :, to] = sides[1][1][j, p]
                dsl[:, 5, p, :, to] = slope[j, p][:, 2]
            part = act[j, 0] + act[j, 1]
            part = part[..., :128] + part[..., 128:]
            ends = [side[0][j, 0] + side[0][j, 1] for side in sides]
            ends = [end[..., :128] + end[..., 128:] for end in ends]
            out = pl.ds(pl.multiple_of(512 * i + 128 * j, 128), 128)
            pooled[:, 0, :, out] = ((part[:, 0] + part[:, 1]) * low).astype(BF)
            pooled[:, 1, :, out] = ((ends[0] + inner[:, 0, :, out]) * 0.125).astype(BF)
            pooled[:, 2, :, out] = ((ends[1] + inner[:, 1, :, out]) * 0.125).astype(BF)
            pooled[:, 3, :, out] = ((part[:, 2] + part[:, 3]) * high).astype(BF)
        return carry

    lax.fori_loop(0, 2, groups, 0)

    shifter = row_picker(3, 1, 4)
    for b in range(cube_count):
        block = pooled[b].reshape(64, 1024)
        block = jnp.concatenate([jnp.zeros((64, 64), BF), block, jnp.zeros((64, 64), BF)], axis=1)
        moved = dot(shifter, block).astype(BF)
        for z in range(4):
            for v in range(3):
                pools[b, z, v] = moved[48 * z + 16 * v : 48 * z + 16 * v + 16]

    rows_b = cube_count * 2 * 16
    columns = []
    for dz in range(3):
        for dy in range(3):
            columns.append(
                jnp.concatenate(
                    [
                        pools[:, dz : dz + 2, dy, :, 128 * g : 128 * g + 256].reshape(rows_b, 256)
                        for g in range(8)
                    ],
                    axis=0,
                )
            )
    pre_b = dot(jnp.concatenate(columns, axis=1), tb[...])
    squash = sigmoid(pre_b)
    slope_b = squash + pre_b * squash * (1.0 - squash)
    row = lax.broadcasted_iota(jnp.int32, (16, 8), 0)
    twice = jnp.where(row // 2 == lax.broadcasted_iota(jnp.int32, (16, 8), 1), 0.125, 0.0).astype(BF)
    ups = [dot(twice, cot[b, 0]) for b in range(cube_count)]
    for g in range(8):
        part = slope_b[rows_b * g : rows_b * g + rows_b].reshape(cube_count, 2, 16, 256)
        up = jnp.stack([ups[b][:, 128 * g : 128 * g + 128] for b in range(cube_count)])
        for z in range(2):
            for e in range(2):
                at = 256 * g + 128 * e
                grad_b[:, z, :, at : at + 128] = (up * part[:, z, :, 128 * e : 128 * e + 128]).astype(BF)


def spread_grad(target, b, zz, pair, shifter):
    moved = dot(shifter, pair.reshape(32, 2048)).astype(BF)
    for i in range(2):
        for v in range(3):
            target[b, zz + i, v, :, 128:2176] = moved[48 * i + 16 * v : 48 * i + 16 * v + 16]
            target[b, zz + i, v, :, :128] = jnp.zeros((16, 128), BF)
            target[b, zz + i, v, :, 2176:] = jnp.zeros((16, 128), BF)


def terms_b_kernel(pools, grad_b, wa, wb, terms, gs, tat, tbt, back):
    cube_count = grad_b.shape[0]
    shifter = row_picker(3, 1, 2)
    for b in range(cube_count):
        spread_grad(gs, b, 2, grad_b[b], shifter)
    for d in range(9):
        mirror(8 - d, rows_at(wa[96 * d : 96 * d + 96], 0, 128).T[:64], tat)
        block = wb[192 * d : 192 * d + 192]
        turned = []
        for dx in (2, 1, 0):
            part = block[64 * dx : 64 * dx + 64]
            turned.append(jnp.concatenate([part, part], axis=0).T)
        block = jnp.concatenate(turned, axis=0)
        to = 768 * (8 - d)
        for e in range(2):
            tbt[to : to + 768, 128 * e : 128 * e + 128] = halves(
                rows_at(block, 256 * e, 768), rows_at(block, 256 * e + 128, 768)
            )
    rows_b = cube_count * 2 * 16
    grads = jnp.concatenate(
        [grad_b[:, :, :, 256 * g : 256 * g + 256].reshape(rows_b, 256) for g in range(8)], axis=0
    )
    terms[pl.ds(27, C2, stride=28), :] = jnp.zeros((C2, 128), F32)
    for dz in range(3):
        for dy in range(3):
            windows = jnp.concatenate(
                [
                    pools[:, dz : dz + 2, dy, :, 128 * g : 128 * g + 256].reshape(rows_b, 256)
                    for g in range(8)
                ],
                axis=0,
            )
            full = dot_t(windows, grads)
            for dx in range(3):
                term = full[64 * dx : 64 * dx + 64, :128] + full[64 * dx + 64 : 64 * dx + 128, 128:]
                terms[pl.ds(9 * dz + 3 * dy + dx, C2, stride=28), :] = term

    sources = windows_b(gs, ((2, 2),))
    given = [
        dot(sources, tbt[2304 * dz : 2304 * dz + 2304]).reshape(4, cube_count, 2, 16, 256) for dz in range(3)
    ]
    back[:, :, 0] = given[2][:, :, 0]
    back[:, :, 1] = given[1][:, :, 0] + given[2][:, :, 1]
    back[:, :, 2] = given[0][:, :, 0] + given[1][:, :, 1]
    back[:, :, 3] = given[0][:, :, 1]


def windows_b(gs, spans):
    columns = []
    for dy in range(3):
        stacks = []
        for q in range(4):
            parts = [gs[:, first : first + planes, dy, :, 512 * q : 512 * q + 768] for first, planes in spans]
            whole = jnp.concatenate(parts, axis=1) if len(parts) > 1 else parts[0]
            stacks.append(whole.reshape(whole.shape[0] * whole.shape[1] * 16, 768))
        columns.append(jnp.concatenate(stacks, axis=0))
    return jnp.concatenate(columns, axis=1)


def tree(parts):
    while len(parts) > 1:
        parts = [left + right for left, right in zip(parts[::2], parts[1::2])]
    return parts[0]


def scatter_kernel(where, keep, recv, *outs):
    for k, out in enumerate(outs):
        part = where[2] ^ k
        out[...] = (keep[part].astype(F32) + recv[part].astype(F32)).astype(BF)


def add_kernel(after, *refs):
    del after
    parts, out = refs[:-1], refs[-1]
    out[...] = tree([part[...].astype(F32) for part in parts]).astype(BF)


def stack_kernel(where, *refs):
    parts, out = refs[:-1], refs[-1]
    for k, part in enumerate(parts):
        out[where[2] ^ k] = part[...]


def lay_out(pieces, scale, out_a, out_b, whole):
    whole[...] = pieces[...].astype(F32) * scale
    count = pieces.shape[0]
    for width, base, out in ((C2, 0, out_b), (C1 // 2, ROWS_B // (2 * count), out_a)):
        each = width // (2 * count)
        for i in range(width // 2):
            start = base + 28 * (i % each)
            out[:, 128 * i : 128 * i + 128] = whole[i // each, start : start + 27]


def send_half(core, pieces, scale, outs, halves_out, whole, sems):
    lay_out(pieces, scale, *halves_out, whole)
    copies = []
    for i, (out, half) in enumerate(zip(outs, halves_out)):
        width = half.shape[1]
        copies.append(
            pltpu.make_async_copy(half, out.at[:, pl.ds(pl.multiple_of(core * width, width), width)], sems.at[i])
        )
        copies[-1].start()
    for copy in copies:
        copy.wait()


def first_half_kernel(where, scale, pieces, out_a, out_b, whole, half_a, half_b, sems):
    send_half(where[0] % 2, pieces, scale[0], (out_a, out_b), (half_a, half_b), whole, sems)


def finish_kernel(where, scale, pieces, before_a, before_b, out_a, out_b, whole, half_a, half_b, sems):
    del before_a, before_b
    send_half(1 - where[0] % 2, pieces, scale[0], (out_a, out_b), (half_a, half_b), whole, sems)


def backward_kernel(where, own, recv_a, recv_b, tbt, dsl, xs, terms_b, back, ga, keep, send, gs, gpool, acc, term, terms):
    del own
    cube_count = recv_a.shape[0]
    even = where[0] % 2 == 0
    shifter = row_picker(3, 1, 2)
    for b in range(cube_count):
        from_a, from_b = recv_a[b].astype(F32), recv_b[b].astype(F32)
        spread_grad(gs, b, 0, jnp.where(even, from_b, from_a).astype(BF), shifter)
        spread_grad(gs, b, 4, jnp.where(even, from_a, from_b).astype(BF), shifter)

    low = jnp.where(where[0] == 0, 0.0, 0.125)
    high = jnp.where(where[0] == where[1] - 1, 0.0, 0.125)
    parts = [
        dot(windows_b(gs, spans), tbt[2304 * dz : 2304 * dz + 2304]).reshape(4, cube_count, 2, 16, 256)
        for dz, spans in enumerate((((0, 2),), ((1, 1), (4, 1)), ((4, 2),)))
    ]
    extra = (
        parts[0][:, :, 0] + parts[1][:, :, 0],
        parts[0][:, :, 1],
        parts[2][:, :, 0],
        parts[1][:, :, 1] + parts[2][:, :, 1],
    )
    for z in range(4):
        scale = low if z == 0 else high if z == 3 else 0.125
        total = (back[:, :, z] + extra[z]) * scale
        for q in range(4):
            gpool[:, z, :, 256 * q : 256 * q + 256] = total[q]

    ga[:, :, :, :, :128] = jnp.zeros((cube_count, 6, 4, 16, 128), BF)
    ga[:, :, :, :, 2176:] = jnp.zeros((cube_count, 6, 4, 16, 128), BF)
    rows_a = cube_count * 6 * 16
    own_rows = cube_count * 4 * 16
    place = lax.broadcasted_iota(jnp.int32, (rows_a, 128), 0) % 16

    def one_group(g):
        lanes = pl.ds(pl.multiple_of(128 * g, 128), 128)
        up = gpool[:, :, :, lanes]
        up = jnp.concatenate(
            [up[:, 0:1], up[:, 1:2], up[:, 1:2], up[:, 2:3], up[:, 2:3], up[:, 3:4]], axis=1
        ).reshape(rows_a, 128)
        sides = []
        for p in range(2):
            pair = []
            for px in range(2):
                at = pl.ds(pl.multiple_of(256 * g + 128 * px, 128), 128)
                grad = up * dsl[:, :, p, :, at].astype(F32).reshape(rows_a, 128)
                to = pl.ds(pl.multiple_of(256 * g + 128 * px + 128, 128), 128)
                kept = grad.astype(BF).reshape(cube_count, 6, 16, 128)
                ga[:, :, 1 + p, :, to] = kept
                pair.append(kept[:, 1:5].reshape(own_rows, 128))
                if p == 1:
                    moved = jnp.where(place == 0, 0.0, pltpu.roll(grad, 1, 0))
                else:
                    moved = jnp.where(place == 15, 0.0, pltpu.roll(grad, rows_a - 1, 0))
                ga[:, :, 0 if p else 3, :, to] = moved.astype(BF).reshape(cube_count, 6, 16, 128)
            sides.append(jnp.concatenate(pair, axis=1))
        return sides, [windows_a(xs, ((HALO - 1, ZD),), p, 128 * g) for p in range(2)]

    def groups(i, carry):
        first, second = one_group(2 * i), one_group(2 * i + 1)
        grads = jnp.concatenate(first[0] + second[0], axis=0)
        acc[...] += dot_t(jnp.concatenate(first[1] + second[1], axis=0), grads)
        return carry

    acc[...] = jnp.zeros_like(acc)
    lax.fori_loop(0, 4, groups, 0)

    terms[pl.ds(27, C1 // 2, stride=28), :] = jnp.zeros((C1 // 2, 128), F32)
    mask = lanes_below((32, 128), 64)
    for d in range(9):
        full = acc[256 * d : 256 * d + 256]
        for dx in range(3):
            left = full[32 * dx : 32 * dx + 32, :128] + full[32 * dx + 32 : 32 * dx + 64, 128:]
            right = full[32 * dx + 64 : 32 * dx + 96, :128] + full[32 * dx + 96 : 32 * dx + 128, 128:]
            merged = jnp.where(mask, left, right)
            slot = (3 * d + dx) % 4
            term[slot] = merged + pltpu.roll(merged, 64, 1)
            evens = term[slot, pl.ds(0, C1 // 2, stride=2), :]
            odds = term[slot, pl.ds(1, C1 // 2, stride=2), :]
            terms[pl.ds(3 * d + dx, C1 // 2, stride=28), :] = jnp.where(mask[:16], evens, odds)
    low = where[0] % 2 == 0
    count = keep.shape[0]
    for part in range(count):
        sides = []
        for core in range(2):
            at = core * count + part
            rows_b, rows_a = ROWS_B // (2 * count), ROWS_A // (2 * count)
            sides.append(
                jnp.concatenate(
                    [terms_b[rows_b * at : rows_b * at + rows_b], terms[rows_a * at : rows_a * at + rows_a]], axis=0
                )
            )
        keep[part] = jnp.where(low, sides[0], sides[1]).astype(BF)
        send[part] = jnp.where(low, sides[1], sides[0]).astype(BF)


def one_cube(b, ga, tat, out, landed):
    rows = ZD * 16
    sides = []
    for p in range(2):
        columns = []
        for dz in range(3):
            for dy in range(3):
                columns.append(
                    jnp.concatenate(
                        [ga[b, dz : dz + ZD, p + dy, :, 512 * q : 512 * q + 768].reshape(rows, 768) for q in range(4)],
                        axis=0,
                    )
                )
        sides.append(jnp.concatenate(columns, axis=1))
    both = dot(jnp.concatenate(sides, axis=0), tat[...]).astype(BF).reshape(2, 4, ZD, 16, 256)
    row = lax.broadcasted_iota(jnp.int32, (32, 32), 0)
    col = lax.broadcasted_iota(jnp.int32, (32, 32), 1)
    mixer = jnp.where(col == row // 2 + 16 * (row % 2), 1.0, 0.0).astype(BF)
    for z in range(ZD):
        for q in range(4):
            pair = jnp.concatenate([both[0, q, z], both[1, q, z]], axis=0)
            out[z, :, 256 * q : 256 * q + 256] = dot(mixer, pair).astype(BF)
        if landed is not None:
            landed(z)


def early_cube_kernel(b):
    def kernel(ga, tat, out):
        one_cube(b, ga, tat, out, None)

    return kernel


def last_cube_kernel(ga, tat, *rest):
    early, (out, token, block, sems) = rest[:-4], rest[-4:]
    last = len(early)
    copies = [pltpu.make_async_copy(cube, out.at[b], sems.at[b]) for b, cube in enumerate(early)]
    for copy in copies:
        copy.start()

    def landed(z):
        copy = pltpu.make_async_copy(block.at[z], out.at[last, z], sems.at[last + z])
        copy.start()
        copies.append(copy)

    one_cube(last, ga, tat, block, landed)
    token[...] = jnp.zeros_like(token)
    for copy in copies:
        copy.wait()


def call(kernel, args, outs, scratch, flops, smem=0, any_in=(), any_out=(), aliases=None):
    specs = [SMEM if i < smem else ANY if i in any_in else VMEM for i in range(len(args))]
    return pl.pallas_call(
        kernel,
        out_shape=[jax.ShapeDtypeStruct(shape, dtype) for shape, dtype in outs],
        in_specs=specs,
        out_specs=[ANY if i in any_out else VMEM for i in range(len(outs))],
        scratch_shapes=scratch,
        input_output_aliases=aliases or {},
        compiler_params=pltpu.CompilerParams(vmem_limit_bytes=28 * 1024 * 1024),
        cost_estimate=pl.CostEstimate(flops=flops, bytes_accessed=1_000_000, transcendentals=0),
    )(*args)


def swap(first, second, count):
    pairs_a = [(i, i ^ 1) for i in range(count)]
    pairs_b = [(i, ((i + 1) ^ 1) - 1) for i in range(1, count - 1)]
    return lax.ppermute(first, "gz", pairs_a), lax.ppermute(second, "gz", pairs_b)


def swap_along(parts, axis, step):
    count = lax.axis_size(axis)
    return [
        lax.ppermute(part, axis, [(i, i ^ (k * step)) for i in range(count)]) for k, part in enumerate(parts) if k
    ]


def shards(cubes, weight_a, weight_b, cotangent):
    cube_count = cubes.shape[0]
    ring = lax.axis_size("gz")
    samples = lax.axis_size("sample")
    where = jnp.stack([lax.axis_index("gz"), jnp.int32(ring), lax.axis_index("sample")]).astype(jnp.int32)
    outer = lax.dynamic_slice_in_dim(cubes, lax.axis_index("gz") % 2, HALO, axis=1)
    recv_a, recv_b = swap(cubes, outer, ring)

    own_xs, ta, own_slope, inner, edge_low, edge_high, wa = call(
        prepare_kernel,
        [cubes, weight_a],
        [
            ((cube_count, ZD + 2 * HALO, 4, 16, 1152), BF),
            ((2304, 256), BF),
            ((cube_count, 6, 2, 16, 2048), BF),
            ((cube_count, 2, 16, 1024), F32),
            ((cube_count * 256, 256), F32),
            ((cube_count * 256, 256), F32),
            ((27 * C1, 128), F32),
        ],
        [],
        1_000_000_000,
    )
    tb, wb = call(
        prepare_b_kernel, [weight_b], [((2304, 256), BF), ((27 * C2, 128), F32)], [], 500_000_000
    )
    xs, dsl, pools, grad_b = call(
        forward_kernel,
        [where, own_xs, own_slope, inner, edge_low, edge_high, recv_a, recv_b, ta, tb, cotangent],
        [
            ((cube_count, ZD + 2 * HALO, 4, 16, 1152), BF),
            ((cube_count, 6, 2, 16, 2048), BF),
            ((cube_count, 4, 3, 16, 1152), BF),
            ((cube_count, 2, 16, 2048), BF),
        ],
        [pltpu.VMEM((cube_count, 4, 16, 1024), BF)],
        8_000_000_000,
        smem=1,
        aliases={1: 0, 2: 1},
    )
    back_a, back_b = swap(grad_b, grad_b, ring)
    spread = ((cube_count, 6, 3, 16, 2304), BF)
    wide = ((6912, 256), BF)
    terms_b, own_gs, tat, tbt, back = call(
        terms_b_kernel,
        [pools, grad_b, wa, wb],
        [((ROWS_B, 128), F32), spread, wide, wide, ((4, cube_count, 4, 16, 256), F32)],
        [],
        1_000_000_000,
    )
    piece = (ROWS_A + ROWS_B) // (2 * samples)
    pieces = ((samples, piece, 128), BF)
    ga, keep, send, _ = call(
        backward_kernel,
        [where, own_gs, back_a, back_b, tbt, dsl, xs, terms_b, back],
        [((cube_count, 6, 4, 16, 2304), BF), pieces, pieces, spread],
        [
            pltpu.VMEM((cube_count, 4, 16, 1024), F32),
            pltpu.VMEM((2304, 256), F32),
            pltpu.VMEM((4, C1, 128), F32),
            pltpu.VMEM((ROWS_A, 128), F32),
        ],
        6_000_000_000,
        smem=1,
        aliases={1: 3},
    )
    small = [((piece, 128), BF)]
    (recv,) = swap_along([send] * 2, "gz", 1)
    parts = call(scatter_kernel, [where, keep, recv], small * samples, [], 1_000_000, smem=1)
    others = swap_along(parts, "sample", 1)
    cube = (ZD, SIDE, SIDE * C1)
    early = [
        call(early_cube_kernel(b), [ga, tat], [(cube, BF)], [], 2_000_000_000)[0] for b in range(cube_count - 1)
    ]
    (mine,) = call(add_kernel, [early[0], parts[0], *others], small, [], 1_000_000)
    others = swap_along([mine] * (ring // 2), "gz", 2)
    input_grad, done = call(
        last_cube_kernel,
        [ga, tat, *early],
        [((cube_count, *cube), BF), ((8, 128), F32)],
        [pltpu.VMEM(cube, BF), pltpu.SemaphoreType.DMA((cube_count - 1 + ZD,))],
        2_000_000_000,
        any_out=(0,),
    )
    (mine,) = call(add_kernel, [done, mine, *others], small, [], 1_000_000)
    (own,) = call(
        stack_kernel, [where, mine, *swap_along([mine] * samples, "sample", 1)], [pieces], [], 1_000_000, smem=1
    )
    (other,) = swap_along([own] * 2, "gz", 1)
    scale = jnp.full((1,), 1.0 / (cube_count * samples), F32)
    shapes = [((27, C1 * C2), F32), ((27, C2 * C3), F32)]
    scratch = [
        pltpu.VMEM((samples, piece, 128), F32),
        pltpu.VMEM((27, C1 * C2 // 2), F32),
        pltpu.VMEM((27, C2 * C3 // 2), F32),
        pltpu.SemaphoreType.DMA((2,)),
    ]
    totals = call(first_half_kernel, [where, scale, own], shapes, scratch, 1_000_000, smem=2, any_out=(0, 1))
    total_a, total_b = call(
        finish_kernel,
        [where, scale, other, *totals],
        shapes,
        scratch,
        1_000_000,
        smem=2,
        any_in=(3, 4),
        any_out=(0, 1),
        aliases={3: 0, 4: 1},
    )
    return input_grad, total_a, total_b


def solution(mesh):
    in_specs = (P("sample", "gz", None, None), P(), P(), P("sample", "gz", None, None))
    out_specs = (P("sample", "gz", None, None), P(), P())
    return jax.shard_map(shards, mesh=mesh, in_specs=in_specs, out_specs=out_specs, check_vma=False)
```

```python
import functools

import jax
import jax.numpy as jnp
from jax import lax
from jax.experimental import pallas as pl
from jax.experimental.pallas import tpu as pltpu
from jax.sharding import PartitionSpec as P

C1 = 32
C2 = 64
C3 = 128
SIDE = 32
ZD = 4
HALO = 3
ROWS_B = C1 * 2 * 28
ROWS_A = C1 // 2 * 28
BF = jnp.bfloat16
F32 = jnp.float32
VMEM = pl.BlockSpec(memory_space=pltpu.VMEM)
ANY = pl.BlockSpec(memory_space=pl.ANY)


def position():
    return lax.axis_index("gz"), lax.axis_size("gz"), lax.axis_index("sample")


def dot(a, b):
    return jnp.dot(a, b, preferred_element_type=F32)


def dot_t(a, b):
    return lax.dot_general(a, b, (((0,), (0,)), ((), ())), preferred_element_type=F32)


def sigmoid(v):
    return pl.reciprocal(1.0 + jnp.exp(-v), approx=True)


def row_picker(variants, stride, planes):
    size = 16 * stride
    shape = (planes * variants * 16, planes * size)
    row = lax.broadcasted_iota(jnp.int32, shape, 0)
    col = lax.broadcasted_iota(jnp.int32, shape, 1)
    want = stride * (row % 16) + row // 16 % variants - 1
    hit = (col == row // (16 * variants) * size + want) & (want >= 0) & (want < size)
    return jnp.where(hit, 1.0, 0.0).astype(BF)


def rows_at(block, before, total):
    rows, lanes = block.shape
    parts = []
    if before:
        parts.append(jnp.zeros((before, lanes), block.dtype))
    parts.append(block)
    if total - before - rows:
        parts.append(jnp.zeros((total - before - rows, lanes), block.dtype))
    return jnp.concatenate(parts, axis=0) if len(parts) > 1 else block


def lanes_below(shape, bound):
    return lax.broadcasted_iota(jnp.int32, shape, 1) < bound


def halves(left, right):
    return jnp.where(lanes_below(left.shape, 64), left, right).astype(BF)


def silu(pre):
    squash = sigmoid(pre)
    act = pre * squash
    return act, (squash + act * (1.0 - squash)).astype(BF)


def windows_a(xs, spans, p, start, offsets=(0, 1, 2)):
    lanes = pl.ds(start if isinstance(start, int) else pl.multiple_of(start, 128), 256)
    columns = []
    for dz in offsets:
        for dy in range(3):
            parts = [xs[:, first + dz : first + dz + planes, p + dy, :, lanes] for first, planes in spans]
            whole = jnp.concatenate(parts, axis=1) if len(parts) > 1 else parts[0]
            columns.append(whole.reshape(whole.shape[0] * whole.shape[1] * 16, 256))
    return jnp.concatenate(columns, axis=1)


def spread_input(target, b, zz, planes, picker):
    rows = 32 * len(planes)
    block = jnp.concatenate(planes, axis=0)
    block = jnp.concatenate([jnp.zeros((rows, 32), BF), block, jnp.zeros((rows, 96), BF)], axis=1)
    moved = dot(picker, block).astype(BF)
    for i in range(len(planes)):
        for v in range(4):
            target[b, zz + i, v] = moved[64 * i + 16 * v : 64 * i + 16 * v + 16]


RANKS = (-3, -1, 0, 2, 1, 3, 4, 6, 5, 7, 8, 10)


def mirror(d, block, tat):
    lane = lax.broadcasted_iota(jnp.int32, (64, 128), 1)
    turned = [block if s == 0 else pltpu.roll(block, 32 * s, 1) for s in range(4)]
    for slot, rank in enumerate(RANKS):
        for half in range(2):
            start = 32 * (rank - 1 - 4 * half)
            keep = (lane >= start) & (lane < start + 96)
            value = jnp.where(keep, turned[(rank - 1) % 4], 0.0).astype(BF)
            tat[768 * d + 64 * slot : 768 * d + 64 * slot + 64, 128 * half : 128 * half + 128] = value


def prepare_kernel(cubes, weight_a, xs, ta, dsl, inner, edge_low, edge_high, wa):
    mask = lanes_below((27, 128), 64)
    for j in range(C1 // 2):
        both = weight_a[:, 128 * j : 128 * j + 128].astype(F32)
        other = pltpu.roll(both, 64, 1)
        wa[pl.ds(2 * j, 27, stride=C1), :] = jnp.where(mask, both, other)
        wa[pl.ds(2 * j + 1, 27, stride=C1), :] = jnp.where(mask, other, both)
    picker = row_picker(4, 2, ZD)
    for b in range(cubes.shape[0]):
        spread_input(xs, b, HALO, [cubes[b, z] for z in range(ZD)], picker)
    for d in range(9):
        block = wa[96 * d : 96 * d + 96]
        for px in range(2):
            ta[256 * d : 256 * d + 256, 128 * px : 128 * px + 128] = halves(
                rows_at(block, 32 * px, 256), rows_at(block, 64 + 32 * px, 256)
            )

    cube_count = cubes.shape[0]
    pre = dot(
        jnp.concatenate(
            [windows_a(xs, ((HALO, 2),), p, 128 * g) for g in range(8) for p in range(2)], axis=0
        ),
        ta[...],
    )
    act, slope = silu(pre)
    slope = slope.reshape(8, 2, cube_count, 2, 16, 256)
    act = act.reshape(8, 2, cube_count, 2, 16, 256)
    for g in range(8):
        for p in range(2):
            dsl[:, 2:4, p, :, 256 * g : 256 * g + 256] = slope[g, p]
        part = act[g, 0] + act[g, 1]
        inner[:, :, :, 128 * g : 128 * g + 128] = part[..., :128] + part[..., 128:]
    for edge, first, offsets in ((edge_low, HALO - 1, (1, 2)), (edge_high, HALO + 2, (0, 1))):
        rows = jnp.concatenate(
            [windows_a(xs, ((first, 1),), p, 128 * g, offsets) for g in range(8) for p in range(2)], axis=0
        )
        edge[...] = dot(rows, ta[768 * offsets[0] : 768 * offsets[0] + 1536])


def prepare_b_kernel(weight_b, tb, wb):
    for i in range(C2):
        wb[pl.ds(i, 27, stride=C2), :] = weight_b[:, 128 * i : 128 * i + 128].astype(F32)
    for d in range(9):
        block = wb[192 * d : 192 * d + 192].astype(BF)
        for e in range(2):
            tb[256 * d : 256 * d + 256, 128 * e : 128 * e + 128] = rows_at(block, 64 * e, 256)


def forward_kernel(own, own_slope, inner, edge_low, edge_high, recv_a, recv_b, ta, tb, cot, xs, dsl, pools, grad_b, pooled):
    del own, own_slope
    where = position()
    cube_count = xs.shape[0]
    even = where[0] % 2 == 0
    picker = row_picker(4, 2, HALO)
    for b in range(cube_count):
        below, above = [], []
        for z in range(HALO):
            far = ZD - HALO + z
            below.append(jnp.where(even, recv_b[b, z].astype(F32), recv_a[b, far].astype(F32)).astype(BF))
            above.append(jnp.where(even, recv_a[b, z].astype(F32), recv_b[b, z].astype(F32)).astype(BF))
        spread_input(xs, b, 0, below, picker)
        spread_input(xs, b, HALO + ZD, above, picker)

    low = jnp.where(where[0] == 0, 0.0, 0.125)
    high = jnp.where(where[0] == where[1] - 1, 0.0, 0.125)

    def groups(i, carry):
        def stack(spans, offsets=(0, 1, 2)):
            return jnp.concatenate(
                [windows_a(xs, spans, p, 512 * i + 128 * j, offsets) for j in range(4) for p in range(2)], axis=0
            )

        act, slope = silu(dot(stack(((0, 2), (HALO + ZD - 1, 2))), ta[...]))
        slope = slope.reshape(4, 2, cube_count, 4, 16, 256)
        act = act.reshape(4, 2, cube_count, 4, 16, 256)
        rows = cube_count * 128
        here = pl.ds(pl.multiple_of(rows * i, rows), rows)
        sides = []
        for edge, first, dz in ((edge_low, HALO - 1, 0), (edge_high, HALO + 2, 2)):
            pre = edge[here] + dot(stack(((first, 1),), (dz,)), ta[768 * dz : 768 * dz + 768])
            edge_act, edge_slope = silu(pre)
            edge_act = edge_act.reshape(4, 2, cube_count, 16, 256)
            sides.append((edge_act, edge_slope.reshape(4, 2, cube_count, 16, 256)))
        for j in range(4):
            for p in range(2):
                to = pl.ds(pl.multiple_of(1024 * i + 256 * j, 256), 256)
                dsl[:, 0, p, :, to] = slope[j, p][:, 1]
                dsl[:, 1, p, :, to] = sides[0][1][j, p]
                dsl[:, 4, p, :, to] = sides[1][1][j, p]
                dsl[:, 5, p, :, to] = slope[j, p][:, 2]
            part = act[j, 0] + act[j, 1]
            part = part[..., :128] + part[..., 128:]
            ends = [side[0][j, 0] + side[0][j, 1] for side in sides]
            ends = [end[..., :128] + end[..., 128:] for end in ends]
            out = pl.ds(pl.multiple_of(512 * i + 128 * j, 128), 128)
            pooled[:, 0, :, out] = ((part[:, 0] + part[:, 1]) * low).astype(BF)
            pooled[:, 1, :, out] = ((ends[0] + inner[:, 0, :, out]) * 0.125).astype(BF)
            pooled[:, 2, :, out] = ((ends[1] + inner[:, 1, :, out]) * 0.125).astype(BF)
            pooled[:, 3, :, out] = ((part[:, 2] + part[:, 3]) * high).astype(BF)
        return carry

    lax.fori_loop(0, 2, groups, 0)

    shifter = row_picker(3, 1, 4)
    for b in range(cube_count):
        block = pooled[b].reshape(64, 1024)
        block = jnp.concatenate([jnp.zeros((64, 64), BF), block, jnp.zeros((64, 64), BF)], axis=1)
        moved = dot(shifter, block).astype(BF)
        for z in range(4):
            for v in range(3):
                pools[b, z, v] = moved[48 * z + 16 * v : 48 * z + 16 * v + 16]

    rows_b = cube_count * 2 * 16
    columns = []
    for dz in range(3):
        for dy in range(3):
            columns.append(
                jnp.concatenate(
                    [
                        pools[:, dz : dz + 2, dy, :, 128 * g : 128 * g + 256].reshape(rows_b, 256)
                        for g in range(8)
                    ],
                    axis=0,
                )
            )
    pre_b = dot(jnp.concatenate(columns, axis=1), tb[...])
    squash = sigmoid(pre_b)
    slope_b = squash + pre_b * squash * (1.0 - squash)
    row = lax.broadcasted_iota(jnp.int32, (16, 8), 0)
    twice = jnp.where(row // 2 == lax.broadcasted_iota(jnp.int32, (16, 8), 1), 0.125, 0.0).astype(BF)
    ups = [dot(twice, cot[b, 0]) for b in range(cube_count)]
    for g in range(8):
        part = slope_b[rows_b * g : rows_b * g + rows_b].reshape(cube_count, 2, 16, 256)
        up = jnp.stack([ups[b][:, 128 * g : 128 * g + 128] for b in range(cube_count)])
        for z in range(2):
            for e in range(2):
                at = 256 * g + 128 * e
                grad_b[:, z, :, at : at + 128] = (up * part[:, z, :, 128 * e : 128 * e + 128]).astype(BF)


def spread_grad(target, b, zz, pair, shifter):
    moved = dot(shifter, pair.reshape(32, 2048)).astype(BF)
    for i in range(2):
        for v in range(3):
            target[b, zz + i, v, :, 128:2176] = moved[48 * i + 16 * v : 48 * i + 16 * v + 16]
            target[b, zz + i, v, :, :128] = jnp.zeros((16, 128), BF)
            target[b, zz + i, v, :, 2176:] = jnp.zeros((16, 128), BF)


def terms_b_kernel(pools, grad_b, wa, wb, terms, gs, tat, tbt, back):
    cube_count = grad_b.shape[0]
    shifter = row_picker(3, 1, 2)
    for b in range(cube_count):
        spread_grad(gs, b, 2, grad_b[b], shifter)
    for d in range(9):
        mirror(8 - d, rows_at(wa[96 * d : 96 * d + 96], 0, 128).T[:64], tat)
        block = wb[192 * d : 192 * d + 192]
        turned = []
        for dx in (2, 1, 0):
            part = block[64 * dx : 64 * dx + 64]
            turned.append(jnp.concatenate([part, part], axis=0).T)
        block = jnp.concatenate(turned, axis=0)
        to = 768 * (8 - d)
        for e in range(2):
            tbt[to : to + 768, 128 * e : 128 * e + 128] = halves(
                rows_at(block, 256 * e, 768), rows_at(block, 256 * e + 128, 768)
            )
    rows_b = cube_count * 2 * 16
    grads = jnp.concatenate(
        [grad_b[:, :, :, 256 * g : 256 * g + 256].reshape(rows_b, 256) for g in range(8)], axis=0
    )
    terms[pl.ds(27, C2, stride=28), :] = jnp.zeros((C2, 128), F32)
    for dz in range(3):
        for dy in range(3):
            windows = jnp.concatenate(
                [
                    pools[:, dz : dz + 2, dy, :, 128 * g : 128 * g + 256].reshape(rows_b, 256)
                    for g in range(8)
                ],
                axis=0,
            )
            full = dot_t(windows, grads)
            for dx in range(3):
                term = full[64 * dx : 64 * dx + 64, :128] + full[64 * dx + 64 : 64 * dx + 128, 128:]
                terms[pl.ds(9 * dz + 3 * dy + dx, C2, stride=28), :] = term

    sources = windows_b(gs, ((2, 2),))
    given = [
        dot(sources, tbt[2304 * dz : 2304 * dz + 2304]).reshape(4, cube_count, 2, 16, 256) for dz in range(3)
    ]
    back[:, :, 0] = given[2][:, :, 0]
    back[:, :, 1] = given[1][:, :, 0] + given[2][:, :, 1]
    back[:, :, 2] = given[0][:, :, 0] + given[1][:, :, 1]
    back[:, :, 3] = given[0][:, :, 1]


def windows_b(gs, spans):
    columns = []
    for dy in range(3):
        stacks = []
        for q in range(4):
            parts = [gs[:, first : first + planes, dy, :, 512 * q : 512 * q + 768] for first, planes in spans]
            whole = jnp.concatenate(parts, axis=1) if len(parts) > 1 else parts[0]
            stacks.append(whole.reshape(whole.shape[0] * whole.shape[1] * 16, 768))
        columns.append(jnp.concatenate(stacks, axis=0))
    return jnp.concatenate(columns, axis=1)


def tree(parts):
    while len(parts) > 1:
        parts = [left + right for left, right in zip(parts[::2], parts[1::2])]
    return parts[0]


def scatter_kernel(keep, recv, *outs):
    where = position()
    for k, out in enumerate(outs):
        part = where[2] ^ k
        out[...] = (keep[part].astype(F32) + recv[part].astype(F32)).astype(BF)


def add_kernel(after, *refs):
    del after
    parts, out = refs[:-1], refs[-1]
    out[...] = tree([part[...].astype(F32) for part in parts]).astype(BF)


def stack_kernel(*refs):
    where = position()
    parts, out = refs[:-1], refs[-1]
    for k, part in enumerate(parts):
        out[where[2] ^ k] = part[...]


def lay_out(pieces, scale, out_a, out_b, whole):
    whole[...] = pieces[...].astype(F32) * scale
    count = pieces.shape[0]
    for width, base, out in ((C2, 0, out_b), (C1 // 2, ROWS_B // (2 * count), out_a)):
        each = width // (2 * count)
        for i in range(width // 2):
            start = base + 28 * (i % each)
            out[:, 128 * i : 128 * i + 128] = whole[i // each, start : start + 27]


def send_half(core, pieces, scale, outs, halves_out, whole, sems):
    lay_out(pieces, scale, *halves_out, whole)
    copies = []
    for i, (out, half) in enumerate(zip(outs, halves_out)):
        width = half.shape[1]
        copies.append(
            pltpu.make_async_copy(half, out.at[:, pl.ds(pl.multiple_of(core * width, width), width)], sems.at[i])
        )
        copies[-1].start()
    for copy in copies:
        copy.wait()


def first_half_kernel(scale, pieces, out_a, out_b, whole, half_a, half_b, sems):
    send_half(position()[0] % 2, pieces, scale, (out_a, out_b), (half_a, half_b), whole, sems)


def finish_kernel(scale, pieces, before_a, before_b, out_a, out_b, whole, half_a, half_b, sems):
    del before_a, before_b
    send_half(1 - position()[0] % 2, pieces, scale, (out_a, out_b), (half_a, half_b), whole, sems)


def backward_kernel(own, recv_a, recv_b, tbt, dsl, xs, terms_b, back, ga, keep, send, gs, gpool, acc, term, terms):
    del own
    where = position()
    cube_count = recv_a.shape[0]
    even = where[0] % 2 == 0
    shifter = row_picker(3, 1, 2)
    for b in range(cube_count):
        from_a, from_b = recv_a[b].astype(F32), recv_b[b].astype(F32)
        spread_grad(gs, b, 0, jnp.where(even, from_b, from_a).astype(BF), shifter)
        spread_grad(gs, b, 4, jnp.where(even, from_a, from_b).astype(BF), shifter)

    low = jnp.where(where[0] == 0, 0.0, 0.125)
    high = jnp.where(where[0] == where[1] - 1, 0.0, 0.125)
    parts = [
        dot(windows_b(gs, spans), tbt[2304 * dz : 2304 * dz + 2304]).reshape(4, cube_count, 2, 16, 256)
        for dz, spans in enumerate((((0, 2),), ((1, 1), (4, 1)), ((4, 2),)))
    ]
    extra = (
        parts[0][:, :, 0] + parts[1][:, :, 0],
        parts[0][:, :, 1],
        parts[2][:, :, 0],
        parts[1][:, :, 1] + parts[2][:, :, 1],
    )
    for z in range(4):
        scale = low if z == 0 else high if z == 3 else 0.125
        total = (back[:, :, z] + extra[z]) * scale
        for q in range(4):
            gpool[:, z, :, 256 * q : 256 * q + 256] = total[q]

    ga[:, :, :, :, :128] = jnp.zeros((cube_count, 6, 4, 16, 128), BF)
    ga[:, :, :, :, 2176:] = jnp.zeros((cube_count, 6, 4, 16, 128), BF)
    rows_a = cube_count * 6 * 16
    own_rows = cube_count * 4 * 16
    place = lax.broadcasted_iota(jnp.int32, (rows_a, 128), 0) % 16

    def one_group(g):
        lanes = pl.ds(pl.multiple_of(128 * g, 128), 128)
        up = gpool[:, :, :, lanes]
        up = jnp.concatenate(
            [up[:, 0:1], up[:, 1:2], up[:, 1:2], up[:, 2:3], up[:, 2:3], up[:, 3:4]], axis=1
        ).reshape(rows_a, 128)
        sides = []
        for p in range(2):
            pair = []
            for px in range(2):
                at = pl.ds(pl.multiple_of(256 * g + 128 * px, 128), 128)
                grad = up * dsl[:, :, p, :, at].astype(F32).reshape(rows_a, 128)
                to = pl.ds(pl.multiple_of(256 * g + 128 * px + 128, 128), 128)
                kept = grad.astype(BF).reshape(cube_count, 6, 16, 128)
                ga[:, :, 1 + p, :, to] = kept
                pair.append(kept[:, 1:5].reshape(own_rows, 128))
                if p == 1:
                    moved = jnp.where(place == 0, 0.0, pltpu.roll(grad, 1, 0))
                else:
                    moved = jnp.where(place == 15, 0.0, pltpu.roll(grad, rows_a - 1, 0))
                ga[:, :, 0 if p else 3, :, to] = moved.astype(BF).reshape(cube_count, 6, 16, 128)
            sides.append(jnp.concatenate(pair, axis=1))
        return sides, [windows_a(xs, ((HALO - 1, ZD),), p, 128 * g) for p in range(2)]

    def groups(i, carry):
        first, second = one_group(2 * i), one_group(2 * i + 1)
        grads = jnp.concatenate(first[0] + second[0], axis=0)
        acc[...] += dot_t(jnp.concatenate(first[1] + second[1], axis=0), grads)
        return carry

    acc[...] = jnp.zeros_like(acc)
    lax.fori_loop(0, 4, groups, 0)

    terms[pl.ds(27, C1 // 2, stride=28), :] = jnp.zeros((C1 // 2, 128), F32)
    mask = lanes_below((32, 128), 64)
    for d in range(9):
        full = acc[256 * d : 256 * d + 256]
        for dx in range(3):
            left = full[32 * dx : 32 * dx + 32, :128] + full[32 * dx + 32 : 32 * dx + 64, 128:]
            right = full[32 * dx + 64 : 32 * dx + 96, :128] + full[32 * dx + 96 : 32 * dx + 128, 128:]
            merged = jnp.where(mask, left, right)
            slot = (3 * d + dx) % 4
            term[slot] = merged + pltpu.roll(merged, 64, 1)
            evens = term[slot, pl.ds(0, C1 // 2, stride=2), :]
            odds = term[slot, pl.ds(1, C1 // 2, stride=2), :]
            terms[pl.ds(3 * d + dx, C1 // 2, stride=28), :] = jnp.where(mask[:16], evens, odds)
    low = where[0] % 2 == 0
    count = keep.shape[0]
    for part in range(count):
        sides = []
        for core in range(2):
            at = core * count + part
            rows_b, rows_a = ROWS_B // (2 * count), ROWS_A // (2 * count)
            sides.append(
                jnp.concatenate(
                    [terms_b[rows_b * at : rows_b * at + rows_b], terms[rows_a * at : rows_a * at + rows_a]], axis=0
                )
            )
        keep[part] = jnp.where(low, sides[0], sides[1]).astype(BF)
        send[part] = jnp.where(low, sides[1], sides[0]).astype(BF)


def one_cube(b, ga, tat, out, landed):
    rows = ZD * 16
    sides = []
    for p in range(2):
        columns = []
        for dz in range(3):
            for dy in range(3):
                columns.append(
                    jnp.concatenate(
                        [ga[b, dz : dz + ZD, p + dy, :, 512 * q : 512 * q + 768].reshape(rows, 768) for q in range(4)],
                        axis=0,
                    )
                )
        sides.append(jnp.concatenate(columns, axis=1))
    both = dot(jnp.concatenate(sides, axis=0), tat[...]).astype(BF).reshape(2, 4, ZD, 16, 256)
    row = lax.broadcasted_iota(jnp.int32, (32, 32), 0)
    col = lax.broadcasted_iota(jnp.int32, (32, 32), 1)
    mixer = jnp.where(col == row // 2 + 16 * (row % 2), 1.0, 0.0).astype(BF)
    for z in range(ZD):
        for q in range(4):
            pair = jnp.concatenate([both[0, q, z], both[1, q, z]], axis=0)
            out[z, :, 256 * q : 256 * q + 256] = dot(mixer, pair).astype(BF)
        if landed is not None:
            landed(z)


def early_cube_kernel(b):
    def kernel(ga, tat, out):
        one_cube(b, ga, tat, out, None)

    return kernel


def last_cube_kernel(ga, tat, *rest):
    early, (out, token, block, sems) = rest[:-4], rest[-4:]
    last = len(early)
    copies = [pltpu.make_async_copy(cube, out.at[b], sems.at[b]) for b, cube in enumerate(early)]
    for copy in copies:
        copy.start()

    def landed(z):
        copy = pltpu.make_async_copy(block.at[z], out.at[last, z], sems.at[last + z])
        copy.start()
        copies.append(copy)

    one_cube(last, ga, tat, block, landed)
    token[...] = jnp.zeros_like(token)
    for copy in copies:
        copy.wait()


def call(kernel, args, outs, scratch, flops, any_in=(), any_out=(), aliases=None):
    specs = [ANY if i in any_in else VMEM for i in range(len(args))]
    return pl.pallas_call(
        kernel,
        out_shape=[jax.ShapeDtypeStruct(shape, dtype) for shape, dtype in outs],
        in_specs=specs,
        out_specs=[ANY if i in any_out else VMEM for i in range(len(outs))],
        scratch_shapes=scratch,
        input_output_aliases=aliases or {},
        compiler_params=pltpu.CompilerParams(vmem_limit_bytes=28 * 1024 * 1024),
        cost_estimate=pl.CostEstimate(flops=flops, bytes_accessed=1_000_000, transcendentals=0),
    )(*args)


def swap(first, second, count):
    pairs_a = [(i, i ^ 1) for i in range(count)]
    pairs_b = [(i, ((i + 1) ^ 1) - 1) for i in range(1, count - 1)]
    return lax.ppermute(first, "gz", pairs_a), lax.ppermute(second, "gz", pairs_b)


def swap_along(parts, axis, step):
    count = lax.axis_size(axis)
    return [
        lax.ppermute(part, axis, [(i, i ^ (k * step)) for i in range(count)]) for k, part in enumerate(parts) if k
    ]


def shards(cubes, weight_a, weight_b, cotangent):
    cube_count = cubes.shape[0]
    ring = lax.axis_size("gz")
    samples = lax.axis_size("sample")
    outer = lax.dynamic_slice_in_dim(cubes, lax.axis_index("gz") % 2, HALO, axis=1)
    recv_a, recv_b = swap(cubes, outer, ring)

    own_xs, ta, own_slope, inner, edge_low, edge_high, wa = call(
        prepare_kernel,
        [cubes, weight_a],
        [
            ((cube_count, ZD + 2 * HALO, 4, 16, 1152), BF),
            ((2304, 256), BF),
            ((cube_count, 6, 2, 16, 2048), BF),
            ((cube_count, 2, 16, 1024), F32),
            ((cube_count * 256, 256), F32),
            ((cube_count * 256, 256), F32),
            ((27 * C1, 128), F32),
        ],
        [],
        1_000_000_000,
    )
    tb, wb = call(
        prepare_b_kernel, [weight_b], [((2304, 256), BF), ((27 * C2, 128), F32)], [], 500_000_000
    )
    xs, dsl, pools, grad_b = call(
        forward_kernel,
        [own_xs, own_slope, inner, edge_low, edge_high, recv_a, recv_b, ta, tb, cotangent],
        [
            ((cube_count, ZD + 2 * HALO, 4, 16, 1152), BF),
            ((cube_count, 6, 2, 16, 2048), BF),
            ((cube_count, 4, 3, 16, 1152), BF),
            ((cube_count, 2, 16, 2048), BF),
        ],
        [pltpu.VMEM((cube_count, 4, 16, 1024), BF)],
        8_000_000_000,
        aliases={0: 0, 1: 1},
    )
    back_a, back_b = swap(grad_b, grad_b, ring)
    spread = ((cube_count, 6, 3, 16, 2304), BF)
    wide = ((6912, 256), BF)
    terms_b, own_gs, tat, tbt, back = call(
        terms_b_kernel,
        [pools, grad_b, wa, wb],
        [((ROWS_B, 128), F32), spread, wide, wide, ((4, cube_count, 4, 16, 256), F32)],
        [],
        1_000_000_000,
    )
    piece = (ROWS_A + ROWS_B) // (2 * samples)
    pieces = ((samples, piece, 128), BF)
    ga, keep, send, _ = call(
        backward_kernel,
        [own_gs, back_a, back_b, tbt, dsl, xs, terms_b, back],
        [((cube_count, 6, 4, 16, 2304), BF), pieces, pieces, spread],
        [
            pltpu.VMEM((cube_count, 4, 16, 1024), F32),
            pltpu.VMEM((2304, 256), F32),
            pltpu.VMEM((4, C1, 128), F32),
            pltpu.VMEM((ROWS_A, 128), F32),
        ],
        6_000_000_000,
        aliases={0: 3},
    )
    small = [((piece, 128), BF)]
    (recv,) = swap_along([send] * 2, "gz", 1)
    parts = call(scatter_kernel, [keep, recv], small * samples, [], 1_000_000)
    others = swap_along(parts, "sample", 1)
    cube = (ZD, SIDE, SIDE * C1)
    early = [
        call(early_cube_kernel(b), [ga, tat], [(cube, BF)], [], 2_000_000_000)[0] for b in range(cube_count - 1)
    ]
    (mine,) = call(add_kernel, [early[0], parts[0], *others], small, [], 1_000_000)
    others = swap_along([mine] * (ring // 2), "gz", 2)
    input_grad, done = call(
        last_cube_kernel,
        [ga, tat, *early],
        [((cube_count, *cube), BF), ((8, 128), F32)],
        [pltpu.VMEM(cube, BF), pltpu.SemaphoreType.DMA((cube_count - 1 + ZD,))],
        2_000_000_000,
        any_out=(0,),
    )
    (mine,) = call(add_kernel, [done, mine, *others], small, [], 1_000_000)
    (own,) = call(
        stack_kernel, [mine, *swap_along([mine] * samples, "sample", 1)], [pieces], [], 1_000_000
    )
    (other,) = swap_along([own] * 2, "gz", 1)
    scale = 1.0 / (cube_count * samples)
    shapes = [((27, C1 * C2), F32), ((27, C2 * C3), F32)]
    scratch = [
        pltpu.VMEM((samples, piece, 128), F32),
        pltpu.VMEM((27, C1 * C2 // 2), F32),
        pltpu.VMEM((27, C2 * C3 // 2), F32),
        pltpu.SemaphoreType.DMA((2,)),
    ]
    totals = call(functools.partial(first_half_kernel, scale), [own], shapes, scratch, 1_000_000, any_out=(0, 1))
    total_a, total_b = call(
        functools.partial(finish_kernel, scale),
        [other, *totals],
        shapes,
        scratch,
        1_000_000,
        any_in=(1, 2),
        any_out=(0, 1),
        aliases={1: 0, 2: 1},
    )
    return input_grad, total_a, total_b


def solution(mesh):
    in_specs = (P("sample", "gz", None, None), P(), P(), P("sample", "gz", None, None))
    out_specs = (P("sample", "gz", None, None), P(), P())
    return jax.shard_map(shards, mesh=mesh, in_specs=in_specs, out_specs=out_specs, check_vma=False)
```

```python
import functools

import jax
import jax.numpy as jnp
from jax import lax
from jax.experimental import pallas as pl
from jax.experimental.pallas import tpu as pltpu
from jax.sharding import PartitionSpec as P

C1 = 32
C2 = 64
C3 = 128
SIDE = 32
ZD = 4
HALO = 3
ROWS_B = C1 * 2 * 28
ROWS_A = C1 // 2 * 28
BF = jnp.bfloat16
F32 = jnp.float32
VMEM = pl.BlockSpec(memory_space=pltpu.VMEM)
ANY = pl.BlockSpec(memory_space=pl.ANY)


def position():
    return lax.axis_index("gz"), lax.axis_size("gz"), lax.axis_index("sample")


def dot(a, b):
    return jnp.dot(a, b, preferred_element_type=F32)


def dot_t(a, b):
    return lax.dot_general(a, b, (((0,), (0,)), ((), ())), preferred_element_type=F32)


def sigmoid(v):
    return pl.reciprocal(1.0 + jnp.exp(-v), approx=True)


def row_picker(variants, stride, planes):
    size = 16 * stride
    shape = (planes * variants * 16, planes * size)
    row = lax.broadcasted_iota(jnp.int32, shape, 0)
    col = lax.broadcasted_iota(jnp.int32, shape, 1)
    want = stride * (row % 16) + row // 16 % variants - 1
    hit = (col == row // (16 * variants) * size + want) & (want >= 0) & (want < size)
    return jnp.where(hit, 1.0, 0.0).astype(BF)


def rows_at(block, before, total):
    rows, lanes = block.shape
    parts = []
    if before:
        parts.append(jnp.zeros((before, lanes), block.dtype))
    parts.append(block)
    if total - before - rows:
        parts.append(jnp.zeros((total - before - rows, lanes), block.dtype))
    return jnp.concatenate(parts, axis=0) if len(parts) > 1 else block


def lanes_below(shape, bound):
    return lax.broadcasted_iota(jnp.int32, shape, 1) < bound


def halves(left, right):
    return jnp.where(lanes_below(left.shape, 64), left, right).astype(BF)


def silu(pre):
    squash = sigmoid(pre)
    act = pre * squash
    return act, (squash + act * (1.0 - squash)).astype(BF)


def windows_a(xs, spans, p, start, offsets=(0, 1, 2)):
    lanes = pl.ds(start if isinstance(start, int) else pl.multiple_of(start, 128), 256)
    columns = []
    for dz in offsets:
        for dy in range(3):
            parts = [xs[:, first + dz : first + dz + planes, p + dy, :, lanes] for first, planes in spans]
            whole = jnp.concatenate(parts, axis=1) if len(parts) > 1 else parts[0]
            columns.append(whole.reshape(whole.shape[0] * whole.shape[1] * 16, 256))
    return jnp.concatenate(columns, axis=1)


def spread_input(target, b, zz, planes, picker):
    rows = 32 * len(planes)
    block = jnp.concatenate(planes, axis=0)
    block = jnp.concatenate([jnp.zeros((rows, 32), BF), block, jnp.zeros((rows, 96), BF)], axis=1)
    moved = dot(picker, block).astype(BF)
    for i in range(len(planes)):
        for v in range(4):
            target[b, zz + i, v] = moved[64 * i + 16 * v : 64 * i + 16 * v + 16]


RANKS = (-3, -1, 0, 2, 1, 3, 4, 6, 5, 7, 8, 10)


def mirror(d, block, tat):
    lane = lax.broadcasted_iota(jnp.int32, (64, 128), 1)
    turned = [block if s == 0 else pltpu.roll(block, 32 * s, 1) for s in range(4)]
    for slot, rank in enumerate(RANKS):
        for half in range(2):
            start = 32 * (rank - 1 - 4 * half)
            keep = (lane >= start) & (lane < start + 96)
            value = jnp.where(keep, turned[(rank - 1) % 4], 0.0).astype(BF)
            tat[768 * d + 64 * slot : 768 * d + 64 * slot + 64, 128 * half : 128 * half + 128] = value


def prepare_kernel(cubes, weight_a, xs, ta, dsl, inner, edge_low, edge_high, wa):
    mask = lanes_below((27, 128), 64)
    for j in range(C1 // 2):
        both = weight_a[:, 128 * j : 128 * j + 128].astype(F32)
        other = pltpu.roll(both, 64, 1)
        wa[pl.ds(2 * j, 27, stride=C1), :] = jnp.where(mask, both, other)
        wa[pl.ds(2 * j + 1, 27, stride=C1), :] = jnp.where(mask, other, both)
    picker = row_picker(4, 2, ZD)
    for b in range(cubes.shape[0]):
        spread_input(xs, b, HALO, [cubes[b, z] for z in range(ZD)], picker)
    for d in range(9):
        block = wa[96 * d : 96 * d + 96]
        for px in range(2):
            ta[256 * d : 256 * d + 256, 128 * px : 128 * px + 128] = halves(
                rows_at(block, 32 * px, 256), rows_at(block, 64 + 32 * px, 256)
            )

    cube_count = cubes.shape[0]
    pre = dot(
        jnp.concatenate(
            [windows_a(xs, ((HALO, 2),), p, 128 * g) for g in range(8) for p in range(2)], axis=0
        ),
        ta[...],
    )
    act, slope = silu(pre)
    slope = slope.reshape(8, 2, cube_count, 2, 16, 256)
    act = act.reshape(8, 2, cube_count, 2, 16, 256)
    for g in range(8):
        for p in range(2):
            dsl[:, 2:4, p, :, 256 * g : 256 * g + 256] = slope[g, p]
        part = act[g, 0] + act[g, 1]
        inner[:, :, :, 128 * g : 128 * g + 128] = part[..., :128] + part[..., 128:]
    for edge, first, offsets in ((edge_low, HALO - 1, (1, 2)), (edge_high, HALO + 2, (0, 1))):
        rows = jnp.concatenate(
            [windows_a(xs, ((first, 1),), p, 128 * g, offsets) for g in range(8) for p in range(2)], axis=0
        )
        edge[...] = dot(rows, ta[768 * offsets[0] : 768 * offsets[0] + 1536])


def prepare_b_kernel(weight_b, tb, wb):
    for i in range(C2):
        wb[pl.ds(i, 27, stride=C2), :] = weight_b[:, 128 * i : 128 * i + 128].astype(F32)
    for d in range(9):
        block = wb[192 * d : 192 * d + 192].astype(BF)
        for e in range(2):
            tb[256 * d : 256 * d + 256, 128 * e : 128 * e + 128] = rows_at(block, 64 * e, 256)


def forward_kernel(own, own_slope, inner, edge_low, edge_high, recv_a, recv_b, ta, tb, cot, xs, dsl, pools, grad_b, pooled):
    del own, own_slope
    where = position()
    cube_count = xs.shape[0]
    even = where[0] % 2 == 0
    picker = row_picker(4, 2, HALO)
    for b in range(cube_count):
        below, above = [], []
        for z in range(HALO):
            far = ZD - HALO + z
            below.append(jnp.where(even, recv_b[b, z].astype(F32), recv_a[b, far].astype(F32)).astype(BF))
            above.append(jnp.where(even, recv_a[b, z].astype(F32), recv_b[b, z].astype(F32)).astype(BF))
        spread_input(xs, b, 0, below, picker)
        spread_input(xs, b, HALO + ZD, above, picker)

    low = jnp.where(where[0] == 0, 0.0, 0.125)
    high = jnp.where(where[0] == where[1] - 1, 0.0, 0.125)

    def groups(i, carry):
        def stack(spans, offsets=(0, 1, 2)):
            return jnp.concatenate(
                [windows_a(xs, spans, p, 512 * i + 128 * j, offsets) for j in range(4) for p in range(2)], axis=0
            )

        act, slope = silu(dot(stack(((0, 2), (HALO + ZD - 1, 2))), ta[...]))
        slope = slope.reshape(4, 2, cube_count, 4, 16, 256)
        act = act.reshape(4, 2, cube_count, 4, 16, 256)
        rows = cube_count * 128
        here = pl.ds(pl.multiple_of(rows * i, rows), rows)
        sides = []
        for edge, first, dz in ((edge_low, HALO - 1, 0), (edge_high, HALO + 2, 2)):
            pre = edge[here] + dot(stack(((first, 1),), (dz,)), ta[768 * dz : 768 * dz + 768])
            edge_act, edge_slope = silu(pre)
            edge_act = edge_act.reshape(4, 2, cube_count, 16, 256)
            sides.append((edge_act, edge_slope.reshape(4, 2, cube_count, 16, 256)))
        for j in range(4):
            for p in range(2):
                to = pl.ds(pl.multiple_of(1024 * i + 256 * j, 256), 256)
                dsl[:, 0, p, :, to] = slope[j, p][:, 1]
                dsl[:, 1, p, :, to] = sides[0][1][j, p]
                dsl[:, 4, p, :, to] = sides[1][1][j, p]
                dsl[:, 5, p, :, to] = slope[j, p][:, 2]
            part = act[j, 0] + act[j, 1]
            part = part[..., :128] + part[..., 128:]
            ends = [side[0][j, 0] + side[0][j, 1] for side in sides]
            ends = [end[..., :128] + end[..., 128:] for end in ends]
            out = pl.ds(pl.multiple_of(512 * i + 128 * j, 128), 128)
            pooled[:, 0, :, out] = ((part[:, 0] + part[:, 1]) * low).astype(BF)
            pooled[:, 1, :, out] = ((ends[0] + inner[:, 0, :, out]) * 0.125).astype(BF)
            pooled[:, 2, :, out] = ((ends[1] + inner[:, 1, :, out]) * 0.125).astype(BF)
            pooled[:, 3, :, out] = ((part[:, 2] + part[:, 3]) * high).astype(BF)
        return carry

    lax.fori_loop(0, 2, groups, 0)

    shifter = row_picker(3, 1, 4)
    for b in range(cube_count):
        block = pooled[b].reshape(64, 1024)
        block = jnp.concatenate([jnp.zeros((64, 64), BF), block, jnp.zeros((64, 64), BF)], axis=1)
        moved = dot(shifter, block).astype(BF)
        for z in range(4):
            for v in range(3):
                pools[b, z, v] = moved[48 * z + 16 * v : 48 * z + 16 * v + 16]

    rows_b = cube_count * 2 * 16
    columns = []
    for dz in range(3):
        for dy in range(3):
            columns.append(
                jnp.concatenate(
                    [
                        pools[:, dz : dz + 2, dy, :, 128 * g : 128 * g + 256].reshape(rows_b, 256)
                        for g in range(8)
                    ],
                    axis=0,
                )
            )
    pre_b = dot(jnp.concatenate(columns, axis=1), tb[...])
    squash = sigmoid(pre_b)
    slope_b = squash + pre_b * squash * (1.0 - squash)
    row = lax.broadcasted_iota(jnp.int32, (16, 8), 0)
    twice = jnp.where(row // 2 == lax.broadcasted_iota(jnp.int32, (16, 8), 1), 0.125, 0.0).astype(BF)
    ups = [dot(twice, cot[b, 0]) for b in range(cube_count)]
    for g in range(8):
        part = slope_b[rows_b * g : rows_b * g + rows_b].reshape(cube_count, 2, 16, 256)
        up = jnp.stack([ups[b][:, 128 * g : 128 * g + 128] for b in range(cube_count)])
        for z in range(2):
            for e in range(2):
                at = 256 * g + 128 * e
                grad_b[:, z, :, at : at + 128] = (up * part[:, z, :, 128 * e : 128 * e + 128]).astype(BF)


def spread_grad(target, b, zz, pair, shifter):
    moved = dot(shifter, pair.reshape(32, 2048)).astype(BF)
    for i in range(2):
        for v in range(3):
            target[b, zz + i, v, :, 128:2176] = moved[48 * i + 16 * v : 48 * i + 16 * v + 16]
            target[b, zz + i, v, :, :128] = jnp.zeros((16, 128), BF)
            target[b, zz + i, v, :, 2176:] = jnp.zeros((16, 128), BF)


def terms_b_kernel(pools, grad_b, wa, wb, terms, gs, tat, tbt, back):
    cube_count = grad_b.shape[0]
    shifter = row_picker(3, 1, 2)
    for b in range(cube_count):
        spread_grad(gs, b, 2, grad_b[b], shifter)
    for d in range(9):
        mirror(8 - d, rows_at(wa[96 * d : 96 * d + 96], 0, 128).T[:64], tat)
        block = wb[192 * d : 192 * d + 192]
        turned = []
        for dx in (2, 1, 0):
            part = block[64 * dx : 64 * dx + 64]
            turned.append(jnp.concatenate([part, part], axis=0).T)
        block = jnp.concatenate(turned, axis=0)
        to = 768 * (8 - d)
        for e in range(2):
            tbt[to : to + 768, 128 * e : 128 * e + 128] = halves(
                rows_at(block, 256 * e, 768), rows_at(block, 256 * e + 128, 768)
            )
    rows_b = cube_count * 2 * 16
    grads = jnp.concatenate(
        [grad_b[:, :, :, 256 * g : 256 * g + 256].reshape(rows_b, 256) for g in range(8)], axis=0
    )
    terms[pl.ds(27, C2, stride=28), :] = jnp.zeros((C2, 128), F32)
    for dz in range(3):
        for dy in range(3):
            windows = jnp.concatenate(
                [
                    pools[:, dz : dz + 2, dy, :, 128 * g : 128 * g + 256].reshape(rows_b, 256)
                    for g in range(8)
                ],
                axis=0,
            )
            full = dot_t(windows, grads)
            for dx in range(3):
                term = full[64 * dx : 64 * dx + 64, :128] + full[64 * dx + 64 : 64 * dx + 128, 128:]
                terms[pl.ds(9 * dz + 3 * dy + dx, C2, stride=28), :] = term

    sources = windows_b(gs, ((2, 2),))
    given = [
        dot(sources, tbt[2304 * dz : 2304 * dz + 2304]).reshape(4, cube_count, 2, 16, 256) for dz in range(3)
    ]
    back[:, :, 0] = given[2][:, :, 0]
    back[:, :, 1] = given[1][:, :, 0] + given[2][:, :, 1]
    back[:, :, 2] = given[0][:, :, 0] + given[1][:, :, 1]
    back[:, :, 3] = given[0][:, :, 1]


def windows_b(gs, spans):
    columns = []
    for dy in range(3):
        stacks = []
        for q in range(4):
            parts = [gs[:, first : first + planes, dy, :, 512 * q : 512 * q + 768] for first, planes in spans]
            whole = jnp.concatenate(parts, axis=1) if len(parts) > 1 else parts[0]
            stacks.append(whole.reshape(whole.shape[0] * whole.shape[1] * 16, 768))
        columns.append(jnp.concatenate(stacks, axis=0))
    return jnp.concatenate(columns, axis=1)


def tree(parts):
    while len(parts) > 1:
        parts = [left + right for left, right in zip(parts[::2], parts[1::2])]
    return parts[0]


def scatter_kernel(keep, recv, *outs):
    where = position()
    for k, out in enumerate(outs):
        part = where[2] ^ k
        out[...] = (keep[part].astype(F32) + recv[part].astype(F32)).astype(BF)


def add_kernel(after, *refs):
    del after
    parts, out = refs[:-1], refs[-1]
    out[...] = tree([part[...].astype(F32) for part in parts]).astype(BF)


def stack_kernel(*refs):
    where = position()
    parts, out = refs[:-1], refs[-1]
    for k, part in enumerate(parts):
        out[where[2] ^ k] = part[...]


def lay_out(pieces, scale, out_a, out_b, whole):
    whole[...] = pieces[...].astype(F32) * scale
    count = pieces.shape[0]
    for width, base, out in ((C2, 0, out_b), (C1 // 2, ROWS_B // (2 * count), out_a)):
        each = width // (2 * count)
        for i in range(width // 2):
            start = base + 28 * (i % each)
            out[:, 128 * i : 128 * i + 128] = whole[i // each, start : start + 27]


def send_half(core, pieces, scale, outs, halves_out, whole, sems):
    lay_out(pieces, scale, *halves_out, whole)
    copies = []
    for i, (out, half) in enumerate(zip(outs, halves_out)):
        width = half.shape[1]
        copies.append(
            pltpu.make_async_copy(half, out.at[:, pl.ds(pl.multiple_of(core * width, width), width)], sems.at[i])
        )
        copies[-1].start()
    for copy in copies:
        copy.wait()


def first_half_kernel(scale, pieces, out_a, out_b, whole, half_a, half_b, sems):
    send_half(position()[0] % 2, pieces, scale, (out_a, out_b), (half_a, half_b), whole, sems)


def finish_kernel(scale, pieces, before_a, before_b, out_a, out_b, whole, half_a, half_b, sems):
    del before_a, before_b
    send_half(1 - position()[0] % 2, pieces, scale, (out_a, out_b), (half_a, half_b), whole, sems)


def backward_kernel(own, recv_a, recv_b, tbt, dsl, xs, terms_b, back, ga, keep, send, gs, gpool, acc, term, terms):
    del own
    where = position()
    cube_count = recv_a.shape[0]
    even = where[0] % 2 == 0
    shifter = row_picker(3, 1, 2)
    for b in range(cube_count):
        from_a, from_b = recv_a[b].astype(F32), recv_b[b].astype(F32)
        spread_grad(gs, b, 0, jnp.where(even, from_b, from_a).astype(BF), shifter)
        spread_grad(gs, b, 4, jnp.where(even, from_a, from_b).astype(BF), shifter)

    low = jnp.where(where[0] == 0, 0.0, 0.125)
    high = jnp.where(where[0] == where[1] - 1, 0.0, 0.125)
    parts = [
        dot(windows_b(gs, spans), tbt[2304 * dz : 2304 * dz + 2304]).reshape(4, cube_count, 2, 16, 256)
        for dz, spans in enumerate((((0, 2),), ((1, 1), (4, 1)), ((4, 2),)))
    ]
    extra = (
        parts[0][:, :, 0] + parts[1][:, :, 0],
        parts[0][:, :, 1],
        parts[2][:, :, 0],
        parts[1][:, :, 1] + parts[2][:, :, 1],
    )
    for z in range(4):
        scale = low if z == 0 else high if z == 3 else 0.125
        total = (back[:, :, z] + extra[z]) * scale
        for q in range(4):
            gpool[:, z, :, 256 * q : 256 * q + 256] = total[q]

    ga[:, :, :, :, :128] = jnp.zeros((cube_count, 6, 4, 16, 128), BF)
    ga[:, :, :, :, 2176:] = jnp.zeros((cube_count, 6, 4, 16, 128), BF)
    rows_a = cube_count * 6 * 16
    own_rows = cube_count * 4 * 16
    place = lax.broadcasted_iota(jnp.int32, (rows_a, 128), 0) % 16

    def one_group(g):
        lanes = pl.ds(pl.multiple_of(128 * g, 128), 128)
        up = gpool[:, :, :, lanes]
        up = jnp.concatenate(
            [up[:, 0:1], up[:, 1:2], up[:, 1:2], up[:, 2:3], up[:, 2:3], up[:, 3:4]], axis=1
        ).reshape(rows_a, 128)
        sides = []
        for p in range(2):
            pair = []
            for px in range(2):
                at = pl.ds(pl.multiple_of(256 * g + 128 * px, 128), 128)
                grad = up * dsl[:, :, p, :, at].astype(F32).reshape(rows_a, 128)
                to = pl.ds(pl.multiple_of(256 * g + 128 * px + 128, 128), 128)
                kept = grad.astype(BF).reshape(cube_count, 6, 16, 128)
                ga[:, :, 1 + p, :, to] = kept
                pair.append(kept[:, 1:5].reshape(own_rows, 128))
                if p == 1:
                    moved = jnp.where(place == 0, 0.0, pltpu.roll(grad, 1, 0))
                else:
                    moved = jnp.where(place == 15, 0.0, pltpu.roll(grad, rows_a - 1, 0))
                ga[:, :, 0 if p else 3, :, to] = moved.astype(BF).reshape(cube_count, 6, 16, 128)
            sides.append(jnp.concatenate(pair, axis=1))
        return sides, [windows_a(xs, ((HALO - 1, ZD),), p, 128 * g) for p in range(2)]

    def groups(i, carry):
        first, second = one_group(2 * i), one_group(2 * i + 1)
        grads = jnp.concatenate(first[0] + second[0], axis=0)
        acc[...] += dot_t(jnp.concatenate(first[1] + second[1], axis=0), grads)
        return carry

    acc[...] = jnp.zeros_like(acc)
    lax.fori_loop(0, 4, groups, 0)

    terms[pl.ds(27, C1 // 2, stride=28), :] = jnp.zeros((C1 // 2, 128), F32)
    mask = lanes_below((32, 128), 64)
    for d in range(9):
        full = acc[256 * d : 256 * d + 256]
        for dx in range(3):
            left = full[32 * dx : 32 * dx + 32, :128] + full[32 * dx + 32 : 32 * dx + 64, 128:]
            right = full[32 * dx + 64 : 32 * dx + 96, :128] + full[32 * dx + 96 : 32 * dx + 128, 128:]
            merged = jnp.where(mask, left, right)
            slot = (3 * d + dx) % 4
            term[slot] = merged + pltpu.roll(merged, 64, 1)
            evens = term[slot, pl.ds(0, C1 // 2, stride=2), :]
            odds = term[slot, pl.ds(1, C1 // 2, stride=2), :]
            terms[pl.ds(3 * d + dx, C1 // 2, stride=28), :] = jnp.where(mask[:16], evens, odds)
    low = where[0] % 2 == 0
    count = keep.shape[0]
    for part in range(count):
        sides = []
        for core in range(2):
            at = core * count + part
            rows_b, rows_a = ROWS_B // (2 * count), ROWS_A // (2 * count)
            sides.append(
                jnp.concatenate(
                    [terms_b[rows_b * at : rows_b * at + rows_b], terms[rows_a * at : rows_a * at + rows_a]], axis=0
                )
            )
        keep[part] = jnp.where(low, sides[0], sides[1]).astype(BF)
        send[part] = jnp.where(low, sides[1], sides[0]).astype(BF)


def one_cube(b, ga, tat, out, landed):
    rows = ZD * 16
    sides = []
    for p in range(2):
        columns = []
        for dz in range(3):
            for dy in range(3):
                columns.append(
                    jnp.concatenate(
                        [ga[b, dz : dz + ZD, p + dy, :, 512 * q : 512 * q + 768].reshape(rows, 768) for q in range(4)],
                        axis=0,
                    )
                )
        sides.append(jnp.concatenate(columns, axis=1))
    both = dot(jnp.concatenate(sides, axis=0), tat[...]).astype(BF).reshape(2, 4, ZD, 16, 256)
    row = lax.broadcasted_iota(jnp.int32, (32, 32), 0)
    col = lax.broadcasted_iota(jnp.int32, (32, 32), 1)
    mixer = jnp.where(col == row // 2 + 16 * (row % 2), 1.0, 0.0).astype(BF)
    for z in range(ZD):
        for q in range(4):
            pair = jnp.concatenate([both[0, q, z], both[1, q, z]], axis=0)
            out[z, :, 256 * q : 256 * q + 256] = dot(mixer, pair).astype(BF)
        if landed is not None:
            landed(z)


def early_cube_kernel(b):
    def kernel(ga, tat, out):
        one_cube(b, ga, tat, out, None)

    return kernel


def last_cube_kernel(ga, tat, *rest):
    early, (out, token, block, sems) = rest[:-4], rest[-4:]
    last = len(early)
    copies = [pltpu.make_async_copy(cube, out.at[b], sems.at[b]) for b, cube in enumerate(early)]
    for copy in copies:
        copy.start()

    def landed(z):
        copy = pltpu.make_async_copy(block.at[z], out.at[last, z], sems.at[last + z])
        copy.start()
        copies.append(copy)

    one_cube(last, ga, tat, block, landed)
    token[...] = jnp.zeros_like(token)
    for copy in copies:
        copy.wait()


def call(kernel, args, outs, scratch, flops, any_in=(), any_out=(), aliases=None):
    specs = [ANY if i in any_in else VMEM for i in range(len(args))]
    return pl.pallas_call(
        kernel,
        out_shape=[jax.ShapeDtypeStruct(shape, dtype) for shape, dtype in outs],
        in_specs=specs,
        out_specs=[ANY if i in any_out else VMEM for i in range(len(outs))],
        scratch_shapes=scratch,
        input_output_aliases=aliases or {},
        compiler_params=pltpu.CompilerParams(vmem_limit_bytes=28 * 1024 * 1024),
        cost_estimate=pl.CostEstimate(flops=flops, bytes_accessed=1_000_000, transcendentals=0),
    )(*args)


def swap(first, second, count):
    pairs_a = [(i, i ^ 1) for i in range(count)]
    pairs_b = [(i, ((i + 1) ^ 1) - 1) for i in range(1, count - 1)]
    return lax.ppermute(first, "gz", pairs_a), lax.ppermute(second, "gz", pairs_b)


def swap_along(parts, axis, step):
    count = lax.axis_size(axis)
    return [
        lax.ppermute(part, axis, [(i, i ^ (k * step)) for i in range(count)]) for k, part in enumerate(parts) if k
    ]


def shards(cubes, weight_a, weight_b, cotangent):
    cube_count = cubes.shape[0]
    ring = lax.axis_size("gz")
    samples = lax.axis_size("sample")
    outer = lax.dynamic_slice_in_dim(cubes, lax.axis_index("gz") % 2, HALO, axis=1)
    recv_a, recv_b = swap(cubes, outer, ring)

    own_xs, ta, own_slope, inner, edge_low, edge_high, wa = call(
        prepare_kernel,
        [cubes, weight_a],
        [
            ((cube_count, ZD + 2 * HALO, 4, 16, 1152), BF),
            ((2304, 256), BF),
            ((cube_count, 6, 2, 16, 2048), BF),
            ((cube_count, 2, 16, 1024), F32),
            ((cube_count * 256, 256), F32),
            ((cube_count * 256, 256), F32),
            ((32 * C1, 128), F32),
        ],
        [],
        1_000_000_000,
    )
    tb, wb = call(
        prepare_b_kernel, [weight_b], [((2304, 256), BF), ((32 * C2, 128), F32)], [], 500_000_000
    )
    xs, dsl, pools, grad_b = call(
        forward_kernel,
        [own_xs, own_slope, inner, edge_low, edge_high, recv_a, recv_b, ta, tb, cotangent],
        [
            ((cube_count, ZD + 2 * HALO, 4, 16, 1152), BF),
            ((cube_count, 6, 2, 16, 2048), BF),
            ((cube_count, 4, 3, 16, 1152), BF),
            ((cube_count, 2, 16, 2048), BF),
        ],
        [pltpu.VMEM((cube_count, 4, 16, 1024), BF)],
        8_000_000_000,
        aliases={0: 0, 1: 1},
    )
    back_a, back_b = swap(grad_b, grad_b, ring)
    spread = ((cube_count, 6, 3, 16, 2304), BF)
    wide = ((6912, 256), BF)
    terms_b, own_gs, tat, tbt, back = call(
        terms_b_kernel,
        [pools, grad_b, wa, wb],
        [((ROWS_B, 128), F32), spread, wide, wide, ((4, cube_count, 4, 16, 256), F32)],
        [],
        1_000_000_000,
    )
    piece = (ROWS_A + ROWS_B) // (2 * samples)
    pieces = ((samples, piece, 128), BF)
    ga, keep, send, _ = call(
        backward_kernel,
        [own_gs, back_a, back_b, tbt, dsl, xs, terms_b, back],
        [((cube_count, 6, 4, 16, 2304), BF), pieces, pieces, spread],
        [
            pltpu.VMEM((cube_count, 4, 16, 1024), F32),
            pltpu.VMEM((2304, 256), F32),
            pltpu.VMEM((4, C1, 128), F32),
            pltpu.VMEM((ROWS_A, 128), F32),
        ],
        6_000_000_000,
        aliases={0: 3},
    )
    small = [((piece, 128), BF)]
    (recv,) = swap_along([send] * 2, "gz", 1)
    parts = call(scatter_kernel, [keep, recv], small * samples, [], 1_000_000)
    others = swap_along(parts, "sample", 1)
    cube = (ZD, SIDE, SIDE * C1)
    early = [
        call(early_cube_kernel(b), [ga, tat], [(cube, BF)], [], 2_000_000_000)[0] for b in range(cube_count - 1)
    ]
    (mine,) = call(add_kernel, [early[0], parts[0], *others], small, [], 1_000_000)
    others = swap_along([mine] * (ring // 2), "gz", 2)
    input_grad, done = call(
        last_cube_kernel,
        [ga, tat, *early],
        [((cube_count, *cube), BF), ((8, 128), F32)],
        [pltpu.VMEM(cube, BF), pltpu.SemaphoreType.DMA((cube_count - 1 + ZD,))],
        2_000_000_000,
        any_out=(0,),
    )
    (mine,) = call(add_kernel, [done, mine, *others], small, [], 1_000_000)
    (own,) = call(
        stack_kernel, [mine, *swap_along([mine] * samples, "sample", 1)], [pieces], [], 1_000_000
    )
    (other,) = swap_along([own] * 2, "gz", 1)
    scale = 1.0 / (cube_count * samples)
    shapes = [((27, C1 * C2), F32), ((27, C2 * C3), F32)]
    scratch = [
        pltpu.VMEM((samples, piece, 128), F32),
        pltpu.VMEM((27, C1 * C2 // 2), F32),
        pltpu.VMEM((27, C2 * C3 // 2), F32),
        pltpu.SemaphoreType.DMA((2,)),
    ]
    totals = call(functools.partial(first_half_kernel, scale), [own], shapes, scratch, 1_000_000, any_out=(0, 1))
    total_a, total_b = call(
        functools.partial(finish_kernel, scale),
        [other, *totals],
        shapes,
        scratch,
        1_000_000,
        any_in=(1, 2),
        any_out=(0, 1),
        aliases={1: 0, 2: 1},
    )
    return input_grad, total_a, total_b


def solution(mesh):
    in_specs = (P("sample", "gz", None, None), P(), P(), P("sample", "gz", None, None))
    out_specs = (P("sample", "gz", None, None), P(), P())
    return jax.shard_map(shards, mesh=mesh, in_specs=in_specs, out_specs=out_specs, check_vma=False)
```
